32 devices in a mesh: rep: 4 (over y, x), shard: 8 (over z, core).
Axes of the slice: x: 2, y: 2, z: 4, core: 2. Of those that a mesh axis runs over, the one named last changes fastest.
Arguments:
- tokens: bfloat16 [8, 512, 2560], P('shard', 'rep'), may hold values from -6 to 6
- cotangent: bfloat16 [8, 512, 2560], P('shard', 'rep'), may hold values from -6 to 6
- doc_lengths: int32 [8, 4], P('shard'), may hold values from 1 to 509, as said below
- gain_attn: bfloat16 [2560], P('shard'), may hold values from 0.25 to 1.75
- query_down: bfloat16 [2560, 768], P('shard'), may hold values from -0.125 to 0.125
- gain_query: bfloat16 [768], P('shard'), may hold values from 0.25 to 1.75
- query_up: bfloat16 [768, 3840], P('shard'), may hold values from -0.3125 to 0.3125
- latent_down: bfloat16 [2560, 288], P('shard'), may hold values from -0.125 to 0.125
- gain_latent: bfloat16 [256], P('shard'), may hold values from 0.25 to 1.75
- latent_up: bfloat16 [256, 5120], P('shard'), may hold values from -0.375 to 0.375
- attn_out: bfloat16 [2560, 2560], P('shard'), may hold values from -6 to 6
- gain_ffn: bfloat16 [2560], P('shard'), may hold values from 0.25 to 1.75
- w_gate: bfloat16 [2560, 6400], P('shard'), may hold values from -0.125 to 0.125
- w_up: bfloat16 [2560, 6400], P('shard'), may hold values from -0.125 to 0.125
- w_down: bfloat16 [6400, 2560], P('shard'), may hold values from -0.4375 to 0.4375
Outputs:
- layer_out: bfloat16 [8, 512, 2560], P('shard', 'rep')
- tokens_grad: bfloat16 [8, 512, 2560], P('shard', 'rep')
- gain_attn_grad: float32 [2560], P('shard')
- query_down_grad: float32 [2560, 768], P('shard')
- gain_query_grad: float32 [768], P('shard')
- query_up_grad: float32 [768, 3840], P('shard')
- latent_down_grad: float32 [2560, 288], P('shard')
- gain_latent_grad: float32 [256], P('shard')
- latent_up_grad: float32 [256, 5120], P('shard')
- attn_out_grad: float32 [2560, 2560], P('shard')
- gain_ffn_grad: float32 [2560], P('shard')
- w_gate_grad: float32 [2560, 6400], P('shard')
- w_up_grad: float32 [2560, 6400], P('shard')
- w_down_grad: float32 [6400, 2560], P('shard')
The draws below stay inside these ranges and needn't reach their ends.
Inputs may be any that keep to these rules, and one draw needn't show every extreme that they name: `doc_lengths`: each row holds the lengths of the 4 documents of one sequence, in order, and sums to 512; the second document begins within the sequence's first 128 tokens and ends within its last 128; in some sequence every document but the second has length 1.
All inputs are finite; a program needn't handle non-finite values.
Results may differ from the reference program's by a relative error of at most 0.022.
Values may be sent and summed in bfloat16 or wider, within the bound.
A program may use at most 640 MiB of HBM per device.

```python
import math
import jax
import jax.numpy as jnp
from jax import lax

D = 2560
QR = 768
KR = 256
H = 40
ND = 64
RD = 32
VD = 64
FF = 6400
TOK_DEV = 128
DOCS = 4
LENGTH = 512
SEQS = 8


def draw_doc_lengths(key, part):
    key = jax.random.fold_in(key, 7)
    key_head, key_tail, key_pick = jax.random.split(key, 3)
    leading = jax.random.randint(key_head, (SEQS, 1), 1, TOK_DEV, dtype=jnp.int32)
    trailing = jax.random.randint(key_tail, (SEQS, DOCS - 2), 1, TOK_DEV // (DOCS - 2), dtype=jnp.int32)
    picked = jax.random.randint(key_pick, (), 0, SEQS, dtype=jnp.int32)
    chosen_row = (jnp.arange(SEQS, dtype=jnp.int32) == picked)[:, None]
    leading = jnp.where(chosen_row, jnp.ones_like(leading), leading).astype(jnp.int32)
    trailing = jnp.where(chosen_row, jnp.ones_like(trailing), trailing).astype(jnp.int32)
    middle = LENGTH - leading - jnp.sum(trailing, axis=1, keepdims=True)
    return jnp.concatenate([leading, middle, trailing], axis=1).astype(jnp.int32)


def level_of(key, shape, cuts, least, high):
    def one(dim, blocks):
        draws = jax.random.uniform(jax.random.fold_in(jax.random.fold_in(key, 6), dim), (blocks,), jnp.float32, least / len(cuts), high / len(cuts))
        return jnp.repeat(jnp.exp(draws), shape[dim] // blocks).reshape((-1,) + (1,) * (len(shape) - dim - 1))

    loudness = one(*cuts[0])
    for cut in cuts[1:]:
        loudness = loudness * one(*cut)
    return loudness


def noise(own_key, dims, spread, bound, cuts=(), kind=jnp.bfloat16):
    entries = spread * jax.random.normal(own_key, dims, jnp.float32)
    if cuts:
        entries = entries * level_of(own_key, dims, cuts, -0.22, 0.18)
    return jnp.clip(entries, -bound, bound).astype(kind)


def setup_inputs(seed: int = 0) -> dict:
    seeds = jax.random.split(jax.random.key(seed), 16)
    tokens = noise(seeds[0], (SEQS, LENGTH, D), 1.0, 6.0, ((0, 8), (1, 4)))
    cotangent = noise(seeds[1], (SEQS, LENGTH, D), 1.0, 6.0, ((0, 8), (1, 4)))
    doc_lengths = draw_doc_lengths(jax.random.fold_in(seeds[15], 71), 0)
    gain_attn = jnp.clip(1.0 + 0.15 * jax.random.normal(seeds[3], (D,), jnp.float32), 0.25, 1.75).astype(jnp.bfloat16)
    query_down = noise(seeds[4], (D, QR), D ** -0.5, 0.125, ((0, 8),))
    gain_query = jnp.clip(1.0 + 0.15 * jax.random.normal(seeds[5], (QR,), jnp.float32), 0.25, 1.75).astype(jnp.bfloat16)
    query_up = noise(seeds[6], (QR, H * (ND + RD)), (QR // 2) ** -0.5, 0.3125, ((0, 8),))
    latent_down = noise(seeds[7], (D, KR + RD), D ** -0.5, 0.125, ((0, 8),))
    gain_latent = jnp.clip(1.0 + 0.15 * jax.random.normal(seeds[8], (KR,), jnp.float32), 0.25, 1.75).astype(jnp.bfloat16)
    latent_up = noise(seeds[9], (KR, H * (ND + VD)), KR ** -0.5, 0.375, ((0, 8),))
    attn_out = noise(seeds[10], (H * VD, D), 1 ** -0.5, 6.0, ((0, 8),))
    gain_ffn = jnp.clip(1.0 + 0.15 * jax.random.normal(seeds[11], (D,), jnp.float32), 0.25, 1.75).astype(jnp.bfloat16)
    w_gate = noise(seeds[12], (D, FF), D ** -0.5, 0.125, ((0, 8),))
    w_up = noise(seeds[13], (D, FF), D ** -0.5, 0.125, ((0, 8),))
    w_down = noise(seeds[14], (FF, D), (FF // 32) ** -0.5, 0.4375, ((0, 8),))
    return dict(tokens=tokens, cotangent=cotangent, doc_lengths=doc_lengths, gain_attn=gain_attn, query_down=query_down, gain_query=gain_query, query_up=query_up, latent_down=latent_down, gain_latent=gain_latent, latent_up=latent_up, attn_out=attn_out, gain_ffn=gain_ffn, w_gate=w_gate, w_up=w_up, w_down=w_down)


epsilon = 1e-05
residual_scale = 1.4 / math.sqrt(62.0)
rope_base = 10000.0
masked_score = -1e+30

@jax.custom_vjp
def low(v):
    return lax.optimization_barrier(v.astype(jnp.bfloat16)).astype(jnp.float32)

@jax.custom_vjp
def low_back(v):
    return v

def low_keep(v):
    return (low(v), None)

def low_pass(kept, grad):
    return (grad,)

def back_keep(v):
    return (v, None)

def back_low(kept, grad):
    return (low(grad),)
low.defvjp(low_keep, low_pass)
low_back.defvjp(back_keep, back_low)

def rms_scale(values, gain):
    return values * lax.rsqrt(lax.optimization_barrier(jnp.mean(values * values, axis=-1, keepdims=True)) + epsilon) * gain

def rotate(values, cos_part, sin_part):
    midpoint = values.shape[-1] // 2
    former = values[..., :midpoint]
    latter = values[..., midpoint:]
    return jnp.concatenate([former * cos_part - latter * sin_part, latter * cos_part + former * sin_part], axis=-1)

def segment_of(lengths, positions):
    doc_ends = jnp.cumsum(lengths).astype(jnp.int32)
    doc_starts = (doc_ends - lengths).astype(jnp.int32)
    segment = lax.optimization_barrier(jnp.sum((positions[:, None] >= doc_ends[None, :]).astype(jnp.int32), axis=1)).astype(jnp.int32)
    chosen = segment[:, None] == jnp.arange(lengths.shape[0], dtype=jnp.int32)[None, :]
    offsets = positions - lax.optimization_barrier(jnp.sum(jnp.where(chosen, doc_starts[None, :], 0), axis=1)).astype(jnp.int32)
    return (segment, offsets)

def rope_tables(offsets, rope_width):
    exponents = jnp.arange(0, rope_width, 2, dtype=jnp.float32) / rope_width
    angles = offsets.astype(jnp.float32)[:, None] * (rope_base ** (-exponents))[None, :]
    return (jnp.cos(angles), jnp.sin(angles))

def product(leading, trailing):
    return jnp.dot(leading, trailing, precision=lax.Precision.HIGHEST, preferred_element_type=jnp.float32)

def reference(tokens, cotangent, doc_lengths, gain_attn, query_down, gain_query, query_up, latent_down, gain_latent, latent_up, attn_out, gain_ffn, w_gate, w_up, w_down):
    head_dim = ND + RD
    softmax_scale = head_dim ** (-0.5)

    def layer(inputs, g_attn, q_down, g_query, q_up, l_down, g_latent, l_up, a_out, g_ffn, gate_mat, up_mat, down_mat):

        def one_sequence(carry, pair):
            seq_in, seq_lengths = pair
            positions = jnp.arange(LENGTH, dtype=jnp.int32)
            segment, offsets = segment_of(seq_lengths, positions)
            allowed = (segment[:, None] == segment[None, :]) & (positions[None, :] <= positions[:, None])
            cos_part, sin_part = rope_tables(offsets, RD)
            normed = low(rms_scale(seq_in, g_attn))
            query_lat = low_back(product(normed, q_down))
            query_norm = low(rms_scale(query_lat, g_query))
            query_full = low_back(product(query_norm, q_up)).reshape(LENGTH, H, head_dim)
            query_used = low(jnp.concatenate([query_full[..., :ND], rotate(query_full[..., ND:], cos_part[:, None, :], sin_part[:, None, :])], axis=-1))
            latent_full = low_back(product(normed, l_down))
            latent_norm = low(rms_scale(latent_full[:, :KR], g_latent))
            key_rope = low(rotate(latent_full[:, KR:], cos_part, sin_part))
            keyvals = low(low_back(product(latent_norm, l_up))).reshape(LENGTH, H, ND + VD)

            def one_head(pieces):
                query_head, keyval_head = pieces
                keys = jnp.concatenate([keyval_head[:, :ND], key_rope], axis=-1)
                scores = low_back(product(query_head, keys.T) * softmax_scale)
                scores = jnp.where(allowed, scores, masked_score)
                row_max = lax.optimization_barrier(jnp.max(scores, axis=-1, keepdims=True))
                exp_scores = jnp.exp(scores - row_max)
                probs = low(exp_scores / lax.optimization_barrier(jnp.sum(exp_scores, axis=-1, keepdims=True)))
                return product(probs, keyval_head[:, ND:])
            mixed_heads = lax.map(jax.checkpoint(one_head), (query_used.transpose(1, 0, 2), keyvals.transpose(1, 0, 2)))
            mixed = low(low_back(mixed_heads.transpose(1, 0, 2).reshape(LENGTH, H * VD)))
            branch = low_back(product(mixed, a_out))
            residual = seq_in + residual_scale * branch
            normed_ffn = low(rms_scale(residual, g_ffn))
            gate_vals = low_back(product(normed_ffn, gate_mat))
            up_vals = low_back(product(normed_ffn, up_mat))
            hidden = low(jax.nn.silu(gate_vals) * up_vals)
            result = residual + residual_scale * low_back(product(hidden, down_mat))
            return (carry, result)
        start_carry = jnp.zeros((), jnp.float32)
        final_carry, stacked = lax.scan(jax.checkpoint(one_sequence), start_carry, (inputs, doc_lengths))
        return stacked
    params = tuple((matrix.astype(jnp.float32) for matrix in (gain_attn, query_down, gain_query, query_up, latent_down, gain_latent, latent_up, attn_out, gain_ffn, w_gate, w_up, w_down)))
    outputs, pullback = jax.vjp(layer, tokens.astype(jnp.float32), *params)
    grads = pullback(cotangent.astype(jnp.float32))
    return (outputs.astype(jnp.bfloat16), grads[0].astype(jnp.bfloat16), grads[1], grads[2], grads[3], grads[4], grads[5], grads[6], grads[7], grads[8], grads[9], grads[10], grads[11], grads[12])
```

```python
import functools
import math

import jax
import jax.numpy as jnp
from jax import lax
from jax.experimental import pallas as pl
from jax.experimental.pallas import tpu as pltpu
from jax.sharding import PartitionSpec as P

KR = 256
H = 40
ND = 64
RD = 32
VD = 64
FF = 6400


epsilon = 1e-05
residual_scale = 1.4 / math.sqrt(62.0)
rope_base = 10000.0
masked_score = -1e30


def rms_scale(values, gain):
    return values * lax.rsqrt(jnp.mean(values * values, axis=-1, keepdims=True) + epsilon) * gain


def rotate(values, cos_part, sin_part):
    midpoint = values.shape[-1] // 2
    former = values[..., :midpoint]
    latter = values[..., midpoint:]
    return jnp.concatenate(
        [former * cos_part - latter * sin_part, latter * cos_part + former * sin_part], axis=-1
    )


def segment_of(lengths, positions):
    doc_ends = jnp.cumsum(lengths)
    doc_starts = doc_ends - lengths
    segment = jnp.sum((positions[:, None] >= doc_ends[None, :]).astype(jnp.int32), axis=1)
    chosen = segment[:, None] == jnp.arange(lengths.shape[0], dtype=jnp.int32)[None, :]
    offsets = positions - jnp.sum(jnp.where(chosen, doc_starts[None, :], 0), axis=1)
    return (segment, offsets)


def rope_tables(offsets, rope_width):
    exponents = jnp.arange(0, rope_width, 2, dtype=jnp.float32) / rope_width
    angles = offsets.astype(jnp.float32)[:, None] * (rope_base ** (-exponents))[None, :]
    return (jnp.cos(angles), jnp.sin(angles))


def swiglu(gate_vals, up_vals):
    return jax.nn.silu(gate_vals) * up_vals


def inner_rows(leading, trailing):
    return lax.dot_general(
        leading, trailing, (((0,), (0,)), ((), ())), preferred_element_type=jnp.float32
    )


def outer_cols(leading, trailing):
    return lax.dot_general(
        leading, trailing, (((1,), (1,)), ((), ())), preferred_element_type=jnp.float32
    )


MESH = pl.DeviceIdType.MESH
ANY = pl.BlockSpec(memory_space=pl.ANY)

def place():
    rep = lax.axis_index("rep")
    shard = lax.axis_index("shard")
    zpos, core = shard // 2, shard % 2
    return rep, zpos, core

def mult(value, by):
    return pl.multiple_of(value, by)

def greet(rep, zpos, core, plane=0, column=False):
    barrier = pltpu.get_barrier_semaphore()
    shard = zpos * 2 + core

    def signal(r, s):
        pl.semaphore_signal(barrier, inc=1, device_id=(r, s), device_id_type=MESH)

    if column:
        for m in range(1, 8):
            signal(rep, column_place(zpos, core, m))
        count = 7
    else:
        signal(rep, zpos * 2 + 1 - core)

        @pl.when(zpos > 0)
        def _():
            signal(rep, shard - 2)

        @pl.when(zpos < 3)
        def _():
            signal(rep, shard + 2)

        count = 1 + jnp.minimum(zpos, 1) + jnp.minimum(3 - zpos, 1)
    if plane:
        for other in plane_places(rep)[:plane]:
            signal(other, shard)
        count = count + plane
    pl.semaphore_wait(barrier, count)


def plane_places(rep):
    return rep + 1 - 2 * (rep % 2), (rep + 2) % 4, 3 - rep


def column_place(zpos, core, m, back=False):
    step = 4 - m // 2 if back else m // 2
    return ((zpos + step) % 4) * 2 + (core + m) % 2


def remote(src, dst, ssem, rsem, r, s):
    return pltpu.make_async_remote_copy(
        src_ref=src, dst_ref=dst, send_sem=ssem, recv_sem=rsem, device_id=(r, s), device_id_type=MESH
    )


def dma_sems(*dims):
    return pltpu.SemaphoreType.DMA(dims)


class Gather:
    def __init__(self, ins, outs, sems):
        self.ins, self.outs = ins, outs
        self.zsend, self.zrecv, self.csend, self.crecv, self.own = sems
        self.rep, self.zpos, self.core = place()
        self.held = None

    @staticmethod
    def scratch(n):
        return [dma_sems(2, 3, n), dma_sems(2, 3, n), dma_sems(7, n), dma_sems(7, n), dma_sems(2, n)]

    def at(self, a, z, c):
        rows = self.ins[a].shape[0]
        return self.outs[a].at[pl.ds(mult((z * 2 + c) * rows, rows), rows)]

    def hop_copy(self, a, way, hop, z, src=None):
        dst = self.at(a, z, self.core)
        return remote(dst if src is None else src, dst, self.zsend.at[way, hop, a], self.zrecv.at[way, hop, a],
                      self.rep, (self.zpos + (1 - 2 * way)) * 2 + self.core)

    def core_copy(self, a, slot, z, c, src=None):
        dst = self.at(a, z, c)
        return remote(dst if src is None else src, dst, self.csend.at[slot, a], self.crecv.at[slot, a],
                      self.rep, self.zpos * 2 + 1 - self.core)

    def keep(self, a):
        return pltpu.make_async_copy(self.ins[a], self.at(a, self.zpos, self.core), self.own.at[0, a])

    def onward(self, way):
        return self.zpos < 3 if way == 0 else self.zpos > 0

    def source(self, way, hop):
        z = self.zpos - hop if way == 0 else self.zpos + hop
        return z, (z >= 0 if way == 0 else z <= 3)

    def start(self, which=None):
        which = range(len(self.ins)) if which is None else which
        for way in range(2):
            @pl.when(self.onward(way))
            def _():
                for a in which:
                    self.hop_copy(a, way, 0, self.zpos, src=self.ins[a]).start()
        for a in which:
            self.core_copy(a, 0, self.zpos, self.core, src=self.ins[a]).start()
            self.keep(a).start()

    def hop(self, hop, which=None):
        which = range(len(self.ins)) if which is None else which
        for way in range(2):
            z, there = self.source(way, hop)

            @pl.when(there)
            def _():
                for a in which:
                    self.hop_copy(a, way, hop - 1, z).wait_recv()
                    if hop < 3:
                        @pl.when(self.onward(way))
                        def _():
                            self.hop_copy(a, way, hop, z).start()
                    self.core_copy(a, way * 3 + hop, z, self.core).start()

    def finish(self):
        arrays = range(len(self.ins))
        for way in range(2):
            for hop in range(3):
                z, there = self.source(way, hop)

                @pl.when(there & self.onward(way))
                def _():
                    for a in arrays:
                        self.hop_copy(a, way, hop, z).wait_send()
        for a in arrays:
            self.keep(a).wait()
            self.core_copy(a, 0, self.zpos, self.core, src=self.ins[a]).wait_send()
            self.core_copy(a, 0, self.zpos, 1 - self.core).wait_recv()
        for way in range(2):
            for hop in range(1, 4):
                z, there = self.source(way, hop)

                @pl.when(there)
                def _():
                    for a in arrays:
                        self.core_copy(a, way * 3 + hop, z, self.core).wait_send()
                        self.core_copy(a, way * 3 + hop, z, 1 - self.core).wait_recv()


class Total:
    def __init__(self, term, out, bufs, sems):
        self.term, self.out = term, out
        self.mine, self.theirs, self.stage, self.landed = bufs
        self.zsend, self.zrecv, self.csend, self.crecv, self.own = sems
        self.rep, self.zpos, self.core = place()

    @staticmethod
    def scratch(term):
        four = pltpu.VMEM((4,) + term.shape[1:], term.dtype)
        return [four] * 3 + [pltpu.VMEM((2, 4) + term.shape[1:], term.dtype),
                             dma_sems(2, 4), dma_sems(2, 4), dma_sems(4), dma_sems(4), dma_sems(4)]

    def pair_copy(self, z):
        return remote(self.term.at[z * 2 + 1 - self.core], self.theirs.at[z], self.csend.at[z], self.crecv.at[z],
                      self.rep, self.zpos * 2 + 1 - self.core)

    def load(self, z):
        return pltpu.make_async_copy(self.term.at[z * 2 + self.core], self.mine.at[z], self.own.at[z])

    def hop_copy(self, way, z):
        return remote(self.stage.at[z], self.landed.at[way, z], self.zsend.at[way, z], self.zrecv.at[way, z],
                      self.rep, (self.zpos + (1 - 2 * way)) * 2 + self.core)

    def each(self, step):
        for way in range(2):
            behind = self.zpos if way == 0 else 3 - self.zpos
            target = self.zpos + 3 - step if way == 0 else self.zpos - 3 + step
            yield way, behind, target, (behind <= step) & (behind < 3)

    def start(self):
        for z in (3, 0, 2, 1):
            self.pair_copy(z).start()
            self.load(z).start()

    def pair(self):
        for z in (3, 0, 2, 1):
            self.load(z).wait()
            self.pair_copy(z).wait_recv()

    def step(self, step):
        wide = jnp.float32
        for way, behind, target, there in self.each(step):
            @pl.when(there)
            def _():
                total = self.mine[target].astype(wide) + self.theirs[target].astype(wide)

                @pl.when(behind == 0)
                def _():
                    self.stage[target] = total.astype(self.stage.dtype)

                @pl.when(behind > 0)
                def _():
                    self.hop_copy(way, target).wait_recv()
                    self.stage[target] = (total + self.landed[way, target].astype(wide)).astype(self.stage.dtype)
                self.hop_copy(way, target).start()

    def finish(self):
        wide = jnp.float32
        self.out[...] = self.mine[self.zpos].astype(wide) + self.theirs[self.zpos].astype(wide)
        for way in range(2):
            @pl.when(self.zpos > 0 if way == 0 else self.zpos < 3)
            def _():
                self.hop_copy(way, self.zpos).wait_recv()
                self.out[...] += self.landed[way, self.zpos].astype(wide)
        for step in range(3):
            for way, behind, target, there in self.each(step):
                @pl.when(there)
                def _():
                    self.hop_copy(way, target).wait_send()
        for z in range(4):
            self.pair_copy(z).wait_send()


def kernel_params(cid):
    return pltpu.CompilerParams(collective_id=cid, has_side_effects=True, vmem_limit_bytes=56 * 2**20)


VMEM = pl.BlockSpec(memory_space=pltpu.VMEM)


def chain_gather_kernel(n, *refs):
    gather = Gather(refs[:n], refs[n : 2 * n], refs[2 * n :])
    greet(*place())
    gather.start()
    for hop in range(1, 4):
        gather.hop(hop)
    gather.finish()


def chain_gather(cid, *arrays):
    n = len(arrays)
    out = [jax.ShapeDtypeStruct((a.shape[0] * 8,) + a.shape[1:], a.dtype) for a in arrays]
    return pl.pallas_call(
        functools.partial(chain_gather_kernel, n), out_shape=out, in_specs=[ANY] * n, out_specs=[ANY] * n,
        scratch_shapes=Gather.scratch(n), compiler_params=kernel_params(cid),
    )(*arrays)


def chain_sum_kernel(term, out, *refs):
    total = Total(term, out, refs[:4], refs[4:])
    greet(*place())
    total.start()
    total.pair()
    for step in range(3):
        total.step(step)
    total.finish()


def chain_sum(cid, term):
    return pl.pallas_call(
        chain_sum_kernel, out_shape=jax.ShapeDtypeStruct(term.shape[1:], jnp.float32), in_specs=[ANY], out_specs=VMEM,
        scratch_shapes=Total.scratch(term), compiler_params=kernel_params(cid),
    )(term)


def late_kernel(*refs):
    branch, lat, cols, term, parts, down = refs[:6]
    branch_all, lat_all, cols_all, out, parts_all, down_all = refs[6:12]
    scratch = list(refs[12:])
    rep, zpos, core = place()
    shard = zpos * 2 + core
    xrep, yrep, drep = plane_places(rep)
    gather = Gather((branch, lat), (branch_all, lat_all), scratch[:5])
    total = Total(term, out, scratch[5:9], scratch[9:14])
    asend, arecv, esend, erecv, psend, precv, dsend, drecv, own = scratch[14:]

    def cols_copy(m, back=False):
        s2 = column_place(zpos, core, m, back)
        here = cols_all.at[s2 if back else shard]
        return remote(cols.at[s2], here, asend.at[m - 1], arecv.at[m - 1], rep, s2)

    def parts_copy(m, which, back=False):
        s2 = column_place(zpos, core, m, back)
        return remote(parts.at[s2, which], parts_all.at[s2 if back else shard, rep, which],
                      esend.at[m - 1, which], erecv.at[m - 1, which], rep, s2)

    def parts_plane(m, which, quarter, kind, r):
        ref = parts_all.at[column_place(zpos, core, m, True), quarter, which]
        src = parts.at[shard, which] if m == 0 and kind < 2 else ref
        return remote(src, ref, psend.at[kind, m, which], precv.at[kind, m, which], r, shard)

    def down_plane(half, quarter, kind, r):
        width = down.shape[1] // 2
        at = (slice(None), pl.ds(half * width, width))
        dst = down_all.at[(quarter,) + at]
        return remote(down.at[at] if kind < 2 else dst, dst, dsend.at[kind, half], drecv.at[kind, half], r, shard)

    def own_copies():
        return (pltpu.make_async_copy(cols.at[shard], cols_all.at[shard], own.at[0]),
                pltpu.make_async_copy(parts.at[shard], parts_all.at[shard, rep], own.at[1]),
                pltpu.make_async_copy(down, down_all.at[rep], own.at[2]))

    greet(rep, zpos, core, plane=2, column=True)
    near = (1, 2, 6, 3, 7, 4, 5)
    for m in near:
        for which in range(2):
            parts_copy(m, which).start()
    total.start()
    for half in range(2):
        down_plane(half, rep, 0, xrep).start()
        down_plane(half, rep, 1, yrep).start()
        parts_plane(0, half, rep, 0, xrep).start()
        parts_plane(0, half, rep, 1, yrep).start()
    gather.start()
    for m in near:
        cols_copy(m).start()
    for copy in own_copies():
        copy.start()

    def onward(kind_of, half, *first):
        kind_of(*first, half, xrep, 0, xrep).wait_recv()
        kind_of(*first, half, yrep, 1, yrep).wait_recv()
        if half == 0:
            kind_of(*first, half, xrep, 2, yrep).start()
        else:
            kind_of(*first, half, yrep, 2, xrep).start()

    def from_column(m):
        for which in range(2):
            parts_copy(m, which, True).wait_recv()
            parts_plane(m, which, rep, 0, xrep).start()
            parts_plane(m, which, rep, 1, yrep).start()

    total.pair()
    total.step(0)
    for m in near[:3]:
        from_column(m)
    for half in range(2):
        onward(down_plane, half)
        onward(parts_plane, half, 0)
    gather.hop(1)
    total.step(1)
    for m in near[3:]:
        from_column(m)
    for m in near[:3]:
        for half in range(2):
            onward(parts_plane, half, m)
    gather.hop(2)
    total.step(2)
    for m in near[3:]:
        for half in range(2):
            onward(parts_plane, half, m)
    gather.hop(3)
    total.finish()
    gather.finish()
    for m in near:
        cols_copy(m).wait_send()
        cols_copy(m, True).wait_recv()
        for which in range(2):
            parts_copy(m, which).wait_send()

    def settle(kind_of, half, *first):
        kind_of(*first, half, rep, 0, xrep).wait_send()
        kind_of(*first, half, rep, 1, yrep).wait_send()
        if half == 0:
            kind_of(*first, half, xrep, 2, yrep).wait_send()
        else:
            kind_of(*first, half, yrep, 2, xrep).wait_send()
        kind_of(*first, half, drep, 2, drep).wait_recv()

    for half in range(2):
        settle(down_plane, half)
        for m in range(8):
            settle(parts_plane, half, m)
    for copy in own_copies():
        copy.wait()


def late_exchange(cid, branch, lat, cols, term, parts, down):
    out = [jax.ShapeDtypeStruct((8 * branch.shape[0], branch.shape[1]), branch.dtype),
           jax.ShapeDtypeStruct((8 * lat.shape[0], lat.shape[1]), lat.dtype),
           jax.ShapeDtypeStruct(cols.shape, cols.dtype),
           jax.ShapeDtypeStruct(term.shape[1:], jnp.float32),
           jax.ShapeDtypeStruct((8, 4) + parts.shape[1:], parts.dtype),
           jax.ShapeDtypeStruct((4,) + down.shape, down.dtype)]
    return pl.pallas_call(
        late_kernel, out_shape=out, in_specs=[ANY] * 6, out_specs=[ANY, ANY, ANY, VMEM, ANY, ANY],
        scratch_shapes=Gather.scratch(2) + Total.scratch(term) + [
            dma_sems(7), dma_sems(7), dma_sems(7, 2), dma_sems(7, 2), dma_sems(3, 8, 2), dma_sems(3, 8, 2),
            dma_sems(3, 2), dma_sems(3, 2), dma_sems(3)],
        compiler_params=kernel_params(cid),
    )(branch, lat, cols, term, parts, down)


def last_kernel(n, *refs):
    terms, gain = refs[:n], refs[n]
    outs, gain_out = refs[n + 1 : 2 * n + 1], refs[2 * n + 1]
    scratch = list(refs[2 * n + 2 :])
    landed, sums = scratch[:n], scratch[n : 2 * n]
    gain_landed, gain_sum, gain_plane, ssend, srecv, tsend, trecv, gsend, grecv, hsend, hrecv = scratch[2 * n :]
    rep, zpos, core = place()
    shard = zpos * 2 + core
    places = plane_places(rep)
    wide = jnp.float32
    greet(rep, zpos, core, plane=3, column=True)

    def term_copy(a, k):
        return remote(terms[a].at[places[k]], landed[a].at[k], ssend.at[k, a], srecv.at[k, a], places[k], shard)

    def sum_copy(a, k, back=False):
        return remote(sums[a], outs[a].at[places[k] if back else rep], tsend.at[k, a], trecv.at[k, a], places[k], shard)

    def gain_copy(m):
        s2 = column_place(zpos, core, m)
        return remote(gain.at[s2], gain_landed.at[m - 1], gsend.at[m - 1], grecv.at[m - 1], rep, s2)

    def gain_on(k):
        return remote(gain_sum, gain_plane.at[k], hsend.at[k], hrecv.at[k], places[k], shard)

    for m in range(1, 8):
        gain_copy(m).start()
    for a in range(n):
        for k in range(3):
            term_copy(a, k).start()
    gain_sum[...] = gain[shard]
    for m in range(1, 8):
        gain_copy(m).wait_recv()
        gain_sum[...] += gain_landed[m - 1]
    for k in range(3):
        gain_on(k).start()
    for a in range(n):
        total = terms[a][rep].astype(wide)
        for k in range(3):
            term_copy(a, k).wait_recv()
            total = total + landed[a][k].astype(wide)
        sums[a][...] = total.astype(jnp.bfloat16)
        for k in range(3):
            sum_copy(a, k).start()
        outs[a][rep] = sums[a][...]
    gain_out[...] = gain_sum[...]
    for k in range(3):
        gain_on(k).wait_recv()
        gain_out[...] += gain_plane[k]
    for k in range(3):
        gain_on(k).wait_send()
        for a in range(n):
            term_copy(a, k).wait_send()
            sum_copy(a, k).wait_send()
            sum_copy(a, k, True).wait_recv()
    for m in range(1, 8):
        gain_copy(m).wait_send()


def last_sums(cid, terms, gain):
    n = len(terms)
    out = [jax.ShapeDtypeStruct(t.shape, jnp.bfloat16) for t in terms] + [jax.ShapeDtypeStruct(gain.shape[1:], gain.dtype)]
    block = pltpu.VMEM(gain.shape[1:], gain.dtype)
    return pl.pallas_call(
        functools.partial(last_kernel, n), out_shape=out, in_specs=[VMEM] * (n + 1), out_specs=[VMEM] * (n + 1),
        scratch_shapes=[pltpu.VMEM((3,) + t.shape[1:], t.dtype) for t in terms]
        + [pltpu.VMEM(t.shape[1:], t.dtype) for t in terms]
        + [pltpu.VMEM((7,) + gain.shape[1:], gain.dtype), block, pltpu.VMEM((3,) + gain.shape[1:], gain.dtype)]
        + [dma_sems(3, n)] * 4 + [dma_sems(7)] * 2 + [dma_sems(3)] * 2,
        compiler_params=kernel_params(cid),
    )(*terms, gain)

def start_kernel(*refs):
    ins, (gate, up) = refs[:7], refs[7:9]
    outs, cols = refs[9:16], refs[16:18]
    (zsend, zrecv, xsend, xrecv, ysend, yrecv, dsend, drecv, csend, crecv, own, gsend, grecv, psend, precv) = refs[18:33]
    held, strips = refs[33:40], refs[40:42]
    rep, zpos, core = place()
    xrep, yrep, drep = plane_places(rep)
    shard = zpos * 2 + core

    def whole(a, z, c):
        rows = ins[a].shape[0]
        return outs[a].at[pl.ds(mult((z * 2 + c) * rows, rows), rows)]

    def pieces(a, z, c, quarter, act, own_ref=False):
        def part(b, first, rows):
            full = ins[b].shape[0]
            if own_ref:
                return ins[b].at[pl.ds(mult(first, 16), rows)]
            return outs[b].at[pl.ds(mult((z * 2 + c) * full + first, 16), rows)]

        if a < 3:
            rows = ins[a].shape[0] // 4
            act(part(a, quarter * rows, rows))
        elif a == 3:
            @pl.when(quarter < 3)
            def _():
                act(part(3, jnp.minimum(quarter, 2) * 32, 32))

            @pl.when(quarter == 3)
            def _():
                act(part(4, 0, 32))
        else:
            act(ins[a + 1] if own_ref else whole(a + 1, z, c))

    copy = remote

    def hop(a, way, h, z, what):
        def act(ref):
            c = copy(ref, ref, zsend.at[way, h, a], zrecv.at[way, h, a], rep, (zpos + 1 - 2 * way) * 2 + core)
            getattr(c, what)()
        pieces(a, z, core, rep, act)

    def to_plane(a, k, z, quarter, what, sems, r):
        def act(ref):
            getattr(copy(ref, ref, sems[0].at[k, a], sems[1].at[k, a], r, shard), what)()
        pieces(a, z, core, quarter, act)

    def to_core(a, slot, z, c, what, src=None):
        ref = whole(a, z, c)
        getattr(copy(ref if src is None else src, ref, csend.at[slot, a], crecv.at[slot, a], rep, zpos * 2 + 1 - core), what)()

    greet(rep, zpos, core, plane=2, column=True)
    def send_own(a):
        def first(way):
            def go(src):
                def act(ref):
                    copy(src, ref, zsend.at[way, 0, a], zrecv.at[way, 0, a], rep, (zpos + 1 - 2 * way) * 2 + core).start()
                return act
            return go
        for way in range(2):
            @pl.when(zpos < 3 if way == 0 else zpos > 0)
            def _():
                if a < 3:
                    rows = ins[a].shape[0] // 4
                    src = ins[a].at[pl.ds(mult(rep * rows, 16), rows)]
                    pieces(a, zpos, core, rep, first(way)(src))
                elif a == 3:
                    @pl.when(rep < 3)
                    def _():
                        start = mult(jnp.minimum(rep, 2) * 32, 16)
                        src = ins[3].at[pl.ds(start, 32)]
                        dst = outs[3].at[pl.ds(mult(shard * 96 + start, 16), 32)]
                        first(way)(src)(dst)

                    @pl.when(rep == 3)
                    def _():
                        first(way)(ins[4])(whole(4, zpos, core))
                else:
                    first(way)(ins[a + 1])(whole(a + 1, zpos, core))

    def keep(a, half):
        if half == 0:
            return pltpu.make_async_copy(ins[a], held[a], own.at[0, a])
        return pltpu.make_async_copy(held[a], whole(a, zpos, core), own.at[1, a])

    for a in range(4):
        send_own(a)

    strip = cols[0].shape[1]
    quarter_rows = gate.shape[0] // 4

    def slice_of(which, s, first, rows):
        start = mult((s * 25 // 4) * 128, 128)
        return (gate, up)[which].at[pl.ds(mult(first, 16), rows), pl.ds(start, strip)]

    def rows_of(which, s, quarter):
        return cols[which].at[pl.ds(mult(s * gate.shape[0] + quarter * quarter_rows, 16), quarter_rows)]

    def slice_copy(m, which):
        s2 = column_place(zpos, core, m)
        return remote(slice_of(which, s2, rep * quarter_rows, quarter_rows), rows_of(which, shard, rep),
                      gsend.at[m - 1, which], grecv.at[m - 1, which], rep, s2)

    def slice_plane(m, which, quarter, kind, r):
        ref = rows_of(which, column_place(zpos, core, m, back=True), quarter)
        return remote(ref, ref, psend.at[kind, m - 1, which], precv.at[kind, m - 1, which], r, shard)

    def own_slice(which, half):
        if half == 0:
            return pltpu.make_async_copy(slice_of(which, shard, 0, gate.shape[0]), strips[which], own.at[0, 7 + which])
        rows = gate.shape[0]
        return pltpu.make_async_copy(strips[which], cols[which].at[pl.ds(mult(shard * rows, rows), rows)], own.at[1, 7 + which])

    near = (1, 2, 6, 3, 7, 4, 5)
    for a in range(7):
        to_core(a, 0, zpos, core, "start", src=ins[a])
        keep(a, 0).start()
    for which in range(2):
        own_slice(which, 0).start()
    for a in range(7):
        keep(a, 0).wait()
        keep(a, 1).start()
    for which in range(2):
        own_slice(which, 0).wait()
        own_slice(which, 1).start()

    def slices_from_column(m):
        for which in range(2):
            s2 = column_place(zpos, core, m, back=True)
            ref = rows_of(which, s2, rep)
            remote(ref, ref, gsend.at[m - 1, which], grecv.at[m - 1, which], rep, s2).wait_recv()
            slice_plane(m, which, rep, 0, xrep).start()
            slice_plane(m, which, rep, 1, yrep).start()

    def slices_from_plane(m):
        for which in range(2):
            slice_plane(m, which, xrep, 0, xrep).wait_recv()
            slice_plane(m, which, yrep, 1, yrep).wait_recv()
            if which == 0:
                slice_plane(m, which, xrep, 2, yrep).start()
            else:
                slice_plane(m, which, yrep, 2, xrep).start()

    def from_column(h, way, z, slots=range(4)):
        for a in slots:
            hop(a, way, h - 1, z, "wait_recv")
            if h < 3:
                @pl.when(zpos < 3 if way == 0 else zpos > 0)
                def _():
                    hop(a, way, h, z, "start")
            if a < 4:
                to_plane(a, way * 3 + h - 1, z, rep, "start", (xsend, xrecv), xrep)
                to_plane(a, way * 3 + h - 1, z, rep, "start", (ysend, yrecv), yrep)
            else:
                to_core(a + 1, way * 3 + h, z, core, "start")

    def from_plane(h, way, z):
        k = way * 3 + h - 1
        for a in range(4):
            to_plane(a, k, z, xrep, "wait_recv", (xsend, xrecv), xrep)
            if a == 0:
                to_plane(a, k, z, xrep, "start", (dsend, drecv), yrep)
            to_plane(a, k, z, yrep, "wait_recv", (ysend, yrecv), yrep)
            if a > 0:
                to_plane(a, k, z, yrep, "start", (dsend, drecv), xrep)

    def from_corner(h, way, z):
        k = way * 3 + h - 1
        for a in range(4):
            to_plane(a, k, z, drep, "wait_recv", (dsend, drecv), drep)
        for a in range(5):
            to_core(a, k + 1, z, core, "start")

    def by_hop(stage, h, *more):
        for way in range(2):
            z = zpos - h if way == 0 else zpos + h

            @pl.when(z >= 0 if way == 0 else z <= 3)
            def _():
                stage(h, way, z, *more)

    by_hop(from_column, 1)
    by_hop(from_column, 2)
    for m in near:
        for which in range(2):
            slice_copy(m, which).start()
    by_hop(from_plane, 1)
    by_hop(from_column, 3)
    by_hop(from_plane, 2)
    by_hop(from_corner, 1)
    for m in near[:3]:
        slices_from_column(m)
    send_own(4)
    send_own(5)
    by_hop(from_plane, 3)
    for m in near[3:]:
        slices_from_column(m)
    by_hop(from_corner, 2)
    for m in near[:3]:
        slices_from_plane(m)
    by_hop(from_column, 1, (5, 4))
    by_hop(from_corner, 3)
    for m in near[3:]:
        slices_from_plane(m)
    by_hop(from_column, 2, (5, 4))
    by_hop(from_column, 3, (5, 4))
    for a in range(7):
        to_core(a, 0, zpos, core, "wait_send", src=ins[a])
        to_core(a, 0, zpos, 1 - core, "wait_recv")
        keep(a, 1).wait()
    for which in range(2):
        own_slice(which, 1).wait()
        for m in near:
            slice_copy(m, which).wait_send()
            slice_plane(m, which, rep, 0, xrep).wait_send()
            slice_plane(m, which, rep, 1, yrep).wait_send()
            if which == 0:
                slice_plane(m, which, xrep, 2, yrep).wait_send()
            else:
                slice_plane(m, which, yrep, 2, xrep).wait_send()
            slice_plane(m, which, drep, 2, drep).wait_recv()
    for way in range(2):
        for h in range(3):
            z = zpos - h if way == 0 else zpos + h

            @pl.when((z >= 0) & (zpos < 3) if way == 0 else (z <= 3) & (zpos > 0))
            def _():
                for a in range(6):
                    hop(a, way, h, z, "wait_send")
    for h in range(1, 4):
        for way in range(2):
            z = zpos - h if way == 0 else zpos + h
            k = way * 3 + h - 1

            @pl.when(z >= 0 if way == 0 else z <= 3)
            def _():
                for a in range(4):
                    to_plane(a, k, z, rep, "wait_send", (xsend, xrecv), xrep)
                    to_plane(a, k, z, rep, "wait_send", (ysend, yrecv), yrep)
                    to_plane(a, k, z, xrep if a == 0 else yrep, "wait_send", (dsend, drecv), yrep)
                for a in range(7):
                    to_core(a, k + 1, z, core, "wait_send")
                    to_core(a, k + 1, z, 1 - core, "wait_recv")

def start_gather(cid, weights, gate, up, strip):
    out = [jax.ShapeDtypeStruct((a.shape[0] * 8,) + a.shape[1:], a.dtype) for a in weights]
    out += [jax.ShapeDtypeStruct((gate.shape[0] * 8, strip), gate.dtype)] * 2
    return pl.pallas_call(
        start_kernel, out_shape=out, in_specs=[ANY] * 9, out_specs=[ANY] * 9,
        scratch_shapes=[dma_sems(2, 3, 6), dma_sems(2, 3, 6)] + [dma_sems(6, 4)] * 6
        + [dma_sems(7, 7), dma_sems(7, 7), dma_sems(2, 9), dma_sems(7, 2), dma_sems(7, 2), dma_sems(3, 7, 2), dma_sems(3, 7, 2)]
        + [pltpu.VMEM(a.shape, a.dtype) for a in weights] + [pltpu.VMEM((gate.shape[0], strip), gate.dtype)] * 2,
        compiler_params=kernel_params(cid),
    )(*weights, gate, up)

def plane_swap(values, j):
    return lax.ppermute(values, "rep", [(i, i ^ j) for i in range(4)])


def column_body(
    tokens,
    cotangent,
    doc_lengths,
    gain_attn,
    query_down,
    gain_query,
    query_up,
    latent_down,
    gain_latent,
    latent_up,
    attn_out,
    gain_ffn,
    w_gate,
    w_up,
    w_down,
):
    low = jnp.bfloat16
    wide = jnp.float32
    rows, width = tokens.shape[1], tokens.shape[2]
    seq_len = rows * 4
    head_dim = ND + RD
    group = 8
    groups = H // group
    scale = head_dim ** (-0.5)
    rep, shard = lax.axis_index("rep"), lax.axis_index("shard")
    slice_ff = FF // 8
    strip = 896
    shift = (slice_ff * shard) % 128

    small = jnp.concatenate(
        [v.astype(wide) for v in (gain_attn, gain_ffn, gain_query, gain_latent)]
        + [jnp.zeros((1024 - 768,), wide)]
    ).reshape(8, 128)
    grad_out = cotangent[0].astype(wide)
    grad_down_in = (residual_scale * grad_out).astype(low)
    aout, qdown, ldown, qup, lup, gd_all, small_all, gate_w, up_w = start_gather(
        0, (attn_out, query_down, latent_down, query_up, latent_up, grad_down_in, small), w_gate, w_up, strip
    )
    small_all = small_all.reshape(8, 1024)
    gain_in = small_all[:, :320].reshape(-1)
    gain_f = small_all[:, 320:640].reshape(-1)
    gain_q = small_all[:, 640:736].reshape(-1)
    gain_l = small_all[:, 736:768].reshape(-1)

    down_w = lax.dynamic_update_slice(jnp.zeros((strip, width), low), w_down, (shift, 0))

    local_pos = rep * rows + jnp.arange(rows, dtype=jnp.int32)
    key_pos = jnp.concatenate(
        [(rep ^ j) * rows + jnp.arange(rows, dtype=jnp.int32) for j in range(4)]
    )
    query_seg, query_off = segment_of(doc_lengths[0], local_pos)
    key_seg = segment_of(doc_lengths[0], key_pos)[0]
    allowed = (query_seg[:, None] == key_seg[None, :]) & (key_pos[None, :] <= local_pos[:, None])
    cos_part, sin_part = rope_tables(query_off, RD)
    inputs = tokens[0].astype(wide)
    normed, norm_in_back = jax.vjp(rms_scale, inputs, gain_in)
    normed_low = normed.astype(low)
    latent_proj = jnp.dot(normed_low, ldown, preferred_element_type=wide)
    latent_norm, norm_l_back = jax.vjp(rms_scale, latent_proj[:, :KR], gain_l)

    def key_rotate(values):
        return rotate(values, cos_part, sin_part)

    key_rot, key_back = jax.vjp(key_rotate, latent_proj[:, KR:])
    latents = jnp.concatenate([latent_norm.astype(low), key_rot.astype(low)], axis=1)
    latents = jnp.concatenate([latents] + [plane_swap(latents, j) for j in range(1, 4)], axis=0)
    latent_low, all_rope = latents[:, :KR], latents[:, KR:]
    query_lat = jnp.dot(normed_low, qdown, preferred_element_type=wide)
    query_norm, norm_q_back = jax.vjp(rms_scale, query_lat, gain_q)
    query_low = query_norm.astype(low)
    query_proj = jnp.dot(query_low, qup, preferred_element_type=wide).reshape(rows, H, head_dim)

    def query_rope(values):
        return jnp.concatenate(
            [
                values[..., :ND],
                rotate(values[..., ND:], cos_part[:, None, :], sin_part[:, None, :]),
            ],
            axis=-1,
        )

    query_rot, query_back = jax.vjp(query_rope, query_proj)
    query_used = query_rot.astype(low)
    keyvals = jnp.dot(latent_low, lup, preferred_element_type=wide).astype(low)
    queries = query_used.reshape(rows, groups, group, head_dim).transpose(1, 0, 2, 3)
    key_groups = keyvals.reshape(seq_len, groups, group, ND + VD).transpose(1, 0, 2, 3)

    def scores_of(query_blk, key_blk):
        nope_part = jnp.einsum(
            "thd,shd->hts", query_blk[..., :ND], key_blk[..., :ND], preferred_element_type=wide
        )
        rope_part = jnp.einsum(
            "thd,sd->hts", query_blk[..., ND:], all_rope, preferred_element_type=wide
        )
        return jnp.where(allowed[None], (nope_part + rope_part) * scale, masked_score)

    def forward_group(carry, blocks):
        query_blk, key_blk = blocks
        scores = scores_of(query_blk, key_blk)
        row_max = jnp.max(scores, axis=-1, keepdims=True)
        exp_scores = jnp.exp(scores - row_max)
        totals = jnp.sum(exp_scores, axis=-1, keepdims=True)
        probs = (exp_scores / totals).astype(low)
        mixed = jnp.einsum("hts,shd->thd", probs, key_blk[..., ND:], preferred_element_type=wide)
        return (carry, (mixed, row_max + jnp.log(totals)))

    _, (mixed_groups, log_totals) = lax.scan(
        forward_group, jnp.zeros((), wide), (queries, key_groups)
    )
    mixed_low = mixed_groups.transpose(1, 0, 2, 3).reshape(rows, H * VD).astype(low)
    branch = jnp.dot(mixed_low, aout, preferred_element_type=wide)
    residual = inputs + residual_scale * branch
    normed_ffn, norm_f_back = jax.vjp(rms_scale, residual, gain_f)
    ffn_low = normed_ffn.astype(low)

    (ffn_all,) = chain_gather(1, ffn_low)
    gate_pre = jnp.dot(ffn_all, gate_w, preferred_element_type=wide)
    up_pre = jnp.dot(ffn_all, up_w, preferred_element_type=wide)
    hidden, act_back = jax.vjp(swiglu, gate_pre, up_pre)
    hidden_low = hidden.astype(low)
    grad_hidden = outer_cols(gd_all, down_w)
    grad_gate_f, grad_up_f = act_back(grad_hidden)
    grad_gate = grad_gate_f.astype(low)
    grad_up = grad_up_f.astype(low)
    ffn_in_part = (outer_cols(grad_gate, gate_w) + outer_cols(grad_up, up_w)).astype(low)
    grad_ffn_in = chain_sum(2, ffn_in_part.reshape(8, rows, width))
    out_part = jnp.dot(hidden_low, down_w, preferred_element_type=wide).astype(low)
    down_part = lax.dynamic_slice(
        inner_rows(hidden_low, gd_all).astype(low), (shift, 0), (slice_ff, width)
    )
    gate_part = inner_rows(ffn_all, grad_gate).astype(low)
    up_part = inner_rows(ffn_all, grad_up).astype(low)
    down_own = lax.psum_scatter(
        down_part.reshape(4, slice_ff // 4, width), "rep", scatter_dimension=0, tiled=False
    )
    parts_own = lax.psum_scatter(
        jnp.stack([gate_part.reshape(8, 4, 80, strip), up_part.reshape(8, 4, 80, strip)])
        .transpose(2, 1, 0, 3, 4),
        "rep",
        scatter_dimension=0,
        tiled=False,
    )

    grad_res_norm, grad_gain_ffn = norm_f_back(grad_ffn_in)
    grad_resid = grad_out + grad_res_norm
    grad_branch = (residual_scale * grad_resid).astype(low)
    grad_mixed = outer_cols(grad_branch, aout).astype(low)
    grad_groups = grad_mixed.reshape(rows, groups, group, VD).transpose(1, 0, 2, 3)

    def backward_group(rope_acc, blocks):
        query_blk, key_blk, grad_blk, log_blk = blocks
        scores = scores_of(query_blk, key_blk)
        probs = jnp.exp(scores - log_blk)
        grad_probs = jnp.einsum(
            "thd,shd->hts", grad_blk, key_blk[..., ND:], preferred_element_type=wide
        )
        delta = jnp.sum(probs * grad_probs, axis=-1, keepdims=True)
        grad_scores = (probs * (grad_probs - delta)).astype(low)
        grad_query = (
            jnp.concatenate(
                [
                    jnp.einsum(
                        "hts,shd->thd",
                        grad_scores,
                        key_blk[..., :ND],
                        preferred_element_type=wide,
                    ),
                    jnp.einsum(
                        "hts,sd->thd", grad_scores, all_rope, preferred_element_type=wide
                    ),
                ],
                axis=-1,
            )
            * scale
        )
        grad_key = (
            jnp.einsum(
                "hts,thd->shd", grad_scores, query_blk[..., :ND], preferred_element_type=wide
            )
            * scale
        )
        grad_value = jnp.einsum(
            "hts,thd->shd", probs.astype(low), grad_blk, preferred_element_type=wide
        )
        rope_acc = (
            rope_acc
            + jnp.einsum(
                "hts,thd->sd", grad_scores, query_blk[..., ND:], preferred_element_type=wide
            )
            * scale
        )
        return (rope_acc, (grad_query, jnp.concatenate([grad_key, grad_value], axis=-1)))

    rope_sum, (grad_q_groups, grad_kv_groups) = lax.scan(
        backward_group,
        jnp.zeros((seq_len, RD), wide),
        (queries, key_groups, grad_groups, log_totals),
    )
    grad_kv = grad_kv_groups.transpose(1, 0, 2, 3).reshape(seq_len, H * (ND + VD)).astype(low)
    grad_lat_part = jnp.concatenate([outer_cols(grad_kv, lup), rope_sum], axis=1).astype(low)
    grad_lat_own = grad_lat_part[:rows].astype(wide)
    for j in range(1, 4):
        grad_lat_own = grad_lat_own + plane_swap(
            grad_lat_part[j * rows : (j + 1) * rows], j
        ).astype(wide)
    grad_q_full = grad_q_groups.transpose(1, 0, 2, 3).reshape(rows, H, head_dim)
    grad_q_proj = query_back(grad_q_full)[0].reshape(rows, H * head_dim).astype(low)
    grad_q_lat_f, grad_gain_query = norm_q_back(outer_cols(grad_q_proj, qup))
    grad_q_lat = grad_q_lat_f.astype(low)
    grad_lat_c, grad_gain_latent = norm_l_back(grad_lat_own[:, :KR])
    grad_lat_r = key_back(grad_lat_own[:, KR:])[0]
    grad_lat = jnp.concatenate([grad_lat_c, grad_lat_r], axis=1).astype(low)
    grad_normed = outer_cols(grad_q_lat, qdown) + outer_cols(grad_lat, ldown)
    grad_in_norm, grad_gain_attn = norm_in_back(grad_normed)
    tokens_grad = (grad_resid + grad_in_norm).astype(low)

    qup_grad = inner_rows(query_low, grad_q_proj).astype(low)
    lup_grad = inner_rows(latent_low, grad_kv).astype(low)

    def scattered(grad):
        grad = grad.reshape(8, 4, grad.shape[0] // 32, grad.shape[1])
        part = lax.psum_scatter(grad, "rep", scatter_dimension=1, tiled=False)
        part = lax.psum_scatter(part, "shard", scatter_dimension=0, tiled=False)
        return lax.all_gather(part, "rep", axis=0, tiled=True).astype(wide)

    qup_own, lup_own = scattered(qup_grad), scattered(lup_grad)
    grad_lats = jnp.concatenate([grad_q_lat, grad_lat], axis=1)
    cols = jnp.stack([mixed_low, normed_low]).reshape(2, rows, 8, width // 8).transpose(2, 0, 1, 3)
    branch_all, lat_all, cols_all, out_sum, parts_all, down_all = late_exchange(
        3, grad_branch, grad_lats, cols, out_part.reshape(8, rows, width), parts_own, down_own
    )
    layer_out = (residual + residual_scale * out_sum).astype(low)
    down_grad = down_all.reshape(slice_ff, width).astype(wide)

    def slices(which):
        return jnp.concatenate(
            [
                parts_all[s, :, which, :, (slice_ff * s) % 128 : (slice_ff * s) % 128 + slice_ff]
                for s in range(8)
            ],
            axis=-1,
        ).reshape(-1, FF).astype(wide)

    gate_grad, up_grad = slices(0), slices(1)
    mixed_cols = cols_all[:, 0].reshape(8 * rows, width // 8)
    normed_cols = cols_all[:, 1].reshape(8 * rows, width // 8)
    aout_part = inner_rows(mixed_cols, branch_all).astype(low)
    lat_part = inner_rows(normed_cols, lat_all).astype(low)
    gains = jnp.concatenate(
        [
            v.reshape(8, -1)
            for v in (grad_gain_attn, grad_gain_ffn, grad_gain_query, grad_gain_latent)
        ]
        + [jnp.zeros((8, 1024 - 768), wide)],
        axis=1,
    ).reshape(8, 8, 128)
    aout_own, lat_own, gain_own = last_sums(
        4, (aout_part.reshape(4, 80, width), lat_part.reshape(4, 80, -1)), gains
    )
    aout_own = aout_own.reshape(320, width).astype(wide)
    lat_own = lat_own.reshape(320, -1).astype(wide)
    gain_own = gain_own.reshape(1024)

    return (
        layer_out[None],
        tokens_grad[None],
        gain_own[:320],
        lat_own[:, : query_down.shape[1]],
        gain_own[640:736],
        qup_own,
        lat_own[:, query_down.shape[1] :],
        gain_own[736:768],
        lup_own,
        aout_own,
        gain_own[320:640],
        gate_grad,
        up_grad,
        down_grad,
    )


def body(
    tokens,
    cotangent,
    doc_lengths,
    gain_attn,
    query_down,
    gain_query,
    query_up,
    latent_down,
    gain_latent,
    latent_up,
    attn_out,
    gain_ffn,
    w_gate,
    w_up,
    w_down,
):
    low_type = jnp.bfloat16
    wide_type = jnp.float32
    tok_rows = tokens.shape[1]
    seq_len = tok_rows * lax.axis_size("rep")
    head_dim = ND + RD
    group_size = math.gcd(H, 8)
    group_count = H // group_size
    softmax_scale = head_dim ** (-0.5)
    local_pos = lax.axis_index("rep") * tok_rows + jnp.arange(tok_rows, dtype=jnp.int32)
    key_pos = jnp.arange(seq_len, dtype=jnp.int32)
    query_seg, query_off = segment_of(doc_lengths[0], local_pos)
    key_seg = segment_of(doc_lengths[0], key_pos)[0]
    allowed = (query_seg[:, None] == key_seg[None, :]) & (key_pos[None, :] <= local_pos[:, None])
    cos_part, sin_part = rope_tables(query_off, RD)
    (
        gain_in_full,
        qdown_full,
        gain_q_full,
        qup_full,
        ldown_full,
        gain_l_full,
        lup_full,
        aout_full,
        gain_f_full,
    ) = (
        lax.all_gather(gain_attn, "shard", axis=0, tiled=True),
        lax.all_gather(query_down, "shard", axis=0, tiled=True),
        lax.all_gather(gain_query, "shard", axis=0, tiled=True),
        lax.all_gather(query_up, "shard", axis=0, tiled=True),
        lax.all_gather(latent_down, "shard", axis=0, tiled=True),
        lax.all_gather(gain_latent, "shard", axis=0, tiled=True),
        lax.all_gather(latent_up, "shard", axis=0, tiled=True),
        lax.all_gather(attn_out, "shard", axis=0, tiled=True),
        lax.all_gather(gain_ffn, "shard", axis=0, tiled=True),
    )
    inputs = tokens[0].astype(wide_type)
    normed, norm_in_back = jax.vjp(rms_scale, inputs, gain_in_full.astype(wide_type))
    normed_low = normed.astype(low_type)
    query_lat = jnp.dot(normed_low, qdown_full, preferred_element_type=wide_type)
    query_norm, norm_q_back = jax.vjp(rms_scale, query_lat, gain_q_full.astype(wide_type))
    query_low = query_norm.astype(low_type)
    query_proj = jnp.dot(query_low, qup_full, preferred_element_type=wide_type).reshape(
        tok_rows, H, head_dim
    )

    def query_rope(values):
        return jnp.concatenate(
            [
                values[..., :ND],
                rotate(values[..., ND:], cos_part[:, None, :], sin_part[:, None, :]),
            ],
            axis=-1,
        )

    query_rot, query_back = jax.vjp(query_rope, query_proj)
    query_used = query_rot.astype(low_type)
    latent_proj = jnp.dot(normed_low, ldown_full, preferred_element_type=wide_type)
    latent_norm, norm_l_back = jax.vjp(
        rms_scale, latent_proj[:, :KR], gain_l_full.astype(wide_type)
    )
    latent_low = latent_norm.astype(low_type)

    def key_rotate(values):
        return rotate(values, cos_part, sin_part)

    key_rot, key_back = jax.vjp(key_rotate, latent_proj[:, KR:])
    key_rope = key_rot.astype(low_type)
    keyvals = jnp.dot(latent_low, lup_full, preferred_element_type=wide_type).astype(low_type)
    all_keyvals, all_rope = (
        lax.all_gather(keyvals, "rep", axis=0, tiled=True),
        lax.all_gather(key_rope, "rep", axis=0, tiled=True),
    )
    queries = query_used.reshape(tok_rows, group_count, group_size, head_dim).transpose(1, 0, 2, 3)
    key_groups = all_keyvals.reshape(seq_len, group_count, group_size, ND + VD).transpose(
        1, 0, 2, 3
    )

    def scores_of(query_blk, key_blk):
        nope_part = jnp.einsum(
            "thd,shd->hts", query_blk[..., :ND], key_blk[..., :ND], preferred_element_type=wide_type
        )
        rope_part = jnp.einsum(
            "thd,sd->hts", query_blk[..., ND:], all_rope, preferred_element_type=wide_type
        )
        return jnp.where(allowed[None], (nope_part + rope_part) * softmax_scale, masked_score)

    def forward_group(carry, blocks):
        query_blk, key_blk = blocks
        scores = scores_of(query_blk, key_blk)
        row_max = jnp.max(scores, axis=-1, keepdims=True)
        exp_scores = jnp.exp(scores - row_max)
        totals = jnp.sum(exp_scores, axis=-1, keepdims=True)
        probs = (exp_scores / totals).astype(low_type)
        mixed = jnp.einsum(
            "hts,shd->thd", probs, key_blk[..., ND:], preferred_element_type=wide_type
        )
        return (carry, (mixed, row_max + jnp.log(totals)))

    start_carry = jnp.zeros((), wide_type)
    final_carry, (mixed_groups, log_totals) = lax.scan(
        forward_group, start_carry, (queries, key_groups)
    )
    mixed_low = mixed_groups.transpose(1, 0, 2, 3).reshape(tok_rows, H * VD).astype(low_type)
    branch = jnp.dot(mixed_low, aout_full, preferred_element_type=wide_type)
    residual = inputs + residual_scale * branch
    normed_ffn, norm_f_back = jax.vjp(rms_scale, residual, gain_f_full.astype(wide_type))
    ffn_low = normed_ffn.astype(low_type)
    gate_full, up_full, down_full = (
        lax.all_gather(w_gate, "shard", axis=0, tiled=True),
        lax.all_gather(w_up, "shard", axis=0, tiled=True),
        lax.all_gather(w_down, "shard", axis=0, tiled=True),
    )
    gate_pre = jnp.dot(ffn_low, gate_full, preferred_element_type=wide_type)
    up_pre = jnp.dot(ffn_low, up_full, preferred_element_type=wide_type)
    hidden, act_back = jax.vjp(swiglu, gate_pre, up_pre)
    hidden_low = hidden.astype(low_type)
    ffn_branch = jnp.dot(hidden_low, down_full, preferred_element_type=wide_type)
    layer_out = residual + residual_scale * ffn_branch
    grad_out = cotangent[0].astype(wide_type)
    grad_down_in = (residual_scale * grad_out).astype(low_type)
    gate_back_w, up_back_w, down_back_w = (
        lax.all_gather(w_gate, "shard", axis=0, tiled=True),
        lax.all_gather(w_up, "shard", axis=0, tiled=True),
        lax.all_gather(w_down, "shard", axis=0, tiled=True),
    )
    grad_hidden = outer_cols(grad_down_in, down_back_w)
    grad_gate_f, grad_up_f = act_back(grad_hidden)
    grad_gate = grad_gate_f.astype(low_type)
    grad_up = grad_up_f.astype(low_type)
    grad_ffn_in = outer_cols(grad_gate, gate_back_w) + outer_cols(grad_up, up_back_w)
    down_grad = lax.psum_scatter(
        inner_rows(hidden_low, grad_down_in).astype(jnp.bfloat16),
        "shard",
        scatter_dimension=0,
        tiled=True,
    )
    gate_up_in = jnp.concatenate([grad_gate, grad_up], axis=1)
    gate_up_grad = lax.psum_scatter(
        inner_rows(ffn_low, gate_up_in).astype(jnp.bfloat16),
        "shard",
        scatter_dimension=0,
        tiled=True,
    ).astype(jnp.float32)
    gate_grad = gate_up_grad[:, :FF]
    up_grad = gate_up_grad[:, FF:]
    grad_res_norm, grad_gain_ffn = norm_f_back(grad_ffn_in)
    grad_resid = grad_out + grad_res_norm
    qdown_back, qup_back, ldown_back, lup_back, aout_back = (
        lax.all_gather(query_down, "shard", axis=0, tiled=True),
        lax.all_gather(query_up, "shard", axis=0, tiled=True),
        lax.all_gather(latent_down, "shard", axis=0, tiled=True),
        lax.all_gather(latent_up, "shard", axis=0, tiled=True),
        lax.all_gather(attn_out, "shard", axis=0, tiled=True),
    )
    grad_branch = (residual_scale * grad_resid).astype(low_type)
    aout_grad = inner_rows(mixed_low, grad_branch)
    grad_mixed = outer_cols(grad_branch, aout_back).astype(low_type)
    grad_groups = grad_mixed.reshape(tok_rows, group_count, group_size, VD).transpose(1, 0, 2, 3)

    def backward_group(rope_acc, blocks):
        query_blk, key_blk, grad_blk, log_blk = blocks
        scores = scores_of(query_blk, key_blk)
        probs = jnp.exp(scores - log_blk)
        grad_probs = jnp.einsum(
            "thd,shd->hts", grad_blk, key_blk[..., ND:], preferred_element_type=wide_type
        )
        delta = jnp.sum(probs * grad_probs, axis=-1, keepdims=True)
        grad_scores = (probs * (grad_probs - delta)).astype(low_type)
        grad_query = (
            jnp.concatenate(
                [
                    jnp.einsum(
                        "hts,shd->thd",
                        grad_scores,
                        key_blk[..., :ND],
                        preferred_element_type=wide_type,
                    ),
                    jnp.einsum(
                        "hts,sd->thd", grad_scores, all_rope, preferred_element_type=wide_type
                    ),
                ],
                axis=-1,
            )
            * softmax_scale
        )
        grad_key = (
            jnp.einsum(
                "hts,thd->shd", grad_scores, query_blk[..., :ND], preferred_element_type=wide_type
            )
            * softmax_scale
        )
        grad_value = jnp.einsum(
            "hts,thd->shd", probs.astype(low_type), grad_blk, preferred_element_type=wide_type
        )
        rope_acc = (
            rope_acc
            + jnp.einsum(
                "hts,thd->sd", grad_scores, query_blk[..., ND:], preferred_element_type=wide_type
            )
            * softmax_scale
        )
        return (rope_acc, (grad_query, jnp.concatenate([grad_key, grad_value], axis=-1)))

    rope_start = jnp.zeros((seq_len, RD), wide_type)
    rope_sum, (grad_q_groups, grad_kv_groups) = lax.scan(
        backward_group, rope_start, (queries, key_groups, grad_groups, log_totals)
    )
    grad_kv_all = grad_kv_groups.transpose(1, 0, 2, 3).reshape(seq_len, H * (ND + VD))
    grad_kv_own, grad_rope_own = (
        lax.psum_scatter(
            grad_kv_all.astype(jnp.bfloat16), "rep", scatter_dimension=0, tiled=True
        ).astype(jnp.float32),
        lax.psum_scatter(
            rope_sum.astype(jnp.bfloat16), "rep", scatter_dimension=0, tiled=True
        ).astype(jnp.float32),
    )
    grad_q_full = grad_q_groups.transpose(1, 0, 2, 3).reshape(tok_rows, H, head_dim)
    grad_q_proj = query_back(grad_q_full)[0].reshape(tok_rows, H * head_dim).astype(low_type)
    qup_grad = inner_rows(query_low, grad_q_proj)
    grad_q_lat_f, grad_gain_query = norm_q_back(outer_cols(grad_q_proj, qup_back))
    grad_q_lat = grad_q_lat_f.astype(low_type)
    grad_kv_low = grad_kv_own.astype(low_type)
    lup_grad = inner_rows(latent_low, grad_kv_low)
    grad_lat_c, grad_gain_latent = norm_l_back(outer_cols(grad_kv_low, lup_back))
    grad_lat_r = key_back(grad_rope_own)[0]
    grad_lat = jnp.concatenate([grad_lat_c, grad_lat_r], axis=1).astype(low_type)
    qdown_grad = inner_rows(normed_low, grad_q_lat)
    ldown_grad = inner_rows(normed_low, grad_lat)
    grad_normed = outer_cols(grad_q_lat, qdown_back) + outer_cols(grad_lat, ldown_back)
    grad_in_norm, grad_gain_attn = norm_in_back(grad_normed)
    tokens_grad = (grad_resid + grad_in_norm).astype(low_type)
    (
        owned_gain_attn,
        owned_qdown,
        owned_gain_query,
        owned_qup,
        owned_ldown,
        owned_gain_latent,
        owned_lup,
        owned_aout,
        owned_gain_ffn,
    ) = (
        lax.psum_scatter(
            grad_gain_attn.astype(jnp.bfloat16), "shard", scatter_dimension=0, tiled=True
        ).astype(jnp.float32),
        lax.psum_scatter(
            qdown_grad.astype(jnp.bfloat16), "shard", scatter_dimension=0, tiled=True
        ).astype(jnp.float32),
        lax.psum_scatter(
            grad_gain_query.astype(jnp.bfloat16), "shard", scatter_dimension=0, tiled=True
        ).astype(jnp.float32),
        lax.psum_scatter(
            qup_grad.astype(jnp.bfloat16), "shard", scatter_dimension=0, tiled=True
        ).astype(jnp.float32),
        lax.psum_scatter(
            ldown_grad.astype(jnp.bfloat16), "shard", scatter_dimension=0, tiled=True
        ).astype(jnp.float32),
        lax.psum_scatter(
            grad_gain_latent.astype(jnp.bfloat16), "shard", scatter_dimension=0, tiled=True
        ).astype(jnp.float32),
        lax.psum_scatter(
            lup_grad.astype(jnp.bfloat16), "shard", scatter_dimension=0, tiled=True
        ).astype(jnp.float32),
        lax.psum_scatter(
            aout_grad.astype(jnp.bfloat16), "shard", scatter_dimension=0, tiled=True
        ).astype(jnp.float32),
        lax.psum_scatter(
            grad_gain_ffn.astype(jnp.bfloat16), "shard", scatter_dimension=0, tiled=True
        ).astype(jnp.float32),
    )
    summed = (
        lax.psum(owned_gain_attn.astype(jnp.bfloat16), "rep").astype(jnp.float32),
        lax.psum(owned_qdown.astype(jnp.bfloat16), "rep").astype(jnp.float32),
        lax.psum(owned_gain_query.astype(jnp.bfloat16), "rep").astype(jnp.float32),
        lax.psum(owned_qup.astype(jnp.bfloat16), "rep").astype(jnp.float32),
        lax.psum(owned_ldown.astype(jnp.bfloat16), "rep").astype(jnp.float32),
        lax.psum(owned_gain_latent.astype(jnp.bfloat16), "rep").astype(jnp.float32),
        lax.psum(owned_lup.astype(jnp.bfloat16), "rep").astype(jnp.float32),
        lax.psum(owned_aout.astype(jnp.bfloat16), "rep").astype(jnp.float32),
        lax.psum(owned_gain_ffn.astype(jnp.bfloat16), "rep").astype(jnp.float32),
        lax.psum(gate_grad.astype(jnp.bfloat16), "rep").astype(jnp.float32),
        lax.psum(up_grad.astype(jnp.bfloat16), "rep").astype(jnp.float32),
        lax.psum(down_grad, "rep").astype(jnp.float32),
    )
    return (
        layer_out.astype(low_type)[None],
        tokens_grad[None],
        summed[0],
        summed[1],
        summed[2],
        summed[3],
        summed[4],
        summed[5],
        summed[6],
        summed[7],
        summed[8],
        summed[9],
        summed[10],
        summed[11],
    )


def solution(mesh):
    placed = (
        P("shard", "rep", None),
        P("shard", "rep", None),
        P("shard", None),
        P("shard"),
        P("shard", None),
        P("shard"),
        P("shard", None),
        P("shard", None),
        P("shard"),
        P("shard", None),
        P("shard", None),
        P("shard"),
        P("shard", None),
        P("shard", None),
        P("shard", None),
    )
    fits = mesh.shape["rep"] == 4 and mesh.shape["shard"] == 8
    return jax.shard_map(
        column_body if fits else body,
        mesh=mesh,
        in_specs=placed,
        out_specs=(
            P("shard", "rep", None),
            P("shard", "rep", None),
            P("shard"),
            P("shard", None),
            P("shard"),
            P("shard", None),
            P("shard", None),
            P("shard"),
            P("shard", None),
            P("shard", None),
            P("shard"),
            P("shard", None),
            P("shard", None),
            P("shard", None),
        ),
        check_vma=False,
    )
```

```python
import functools
import math

import jax
import jax.numpy as jnp
from jax import lax
from jax.experimental import pallas as pl
from jax.experimental.pallas import tpu as pltpu
from jax.sharding import PartitionSpec as P

KR = 256
H = 40
ND = 64
RD = 32
VD = 64
FF = 6400


epsilon = 1e-05
residual_scale = 1.4 / math.sqrt(62.0)
rope_base = 10000.0
masked_score = -1e30


def rms_scale(values, gain):
    return values * lax.rsqrt(jnp.mean(values * values, axis=-1, keepdims=True) + epsilon) * gain


def rotate(values, cos_part, sin_part):
    midpoint = values.shape[-1] // 2
    former = values[..., :midpoint]
    latter = values[..., midpoint:]
    return jnp.concatenate(
        [former * cos_part - latter * sin_part, latter * cos_part + former * sin_part], axis=-1
    )


def segment_of(lengths, positions):
    doc_ends = jnp.cumsum(lengths)
    doc_starts = doc_ends - lengths
    segment = jnp.sum((positions[:, None] >= doc_ends[None, :]).astype(jnp.int32), axis=1)
    chosen = segment[:, None] == jnp.arange(lengths.shape[0], dtype=jnp.int32)[None, :]
    offsets = positions - jnp.sum(jnp.where(chosen, doc_starts[None, :], 0), axis=1)
    return (segment, offsets)


def rope_tables(offsets, rope_width):
    exponents = jnp.arange(0, rope_width, 2, dtype=jnp.float32) / rope_width
    angles = offsets.astype(jnp.float32)[:, None] * (rope_base ** (-exponents))[None, :]
    return (jnp.cos(angles), jnp.sin(angles))


def swiglu(gate_vals, up_vals):
    return jax.nn.silu(gate_vals) * up_vals


def inner_rows(leading, trailing):
    return lax.dot_general(
        leading, trailing, (((0,), (0,)), ((), ())), preferred_element_type=jnp.float32
    )


def outer_cols(leading, trailing):
    return lax.dot_general(
        leading, trailing, (((1,), (1,)), ((), ())), preferred_element_type=jnp.float32
    )


MESH = pl.DeviceIdType.MESH
ANY = pl.BlockSpec(memory_space=pl.ANY)

def place():
    rep = lax.axis_index("rep")
    shard = lax.axis_index("shard")
    zpos, core = shard // 2, shard % 2
    return rep, zpos, core

def mult(value, by):
    return pl.multiple_of(value, by)

def greet(rep, zpos, core, plane=0, column=False):
    barrier = pltpu.get_barrier_semaphore()
    shard = zpos * 2 + core

    def signal(r, s):
        pl.semaphore_signal(barrier, inc=1, device_id=(r, s), device_id_type=MESH)

    if column:
        for m in range(1, 8):
            signal(rep, column_place(zpos, core, m))
        count = 7
    else:
        signal(rep, zpos * 2 + 1 - core)

        @pl.when(zpos > 0)
        def _():
            signal(rep, shard - 2)

        @pl.when(zpos < 3)
        def _():
            signal(rep, shard + 2)

        count = 1 + jnp.minimum(zpos, 1) + jnp.minimum(3 - zpos, 1)
    if plane:
        for other in plane_places(rep)[:plane]:
            signal(other, shard)
        count = count + plane
    pl.semaphore_wait(barrier, count)


def plane_places(rep):
    return rep + 1 - 2 * (rep % 2), (rep + 2) % 4, 3 - rep


def column_place(zpos, core, m, back=False):
    step = 4 - m // 2 if back else m // 2
    return ((zpos + step) % 4) * 2 + (core + m) % 2


def remote(src, dst, ssem, rsem, r, s):
    return pltpu.make_async_remote_copy(
        src_ref=src, dst_ref=dst, send_sem=ssem, recv_sem=rsem, device_id=(r, s), device_id_type=MESH
    )


def dma_sems(*dims):
    return pltpu.SemaphoreType.DMA(dims)


def head_tile(h):
    return pl.ds(pl.multiple_of(h * 128, 128), 128)


def turn(values, tables, back=False):
    keep, high, low_part = tables
    if back:
        return values * keep + pltpu.roll(values * high, 112, 1) + pltpu.roll(values * low_part, 16, 1)
    return values * keep + pltpu.roll(values, 16, 1) * high + pltpu.roll(values, 112, 1) * low_part


def dot_nt(a, b):
    return lax.dot_general(a, b, (((1,), (1,)), ((), ())), preferred_element_type=jnp.float32)


def dot_tn(a, b):
    return lax.dot_general(a, b, (((0,), (0,)), ((), ())), preferred_element_type=jnp.float32)


def attend_kernel(scale, proj, kv, rope, bias, turns, query, mixed, logs):
    low = jnp.bfloat16
    heads = kv.shape[1] // 128
    lane = lax.broadcasted_iota(jnp.int32, (1, 128), 1)
    first = lane < 64
    logs[...] = jnp.zeros_like(logs)

    def one(h):
        q = turn(proj[:, head_tile(h)], (turns[0], turns[1], turns[2])).astype(low)
        query[:, head_tile(h)] = q
        keyval = kv[:, head_tile(h)]
        key = jnp.where(first, keyval, rope[...])
        scores = dot_nt(q, key) * scale + bias[...]
        top = jnp.max(scores, axis=1, keepdims=True)
        grown = jnp.exp(scores - top)
        total = jnp.sum(grown, axis=1, keepdims=True)
        probs = (grown / total).astype(low)
        logs[...] = jnp.where(lane == h, top + jnp.log(total), logs[...])
        return jnp.dot(probs, keyval, preferred_element_type=jnp.float32)

    def pair(i, carry):
        even, odd = one(2 * i), one(2 * i + 1)
        mixed[:, head_tile(i)] = jnp.where(first, pltpu.roll(even, 64, 1), odd).astype(low)
        return carry

    lax.fori_loop(0, heads // 2, pair, 0)


def attend(scale, proj, kv, rope, bias, turns):
    rows, cols = proj.shape
    return pl.pallas_call(
        functools.partial(attend_kernel, scale),
        out_shape=[jax.ShapeDtypeStruct((rows, cols), jnp.bfloat16), jax.ShapeDtypeStruct((rows, cols // 2), jnp.bfloat16),
                   jax.ShapeDtypeStruct((rows, 128), jnp.float32)],
        in_specs=[VMEM] * 5, out_specs=[VMEM] * 3,
        compiler_params=pltpu.CompilerParams(vmem_limit_bytes=56 * 2**20),
    )(proj, kv, rope, bias, turns)


def attend_back_heads(scale, query, kv, rope, bias, turns, logs, grad, grad_query, grad_packed, grad_kv, grad_rope, left):
    low = jnp.bfloat16
    rows = query.shape[0]
    lane = lax.broadcasted_iota(jnp.int32, (1, 128), 1)
    first = lane < 64

    def one(h, grad_value):
        q = query[:, head_tile(h)]
        keyval = kv[:, head_tile(h)]
        key = jnp.where(first, keyval, rope[...])
        left[0:rows, 0:128] = q
        left[rows:, 128:256] = grad_value
        both = dot_nt(left[...], jnp.concatenate([key, keyval], axis=1))
        log = jnp.sum(jnp.where(lane == h, logs[...], 0.0), axis=1, keepdims=True)
        probs = jnp.exp(both[:rows] * scale + bias[...] - log)
        weighed = probs * both[rows:]
        delta = jnp.sum(weighed, axis=1, keepdims=True)
        grad_scores = (weighed - probs * delta).astype(low)
        grad_q = jnp.dot(grad_scores, key, preferred_element_type=jnp.float32) * scale
        grad_q = turn(grad_q, (turns[0], turns[1], turns[2]), True)
        grad_query[:, head_tile(h)] = grad_q.astype(low)
        out = dot_tn(jnp.concatenate([grad_scores, probs.astype(low)], axis=0), left[...])
        grad_key = out[:, :128] * scale
        grad_rope[...] += grad_key
        grad_kv[:, head_tile(h)] = jnp.where(first, grad_key, out[:, 128:]).astype(low)
        return grad_q

    def quarter(i, carry):
        rotary = jnp.zeros((rows, 128), jnp.float32)
        for j in range(5):
            both = grad[:, head_tile(5 * i + j)].astype(jnp.float32)
            even = one(10 * i + 2 * j, jnp.where(first, 0.0, pltpu.roll(both, 64, 1)).astype(low))
            odd = one(10 * i + 2 * j + 1, jnp.where(first, 0.0, both).astype(low))
            grad_packed[:, head_tile(8 * i + j)] = jnp.where(first, even, pltpu.roll(odd, 64, 1)).astype(low)
            for k, got in ((2 * j, even), (2 * j + 1, odd)):
                at = 32 * (k % 4)
                moved = got if at == 64 else pltpu.roll(got, (at + 64) % 128, 1)
                rotary = jnp.where((lane >= at) & (lane < at + 32), moved, rotary)
                if k % 4 == 3 or k == 9:
                    grad_packed[:, head_tile(8 * i + 5 + k // 4)] = rotary.astype(low)
                    rotary = jnp.zeros((rows, 128), jnp.float32)
        return carry

    return quarter


def widen_kernel(*refs):
    n = len(refs) // 2
    for strips, out in zip(refs[:n], refs[n:]):
        each = out.shape[1] // 8
        for s in range(8):
            first, last = s * each // 128, (s + 1) * each // 128
            tiles = strips[s, 0].astype(jnp.float32)
            if s * each % 128:
                shared = strips[s - 1, 0, :, (first - (s - 1) * each // 128) * 128 :][:, :128]
                out[:, first * 128 : first * 128 + 128] = tiles[:, :128] + shared.astype(jnp.float32)
                first_full = first + 1
            else:
                first_full = first
            base = s * each // 128
            out[:, first_full * 128 : last * 128] = tiles[:, (first_full - base) * 128 : (last - base) * 128]


def widen(arrays, cols):
    _, quarters, rows, strip = arrays[0].shape
    n = len(arrays)
    return pl.pallas_call(
        widen_kernel, grid=(quarters,),
        out_shape=[jax.ShapeDtypeStruct((quarters * rows, cols), jnp.float32)] * n,
        in_specs=[pl.BlockSpec((8, 1, rows, strip), lambda q: (0, q, 0, 0))] * n,
        out_specs=[pl.BlockSpec((rows, cols), lambda q: (q, 0))] * n,
        compiler_params=pltpu.CompilerParams(vmem_limit_bytes=56 * 2**20),
    )(*arrays)


class Gather:
    def __init__(self, ins, outs, sems):
        self.ins, self.outs = ins, outs
        self.zsend, self.zrecv, self.csend, self.crecv, self.own = sems
        self.rep, self.zpos, self.core = place()
        self.held = None

    @staticmethod
    def scratch(n):
        return [dma_sems(2, 3, n), dma_sems(2, 3, n), dma_sems(7, n), dma_sems(7, n), dma_sems(2, n)]

    def at(self, a, z, c):
        rows = self.ins[a].shape[0]
        return self.outs[a].at[pl.ds(mult((z * 2 + c) * rows, rows), rows)]

    def hop_copy(self, a, way, hop, z, src=None):
        dst = self.at(a, z, self.core)
        return remote(dst if src is None else src, dst, self.zsend.at[way, hop, a], self.zrecv.at[way, hop, a],
                      self.rep, (self.zpos + (1 - 2 * way)) * 2 + self.core)

    def core_copy(self, a, slot, z, c, src=None):
        dst = self.at(a, z, c)
        return remote(dst if src is None else src, dst, self.csend.at[slot, a], self.crecv.at[slot, a],
                      self.rep, self.zpos * 2 + 1 - self.core)

    def keep(self, a):
        return pltpu.make_async_copy(self.ins[a], self.at(a, self.zpos, self.core), self.own.at[0, a])

    def onward(self, way):
        return self.zpos < 3 if way == 0 else self.zpos > 0

    def source(self, way, hop):
        z = self.zpos - hop if way == 0 else self.zpos + hop
        return z, (z >= 0 if way == 0 else z <= 3)

    def start(self, which=None):
        which = range(len(self.ins)) if which is None else which
        for way in range(2):
            @pl.when(self.onward(way))
            def _():
                for a in which:
                    self.hop_copy(a, way, 0, self.zpos, src=self.ins[a]).start()
        for a in which:
            self.core_copy(a, 0, self.zpos, self.core, src=self.ins[a]).start()
            self.keep(a).start()

    def hop(self, hop, which=None):
        which = range(len(self.ins)) if which is None else which
        for way in range(2):
            z, there = self.source(way, hop)

            @pl.when(there)
            def _():
                for a in which:
                    self.hop_copy(a, way, hop - 1, z).wait_recv()
                    if hop < 3:
                        @pl.when(self.onward(way))
                        def _():
                            self.hop_copy(a, way, hop, z).start()
                    self.core_copy(a, way * 3 + hop, z, self.core).start()

    def finish(self):
        arrays = range(len(self.ins))
        for way in range(2):
            for hop in range(3):
                z, there = self.source(way, hop)

                @pl.when(there & self.onward(way))
                def _():
                    for a in arrays:
                        self.hop_copy(a, way, hop, z).wait_send()
        for a in arrays:
            self.keep(a).wait()
            self.core_copy(a, 0, self.zpos, self.core, src=self.ins[a]).wait_send()
            self.core_copy(a, 0, self.zpos, 1 - self.core).wait_recv()
        for way in range(2):
            for hop in range(1, 4):
                z, there = self.source(way, hop)

                @pl.when(there)
                def _():
                    for a in arrays:
                        self.core_copy(a, way * 3 + hop, z, self.core).wait_send()
                        self.core_copy(a, way * 3 + hop, z, 1 - self.core).wait_recv()


class Total:
    def __init__(self, term, out, bufs, sems):
        self.term, self.out = term, out
        self.mine, self.theirs, self.stage, self.landed = bufs
        self.zsend, self.zrecv, self.csend, self.crecv, self.own = sems
        self.rep, self.zpos, self.core = place()

    @staticmethod
    def scratch(term):
        four = pltpu.VMEM((4,) + term.shape[1:], term.dtype)
        return [four] * 3 + [pltpu.VMEM((2, 4) + term.shape[1:], term.dtype),
                             dma_sems(2, 4), dma_sems(2, 4), dma_sems(4), dma_sems(4), dma_sems(4)]

    def pair_copy(self, z):
        return remote(self.term.at[z * 2 + 1 - self.core], self.theirs.at[z], self.csend.at[z], self.crecv.at[z],
                      self.rep, self.zpos * 2 + 1 - self.core)

    def load(self, z):
        return pltpu.make_async_copy(self.term.at[z * 2 + self.core], self.mine.at[z], self.own.at[z])

    def hop_copy(self, way, z):
        return remote(self.stage.at[z], self.landed.at[way, z], self.zsend.at[way, z], self.zrecv.at[way, z],
                      self.rep, (self.zpos + (1 - 2 * way)) * 2 + self.core)

    def each(self, step):
        for way in range(2):
            behind = self.zpos if way == 0 else 3 - self.zpos
            target = self.zpos + 3 - step if way == 0 else self.zpos - 3 + step
            yield way, behind, target, (behind <= step) & (behind < 3)

    def start(self):
        for z in (3, 0, 2, 1):
            self.pair_copy(z).start()
            self.load(z).start()

    def pair(self):
        for z in (3, 0, 2, 1):
            self.load(z).wait()
            self.pair_copy(z).wait_recv()

    def step(self, step):
        wide = jnp.float32
        for way, behind, target, there in self.each(step):
            @pl.when(there)
            def _():
                total = self.mine[target].astype(wide) + self.theirs[target].astype(wide)

                @pl.when(behind == 0)
                def _():
                    self.stage[target] = total.astype(self.stage.dtype)

                @pl.when(behind > 0)
                def _():
                    self.hop_copy(way, target).wait_recv()
                    self.stage[target] = (total + self.landed[way, target].astype(wide)).astype(self.stage.dtype)
                self.hop_copy(way, target).start()

    def finish(self):
        wide = jnp.float32
        self.out[...] = self.mine[self.zpos].astype(wide) + self.theirs[self.zpos].astype(wide)
        for way in range(2):
            @pl.when(self.zpos > 0 if way == 0 else self.zpos < 3)
            def _():
                self.hop_copy(way, self.zpos).wait_recv()
                self.out[...] += self.landed[way, self.zpos].astype(wide)
        for step in range(3):
            for way, behind, target, there in self.each(step):
                @pl.when(there)
                def _():
                    self.hop_copy(way, target).wait_send()
        for z in range(4):
            self.pair_copy(z).wait_send()


def kernel_params(cid):
    return pltpu.CompilerParams(collective_id=cid, has_side_effects=True, vmem_limit_bytes=56 * 2**20)


VMEM = pl.BlockSpec(memory_space=pltpu.VMEM)


def chain_gather_kernel(n, *refs):
    gather = Gather(refs[:n], refs[n : 2 * n], refs[2 * n :])
    greet(*place())
    gather.start()
    for hop in range(1, 4):
        gather.hop(hop)
    gather.finish()


def chain_gather(cid, *arrays):
    n = len(arrays)
    out = [jax.ShapeDtypeStruct((a.shape[0] * 8,) + a.shape[1:], a.dtype) for a in arrays]
    return pl.pallas_call(
        functools.partial(chain_gather_kernel, n), out_shape=out, in_specs=[ANY] * n, out_specs=[ANY] * n,
        scratch_shapes=Gather.scratch(n), compiler_params=kernel_params(cid),
    )(*arrays)


def ffn_gather_kernel(tokens, partial, grad, down, tokens_all, up, grad_hidden, *scratch):
    del partial
    rep, zpos, core = place()
    gather = Gather((tokens,), (tokens_all,), scratch[:5])
    piece = up.shape[0] // 32

    def part(m):
        first = column_place(zpos, core, m, True) * (4 * piece)
        return lambda p: up.at[pl.ds(mult(first + p * piece, 16), piece)]

    spread = PlaneGather([(None, part(m), m % 2) for m in ColumnSwap.near], scratch[5:8])
    greet(rep, zpos, core, plane=2)
    gather.start()
    spread.start()
    chunk = grad.shape[0] // 4

    def product(i):
        at = pl.ds(mult(i * chunk, chunk), chunk)
        grad_hidden[at] = dot_nt(grad[at], down[...])

    def step(i, carry):
        product(i)

        @pl.when(i == 1)
        def _():
            gather.hop(1)

        @pl.when(i == 3)
        def _():
            gather.hop(2)
        return carry

    lax.fori_loop(0, 4, step, 0)
    for i in range(7):
        spread.middle(i)
    gather.hop(3)
    gather.finish()
    spread.finish()


def ffn_gather(cid, tokens, partial, grad, down):
    return pl.pallas_call(
        ffn_gather_kernel,
        out_shape=[jax.ShapeDtypeStruct((8 * tokens.shape[0], tokens.shape[1]), tokens.dtype),
                   jax.ShapeDtypeStruct(partial.shape, partial.dtype),
                   jax.ShapeDtypeStruct((grad.shape[0], down.shape[0]), jnp.float32)],
        in_specs=[ANY, ANY, VMEM, VMEM], out_specs=[ANY, ANY, VMEM], input_output_aliases={1: 1},
        scratch_shapes=Gather.scratch(1) + PlaneGather.scratch(7),
        compiler_params=kernel_params(cid),
    )(tokens, partial, grad, down)


class PlaneSum:
    def __init__(self, items, bufs, sems):
        self.items = items
        self.landed, self.stage, self.last = bufs
        self.asend, self.arecv, self.bsend, self.brecv = sems
        self.rep, self.zpos, self.core = place()
        self.shard = self.zpos * 2 + self.core

    @staticmethod
    def scratch(shapes, dtype):
        n = len(shapes)
        return ([pltpu.VMEM((2,) + s, dtype) for s in shapes] + [pltpu.VMEM(s, dtype) for s in shapes] * 2
                + [dma_sems(n, 2), dma_sems(n, 2), dma_sems(n), dma_sems(n)])

    @staticmethod
    def split(refs, n):
        return (refs[:n], refs[n : 2 * n], refs[2 * n : 3 * n]), refs[3 * n : 3 * n + 4], refs[3 * n + 4 :]

    def ways(self, i):
        xrep, yrep, drep = plane_places(self.rep)
        return (xrep, yrep, drep) if self.items[i][2] == 0 else (yrep, xrep, drep)

    def out(self, i, k):
        near, _, far = self.ways(i)
        return remote(self.items[i][0](far if k else near), self.landed[i].at[k], self.asend.at[i, k], self.arecv.at[i, k],
                      near, self.shard)

    def on(self, i):
        return remote(self.stage[i], self.last[i], self.bsend.at[i], self.brecv.at[i], self.ways(i)[1], self.shard)

    def start(self, which=None):
        for i in range(len(self.items)) if which is None else which:
            for k in (1, 0):
                self.out(i, k).start()

    def middle(self, i):
        wide = jnp.float32
        self.out(i, 1).wait_recv()
        term = self.items[i][0](self.ways(i)[1])
        self.stage[i][...] = (term[...].astype(wide) + self.landed[i][1].astype(wide)).astype(self.stage[i].dtype)
        self.on(i).start()

    def end(self, i):
        wide = jnp.float32
        self.out(i, 0).wait_recv()
        self.on(i).wait_recv()
        total = self.items[i][0](self.rep)[...].astype(wide) + self.landed[i][0].astype(wide)
        own = self.items[i][1]
        own[...] = (total + self.last[i][...].astype(wide)).astype(own.dtype)

    def finish(self):
        for i in range(len(self.items)):
            for k in range(2):
                self.out(i, k).wait_send()
            self.on(i).wait_send()


class PlaneGather:
    def __init__(self, items, sems):
        self.items = items
        self.send, self.recv, self.own = sems
        self.rep, self.zpos, self.core = place()
        self.shard = self.zpos * 2 + self.core

    @staticmethod
    def scratch(n):
        return [dma_sems(3, n), dma_sems(3, n), dma_sems(n)]

    def copy(self, i, kind, quarter, to):
        own, part, _ = self.items[i]
        dst = part(quarter)
        return remote(dst if kind == 2 or own is None else own, dst, self.send.at[kind, i], self.recv.at[kind, i], to, self.shard)

    def keep(self, i):
        return pltpu.make_async_copy(self.items[i][0], self.items[i][1](self.rep), self.own.at[i])

    def start(self, which=None):
        xrep, yrep, _ = plane_places(self.rep)
        for i in range(len(self.items)) if which is None else which:
            self.copy(i, 0, self.rep, xrep).start()
            self.copy(i, 1, self.rep, yrep).start()
            if self.items[i][0] is not None:
                self.keep(i).start()

    def middle(self, i):
        xrep, yrep, _ = plane_places(self.rep)
        self.copy(i, 0, xrep, xrep).wait_recv()
        if self.items[i][2] == 0:
            self.copy(i, 2, xrep, yrep).start()
        self.copy(i, 1, yrep, yrep).wait_recv()
        if self.items[i][2] == 1:
            self.copy(i, 2, yrep, xrep).start()

    def finish(self):
        xrep, yrep, drep = plane_places(self.rep)
        for i, (own, _, first) in enumerate(self.items):
            self.copy(i, 0, self.rep, xrep).wait_send()
            self.copy(i, 1, self.rep, yrep).wait_send()
            self.copy(i, 2, *((xrep, yrep) if first == 0 else (yrep, xrep))).wait_send()
            self.copy(i, 2, drep, drep).wait_recv()
            if own is not None:
                self.keep(i).wait()


class ColumnSwap:
    def __init__(self, items, sems, keeps=True):
        self.items, self.keeps = items, keeps
        self.send, self.recv, self.own = sems
        self.rep, self.zpos, self.core = place()
        self.shard = self.zpos * 2 + self.core

    near = (1, 2, 6, 3, 7, 4, 5)

    @staticmethod
    def scratch(n):
        return [dma_sems(7, n), dma_sems(7, n), dma_sems(n)]

    def copy(self, i, m, back=False):
        s2 = column_place(self.zpos, self.core, m, back)
        block, there = self.items[i]
        return remote(block(s2), there(s2 if back else self.shard), self.send.at[m - 1, i], self.recv.at[m - 1, i], self.rep, s2)

    def keep(self, i):
        return pltpu.make_async_copy(self.items[i][0](self.shard), self.items[i][1](self.shard), self.own.at[i])

    def start(self):
        for m in self.near:
            for i in range(len(self.items)):
                self.copy(i, m).start()
        for i in range(len(self.items) if self.keeps else 0):
            self.keep(i).start()

    def arrive(self, m):
        for i in range(len(self.items)):
            self.copy(i, m, True).wait_recv()

    def finish(self, arrive=True):
        for i in range(len(self.items)):
            if self.keeps:
                self.keep(i).wait()
            for m in self.near:
                self.copy(i, m).wait_send()
                if arrive:
                    self.copy(i, m, True).wait_recv()


def quarter_cols(ref, first, rows, p):
    width = ref.shape[1] // 4
    return ref.at[pl.ds(first, rows), pl.ds(mult(p * width, 128), width)]


def back_kernel(shift_unit, *refs):
    term, down, gate, out, down_own, gate_own = refs[:6]
    scratch = list(refs[6:])
    rep, zpos, core = place()
    total = Total(term, out, scratch[:4], scratch[4:9])
    bufs, sems, _ = PlaneSum.split(scratch[9:], 4)
    half = down_own.shape[0] // 2
    shift = mult((zpos * 2 + core) % 4 * shift_unit, 16)

    def down_item(h):
        return (lambda p: quarter_cols(down, mult(shift + h * half, 16), half, p), down_own.at[pl.ds(h * half, half)], h)

    def gate_item(h):
        return (lambda p: gate.at[pl.ds(4 * h, 4), p], gate_own.at[pl.ds(4 * h, 4)], h)

    sums = PlaneSum([down_item(0), down_item(1), gate_item(0), gate_item(1)], bufs, sems)
    greet(rep, zpos, core, plane=2)
    total.start()
    sums.start()
    total.pair()
    total.step(0)
    sums.middle(0)
    sums.middle(1)
    total.step(1)
    sums.middle(2)
    sums.middle(3)
    total.step(2)
    for i in range(4):
        sums.end(i)
    total.finish()
    sums.finish()


def back_sums(cid, term, down, gate, rows):
    width = down.shape[1] // 4
    kind = down.dtype
    return pl.pallas_call(
        functools.partial(back_kernel, rows % 128),
        out_shape=[jax.ShapeDtypeStruct(term.shape[1:], jnp.float32), jax.ShapeDtypeStruct((rows, width), kind),
                   jax.ShapeDtypeStruct((8,) + gate.shape[2:], kind)],
        in_specs=[ANY, VMEM, VMEM], out_specs=[VMEM] * 3,
        scratch_shapes=Total.scratch(term) + PlaneSum.scratch([(rows // 2, width)] * 2 + [(4,) + gate.shape[2:]] * 2, kind),
        compiler_params=kernel_params(cid),
    )(term, down, gate)


def middle_kernel(scale, *refs):
    branch, cols, term, down, up = refs[:5]
    attend_in = refs[5:12]
    branch_all, cols_all, out, down_all, up_own = refs[12:17]
    attend_out = refs[17:21]
    scratch = list(refs[21:])
    left, scratch = scratch[0], scratch[1:]
    rep, zpos, core = place()
    gather = Gather((branch,), (branch_all,), scratch[:5])
    total = Total(term, out, scratch[5:9], scratch[9:14])
    swap = ColumnSwap([(lambda s: cols.at[s], lambda s: cols_all.at[s])], scratch[14:17])
    half = down.shape[0] // 2
    downs = PlaneGather(
        [(down.at[pl.ds(h * half, half)], functools.partial(quarter_cols, down_all, h * half, half), h) for h in range(2)],
        scratch[17:20])
    bufs, sems, _ = PlaneSum.split(scratch[20:], 2)
    sums = PlaneSum([(lambda p, h=h: up.at[pl.ds(4 * h, 4), p], up_own.at[pl.ds(4 * h, 4)], h) for h in range(2)], bufs, sems)
    greet(rep, zpos, core, plane=2, column=True)
    total.start()
    gather.start()
    sums.start()
    downs.start()
    swap.start()
    left[...] = jnp.zeros_like(left)
    attend_out[3][...] = jnp.zeros_like(attend_out[3])
    quarter = attend_back_heads(scale, *attend_in, *attend_out, left)

    def after_first():
        total.pair()
        total.step(0)

    def after_second():
        gather.hop(1)
        sums.middle(0)
        sums.middle(1)

    def after_third():
        total.step(1)
        downs.middle(0)
        downs.middle(1)

    def after_fourth():
        gather.hop(2)
        total.step(2)

    def step(i, carry):
        quarter(i, carry)
        for k, service in enumerate((after_first, after_second, after_third, after_fourth)):
            pl.when(i == k)(service)
        return carry

    lax.fori_loop(0, 4, step, 0)
    sums.end(0)
    sums.end(1)
    gather.hop(3)
    total.finish()
    gather.finish()
    swap.finish()
    downs.finish()
    sums.finish()


def middle_exchange(cid, scale, branch, cols, term, down, up, attend_in):
    kind = branch.dtype
    query, kv, rope = attend_in[:3]
    rows = query.shape[0]
    return pl.pallas_call(
        functools.partial(middle_kernel, scale),
        out_shape=[jax.ShapeDtypeStruct((8 * branch.shape[0], branch.shape[1]), kind), jax.ShapeDtypeStruct(cols.shape, kind),
                   jax.ShapeDtypeStruct(term.shape[1:], jnp.float32),
                   jax.ShapeDtypeStruct((down.shape[0], 4 * down.shape[1]), kind), jax.ShapeDtypeStruct((8,) + up.shape[2:], kind),
                   jax.ShapeDtypeStruct(query.shape, kind), jax.ShapeDtypeStruct((rows, 4096), kind),
                   jax.ShapeDtypeStruct(kv.shape, kind), jax.ShapeDtypeStruct(rope.shape, jnp.float32)],
        in_specs=[ANY] * 4 + [VMEM] * 8, out_specs=[ANY, ANY, VMEM, ANY] + [VMEM] * 5,
        scratch_shapes=[pltpu.VMEM((2 * rows, 256), kind)]
        + Gather.scratch(1) + Total.scratch(term) + ColumnSwap.scratch(1) + PlaneGather.scratch(2)
        + PlaneSum.scratch([(4,) + up.shape[2:]] * 2, kind),
        compiler_params=kernel_params(cid),
    )(branch, cols, term, down, up, *attend_in)


def late_kernel(lat, gate, up, query_up, latent_up, lat_all, gate_all, up_all, query_sum, latent_sum, *scratch):
    rep, zpos, core = place()
    shard = zpos * 2 + core
    gather = Gather((lat,), (lat_all,), scratch[:5])
    pairs = ((gate, gate_all), (up, up_all))
    swap = ColumnSwap([(lambda s, a=a: a.at[s], lambda s, b=b: b.at[s, rep]) for a, b in pairs], scratch[5:8], keeps=False)

    def part(m, b):
        return lambda p: b.at[shard if m == 0 else column_place(zpos, core, m, True), p]

    spread = PlaneGather(
        [(a.at[shard] if m == 0 else None, part(m, b), h) for m in range(8) for h, (a, b) in enumerate(pairs)], scratch[8:11])
    bufs, sems, rest = PlaneSum.split(scratch[11:], 2)
    query_part = rest[0]
    width = query_up.shape[2] // 4

    def query_item(h):
        return (lambda p: query_up.at[pl.ds(4 * h, 4), :, pl.ds(mult(p * width, 128), width)], query_part.at[pl.ds(4 * h, 4)], h)

    sums = PlaneSum([query_item(0), query_item(1)], bufs, sems)
    query_total = Total(query_part, query_sum, rest[1:5], rest[5:10])
    latent_total = Total(latent_up, latent_sum, rest[10:14], rest[14:19])
    greet(rep, zpos, core, plane=2, column=True)
    sums.start()
    spread.start((0, 1))
    swap.start()
    latent_total.start()
    gather.start()
    near = ColumnSwap.near
    for i, m in enumerate(near):
        swap.arrive(m)
        spread.start((2 * m, 2 * m + 1))
        if i == 0:
            sums.middle(0)
            sums.middle(1)
        before = 0 if i == 0 else near[i - 1]
        spread.middle(2 * before)
        spread.middle(2 * before + 1)
        if i == 2:
            latent_total.pair()
            latent_total.step(0)
            sums.end(0)
            sums.end(1)
            query_total.start()
        if i in (1, 3, 5):
            gather.hop((i + 1) // 2)
        if i == 4:
            latent_total.step(1)
            query_total.pair()
            query_total.step(0)
        if i == 6:
            latent_total.step(2)
            query_total.step(1)
    query_total.step(2)
    spread.middle(2 * near[-1])
    spread.middle(2 * near[-1] + 1)
    latent_total.finish()
    query_total.finish()
    gather.finish()
    swap.finish(arrive=False)
    spread.finish()
    sums.finish()


def late_exchange(cid, lat, gate, up, query_up, latent_up):
    kind = gate.dtype
    part = jax.ShapeDtypeStruct((8, query_up.shape[1], query_up.shape[2] // 4), kind)
    half = (4,) + part.shape[1:]
    return pl.pallas_call(
        late_kernel,
        out_shape=[jax.ShapeDtypeStruct((8 * lat.shape[0], lat.shape[1]), lat.dtype)]
        + [jax.ShapeDtypeStruct((8, 4) + gate.shape[1:], kind)] * 2
        + [jax.ShapeDtypeStruct(part.shape[1:], jnp.float32), jax.ShapeDtypeStruct(latent_up.shape[1:], jnp.float32)],
        in_specs=[ANY] * 3 + [VMEM, ANY], out_specs=[ANY] * 3 + [VMEM] * 2,
        scratch_shapes=Gather.scratch(1) + ColumnSwap.scratch(2) + PlaneGather.scratch(16)
        + PlaneSum.scratch([half] * 2, kind) + [pltpu.VMEM(part.shape, kind)] + Total.scratch(part) + Total.scratch(latent_up),
        compiler_params=kernel_params(cid),
    )(lat, gate, up, query_up, latent_up)


def last_kernel(n, *refs):
    terms, done, gain = refs[:n], refs[n], refs[n + 1]
    outs, done_out, gain_out = refs[n + 2 : 2 * n + 2], refs[2 * n + 2], refs[2 * n + 3]
    scratch = list(refs[2 * n + 4 :])
    landed, sums = scratch[:n], scratch[n : 2 * n + 1]
    gain_landed, gain_sum, gain_plane, ssend, srecv, tsend, trecv, gsend, grecv, hsend, hrecv = scratch[2 * n + 1 :]
    rep, zpos, core = place()
    shard = zpos * 2 + core
    places = plane_places(rep)
    wide = jnp.float32
    greet(rep, zpos, core, plane=3, column=True)

    def quarter(ref, p):
        if len(ref.shape) == 3:
            return ref.at[p]
        return quarter_cols(ref, 0, ref.shape[0], p)

    def term_copy(a, k):
        return remote(quarter(terms[a], places[k]), landed[a].at[k], ssend.at[k, a], srecv.at[k, a], places[k], shard)

    def sum_copy(a, k, back=False):
        out = quarter((*outs, done_out)[a], places[k] if back else rep)
        return remote(sums[a], out, tsend.at[k, a], trecv.at[k, a], places[k], shard)

    def gain_copy(m):
        s2 = column_place(zpos, core, m)
        return remote(gain.at[s2], gain_landed.at[m - 1], gsend.at[m - 1], grecv.at[m - 1], rep, s2)

    def gain_on(k):
        return remote(gain_sum, gain_plane.at[k], hsend.at[k], hrecv.at[k], places[k], shard)

    def hand_on(a):
        for k in range(3):
            sum_copy(a, k).start()
        quarter((*outs, done_out)[a], rep)[...] = sums[a][...]

    for m in range(1, 8):
        gain_copy(m).start()
    for a in range(n):
        for k in range(3):
            term_copy(a, k).start()
    sums[n][...] = done[...].astype(sums[n].dtype)
    hand_on(n)
    gain_sum[...] = gain[shard]
    for m in range(1, 8):
        gain_copy(m).wait_recv()
        gain_sum[...] += gain_landed[m - 1]
    for k in range(3):
        gain_on(k).start()
    for a in range(n):
        total = quarter(terms[a], rep)[...].astype(wide)
        for k in range(3):
            term_copy(a, k).wait_recv()
            total = total + landed[a][k].astype(wide)
        sums[a][...] = total.astype(jnp.bfloat16)
        hand_on(a)
    gain_out[...] = gain_sum[...]
    for k in range(3):
        gain_on(k).wait_recv()
        gain_out[...] += gain_plane[k]
    for k in range(3):
        gain_on(k).wait_send()
        for a in range(n + 1):
            if a < n:
                term_copy(a, k).wait_send()
            sum_copy(a, k).wait_send()
            sum_copy(a, k, True).wait_recv()
    for m in range(1, 8):
        gain_copy(m).wait_send()


def last_sums(cid, terms, done, gain):
    n = len(terms)
    low = jnp.bfloat16
    out = [jax.ShapeDtypeStruct(t.shape, low) for t in terms]
    out += [jax.ShapeDtypeStruct((done.shape[0], 4 * done.shape[1]), low), jax.ShapeDtypeStruct(gain.shape[1:], gain.dtype)]
    cut = [t.shape[1:] if len(t.shape) == 3 else (t.shape[0], t.shape[1] // 4) for t in terms]
    block = pltpu.VMEM(gain.shape[1:], gain.dtype)
    return pl.pallas_call(
        functools.partial(last_kernel, n), out_shape=out, in_specs=[VMEM] * (n + 2), out_specs=[VMEM] * (n + 2),
        scratch_shapes=[pltpu.VMEM((3,) + c, low) for c in cut] + [pltpu.VMEM(c, low) for c in cut] + [pltpu.VMEM(done.shape, low)]
        + [pltpu.VMEM((7,) + gain.shape[1:], gain.dtype), block, pltpu.VMEM((3,) + gain.shape[1:], gain.dtype)]
        + [dma_sems(3, n + 1)] * 4 + [dma_sems(7)] * 2 + [dma_sems(3)] * 2,
        compiler_params=kernel_params(cid),
    )(*terms, done, gain)

def start_kernel(*refs):
    ins, (gate, up) = refs[:7], refs[7:9]
    outs, cols = refs[9:16], refs[16:18]
    (zsend, zrecv, xsend, xrecv, ysend, yrecv, dsend, drecv, csend, crecv, own, gsend, grecv, psend, precv) = refs[18:33]
    held, strips = refs[33:40], refs[40:42]
    rep, zpos, core = place()
    xrep, yrep, drep = plane_places(rep)
    shard = zpos * 2 + core

    def whole(a, z, c):
        rows = ins[a].shape[0]
        return outs[a].at[pl.ds(mult((z * 2 + c) * rows, rows), rows)]

    def pieces(a, z, c, quarter, act, own_ref=False):
        def part(b, first, rows):
            full = ins[b].shape[0]
            if own_ref:
                return ins[b].at[pl.ds(mult(first, 16), rows)]
            return outs[b].at[pl.ds(mult((z * 2 + c) * full + first, 16), rows)]

        if a < 3:
            rows = ins[a].shape[0] // 4
            act(part(a, quarter * rows, rows))
        elif a == 3:
            @pl.when(quarter < 3)
            def _():
                act(part(3, jnp.minimum(quarter, 2) * 32, 32))

            @pl.when(quarter == 3)
            def _():
                act(part(4, 0, 32))
        else:
            act(ins[a + 1] if own_ref else whole(a + 1, z, c))

    copy = remote

    def hop(a, way, h, z, what):
        def act(ref):
            c = copy(ref, ref, zsend.at[way, h, a], zrecv.at[way, h, a], rep, (zpos + 1 - 2 * way) * 2 + core)
            getattr(c, what)()
        pieces(a, z, core, rep, act)

    def to_plane(a, k, z, quarter, what, sems, r):
        def act(ref):
            getattr(copy(ref, ref, sems[0].at[k, a], sems[1].at[k, a], r, shard), what)()
        pieces(a, z, core, quarter, act)

    def to_core(a, slot, z, c, what, src=None):
        ref = whole(a, z, c)
        getattr(copy(ref if src is None else src, ref, csend.at[slot, a], crecv.at[slot, a], rep, zpos * 2 + 1 - core), what)()

    greet(rep, zpos, core, plane=2, column=True)
    def send_own(a):
        def first(way):
            def go(src):
                def act(ref):
                    copy(src, ref, zsend.at[way, 0, a], zrecv.at[way, 0, a], rep, (zpos + 1 - 2 * way) * 2 + core).start()
                return act
            return go
        for way in range(2):
            @pl.when(zpos < 3 if way == 0 else zpos > 0)
            def _():
                if a < 3:
                    rows = ins[a].shape[0] // 4
                    src = ins[a].at[pl.ds(mult(rep * rows, 16), rows)]
                    pieces(a, zpos, core, rep, first(way)(src))
                elif a == 3:
                    @pl.when(rep < 3)
                    def _():
                        start = mult(jnp.minimum(rep, 2) * 32, 16)
                        src = ins[3].at[pl.ds(start, 32)]
                        dst = outs[3].at[pl.ds(mult(shard * 96 + start, 16), 32)]
                        first(way)(src)(dst)

                    @pl.when(rep == 3)
                    def _():
                        first(way)(ins[4])(whole(4, zpos, core))
                else:
                    first(way)(ins[a + 1])(whole(a + 1, zpos, core))

    def keep(a, half):
        if half == 0:
            return pltpu.make_async_copy(ins[a], held[a], own.at[0, a])
        return pltpu.make_async_copy(held[a], whole(a, zpos, core), own.at[1, a])

    for a in range(4):
        send_own(a)

    strip = cols[0].shape[1]
    quarter_rows = gate.shape[0] // 4

    def slice_of(which, s, first, rows):
        start = mult((s * 25 // 4) * 128, 128)
        return (gate, up)[which].at[pl.ds(mult(first, 16), rows), pl.ds(start, strip)]

    def rows_of(which, s, quarter):
        return cols[which].at[pl.ds(mult(s * gate.shape[0] + quarter * quarter_rows, 16), quarter_rows)]

    def slice_copy(m, which):
        s2 = column_place(zpos, core, m)
        return remote(slice_of(which, s2, rep * quarter_rows, quarter_rows), rows_of(which, shard, rep),
                      gsend.at[m - 1, which], grecv.at[m - 1, which], rep, s2)

    def slice_plane(m, quarter, kind, r):
        ref = rows_of(0, column_place(zpos, core, m, back=True), quarter)
        return remote(ref, ref, psend.at[kind, m - 1], precv.at[kind, m - 1], r, shard)

    def own_slice(which, half):
        if half == 0:
            return pltpu.make_async_copy(slice_of(which, shard, 0, gate.shape[0]), strips[which], own.at[0, 7 + which])
        rows = gate.shape[0]
        return pltpu.make_async_copy(strips[which], cols[which].at[pl.ds(mult(shard * rows, rows), rows)], own.at[1, 7 + which])

    near = (1, 2, 6, 3, 7, 4, 5)
    for a in range(7):
        to_core(a, 0, zpos, core, "start", src=ins[a])
        keep(a, 0).start()
    for which in range(2):
        own_slice(which, 0).start()
    for a in range(7):
        keep(a, 0).wait()
        keep(a, 1).start()
    for which in range(2):
        own_slice(which, 0).wait()
        own_slice(which, 1).start()

    def slices_from_column(m):
        for which in range(2):
            s2 = column_place(zpos, core, m, back=True)
            ref = rows_of(which, s2, rep)
            remote(ref, ref, gsend.at[m - 1, which], grecv.at[m - 1, which], rep, s2).wait_recv()
        slice_plane(m, rep, 0, xrep).start()
        slice_plane(m, rep, 1, yrep).start()

    def slices_from_plane(m):
        slice_plane(m, xrep, 0, xrep).wait_recv()
        slice_plane(m, yrep, 1, yrep).wait_recv()
        slice_plane(m, *onward(m)).start()

    def onward(m):
        return (xrep, 2, yrep) if m % 2 else (yrep, 2, xrep)

    def from_column(h, way, z, slots=range(4)):
        for a in slots:
            hop(a, way, h - 1, z, "wait_recv")
            if h < 3:
                @pl.when(zpos < 3 if way == 0 else zpos > 0)
                def _():
                    hop(a, way, h, z, "start")
            if a < 4:
                to_plane(a, way * 3 + h - 1, z, rep, "start", (xsend, xrecv), xrep)
                to_plane(a, way * 3 + h - 1, z, rep, "start", (ysend, yrecv), yrep)
            else:
                to_core(a + 1, way * 3 + h, z, core, "start")

    def from_plane(h, way, z):
        k = way * 3 + h - 1
        for a in range(4):
            to_plane(a, k, z, xrep, "wait_recv", (xsend, xrecv), xrep)
            if a == 0:
                to_plane(a, k, z, xrep, "start", (dsend, drecv), yrep)
            to_plane(a, k, z, yrep, "wait_recv", (ysend, yrecv), yrep)
            if a > 0:
                to_plane(a, k, z, yrep, "start", (dsend, drecv), xrep)

    def from_corner(h, way, z):
        k = way * 3 + h - 1
        for a in range(4):
            to_plane(a, k, z, drep, "wait_recv", (dsend, drecv), drep)
        for a in range(5):
            to_core(a, k + 1, z, core, "start")

    def by_hop(stage, h, *more):
        for way in range(2):
            z = zpos - h if way == 0 else zpos + h

            @pl.when(z >= 0 if way == 0 else z <= 3)
            def _():
                stage(h, way, z, *more)

    by_hop(from_column, 1)
    by_hop(from_column, 2)
    for m in near:
        for which in range(2):
            slice_copy(m, which).start()
    by_hop(from_plane, 1)
    by_hop(from_column, 3)
    by_hop(from_plane, 2)
    by_hop(from_corner, 1)
    for m in near[:3]:
        slices_from_column(m)
    send_own(4)
    send_own(5)
    by_hop(from_plane, 3)
    for m in near[3:]:
        slices_from_column(m)
    by_hop(from_corner, 2)
    for m in near[:3]:
        slices_from_plane(m)
    by_hop(from_column, 1, (5, 4))
    by_hop(from_corner, 3)
    for m in near[3:]:
        slices_from_plane(m)
    by_hop(from_column, 2, (5, 4))
    by_hop(from_column, 3, (5, 4))
    for a in range(7):
        to_core(a, 0, zpos, core, "wait_send", src=ins[a])
        to_core(a, 0, zpos, 1 - core, "wait_recv")
        keep(a, 1).wait()
    for which in range(2):
        own_slice(which, 1).wait()
        for m in near:
            slice_copy(m, which).wait_send()
    for m in near:
        slice_plane(m, rep, 0, xrep).wait_send()
        slice_plane(m, rep, 1, yrep).wait_send()
        slice_plane(m, *onward(m)).wait_send()
        slice_plane(m, drep, 2, drep).wait_recv()
    for way in range(2):
        for h in range(3):
            z = zpos - h if way == 0 else zpos + h

            @pl.when((z >= 0) & (zpos < 3) if way == 0 else (z <= 3) & (zpos > 0))
            def _():
                for a in range(6):
                    hop(a, way, h, z, "wait_send")
    for h in range(1, 4):
        for way in range(2):
            z = zpos - h if way == 0 else zpos + h
            k = way * 3 + h - 1

            @pl.when(z >= 0 if way == 0 else z <= 3)
            def _():
                for a in range(4):
                    to_plane(a, k, z, rep, "wait_send", (xsend, xrecv), xrep)
                    to_plane(a, k, z, rep, "wait_send", (ysend, yrecv), yrep)
                    to_plane(a, k, z, xrep if a == 0 else yrep, "wait_send", (dsend, drecv), yrep)
                for a in range(7):
                    to_core(a, k + 1, z, core, "wait_send")
                    to_core(a, k + 1, z, 1 - core, "wait_recv")

def start_gather(cid, weights, gate, up, strip):
    out = [jax.ShapeDtypeStruct((a.shape[0] * 8,) + a.shape[1:], a.dtype) for a in weights]
    out += [jax.ShapeDtypeStruct((gate.shape[0] * 8, strip), gate.dtype)] * 2
    return pl.pallas_call(
        start_kernel, out_shape=out, in_specs=[ANY] * 9, out_specs=[ANY] * 9,
        scratch_shapes=[dma_sems(2, 3, 6), dma_sems(2, 3, 6)] + [dma_sems(6, 4)] * 6
        + [dma_sems(7, 7), dma_sems(7, 7), dma_sems(2, 9), dma_sems(7, 2), dma_sems(7, 2), dma_sems(3, 7), dma_sems(3, 7)]
        + [pltpu.VMEM(a.shape, a.dtype) for a in weights] + [pltpu.VMEM((gate.shape[0], strip), gate.dtype)] * 2,
        compiler_params=kernel_params(cid),
    )(*weights, gate, up)

def plane_swap(values, j):
    return lax.ppermute(values, "rep", [(i, i ^ j) for i in range(4)])


def column_body(
    tokens,
    cotangent,
    doc_lengths,
    gain_attn,
    query_down,
    gain_query,
    query_up,
    latent_down,
    gain_latent,
    latent_up,
    attn_out,
    gain_ffn,
    w_gate,
    w_up,
    w_down,
):
    low = jnp.bfloat16
    wide = jnp.float32
    rows, width = tokens.shape[1], tokens.shape[2]
    seq_len = rows * 4
    head_dim = ND + RD
    scale = head_dim ** (-0.5)
    rep, shard = lax.axis_index("rep"), lax.axis_index("shard")
    slice_ff = FF // 8
    strip = 896
    shift = (slice_ff * shard) % 128

    small = jnp.concatenate(
        [v.astype(wide) for v in (gain_attn, gain_ffn, gain_query, gain_latent)]
        + [jnp.zeros((1024 - 768,), wide)]
    ).reshape(8, 128)
    tile_up = jnp.pad(
        query_up.reshape(-1, H, head_dim), ((0, 0), (0, 0), (0, 128 - head_dim))
    ).reshape(-1, H * 128)
    grad_out = cotangent[0].astype(wide)
    grad_down_in = (residual_scale * grad_out).astype(low)
    aout, qdown, ldown, qup, lup, gd_all, small_all, gate_w, up_quarter = start_gather(
        0, (attn_out, query_down, latent_down, tile_up, latent_up, grad_down_in, small), w_gate, w_up, strip
    )
    small_all = small_all.reshape(8, 1024)
    gain_in = small_all[:, :320].reshape(-1)
    gain_f = small_all[:, 320:640].reshape(-1)
    gain_q = small_all[:, 640:736].reshape(-1)
    gain_l = small_all[:, 736:768].reshape(-1)

    down_w = lax.dynamic_update_slice(jnp.zeros((strip, width), low), w_down, (shift, 0))

    local_pos = rep * rows + jnp.arange(rows, dtype=jnp.int32)
    key_pos = jnp.concatenate(
        [(rep ^ j) * rows + jnp.arange(rows, dtype=jnp.int32) for j in range(4)]
    )
    query_seg, query_off = segment_of(doc_lengths[0], local_pos)
    key_seg = segment_of(doc_lengths[0], key_pos)[0]
    allowed = (query_seg[:, None] == key_seg[None, :]) & (key_pos[None, :] <= local_pos[:, None])
    bias = jnp.where(allowed, 0.0, masked_score).astype(wide)
    cos_part, sin_part = rope_tables(query_off, RD)
    none = jnp.zeros((rows, RD // 2), wide)
    edge = jnp.zeros((rows, ND), wide)
    tail = jnp.zeros((rows, 128 - head_dim), wide)
    turns = jnp.stack(
        [
            jnp.concatenate([edge + 1.0, cos_part, cos_part, tail], axis=1),
            jnp.concatenate([edge, none, sin_part, tail], axis=1),
            jnp.concatenate([edge, -sin_part, none, tail], axis=1),
        ]
    )
    inputs = tokens[0].astype(wide)
    normed, norm_in_back = jax.vjp(rms_scale, inputs, gain_in)
    normed_low = normed.astype(low)
    latent_proj = jnp.dot(normed_low, ldown, preferred_element_type=wide)
    latent_norm, norm_l_back = jax.vjp(rms_scale, latent_proj[:, :KR], gain_l)

    def key_rotate(values):
        return rotate(values, cos_part, sin_part)

    key_rot, key_back = jax.vjp(key_rotate, latent_proj[:, KR:])
    latents = jnp.concatenate([latent_norm.astype(low), key_rot.astype(low)], axis=1)
    latents = jnp.concatenate([latents] + [plane_swap(latents, j) for j in range(1, 4)], axis=0)
    latent_low, all_rope = latents[:, :KR], latents[:, KR:]
    query_lat = jnp.dot(normed_low, qdown, preferred_element_type=wide)
    query_norm, norm_q_back = jax.vjp(rms_scale, query_lat, gain_q)
    query_low = query_norm.astype(low)
    query_proj = jnp.dot(query_low, qup, preferred_element_type=wide)
    keyvals = jnp.dot(latent_low, lup, preferred_element_type=wide).astype(low)
    rope_tile = jnp.pad(all_rope, ((0, 0), (ND, 128 - head_dim)))
    queries, mixed_low, logs = attend(scale, query_proj, keyvals, rope_tile, bias, turns)
    branch = jnp.dot(mixed_low, aout, preferred_element_type=wide)
    residual = inputs + residual_scale * branch
    normed_ffn, norm_f_back = jax.vjp(rms_scale, residual, gain_f)
    ffn_low = normed_ffn.astype(low)

    ffn_all, up_w, grad_hidden = ffn_gather(1, ffn_low, up_quarter, gd_all, down_w)
    gate_pre = jnp.dot(ffn_all, gate_w, preferred_element_type=wide)
    up_pre = jnp.dot(ffn_all, up_w, preferred_element_type=wide)
    hidden, act_back = jax.vjp(swiglu, gate_pre, up_pre)
    hidden_low = hidden.astype(low)
    grad_gate_f, grad_up_f = act_back(grad_hidden)
    grad_gate = grad_gate_f.astype(low)
    grad_up = grad_up_f.astype(low)
    ffn_in_part = (outer_cols(grad_gate, gate_w) + outer_cols(grad_up, up_w)).astype(low)
    out_part = jnp.dot(hidden_low, down_w, preferred_element_type=wide).astype(low)
    down_part = inner_rows(hidden_low, gd_all).astype(low)
    gate_part = inner_rows(ffn_all, grad_gate).astype(low).reshape(8, 4, -1, strip)
    up_part = inner_rows(ffn_all, grad_up).astype(low).reshape(8, 4, -1, strip)
    grad_ffn_in, down_own, gate_own = back_sums(
        2, ffn_in_part.reshape(8, rows, width), down_part, gate_part, slice_ff
    )

    grad_res_norm, grad_gain_ffn = norm_f_back(grad_ffn_in)
    grad_resid = grad_out + grad_res_norm
    grad_branch = (residual_scale * grad_resid).astype(low)
    grad_mixed = outer_cols(grad_branch, aout).astype(low)
    cols = jnp.stack([mixed_low, normed_low]).reshape(2, rows, 8, width // 8).transpose(2, 0, 1, 3)
    (
        branch_all,
        cols_all,
        out_sum,
        down_all,
        up_own,
        grad_q_proj,
        grad_q_packed,
        grad_kv,
        grad_rope,
    ) = middle_exchange(
        3,
        scale,
        grad_branch,
        cols,
        out_part.reshape(8, rows, width),
        down_own,
        up_part,
        (queries, keyvals, rope_tile, bias, turns, logs, grad_mixed),
    )
    layer_out = (residual + residual_scale * out_sum).astype(low)
    down_grad = down_all.astype(wide)
    rope_sum = grad_rope[:, ND:head_dim]
    grad_lat_part = jnp.concatenate([outer_cols(grad_kv, lup), rope_sum], axis=1).astype(low)
    grad_lat_own = grad_lat_part[:rows].astype(wide)
    for j in range(1, 4):
        grad_lat_own = grad_lat_own + plane_swap(
            grad_lat_part[j * rows : (j + 1) * rows], j
        ).astype(wide)
    grad_q_lat_f, grad_gain_query = norm_q_back(outer_cols(grad_q_proj, qup))
    grad_q_lat = grad_q_lat_f.astype(low)
    grad_lat_c, grad_gain_latent = norm_l_back(grad_lat_own[:, :KR])
    grad_lat_r = key_back(grad_lat_own[:, KR:])[0]
    grad_lat = jnp.concatenate([grad_lat_c, grad_lat_r], axis=1).astype(low)
    grad_normed = outer_cols(grad_q_lat, qdown) + outer_cols(grad_lat, ldown)
    grad_in_norm, grad_gain_attn = norm_in_back(grad_normed)
    tokens_grad = (grad_resid + grad_in_norm).astype(low)

    qup_part = inner_rows(query_low, grad_q_packed).astype(low)
    lup_part = inner_rows(latent_low, grad_kv).astype(low)
    grad_lats = jnp.concatenate([grad_q_lat, grad_lat], axis=1)
    lat_all, gate_all, up_all, qup_sum, lup_sum = late_exchange(
        4, grad_lats, gate_own, up_own,
        qup_part.reshape(8, -1, qup_part.shape[1]), lup_part.reshape(8, -1, lup_part.shape[1]),
    )
    gate_grad, up_grad = widen((gate_all, up_all), FF)
    mixed_cols = cols_all[:, 0].reshape(8 * rows, width // 8)
    normed_cols = cols_all[:, 1].reshape(8 * rows, width // 8)
    aout_part = inner_rows(mixed_cols, branch_all).astype(low)
    lat_part = inner_rows(normed_cols, lat_all).astype(low)
    gains = jnp.concatenate(
        [
            v.reshape(8, -1)
            for v in (grad_gain_attn, grad_gain_ffn, grad_gain_query, grad_gain_latent)
        ]
        + [jnp.zeros((8, 1024 - 768), wide)],
        axis=1,
    ).reshape(8, 8, 128)
    aout_own, lat_own, lup_own, qup_own, gain_own = last_sums(
        5, (aout_part, lat_part.reshape(4, 80, -1), lup_sum.astype(low)), qup_sum, gains
    )
    aout_own = aout_own.astype(wide)
    lat_own = lat_own.reshape(320, -1).astype(wide)
    lup_own = lup_own.astype(wide)
    qup_own = qup_own.reshape(-1, 4, 1024)
    quarter_heads = H // 4
    qup_own = jnp.concatenate(
        [
            qup_own[:, :, : quarter_heads * ND].reshape(-1, H, ND),
            qup_own[:, :, quarter_heads * ND : quarter_heads * head_dim].reshape(-1, H, RD),
        ],
        axis=-1,
    ).reshape(-1, H * head_dim).astype(wide)
    gain_own = gain_own.reshape(1024)

    return (
        layer_out[None],
        tokens_grad[None],
        gain_own[:320],
        lat_own[:, : query_down.shape[1]],
        gain_own[640:736],
        qup_own,
        lat_own[:, query_down.shape[1] :],
        gain_own[736:768],
        lup_own,
        aout_own,
        gain_own[320:640],
        gate_grad,
        up_grad,
        down_grad,
    )


def body(
    tokens,
    cotangent,
    doc_lengths,
    gain_attn,
    query_down,
    gain_query,
    query_up,
    latent_down,
    gain_latent,
    latent_up,
    attn_out,
    gain_ffn,
    w_gate,
    w_up,
    w_down,
):
    low_type = jnp.bfloat16
    wide_type = jnp.float32
    tok_rows = tokens.shape[1]
    seq_len = tok_rows * lax.axis_size("rep")
    head_dim = ND + RD
    group_size = math.gcd(H, 8)
    group_count = H // group_size
    softmax_scale = head_dim ** (-0.5)
    local_pos = lax.axis_index("rep") * tok_rows + jnp.arange(tok_rows, dtype=jnp.int32)
    key_pos = jnp.arange(seq_len, dtype=jnp.int32)
    query_seg, query_off = segment_of(doc_lengths[0], local_pos)
    key_seg = segment_of(doc_lengths[0], key_pos)[0]
    allowed = (query_seg[:, None] == key_seg[None, :]) & (key_pos[None, :] <= local_pos[:, None])
    cos_part, sin_part = rope_tables(query_off, RD)
    (
        gain_in_full,
        qdown_full,
        gain_q_full,
        qup_full,
        ldown_full,
        gain_l_full,
        lup_full,
        aout_full,
        gain_f_full,
    ) = (
        lax.all_gather(gain_attn, "shard", axis=0, tiled=True),
        lax.all_gather(query_down, "shard", axis=0, tiled=True),
        lax.all_gather(gain_query, "shard", axis=0, tiled=True),
        lax.all_gather(query_up, "shard", axis=0, tiled=True),
        lax.all_gather(latent_down, "shard", axis=0, tiled=True),
        lax.all_gather(gain_latent, "shard", axis=0, tiled=True),
        lax.all_gather(latent_up, "shard", axis=0, tiled=True),
        lax.all_gather(attn_out, "shard", axis=0, tiled=True),
        lax.all_gather(gain_ffn, "shard", axis=0, tiled=True),
    )
    inputs = tokens[0].astype(wide_type)
    normed, norm_in_back = jax.vjp(rms_scale, inputs, gain_in_full.astype(wide_type))
    normed_low = normed.astype(low_type)
    query_lat = jnp.dot(normed_low, qdown_full, preferred_element_type=wide_type)
    query_norm, norm_q_back = jax.vjp(rms_scale, query_lat, gain_q_full.astype(wide_type))
    query_low = query_norm.astype(low_type)
    query_proj = jnp.dot(query_low, qup_full, preferred_element_type=wide_type).reshape(
        tok_rows, H, head_dim
    )

    def query_rope(values):
        return jnp.concatenate(
            [
                values[..., :ND],
                rotate(values[..., ND:], cos_part[:, None, :], sin_part[:, None, :]),
            ],
            axis=-1,
        )

    query_rot, query_back = jax.vjp(query_rope, query_proj)
    query_used = query_rot.astype(low_type)
    latent_proj = jnp.dot(normed_low, ldown_full, preferred_element_type=wide_type)
    latent_norm, norm_l_back = jax.vjp(
        rms_scale, latent_proj[:, :KR], gain_l_full.astype(wide_type)
    )
    latent_low = latent_norm.astype(low_type)

    def key_rotate(values):
        return rotate(values, cos_part, sin_part)

    key_rot, key_back = jax.vjp(key_rotate, latent_proj[:, KR:])
    key_rope = key_rot.astype(low_type)
    keyvals = jnp.dot(latent_low, lup_full, preferred_element_type=wide_type).astype(low_type)
    all_keyvals, all_rope = (
        lax.all_gather(keyvals, "rep", axis=0, tiled=True),
        lax.all_gather(key_rope, "rep", axis=0, tiled=True),
    )
    queries = query_used.reshape(tok_rows, group_count, group_size, head_dim).transpose(1, 0, 2, 3)
    key_groups = all_keyvals.reshape(seq_len, group_count, group_size, ND + VD).transpose(
        1, 0, 2, 3
    )

    def scores_of(query_blk, key_blk):
        nope_part = jnp.einsum(
            "thd,shd->hts", query_blk[..., :ND], key_blk[..., :ND], preferred_element_type=wide_type
        )
        rope_part = jnp.einsum(
            "thd,sd->hts", query_blk[..., ND:], all_rope, preferred_element_type=wide_type
        )
        return jnp.where(allowed[None], (nope_part + rope_part) * softmax_scale, masked_score)

    def forward_group(carry, blocks):
        query_blk, key_blk = blocks
        scores = scores_of(query_blk, key_blk)
        row_max = jnp.max(scores, axis=-1, keepdims=True)
        exp_scores = jnp.exp(scores - row_max)
        totals = jnp.sum(exp_scores, axis=-1, keepdims=True)
        probs = (exp_scores / totals).astype(low_type)
        mixed = jnp.einsum(
            "hts,shd->thd", probs, key_blk[..., ND:], preferred_element_type=wide_type
        )
        return (carry, (mixed, row_max + jnp.log(totals)))

    start_carry = jnp.zeros((), wide_type)
    final_carry, (mixed_groups, log_totals) = lax.scan(
        forward_group, start_carry, (queries, key_groups)
    )
    mixed_low = mixed_groups.transpose(1, 0, 2, 3).reshape(tok_rows, H * VD).astype(low_type)
    branch = jnp.dot(mixed_low, aout_full, preferred_element_type=wide_type)
    residual = inputs + residual_scale * branch
    normed_ffn, norm_f_back = jax.vjp(rms_scale, residual, gain_f_full.astype(wide_type))
    ffn_low = normed_ffn.astype(low_type)
    gate_full, up_full, down_full = (
        lax.all_gather(w_gate, "shard", axis=0, tiled=True),
        lax.all_gather(w_up, "shard", axis=0, tiled=True),
        lax.all_gather(w_down, "shard", axis=0, tiled=True),
    )
    gate_pre = jnp.dot(ffn_low, gate_full, preferred_element_type=wide_type)
    up_pre = jnp.dot(ffn_low, up_full, preferred_element_type=wide_type)
    hidden, act_back = jax.vjp(swiglu, gate_pre, up_pre)
    hidden_low = hidden.astype(low_type)
    ffn_branch = jnp.dot(hidden_low, down_full, preferred_element_type=wide_type)
    layer_out = residual + residual_scale * ffn_branch
    grad_out = cotangent[0].astype(wide_type)
    grad_down_in = (residual_scale * grad_out).astype(low_type)
    gate_back_w, up_back_w, down_back_w = (
        lax.all_gather(w_gate, "shard", axis=0, tiled=True),
        lax.all_gather(w_up, "shard", axis=0, tiled=True),
        lax.all_gather(w_down, "shard", axis=0, tiled=True),
    )
    grad_hidden = outer_cols(grad_down_in, down_back_w)
    grad_gate_f, grad_up_f = act_back(grad_hidden)
    grad_gate = grad_gate_f.astype(low_type)
    grad_up = grad_up_f.astype(low_type)
    grad_ffn_in = outer_cols(grad_gate, gate_back_w) + outer_cols(grad_up, up_back_w)
    down_grad = lax.psum_scatter(
        inner_rows(hidden_low, grad_down_in).astype(jnp.bfloat16),
        "shard",
        scatter_dimension=0,
        tiled=True,
    )
    gate_up_in = jnp.concatenate([grad_gate, grad_up], axis=1)
    gate_up_grad = lax.psum_scatter(
        inner_rows(ffn_low, gate_up_in).astype(jnp.bfloat16),
        "shard",
        scatter_dimension=0,
        tiled=True,
    ).astype(jnp.float32)
    gate_grad = gate_up_grad[:, :FF]
    up_grad = gate_up_grad[:, FF:]
    grad_res_norm, grad_gain_ffn = norm_f_back(grad_ffn_in)
    grad_resid = grad_out + grad_res_norm
    qdown_back, qup_back, ldown_back, lup_back, aout_back = (
        lax.all_gather(query_down, "shard", axis=0, tiled=True),
        lax.all_gather(query_up, "shard", axis=0, tiled=True),
        lax.all_gather(latent_down, "shard", axis=0, tiled=True),
        lax.all_gather(latent_up, "shard", axis=0, tiled=True),
        lax.all_gather(attn_out, "shard", axis=0, tiled=True),
    )
    grad_branch = (residual_scale * grad_resid).astype(low_type)
    aout_grad = inner_rows(mixed_low, grad_branch)
    grad_mixed = outer_cols(grad_branch, aout_back).astype(low_type)
    grad_groups = grad_mixed.reshape(tok_rows, group_count, group_size, VD).transpose(1, 0, 2, 3)

    def backward_group(rope_acc, blocks):
        query_blk, key_blk, grad_blk, log_blk = blocks
        scores = scores_of(query_blk, key_blk)
        probs = jnp.exp(scores - log_blk)
        grad_probs = jnp.einsum(
            "thd,shd->hts", grad_blk, key_blk[..., ND:], preferred_element_type=wide_type
        )
        delta = jnp.sum(probs * grad_probs, axis=-1, keepdims=True)
        grad_scores = (probs * (grad_probs - delta)).astype(low_type)
        grad_query = (
            jnp.concatenate(
                [
                    jnp.einsum(
                        "hts,shd->thd",
                        grad_scores,
                        key_blk[..., :ND],
                        preferred_element_type=wide_type,
                    ),
                    jnp.einsum(
                        "hts,sd->thd", grad_scores, all_rope, preferred_element_type=wide_type
                    ),
                ],
                axis=-1,
            )
            * softmax_scale
        )
        grad_key = (
            jnp.einsum(
                "hts,thd->shd", grad_scores, query_blk[..., :ND], preferred_element_type=wide_type
            )
            * softmax_scale
        )
        grad_value = jnp.einsum(
            "hts,thd->shd", probs.astype(low_type), grad_blk, preferred_element_type=wide_type
        )
        rope_acc = (
            rope_acc
            + jnp.einsum(
                "hts,thd->sd", grad_scores, query_blk[..., ND:], preferred_element_type=wide_type
            )
            * softmax_scale
        )
        return (rope_acc, (grad_query, jnp.concatenate([grad_key, grad_value], axis=-1)))

    rope_start = jnp.zeros((seq_len, RD), wide_type)
    rope_sum, (grad_q_groups, grad_kv_groups) = lax.scan(
        backward_group, rope_start, (queries, key_groups, grad_groups, log_totals)
    )
    grad_kv_all = grad_kv_groups.transpose(1, 0, 2, 3).reshape(seq_len, H * (ND + VD))
    grad_kv_own, grad_rope_own = (
        lax.psum_scatter(
            grad_kv_all.astype(jnp.bfloat16), "rep", scatter_dimension=0, tiled=True
        ).astype(jnp.float32),
        lax.psum_scatter(
            rope_sum.astype(jnp.bfloat16), "rep", scatter_dimension=0, tiled=True
        ).astype(jnp.float32),
    )
    grad_q_full = grad_q_groups.transpose(1, 0, 2, 3).reshape(tok_rows, H, head_dim)
    grad_q_proj = query_back(grad_q_full)[0].reshape(tok_rows, H * head_dim).astype(low_type)
    qup_grad = inner_rows(query_low, grad_q_proj)
    grad_q_lat_f, grad_gain_query = norm_q_back(outer_cols(grad_q_proj, qup_back))
    grad_q_lat = grad_q_lat_f.astype(low_type)
    grad_kv_low = grad_kv_own.astype(low_type)
    lup_grad = inner_rows(latent_low, grad_kv_low)
    grad_lat_c, grad_gain_latent = norm_l_back(outer_cols(grad_kv_low, lup_back))
    grad_lat_r = key_back(grad_rope_own)[0]
    grad_lat = jnp.concatenate([grad_lat_c, grad_lat_r], axis=1).astype(low_type)
    qdown_grad = inner_rows(normed_low, grad_q_lat)
    ldown_grad = inner_rows(normed_low, grad_lat)
    grad_normed = outer_cols(grad_q_lat, qdown_back) + outer_cols(grad_lat, ldown_back)
    grad_in_norm, grad_gain_attn = norm_in_back(grad_normed)
    tokens_grad = (grad_resid + grad_in_norm).astype(low_type)
    (
        owned_gain_attn,
        owned_qdown,
        owned_gain_query,
        owned_qup,
        owned_ldown,
        owned_gain_latent,
        owned_lup,
        owned_aout,
        owned_gain_ffn,
    ) = (
        lax.psum_scatter(
            grad_gain_attn.astype(jnp.bfloat16), "shard", scatter_dimension=0, tiled=True
        ).astype(jnp.float32),
        lax.psum_scatter(
            qdown_grad.astype(jnp.bfloat16), "shard", scatter_dimension=0, tiled=True
        ).astype(jnp.float32),
        lax.psum_scatter(
            grad_gain_query.astype(jnp.bfloat16), "shard", scatter_dimension=0, tiled=True
        ).astype(jnp.float32),
        lax.psum_scatter(
            qup_grad.astype(jnp.bfloat16), "shard", scatter_dimension=0, tiled=True
        ).astype(jnp.float32),
        lax.psum_scatter(
            ldown_grad.astype(jnp.bfloat16), "shard", scatter_dimension=0, tiled=True
        ).astype(jnp.float32),
        lax.psum_scatter(
            grad_gain_latent.astype(jnp.bfloat16), "shard", scatter_dimension=0, tiled=True
        ).astype(jnp.float32),
        lax.psum_scatter(
            lup_grad.astype(jnp.bfloat16), "shard", scatter_dimension=0, tiled=True
        ).astype(jnp.float32),
        lax.psum_scatter(
            aout_grad.astype(jnp.bfloat16), "shard", scatter_dimension=0, tiled=True
        ).astype(jnp.float32),
        lax.psum_scatter(
            grad_gain_ffn.astype(jnp.bfloat16), "shard", scatter_dimension=0, tiled=True
        ).astype(jnp.float32),
    )
    summed = (
        lax.psum(owned_gain_attn.astype(jnp.bfloat16), "rep").astype(jnp.float32),
        lax.psum(owned_qdown.astype(jnp.bfloat16), "rep").astype(jnp.float32),
        lax.psum(owned_gain_query.astype(jnp.bfloat16), "rep").astype(jnp.float32),
        lax.psum(owned_qup.astype(jnp.bfloat16), "rep").astype(jnp.float32),
        lax.psum(owned_ldown.astype(jnp.bfloat16), "rep").astype(jnp.float32),
        lax.psum(owned_gain_latent.astype(jnp.bfloat16), "rep").astype(jnp.float32),
        lax.psum(owned_lup.astype(jnp.bfloat16), "rep").astype(jnp.float32),
        lax.psum(owned_aout.astype(jnp.bfloat16), "rep").astype(jnp.float32),
        lax.psum(owned_gain_ffn.astype(jnp.bfloat16), "rep").astype(jnp.float32),
        lax.psum(gate_grad.astype(jnp.bfloat16), "rep").astype(jnp.float32),
        lax.psum(up_grad.astype(jnp.bfloat16), "rep").astype(jnp.float32),
        lax.psum(down_grad, "rep").astype(jnp.float32),
    )
    return (
        layer_out.astype(low_type)[None],
        tokens_grad[None],
        summed[0],
        summed[1],
        summed[2],
        summed[3],
        summed[4],
        summed[5],
        summed[6],
        summed[7],
        summed[8],
        summed[9],
        summed[10],
        summed[11],
    )


def solution(mesh):
    placed = (
        P("shard", "rep", None),
        P("shard", "rep", None),
        P("shard", None),
        P("shard"),
        P("shard", None),
        P("shard"),
        P("shard", None),
        P("shard", None),
        P("shard"),
        P("shard", None),
        P("shard", None),
        P("shard"),
        P("shard", None),
        P("shard", None),
        P("shard", None),
    )
    fits = mesh.shape["rep"] == 4 and mesh.shape["shard"] == 8
    return jax.shard_map(
        column_body if fits else body,
        mesh=mesh,
        in_specs=placed,
        out_specs=(
            P("shard", "rep", None),
            P("shard", "rep", None),
            P("shard"),
            P("shard", None),
            P("shard"),
            P("shard", None),
            P("shard", None),
            P("shard"),
            P("shard", None),
            P("shard", None),
            P("shard"),
            P("shard", None),
            P("shard", None),
            P("shard", None),
        ),
        check_vma=False,
    )
```

```python
import functools
import math

import jax
import jax.numpy as jnp
from jax import lax
from jax.experimental import pallas as pl
from jax.experimental.pallas import tpu as pltpu
from jax.sharding import PartitionSpec as P

KR = 256
H = 40
ND = 64
RD = 32
VD = 64
FF = 6400


epsilon = 1e-05
residual_scale = 1.4 / math.sqrt(62.0)
rope_base = 10000.0
masked_score = -1e30


def rms_scale(values, gain):
    return values * lax.rsqrt(jnp.mean(values * values, axis=-1, keepdims=True) + epsilon) * gain


def rotate(values, cos_part, sin_part):
    midpoint = values.shape[-1] // 2
    former = values[..., :midpoint]
    latter = values[..., midpoint:]
    return jnp.concatenate(
        [former * cos_part - latter * sin_part, latter * cos_part + former * sin_part], axis=-1
    )


def segment_of(lengths, positions):
    doc_ends = jnp.cumsum(lengths)
    doc_starts = doc_ends - lengths
    segment = jnp.sum((positions[:, None] >= doc_ends[None, :]).astype(jnp.int32), axis=1)
    chosen = segment[:, None] == jnp.arange(lengths.shape[0], dtype=jnp.int32)[None, :]
    offsets = positions - jnp.sum(jnp.where(chosen, doc_starts[None, :], 0), axis=1)
    return (segment, offsets)


def rope_tables(offsets, rope_width):
    exponents = jnp.arange(0, rope_width, 2, dtype=jnp.float32) / rope_width
    angles = offsets.astype(jnp.float32)[:, None] * (rope_base ** (-exponents))[None, :]
    return (jnp.cos(angles), jnp.sin(angles))


def swiglu(gate_vals, up_vals):
    return jax.nn.silu(gate_vals) * up_vals


def inner_rows(leading, trailing):
    return lax.dot_general(
        leading, trailing, (((0,), (0,)), ((), ())), preferred_element_type=jnp.float32
    )


def outer_cols(leading, trailing):
    return lax.dot_general(
        leading, trailing, (((1,), (1,)), ((), ())), preferred_element_type=jnp.float32
    )


MESH = pl.DeviceIdType.MESH
ANY = pl.BlockSpec(memory_space=pl.ANY)

def place():
    rep = lax.axis_index("rep")
    shard = lax.axis_index("shard")
    zpos, core = shard // 2, shard % 2
    return rep, zpos, core

def mult(value, by):
    return pl.multiple_of(value, by)

def greet(rep, zpos, core, plane=0, column=False):
    barrier = pltpu.get_barrier_semaphore()
    shard = zpos * 2 + core

    def signal(r, s):
        pl.semaphore_signal(barrier, inc=1, device_id=(r, s), device_id_type=MESH)

    if column:
        for m in range(1, 8):
            signal(rep, column_place(zpos, core, m))
        count = 7
    else:
        signal(rep, zpos * 2 + 1 - core)

        @pl.when(zpos > 0)
        def _():
            signal(rep, shard - 2)

        @pl.when(zpos < 3)
        def _():
            signal(rep, shard + 2)

        count = 1 + jnp.minimum(zpos, 1) + jnp.minimum(3 - zpos, 1)
    if plane:
        for other in plane_places(rep)[:plane]:
            signal(other, shard)
        count = count + plane
    pl.semaphore_wait(barrier, count)


def plane_places(rep):
    return rep + 1 - 2 * (rep % 2), (rep + 2) % 4, 3 - rep


def column_place(zpos, core, m, back=False):
    step = 4 - m // 2 if back else m // 2
    return ((zpos + step) % 4) * 2 + (core + m) % 2


def remote(src, dst, ssem, rsem, r, s):
    return pltpu.make_async_remote_copy(
        src_ref=src, dst_ref=dst, send_sem=ssem, recv_sem=rsem, device_id=(r, s), device_id_type=MESH
    )


def dma_sems(*dims):
    return pltpu.SemaphoreType.DMA(dims)


def head_tile(h):
    return pl.ds(pl.multiple_of(h * 128, 128), 128)


def turn(values, tables, back=False):
    keep, high, low_part = tables
    if back:
        return values * keep + pltpu.roll(values * high, 112, 1) + pltpu.roll(values * low_part, 16, 1)
    return values * keep + pltpu.roll(values, 16, 1) * high + pltpu.roll(values, 112, 1) * low_part


def dot_nt(a, b):
    return lax.dot_general(a, b, (((1,), (1,)), ((), ())), preferred_element_type=jnp.float32)


def dot_tn(a, b):
    return lax.dot_general(a, b, (((0,), (0,)), ((), ())), preferred_element_type=jnp.float32)


def attend_kernel(scale, proj, kv, rope, bias, turns, query, mixed, logs):
    low = jnp.bfloat16
    heads = kv.shape[1] // 128
    lane = lax.broadcasted_iota(jnp.int32, (1, 128), 1)
    first = lane < 64
    logs[...] = jnp.zeros_like(logs)

    def group(i, carry):
        heads_here = [4 * i + j for j in range(4)]
        queries = [turn(proj[:, head_tile(h)], (turns[0], turns[1], turns[2])).astype(low) for h in heads_here]
        keyvals = [kv[:, head_tile(h)] for h in heads_here]
        scores = [dot_nt(q, jnp.where(first, keyval, rope[...])) * scale + bias[...] for q, keyval in zip(queries, keyvals)]
        tops = [jnp.max(s, axis=1, keepdims=True) for s in scores]
        grown = [jnp.exp(s - top) for s, top in zip(scores, tops)]
        totals = [jnp.sum(g, axis=1, keepdims=True) for g in grown]
        outs = [jnp.dot((g / total).astype(low), keyval, preferred_element_type=jnp.float32)
                for g, total, keyval in zip(grown, totals, keyvals)]
        for h, q, top, total in zip(heads_here, queries, tops, totals):
            query[:, head_tile(h)] = q
            logs[...] = jnp.where(lane == h, top + jnp.log(total), logs[...])
        for j in range(2):
            mixed[:, head_tile(2 * i + j)] = jnp.where(first, pltpu.roll(outs[2 * j], 64, 1), outs[2 * j + 1]).astype(low)
        return carry

    lax.fori_loop(0, heads // 4, group, 0)


def attend(scale, proj, kv, rope, bias, turns):
    rows, cols = proj.shape
    return pl.pallas_call(
        functools.partial(attend_kernel, scale),
        out_shape=[jax.ShapeDtypeStruct((rows, cols), jnp.bfloat16), jax.ShapeDtypeStruct((rows, cols // 2), jnp.bfloat16),
                   jax.ShapeDtypeStruct((rows, 128), jnp.float32)],
        in_specs=[VMEM] * 5, out_specs=[VMEM] * 3,
        compiler_params=pltpu.CompilerParams(vmem_limit_bytes=56 * 2**20),
    )(proj, kv, rope, bias, turns)


def attend_back_heads(scale, query, kv, rope, bias, turns, logs, grad, grad_query, grad_packed, grad_kv, grad_rope, left):
    low = jnp.bfloat16
    rows = query.shape[0]
    lane = lax.broadcasted_iota(jnp.int32, (1, 128), 1)
    first = lane < 64

    def one(h, grad_value):
        q = query[:, head_tile(h)]
        keyval = kv[:, head_tile(h)]
        key = jnp.where(first, keyval, rope[...])
        left[0:rows, 0:128] = q
        left[rows:, 128:256] = grad_value
        both = dot_nt(left[...], jnp.concatenate([key, keyval], axis=1))
        log = jnp.sum(jnp.where(lane == h, logs[...], 0.0), axis=1, keepdims=True)
        probs = jnp.exp(both[:rows] * scale + bias[...] - log)
        weighed = probs * both[rows:]
        delta = jnp.sum(weighed, axis=1, keepdims=True)
        grad_scores = (weighed - probs * delta).astype(low)
        grad_q = jnp.dot(grad_scores, key, preferred_element_type=jnp.float32) * scale
        grad_q = turn(grad_q, (turns[0], turns[1], turns[2]), True)
        grad_query[:, head_tile(h)] = grad_q.astype(low)
        out = dot_tn(jnp.concatenate([grad_scores, probs.astype(low)], axis=0), left[...])
        grad_key = out[:, :128] * scale
        grad_rope[...] += grad_key
        grad_kv[:, head_tile(h)] = jnp.where(first, grad_key, out[:, 128:]).astype(low)
        return grad_q

    def quarter(i, carry):
        rotary = jnp.zeros((rows, 128), jnp.float32)
        for j in range(5):
            both = grad[:, head_tile(5 * i + j)].astype(jnp.float32)
            even = one(10 * i + 2 * j, jnp.where(first, 0.0, pltpu.roll(both, 64, 1)).astype(low))
            odd = one(10 * i + 2 * j + 1, jnp.where(first, 0.0, both).astype(low))
            grad_packed[:, head_tile(8 * i + j)] = jnp.where(first, even, pltpu.roll(odd, 64, 1)).astype(low)
            for k, got in ((2 * j, even), (2 * j + 1, odd)):
                at = 32 * (k % 4)
                moved = got if at == 64 else pltpu.roll(got, (at + 64) % 128, 1)
                rotary = jnp.where((lane >= at) & (lane < at + 32), moved, rotary)
                if k % 4 == 3 or k == 9:
                    grad_packed[:, head_tile(8 * i + 5 + k // 4)] = rotary.astype(low)
                    rotary = jnp.zeros((rows, 128), jnp.float32)
        return carry

    return quarter


def widen_kernel(*refs):
    n = len(refs) // 2
    for strips, out in zip(refs[:n], refs[n:]):
        each = out.shape[1] // 8
        for s in range(8):
            first, last = s * each // 128, (s + 1) * each // 128
            tiles = strips[s, 0].astype(jnp.float32)
            if s * each % 128:
                shared = strips[s - 1, 0, :, (first - (s - 1) * each // 128) * 128 :][:, :128]
                out[:, first * 128 : first * 128 + 128] = tiles[:, :128] + shared.astype(jnp.float32)
                first_full = first + 1
            else:
                first_full = first
            base = s * each // 128
            out[:, first_full * 128 : last * 128] = tiles[:, (first_full - base) * 128 : (last - base) * 128]


def unpack_kernel(heads, packed, out):
    pieces = []
    for h in range(heads):
        first, k = h // 10 * 1024, h % 10
        pieces.append(packed[:, first + 64 * k : first + 64 * k + 64])
        pieces.append(packed[:, first + 640 + 32 * k : first + 672 + 32 * k])
    out[...] = jnp.concatenate(pieces, axis=1).astype(jnp.float32)


def unpack(packed, heads):
    return pl.pallas_call(
        functools.partial(unpack_kernel, heads),
        out_shape=jax.ShapeDtypeStruct((packed.shape[0], heads * 96), jnp.float32), in_specs=[VMEM], out_specs=VMEM,
    )(packed)


def widen(arrays, cols):
    _, quarters, rows, strip = arrays[0].shape
    n = len(arrays)
    return pl.pallas_call(
        widen_kernel, grid=(quarters,),
        out_shape=[jax.ShapeDtypeStruct((quarters * rows, cols), jnp.float32)] * n,
        in_specs=[pl.BlockSpec((8, 1, rows, strip), lambda q: (0, q, 0, 0))] * n,
        out_specs=[pl.BlockSpec((rows, cols), lambda q: (q, 0))] * n,
        compiler_params=pltpu.CompilerParams(vmem_limit_bytes=56 * 2**20),
    )(*arrays)


class Gather:
    def __init__(self, ins, outs, sems):
        self.ins, self.outs = ins, outs
        self.zsend, self.zrecv, self.csend, self.crecv, self.own = sems
        self.rep, self.zpos, self.core = place()
        self.held = None

    @staticmethod
    def scratch(n):
        return [dma_sems(2, 3, n), dma_sems(2, 3, n), dma_sems(7, n), dma_sems(7, n), dma_sems(2, n)]

    def at(self, a, z, c):
        rows = self.ins[a].shape[0]
        return self.outs[a].at[pl.ds(mult((z * 2 + c) * rows, rows), rows)]

    def hop_copy(self, a, way, hop, z, src=None):
        dst = self.at(a, z, self.core)
        return remote(dst if src is None else src, dst, self.zsend.at[way, hop, a], self.zrecv.at[way, hop, a],
                      self.rep, (self.zpos + (1 - 2 * way)) * 2 + self.core)

    def core_copy(self, a, slot, z, c, src=None):
        dst = self.at(a, z, c)
        return remote(dst if src is None else src, dst, self.csend.at[slot, a], self.crecv.at[slot, a],
                      self.rep, self.zpos * 2 + 1 - self.core)

    def keep(self, a):
        return pltpu.make_async_copy(self.ins[a], self.at(a, self.zpos, self.core), self.own.at[0, a])

    def onward(self, way):
        return self.zpos < 3 if way == 0 else self.zpos > 0

    def source(self, way, hop):
        z = self.zpos - hop if way == 0 else self.zpos + hop
        return z, (z >= 0 if way == 0 else z <= 3)

    def start(self, which=None):
        which = range(len(self.ins)) if which is None else which
        for way in range(2):
            @pl.when(self.onward(way))
            def _():
                for a in which:
                    self.hop_copy(a, way, 0, self.zpos, src=self.ins[a]).start()
        for a in which:
            self.core_copy(a, 0, self.zpos, self.core, src=self.ins[a]).start()
            self.keep(a).start()

    def hop(self, hop, which=None):
        which = range(len(self.ins)) if which is None else which
        for way in range(2):
            z, there = self.source(way, hop)

            @pl.when(there)
            def _():
                for a in which:
                    self.hop_copy(a, way, hop - 1, z).wait_recv()
                    if hop < 3:
                        @pl.when(self.onward(way))
                        def _():
                            self.hop_copy(a, way, hop, z).start()
                    self.core_copy(a, way * 3 + hop, z, self.core).start()

    def finish(self):
        arrays = range(len(self.ins))
        for way in range(2):
            for hop in range(3):
                z, there = self.source(way, hop)

                @pl.when(there & self.onward(way))
                def _():
                    for a in arrays:
                        self.hop_copy(a, way, hop, z).wait_send()
        for a in arrays:
            self.keep(a).wait()
            self.core_copy(a, 0, self.zpos, self.core, src=self.ins[a]).wait_send()
            self.core_copy(a, 0, self.zpos, 1 - self.core).wait_recv()
        for way in range(2):
            for hop in range(1, 4):
                z, there = self.source(way, hop)

                @pl.when(there)
                def _():
                    for a in arrays:
                        self.core_copy(a, way * 3 + hop, z, self.core).wait_send()
                        self.core_copy(a, way * 3 + hop, z, 1 - self.core).wait_recv()


class Total:
    def __init__(self, term, out, bufs, sems):
        self.term, self.out = term, out
        self.theirs, self.landed = bufs
        self.zsend, self.zrecv, self.csend, self.crecv = sems
        self.rep, self.zpos, self.core = place()

    @staticmethod
    def scratch(term):
        return [pltpu.VMEM((4,) + term.shape[1:], term.dtype), pltpu.VMEM((5,) + term.shape[1:], term.dtype),
                dma_sems(2, 4), dma_sems(2, 4), dma_sems(4), dma_sems(4)]

    @staticmethod
    def split(term, out, refs):
        return Total(term, out, refs[:2], refs[2:6]), refs[6:]

    def pair_copy(self, z):
        return remote(self.term.at[z * 2 + 1 - self.core], self.theirs.at[z], self.csend.at[z], self.crecv.at[z],
                      self.rep, self.zpos * 2 + 1 - self.core)

    def hop_copy(self, way, z):
        return remote(self.theirs.at[z], self.landed.at[z + 1 - way], self.zsend.at[way, z], self.zrecv.at[way, z],
                      self.rep, (self.zpos + (1 - 2 * way)) * 2 + self.core)

    def each(self, step):
        for way in range(2):
            behind = self.zpos if way == 0 else 3 - self.zpos
            target = self.zpos + 3 - step if way == 0 else self.zpos - 3 + step
            yield way, behind, target, (behind <= step) & (behind < 3)

    def start(self):
        for z in (3, 0, 2, 1):
            self.pair_copy(z).start()

    def pair(self):
        for z in (3, 0, 2, 1):
            self.pair_copy(z).wait_recv()

    def both(self, z):
        return self.term[z * 2 + self.core].astype(jnp.float32) + self.theirs[z].astype(jnp.float32)

    def step(self, step):
        for way, behind, target, there in self.each(step):
            @pl.when(there)
            def _():
                total = self.both(target)

                @pl.when(behind == 0)
                def _():
                    self.theirs[target] = total.astype(self.theirs.dtype)

                @pl.when(behind > 0)
                def _():
                    self.hop_copy(way, target).wait_recv()
                    self.theirs[target] = (total + self.landed[target + 1 - way].astype(jnp.float32)).astype(self.theirs.dtype)
                self.hop_copy(way, target).start()

    def finish(self):
        self.out[...] = self.both(self.zpos)
        for way in range(2):
            @pl.when(self.zpos > 0 if way == 0 else self.zpos < 3)
            def _():
                self.hop_copy(way, self.zpos).wait_recv()
                self.out[...] += self.landed[self.zpos + 1 - way].astype(jnp.float32)
        for step in range(3):
            for way, behind, target, there in self.each(step):
                @pl.when(there)
                def _():
                    self.hop_copy(way, target).wait_send()
        for z in range(4):
            self.pair_copy(z).wait_send()


def kernel_params(cid):
    return pltpu.CompilerParams(collective_id=cid, has_side_effects=True, vmem_limit_bytes=56 * 2**20)


VMEM = pl.BlockSpec(memory_space=pltpu.VMEM)


def ffn_gather_kernel(tokens, partial, grad, down, tokens_all, up, grad_hidden, *scratch):
    del partial
    rep, zpos, core = place()
    gather = Gather((tokens,), (tokens_all,), scratch[:5])
    piece = up.shape[0] // 32

    def part(m):
        first = column_place(zpos, core, m, True) * (4 * piece)
        return lambda p: up.at[pl.ds(mult(first + p * piece, 16), piece)]

    spread = PlaneGather([(None, part(m), m % 2) for m in ColumnSwap.near], scratch[5:8])
    greet(rep, zpos, core, plane=2)
    gather.start()
    spread.start()
    chunk = grad.shape[0] // 4

    def product(i):
        at = pl.ds(mult(i * chunk, chunk), chunk)
        grad_hidden[at] = dot_nt(grad[at], down[...])

    def step(i, carry):
        product(i)

        @pl.when(i == 1)
        def _():
            gather.hop(1)

        @pl.when(i == 3)
        def _():
            gather.hop(2)
        return carry

    lax.fori_loop(0, 4, step, 0)
    for i in range(7):
        spread.middle(i)
    gather.hop(3)
    gather.finish()
    spread.finish()


def ffn_gather(cid, tokens, partial, grad, down):
    return pl.pallas_call(
        ffn_gather_kernel,
        out_shape=[jax.ShapeDtypeStruct((8 * tokens.shape[0], tokens.shape[1]), tokens.dtype),
                   jax.ShapeDtypeStruct(partial.shape, partial.dtype),
                   jax.ShapeDtypeStruct((grad.shape[0], down.shape[0]), jnp.float32)],
        in_specs=[ANY, ANY, VMEM, VMEM], out_specs=[ANY, ANY, VMEM], input_output_aliases={1: 1},
        scratch_shapes=Gather.scratch(1) + PlaneGather.scratch(7),
        compiler_params=kernel_params(cid),
    )(tokens, partial, grad, down)


class PlaneSum:
    def __init__(self, items, bufs, sems):
        self.items = items
        self.landed, self.stage, self.last = bufs
        self.asend, self.arecv, self.bsend, self.brecv = sems
        self.rep, self.zpos, self.core = place()
        self.shard = self.zpos * 2 + self.core

    @staticmethod
    def scratch(shapes, dtype):
        n = len(shapes)
        return ([pltpu.VMEM((2,) + s, dtype) for s in shapes] + [pltpu.VMEM(s, dtype) for s in shapes] * 2
                + [dma_sems(n, 2), dma_sems(n, 2), dma_sems(n), dma_sems(n)])

    @staticmethod
    def split(refs, n):
        return (refs[:n], refs[n : 2 * n], refs[2 * n : 3 * n]), refs[3 * n : 3 * n + 4], refs[3 * n + 4 :]

    def ways(self, i):
        xrep, yrep, drep = plane_places(self.rep)
        return (xrep, yrep, drep) if self.items[i][2] == 0 else (yrep, xrep, drep)

    def out(self, i, k):
        near, _, far = self.ways(i)
        return remote(self.items[i][0](far if k else near), self.landed[i].at[k], self.asend.at[i, k], self.arecv.at[i, k],
                      near, self.shard)

    def on(self, i):
        return remote(self.stage[i], self.last[i], self.bsend.at[i], self.brecv.at[i], self.ways(i)[1], self.shard)

    def start(self, which=None):
        for i in range(len(self.items)) if which is None else which:
            for k in (1, 0):
                self.out(i, k).start()

    def middle(self, i):
        wide = jnp.float32
        self.out(i, 1).wait_recv()
        term = self.items[i][0](self.ways(i)[1])
        self.stage[i][...] = (term[...].astype(wide) + self.landed[i][1].astype(wide)).astype(self.stage[i].dtype)
        self.on(i).start()

    def end(self, i):
        wide = jnp.float32
        self.out(i, 0).wait_recv()
        self.on(i).wait_recv()
        total = self.items[i][0](self.rep)[...].astype(wide) + self.landed[i][0].astype(wide)
        own = self.items[i][1]
        own[...] = (total + self.last[i][...].astype(wide)).astype(own.dtype)

    def finish(self):
        for i in range(len(self.items)):
            for k in range(2):
                self.out(i, k).wait_send()
            self.on(i).wait_send()


class PlaneGather:
    def __init__(self, items, sems):
        self.items = items
        self.send, self.recv, self.own = sems
        self.rep, self.zpos, self.core = place()
        self.shard = self.zpos * 2 + self.core

    @staticmethod
    def scratch(n):
        return [dma_sems(3, n), dma_sems(3, n), dma_sems(n)]

    def copy(self, i, kind, quarter, to):
        own, part, _ = self.items[i]
        dst = part(quarter)
        return remote(dst if kind == 2 or own is None else own, dst, self.send.at[kind, i], self.recv.at[kind, i], to, self.shard)

    def keep(self, i):
        return pltpu.make_async_copy(self.items[i][0], self.items[i][1](self.rep), self.own.at[i])

    def start(self, which=None):
        xrep, yrep, _ = plane_places(self.rep)
        for i in range(len(self.items)) if which is None else which:
            self.copy(i, 0, self.rep, xrep).start()
            self.copy(i, 1, self.rep, yrep).start()
            if self.items[i][0] is not None:
                self.keep(i).start()

    def middle(self, i):
        xrep, yrep, _ = plane_places(self.rep)
        self.copy(i, 0, xrep, xrep).wait_recv()
        if self.items[i][2] == 0:
            self.copy(i, 2, xrep, yrep).start()
        self.copy(i, 1, yrep, yrep).wait_recv()
        if self.items[i][2] == 1:
            self.copy(i, 2, yrep, xrep).start()

    def finish(self):
        xrep, yrep, drep = plane_places(self.rep)
        for i, (own, _, first) in enumerate(self.items):
            self.copy(i, 0, self.rep, xrep).wait_send()
            self.copy(i, 1, self.rep, yrep).wait_send()
            self.copy(i, 2, *((xrep, yrep) if first == 0 else (yrep, xrep))).wait_send()
            self.copy(i, 2, drep, drep).wait_recv()
            if own is not None:
                self.keep(i).wait()


class ColumnSwap:
    def __init__(self, items, sems, keeps=True):
        self.items, self.keeps = items, keeps
        self.send, self.recv, self.own = sems
        self.rep, self.zpos, self.core = place()
        self.shard = self.zpos * 2 + self.core

    near = (1, 2, 6, 3, 7, 4, 5)

    @staticmethod
    def scratch(n):
        return [dma_sems(7, n), dma_sems(7, n), dma_sems(n)]

    def copy(self, i, m, back=False):
        s2 = column_place(self.zpos, self.core, m, back)
        block, there = self.items[i]
        return remote(block(s2), there(s2 if back else self.shard), self.send.at[m - 1, i], self.recv.at[m - 1, i], self.rep, s2)

    def keep(self, i):
        return pltpu.make_async_copy(self.items[i][0](self.shard), self.items[i][1](self.shard), self.own.at[i])

    def start(self):
        for m in self.near:
            for i in range(len(self.items)):
                self.copy(i, m).start()
        for i in range(len(self.items) if self.keeps else 0):
            self.keep(i).start()

    def arrive(self, m):
        for i in range(len(self.items)):
            self.copy(i, m, True).wait_recv()

    def finish(self, arrive=True):
        for i in range(len(self.items)):
            if self.keeps:
                self.keep(i).wait()
            for m in self.near:
                self.copy(i, m).wait_send()
                if arrive:
                    self.copy(i, m, True).wait_recv()


def quarter_cols(ref, first, rows, p):
    width = ref.shape[1] // 4
    return ref.at[pl.ds(first, rows), pl.ds(mult(p * width, 128), width)]


def back_kernel(shift_unit, *refs):
    down, tokens, grad_gate, grad_up, gate_w, up_w, out, down_own, gate_own, up = refs[:10]
    term, gate, strips, strip_sems = refs[10:14]
    rep, zpos, core = place()
    total, rest = Total.split(term, out, refs[14:])
    bufs, sems, _ = PlaneSum.split(rest, 4)
    half = down_own.shape[0] // 2
    shift = mult((zpos * 2 + core) % 4 * shift_unit, 16)
    wide = jnp.float32

    def down_item(h):
        return (lambda p: quarter_cols(down, mult(shift + h * half, 16), half, p), down_own.at[pl.ds(h * half, half)], h)

    def gate_item(h):
        return (lambda p: gate.at[pl.ds(4 * h, 4), p], gate_own.at[pl.ds(4 * h, 4)], h)

    sums = PlaneSum([down_item(0), down_item(1), gate_item(0), gate_item(1)], bufs, sems)
    chunk = strips.shape[2]
    chunks = gate_w.shape[0] // chunk

    def strip(i, which):
        return pltpu.make_async_copy(
            (gate_w, up_w)[which].at[pl.ds(mult(i * chunk, 128), chunk)], strips.at[i % 2, which], strip_sems.at[i % 2, which])

    for which in range(2):
        strip(0, which).start()
    greet(rep, zpos, core, plane=2)
    sums.start((0, 1))

    def back(i, carry):
        for which in range(2):
            strip(i, which).wait()

        @pl.when(i < chunks - 1)
        def _():
            for which in range(2):
                strip(i + 1, which).start()

        part = dot_nt(grad_gate[...], strips[i % 2, 0]) + dot_nt(grad_up[...], strips[i % 2, 1])
        term[:, :, pl.ds(mult(i * chunk, 128), chunk)] = part.astype(term.dtype).reshape(8, -1, chunk)
        return carry

    lax.fori_loop(0, chunks, back, 0)
    total.start()
    wide_rows = tokens.shape[1] // 4

    def weight(grad, to, i):
        got = dot_tn(tokens[:, pl.ds(mult(i * wide_rows, 128), wide_rows)], grad[...])
        to[pl.ds(2 * i, 2)] = got.astype(to.dtype).reshape((2,) + to.shape[1:])

    def gate_step(i, carry):
        weight(grad_gate, gate, i)

        @pl.when(i == 2)
        def _():
            total.pair()
            total.step(0)
        return carry

    lax.fori_loop(0, 4, gate_step, 0)
    sums.start((2, 3))

    def up_step(i, carry):
        weight(grad_up, up, i)

        @pl.when(i == 1)
        def _():
            sums.middle(0)
            sums.middle(1)
            total.step(1)
        return carry

    lax.fori_loop(0, 4, up_step, 0)
    sums.end(0)
    sums.end(1)
    total.step(2)
    sums.middle(2)
    sums.middle(3)
    total.finish()
    sums.end(2)
    sums.end(3)
    sums.finish()


def back_sums(cid, down, tokens, grad_gate, grad_up, gate_w, up_w, rows):
    width = down.shape[1] // 4
    kind = down.dtype
    strip = gate_w.shape[1]
    parts = (8, 4, gate_w.shape[0] // 32, strip)
    term = jax.ShapeDtypeStruct((8, tokens.shape[0] // 8, tokens.shape[1]), kind)
    return pl.pallas_call(
        functools.partial(back_kernel, rows % 128),
        out_shape=[jax.ShapeDtypeStruct(term.shape[1:], jnp.float32), jax.ShapeDtypeStruct((rows, width), kind),
                   jax.ShapeDtypeStruct((8,) + parts[2:], kind), jax.ShapeDtypeStruct(parts, kind)],
        in_specs=[VMEM] * 4 + [ANY] * 2, out_specs=[VMEM] * 4,
        scratch_shapes=[pltpu.VMEM(term.shape, kind), pltpu.VMEM(parts, kind),
                        pltpu.VMEM((2, 2, gate_w.shape[0] // 5, strip), kind), dma_sems(2, 2)]
        + Total.scratch(term) + PlaneSum.scratch([(rows // 2, width)] * 2 + [(4,) + parts[2:]] * 2, kind),
        compiler_params=kernel_params(cid),
    )(down, tokens, grad_gate, grad_up, gate_w, up_w)


def middle_kernel(scale, *refs):
    branch, cols, down, up, attn_out, query_low, latent_low = refs[:7]
    query, kv, rope, bias, turns, logs = refs[7:13]
    branch_all, cols_all, down_all, up_own = refs[13:17]
    grad_query, grad_kv, grad_rope, query_up, latent_up = refs[17:22]
    scratch = list(refs[22:])
    left, mixed, packed, strips, strip_sems = scratch[:5]
    scratch = scratch[5:]
    rep, zpos, core = place()
    shard = zpos * 2 + core
    gather = Gather((branch,), (branch_all,), scratch[:5])
    swap = ColumnSwap([(lambda s: cols.at[s], lambda s: cols_all.at[s])], scratch[5:8])
    half = down.shape[0] // 2
    downs = PlaneGather(
        [(down.at[pl.ds(h * half, half)], functools.partial(quarter_cols, down_all, h * half, half), h) for h in range(2)],
        scratch[8:11])
    bufs, sems, _ = PlaneSum.split(scratch[11:], 2)
    sums = PlaneSum([(lambda p, h=h: up.at[pl.ds(4 * h, 4), p], up_own.at[pl.ds(4 * h, 4)], h) for h in range(2)], bufs, sems)
    rows = attn_out.shape[0] // 4

    def strip(i):
        return pltpu.make_async_copy(
            attn_out.at[pl.ds(mult(i * rows, 128), rows)], strips.at[i % 2], strip_sems.at[i % 2])

    strip(0).start()
    greet(rep, zpos, core, plane=2, column=True)
    gather.start()
    sums.start()
    downs.start()
    swap.start()
    left[...] = jnp.zeros_like(left)
    grad_rope[...] = jnp.zeros_like(grad_rope)
    quarter = attend_back_heads(
        scale, query, kv, rope, bias, turns, logs, mixed, grad_query, packed, grad_kv, grad_rope, left)

    def after_second():
        gather.hop(1)
        sums.middle(0)
        sums.middle(1)

    def after_fourth():
        gather.hop(2)
        downs.middle(0)
        downs.middle(1)

    def step(i, carry):
        strip(i).wait()

        @pl.when(i < 3)
        def _():
            strip(i + 1).start()

        mixed[:, pl.ds(mult(i * rows, 128), rows)] = dot_nt(branch[...], strips[i % 2]).astype(mixed.dtype)
        quarter(i, carry)
        pl.when(i == 1)(after_second)
        pl.when(i == 3)(after_fourth)
        return carry

    lax.fori_loop(0, 4, step, 0)

    def terms(i, carry):
        at = pl.ds(mult(i * 1024, 128), 1024)
        query_up[:, at] = dot_tn(query_low[...], packed[:, at]).astype(query_up.dtype)
        width = latent_up.shape[1] // 4
        at = pl.ds(mult(i * width, 128), width)
        latent_up[:, at] = dot_tn(latent_low[...], grad_kv[:, at]).astype(latent_up.dtype)
        return carry

    lax.fori_loop(0, 4, terms, 0)
    sums.end(0)
    sums.end(1)
    gather.hop(3)
    gather.finish()
    swap.finish()
    downs.finish()
    sums.finish()


def middle_exchange(cid, scale, branch, cols, down, up, attn_out, query_low, latent_low, attend_in):
    kind = branch.dtype
    query, kv, rope = attend_in[:3]
    rows = query.shape[0]
    return pl.pallas_call(
        functools.partial(middle_kernel, scale),
        out_shape=[jax.ShapeDtypeStruct((8 * branch.shape[0], branch.shape[1]), kind), jax.ShapeDtypeStruct(cols.shape, kind),
                   jax.ShapeDtypeStruct((down.shape[0], 4 * down.shape[1]), kind), jax.ShapeDtypeStruct((8,) + up.shape[2:], kind),
                   jax.ShapeDtypeStruct(query.shape, kind),
                   jax.ShapeDtypeStruct(kv.shape, kind), jax.ShapeDtypeStruct(rope.shape, jnp.float32),
                   jax.ShapeDtypeStruct((query_low.shape[1], 4096), kind),
                   jax.ShapeDtypeStruct((latent_low.shape[1], kv.shape[1]), kind)],
        in_specs=[VMEM] + [ANY] * 2 + [VMEM, ANY] + [VMEM] * 8, out_specs=[ANY] * 3 + [VMEM] * 6,
        scratch_shapes=[pltpu.VMEM((2 * rows, 256), kind), pltpu.VMEM(branch.shape, kind), pltpu.VMEM((rows, 4096), kind),
                        pltpu.VMEM((2, attn_out.shape[0] // 4, attn_out.shape[1]), kind), dma_sems(2)]
        + Gather.scratch(1) + ColumnSwap.scratch(1) + PlaneGather.scratch(2)
        + PlaneSum.scratch([(4,) + up.shape[2:]] * 2, kind),
        compiler_params=kernel_params(cid),
    )(branch, cols, down, up, attn_out, query_low, latent_low, *attend_in)


def latent_kernel(lat, query_up, latent_up, hidden, down, lat_all, query_part, latent_sum, out_term, *scratch):
    rep, zpos, core = place()
    gather = Gather((lat,), (lat_all,), scratch[:5])
    bufs, sems, rest = PlaneSum.split(scratch[5:], 2)
    width = query_up.shape[2] // 4

    def query_item(h):
        return (lambda p: query_up.at[pl.ds(4 * h, 4), :, pl.ds(mult(p * width, 128), width)], query_part.at[pl.ds(4 * h, 4)], h)

    sums = PlaneSum([query_item(0), query_item(1)], bufs, sems)
    latent_total, _ = Total.split(latent_up, latent_sum, rest)
    greet(rep, zpos, core, plane=2)
    sums.start()
    latent_total.start()
    gather.start()
    rows = lat.shape[0]

    def after_second():
        latent_total.pair()
        latent_total.step(0)

    def after_fourth():
        gather.hop(1)
        latent_total.step(1)

    def after_sixth():
        gather.hop(2)
        latent_total.step(2)

    def step(i, carry):
        out_term[i] = jnp.dot(hidden[pl.ds(mult(i * rows, rows), rows)], down[...],
                              preferred_element_type=jnp.float32).astype(out_term.dtype)
        pl.when(i == 1)(after_second)
        pl.when(i == 3)(after_fourth)
        pl.when(i == 5)(after_sixth)
        return carry

    lax.fori_loop(0, 8, step, 0)
    sums.middle(0)
    sums.middle(1)
    gather.hop(3)
    latent_total.finish()
    gather.finish()
    sums.end(0)
    sums.end(1)
    sums.finish()


def latent_sums(cid, lat, query_up, latent_up, hidden, down):
    kind = query_up.dtype
    part = jax.ShapeDtypeStruct((8, query_up.shape[1], query_up.shape[2] // 4), kind)
    half = (4,) + part.shape[1:]
    return pl.pallas_call(
        latent_kernel,
        out_shape=[jax.ShapeDtypeStruct((8 * lat.shape[0], lat.shape[1]), lat.dtype), part,
                   jax.ShapeDtypeStruct(latent_up.shape[1:], jnp.float32),
                   jax.ShapeDtypeStruct((8, lat.shape[0], down.shape[1]), kind)],
        in_specs=[ANY] + [VMEM] * 4, out_specs=[ANY] + [VMEM] * 3,
        scratch_shapes=Gather.scratch(1) + PlaneSum.scratch([half] * 2, kind) + Total.scratch(latent_up),
        compiler_params=kernel_params(cid),
    )(lat, query_up, latent_up, hidden, down)


def last_kernel(*refs):
    gate, up, term, attn_out, lat, latent_up, query_up, gain = refs[:8]
    gate_all, up_all, out, attn_sum, lat_sum, latent_sum, query_sum, gain_out = refs[8:16]
    scratch = list(refs[16:])
    rep, zpos, core = place()
    shard = zpos * 2 + core
    places = plane_places(rep)
    swap = ColumnSwap([(lambda s, a=a: a.at[s], lambda s, b=b: b.at[s, rep]) for a, b in ((gate, gate_all), (up, up_all))],
                      scratch[:2] + [None], keeps=False)
    spread_sems, scratch = scratch[2:5], scratch[5:]
    total, scratch = Total.split(term, out, scratch)
    owns = scratch[:5]
    gain_landed, gain_sum, gain_plane, gsend, grecv, hsend, hrecv = scratch[5:12]
    query_total, scratch = Total.split(query_up, scratch[12], scratch[13:])
    bufs, sems, _ = PlaneSum.split(scratch, 4)

    def part(m, b):
        return lambda p: b.at[shard if m == 0 else column_place(zpos, core, m, True), p]

    half = attn_out.shape[0] // 2
    sums = PlaneSum(
        [(functools.partial(quarter_cols, attn_out, h * half, half), owns[h], h) for h in range(2)]
        + [(lambda p: lat.at[p], owns[2], 0), (functools.partial(quarter_cols, latent_up, 0, latent_up.shape[0]), owns[3], 1)],
        bufs, sems)
    spread = PlaneGather(
        [(a.at[shard] if m == 0 else None, part(m, b), h) for m in range(8) for h, (a, b) in enumerate(((gate, gate_all), (up, up_all)))]
        + [(owns[h], functools.partial(quarter_cols, attn_sum, h * half, half), h) for h in range(2)]
        + [(owns[2], lambda p: lat_sum.at[p], 0),
           (owns[3], functools.partial(quarter_cols, latent_sum, 0, latent_up.shape[0]), 1),
           (owns[4], functools.partial(quarter_cols, query_sum, 0, query_up.shape[1]), 0)], spread_sems)

    def gain_copy(m):
        s2 = column_place(zpos, core, m)
        return remote(gain.at[s2], gain_landed.at[m - 1], gsend.at[m - 1], grecv.at[m - 1], rep, s2)

    def gain_on(k):
        return remote(gain_sum, gain_plane.at[k], hsend.at[k], hrecv.at[k], places[k], shard)

    greet(rep, zpos, core, plane=3, column=True)
    for m in range(1, 8):
        gain_copy(m).start()
    sums.start()
    swap.start()
    spread.start((0, 1))
    query_total.start()
    total.start()
    gain_sum[...] = gain[shard]
    for m in range(1, 8):
        gain_copy(m).wait_recv()
        gain_sum[...] += gain_landed[m - 1]
    for k in range(3):
        gain_on(k).start()
    near = ColumnSwap.near
    for i, m in enumerate(near):
        swap.arrive(m)
        spread.start((2 * m, 2 * m + 1))
        if i in (1, 2):
            for k in range(2):
                sums.middle(2 * i - 2 + k)
        if i == 1:
            query_total.pair()
        if i in (1, 2, 3):
            query_total.step(i - 1)
        if i == 4:
            query_total.finish()
            owns[4][...] = query_total.out[...].astype(owns[4].dtype)
            spread.start((20,))
        before = 0 if i == 0 else near[i - 1]
        spread.middle(2 * before)
        spread.middle(2 * before + 1)
        if i == 3:
            total.pair()
            total.step(0)
        if i in (3, 4):
            for k in range(2):
                sums.end(2 * i - 6 + k)
                spread.start((2 * i + 10 + k,))
    total.step(1)
    for i in (2 * near[-1], 2 * near[-1] + 1, 20, 16, 17):
        spread.middle(i)
    total.step(2)
    for i in (18, 19):
        spread.middle(i)
    gain_out[...] = gain_sum[...]
    for k in range(3):
        gain_on(k).wait_recv()
        gain_out[...] += gain_plane[k]
    for k in range(3):
        gain_on(k).wait_send()
    for m in range(1, 8):
        gain_copy(m).wait_send()
    total.finish()
    swap.finish(arrive=False)
    sums.finish()
    spread.finish()


def last_sums(cid, gate, up, term, attn_out, lat, latent_up, query_up, gain):
    kind = gate.dtype
    shapes = [(attn_out.shape[0] // 2, attn_out.shape[1] // 4)] * 2 + [
        lat.shape[1:], (latent_up.shape[0], latent_up.shape[1] // 4)]
    block = pltpu.VMEM(gain.shape[1:], gain.dtype)
    return pl.pallas_call(
        last_kernel,
        out_shape=[jax.ShapeDtypeStruct((8, 4) + gate.shape[1:], kind)] * 2
        + [jax.ShapeDtypeStruct(term.shape[1:], jnp.float32)]
        + [jax.ShapeDtypeStruct(a.shape, kind) for a in (attn_out, lat, latent_up)]
        + [jax.ShapeDtypeStruct((query_up.shape[1], 4 * query_up.shape[2]), kind), jax.ShapeDtypeStruct(gain.shape[1:], gain.dtype)],
        in_specs=[ANY] * 2 + [VMEM] * 6, out_specs=[ANY] * 2 + [VMEM] + [ANY] * 4 + [VMEM],
        scratch_shapes=[dma_sems(7, 2), dma_sems(7, 2)] + PlaneGather.scratch(21) + Total.scratch(term)
        + [pltpu.VMEM(s, kind) for s in shapes + [query_up.shape[1:]]]
        + [pltpu.VMEM((7,) + gain.shape[1:], gain.dtype), block, pltpu.VMEM((3,) + gain.shape[1:], gain.dtype)]
        + [dma_sems(7)] * 2 + [dma_sems(3)] * 2 + [pltpu.VMEM(query_up.shape[1:], jnp.float32)] + Total.scratch(query_up)
        + PlaneSum.scratch(shapes, kind),
        compiler_params=kernel_params(cid),
    )(gate, up, term, attn_out, lat, latent_up, query_up, gain)


def start_kernel(*refs):
    ins, (gate, up) = refs[:7], refs[7:9]
    outs, cols = refs[9:16], refs[16:18]
    (zsend, zrecv, xsend, xrecv, ysend, yrecv, dsend, drecv, csend, crecv, own, gsend, grecv, psend, precv) = refs[18:33]
    held, strips = refs[33:40], refs[40:42]
    rep, zpos, core = place()
    xrep, yrep, drep = plane_places(rep)
    shard = zpos * 2 + core

    def whole(a, z, c):
        rows = ins[a].shape[0]
        return outs[a].at[pl.ds(mult((z * 2 + c) * rows, rows), rows)]

    def pieces(a, z, c, quarter, act, own_ref=False):
        def part(b, first, rows):
            full = ins[b].shape[0]
            if own_ref:
                return ins[b].at[pl.ds(mult(first, 16), rows)]
            return outs[b].at[pl.ds(mult((z * 2 + c) * full + first, 16), rows)]

        if a < 3:
            rows = ins[a].shape[0] // 4
            act(part(a, quarter * rows, rows))
        elif a == 3:
            @pl.when(quarter < 3)
            def _():
                act(part(3, jnp.minimum(quarter, 2) * 32, 32))

            @pl.when(quarter == 3)
            def _():
                act(part(4, 0, 32))
        else:
            act(ins[a + 1] if own_ref else whole(a + 1, z, c))

    copy = remote

    def hop(a, way, h, z, what):
        def act(ref):
            c = copy(ref, ref, zsend.at[way, h, a], zrecv.at[way, h, a], rep, (zpos + 1 - 2 * way) * 2 + core)
            getattr(c, what)()
        pieces(a, z, core, rep, act)

    def to_plane(a, k, z, quarter, what, sems, r):
        def act(ref):
            getattr(copy(ref, ref, sems[0].at[k, a], sems[1].at[k, a], r, shard), what)()
        pieces(a, z, core, quarter, act)

    def to_core(a, slot, z, c, what, src=None):
        ref = whole(a, z, c)
        getattr(copy(ref if src is None else src, ref, csend.at[slot, a], crecv.at[slot, a], rep, zpos * 2 + 1 - core), what)()

    greet(rep, zpos, core, plane=2, column=True)
    def send_own(a):
        def first(way):
            def go(src):
                def act(ref):
                    copy(src, ref, zsend.at[way, 0, a], zrecv.at[way, 0, a], rep, (zpos + 1 - 2 * way) * 2 + core).start()
                return act
            return go
        for way in range(2):
            @pl.when(zpos < 3 if way == 0 else zpos > 0)
            def _():
                if a < 3:
                    rows = ins[a].shape[0] // 4
                    src = ins[a].at[pl.ds(mult(rep * rows, 16), rows)]
                    pieces(a, zpos, core, rep, first(way)(src))
                elif a == 3:
                    @pl.when(rep < 3)
                    def _():
                        start = mult(jnp.minimum(rep, 2) * 32, 16)
                        src = ins[3].at[pl.ds(start, 32)]
                        dst = outs[3].at[pl.ds(mult(shard * 96 + start, 16), 32)]
                        first(way)(src)(dst)

                    @pl.when(rep == 3)
                    def _():
                        first(way)(ins[4])(whole(4, zpos, core))
                else:
                    first(way)(ins[a + 1])(whole(a + 1, zpos, core))

    def keep(a, half):
        if half == 0:
            return pltpu.make_async_copy(ins[a], held[a], own.at[0, a])
        return pltpu.make_async_copy(held[a], whole(a, zpos, core), own.at[1, a])

    for a in range(4):
        send_own(a)

    strip = cols[0].shape[1]
    quarter_rows = gate.shape[0] // 4

    def slice_of(which, s, first, rows):
        start = mult((s * 25 // 4) * 128, 128)
        return (gate, up)[which].at[pl.ds(mult(first, 16), rows), pl.ds(start, strip)]

    def rows_of(which, s, quarter):
        return cols[which].at[pl.ds(mult(s * gate.shape[0] + quarter * quarter_rows, 16), quarter_rows)]

    def slice_copy(m, which):
        s2 = column_place(zpos, core, m)
        return remote(slice_of(which, s2, rep * quarter_rows, quarter_rows), rows_of(which, shard, rep),
                      gsend.at[m - 1, which], grecv.at[m - 1, which], rep, s2)

    def slice_plane(m, quarter, kind, r):
        ref = rows_of(0, column_place(zpos, core, m, back=True), quarter)
        return remote(ref, ref, psend.at[kind, m - 1], precv.at[kind, m - 1], r, shard)

    def own_slice(which, half):
        if half == 0:
            return pltpu.make_async_copy(slice_of(which, shard, 0, gate.shape[0]), strips[which], own.at[0, 7 + which])
        rows = gate.shape[0]
        return pltpu.make_async_copy(strips[which], cols[which].at[pl.ds(mult(shard * rows, rows), rows)], own.at[1, 7 + which])

    near = (1, 2, 6, 3, 7, 4, 5)
    for a in range(7):
        to_core(a, 0, zpos, core, "start", src=ins[a])
        keep(a, 0).start()
    for which in range(2):
        own_slice(which, 0).start()
    for a in range(7):
        keep(a, 0).wait()
        keep(a, 1).start()
    for which in range(2):
        own_slice(which, 0).wait()
        own_slice(which, 1).start()

    def slices_from_column(m):
        for which in range(2):
            s2 = column_place(zpos, core, m, back=True)
            ref = rows_of(which, s2, rep)
            remote(ref, ref, gsend.at[m - 1, which], grecv.at[m - 1, which], rep, s2).wait_recv()
        slice_plane(m, rep, 0, xrep).start()
        slice_plane(m, rep, 1, yrep).start()

    def slices_from_plane(m):
        slice_plane(m, xrep, 0, xrep).wait_recv()
        slice_plane(m, yrep, 1, yrep).wait_recv()
        slice_plane(m, *onward(m)).start()

    def onward(m):
        return (xrep, 2, yrep) if m % 2 else (yrep, 2, xrep)

    def from_column(h, way, z, slots=range(4)):
        for a in slots:
            hop(a, way, h - 1, z, "wait_recv")
            if h < 3:
                @pl.when(zpos < 3 if way == 0 else zpos > 0)
                def _():
                    hop(a, way, h, z, "start")
            if a < 4:
                to_plane(a, way * 3 + h - 1, z, rep, "start", (xsend, xrecv), xrep)
                to_plane(a, way * 3 + h - 1, z, rep, "start", (ysend, yrecv), yrep)
            else:
                to_core(a + 1, way * 3 + h, z, core, "start")

    def from_plane(h, way, z):
        k = way * 3 + h - 1
        for a in range(4):
            to_plane(a, k, z, xrep, "wait_recv", (xsend, xrecv), xrep)
            if a == 0:
                to_plane(a, k, z, xrep, "start", (dsend, drecv), yrep)
            to_plane(a, k, z, yrep, "wait_recv", (ysend, yrecv), yrep)
            if a > 0:
                to_plane(a, k, z, yrep, "start", (dsend, drecv), xrep)

    def from_corner(h, way, z):
        k = way * 3 + h - 1
        for a in range(4):
            to_plane(a, k, z, drep, "wait_recv", (dsend, drecv), drep)
        for a in range(5):
            to_core(a, k + 1, z, core, "start")

    def by_hop(stage, h, *more):
        for way in range(2):
            z = zpos - h if way == 0 else zpos + h

            @pl.when(z >= 0 if way == 0 else z <= 3)
            def _():
                stage(h, way, z, *more)

    by_hop(from_column, 1)
    by_hop(from_column, 2)
    for m in near:
        for which in range(2):
            slice_copy(m, which).start()
    by_hop(from_plane, 1)
    by_hop(from_column, 3)
    by_hop(from_plane, 2)
    by_hop(from_corner, 1)
    for m in near[:3]:
        slices_from_column(m)
    send_own(4)
    send_own(5)
    by_hop(from_plane, 3)
    for m in near[3:]:
        slices_from_column(m)
    by_hop(from_corner, 2)
    for m in near[:3]:
        slices_from_plane(m)
    by_hop(from_column, 1, (5, 4))
    by_hop(from_corner, 3)
    for m in near[3:]:
        slices_from_plane(m)
    by_hop(from_column, 2, (5, 4))
    by_hop(from_column, 3, (5, 4))
    for a in range(7):
        to_core(a, 0, zpos, core, "wait_send", src=ins[a])
        to_core(a, 0, zpos, 1 - core, "wait_recv")
        keep(a, 1).wait()
    for which in range(2):
        own_slice(which, 1).wait()
        for m in near:
            slice_copy(m, which).wait_send()
    for m in near:
        slice_plane(m, rep, 0, xrep).wait_send()
        slice_plane(m, rep, 1, yrep).wait_send()
        slice_plane(m, *onward(m)).wait_send()
        slice_plane(m, drep, 2, drep).wait_recv()
    for way in range(2):
        for h in range(3):
            z = zpos - h if way == 0 else zpos + h

            @pl.when((z >= 0) & (zpos < 3) if way == 0 else (z <= 3) & (zpos > 0))
            def _():
                for a in range(6):
                    hop(a, way, h, z, "wait_send")
    for h in range(1, 4):
        for way in range(2):
            z = zpos - h if way == 0 else zpos + h
            k = way * 3 + h - 1

            @pl.when(z >= 0 if way == 0 else z <= 3)
            def _():
                for a in range(4):
                    to_plane(a, k, z, rep, "wait_send", (xsend, xrecv), xrep)
                    to_plane(a, k, z, rep, "wait_send", (ysend, yrecv), yrep)
                    to_plane(a, k, z, xrep if a == 0 else yrep, "wait_send", (dsend, drecv), yrep)
                for a in range(7):
                    to_core(a, k + 1, z, core, "wait_send")
                    to_core(a, k + 1, z, 1 - core, "wait_recv")

def start_gather(cid, weights, gate, up, strip):
    out = [jax.ShapeDtypeStruct((a.shape[0] * 8,) + a.shape[1:], a.dtype) for a in weights]
    out += [jax.ShapeDtypeStruct((gate.shape[0] * 8, strip), gate.dtype)] * 2
    return pl.pallas_call(
        start_kernel, out_shape=out, in_specs=[ANY] * 9, out_specs=[ANY] * 9,
        scratch_shapes=[dma_sems(2, 3, 6), dma_sems(2, 3, 6)] + [dma_sems(6, 4)] * 6
        + [dma_sems(7, 7), dma_sems(7, 7), dma_sems(2, 9), dma_sems(7, 2), dma_sems(7, 2), dma_sems(3, 7), dma_sems(3, 7)]
        + [pltpu.VMEM(a.shape, a.dtype) for a in weights] + [pltpu.VMEM((gate.shape[0], strip), gate.dtype)] * 2,
        compiler_params=kernel_params(cid),
    )(*weights, gate, up)

def plane_swap(values, j):
    return lax.ppermute(values, "rep", [(i, i ^ j) for i in range(4)])


def column_body(
    tokens,
    cotangent,
    doc_lengths,
    gain_attn,
    query_down,
    gain_query,
    query_up,
    latent_down,
    gain_latent,
    latent_up,
    attn_out,
    gain_ffn,
    w_gate,
    w_up,
    w_down,
):
    low = jnp.bfloat16
    wide = jnp.float32
    rows, width = tokens.shape[1], tokens.shape[2]
    seq_len = rows * 4
    head_dim = ND + RD
    scale = head_dim ** (-0.5)
    rep, shard = lax.axis_index("rep"), lax.axis_index("shard")
    slice_ff = FF // 8
    strip = 896
    shift = (slice_ff * shard) % 128

    small = jnp.concatenate(
        [v.astype(wide) for v in (gain_attn, gain_ffn, gain_query, gain_latent)]
        + [jnp.zeros((1024 - 768,), wide)]
    ).reshape(8, 128)
    tile_up = jnp.pad(
        query_up.reshape(-1, H, head_dim), ((0, 0), (0, 0), (0, 128 - head_dim))
    ).reshape(-1, H * 128)
    grad_out = cotangent[0].astype(wide)
    grad_down_in = (residual_scale * grad_out).astype(low)
    aout, qdown, ldown, qup, lup, gd_all, small_all, gate_w, up_quarter = start_gather(
        0, (attn_out, query_down, latent_down, tile_up, latent_up, grad_down_in, small), w_gate, w_up, strip
    )
    small_all = small_all.reshape(8, 1024)
    gain_in = small_all[:, :320].reshape(-1)
    gain_f = small_all[:, 320:640].reshape(-1)
    gain_q = small_all[:, 640:736].reshape(-1)
    gain_l = small_all[:, 736:768].reshape(-1)

    down_w = lax.dynamic_update_slice(jnp.zeros((strip, width), low), w_down, (shift, 0))

    local_pos = rep * rows + jnp.arange(rows, dtype=jnp.int32)
    key_pos = jnp.concatenate(
        [(rep ^ j) * rows + jnp.arange(rows, dtype=jnp.int32) for j in range(4)]
    )
    query_seg, query_off = segment_of(doc_lengths[0], local_pos)
    key_seg = segment_of(doc_lengths[0], key_pos)[0]
    allowed = (query_seg[:, None] == key_seg[None, :]) & (key_pos[None, :] <= local_pos[:, None])
    bias = jnp.where(allowed, 0.0, masked_score).astype(wide)
    cos_part, sin_part = rope_tables(query_off, RD)
    none = jnp.zeros((rows, RD // 2), wide)
    edge = jnp.zeros((rows, ND), wide)
    tail = jnp.zeros((rows, 128 - head_dim), wide)
    turns = jnp.stack(
        [
            jnp.concatenate([edge + 1.0, cos_part, cos_part, tail], axis=1),
            jnp.concatenate([edge, none, sin_part, tail], axis=1),
            jnp.concatenate([edge, -sin_part, none, tail], axis=1),
        ]
    )
    inputs = tokens[0].astype(wide)
    normed, norm_in_back = jax.vjp(rms_scale, inputs, gain_in)
    normed_low = normed.astype(low)
    latent_proj = jnp.dot(normed_low, ldown, preferred_element_type=wide)
    latent_norm, norm_l_back = jax.vjp(rms_scale, latent_proj[:, :KR], gain_l)

    def key_rotate(values):
        return rotate(values, cos_part, sin_part)

    key_rot, key_back = jax.vjp(key_rotate, latent_proj[:, KR:])
    latents = jnp.concatenate([latent_norm.astype(low), key_rot.astype(low)], axis=1)
    latents = jnp.concatenate([latents] + [plane_swap(latents, j) for j in range(1, 4)], axis=0)
    latent_low, all_rope = latents[:, :KR], latents[:, KR:]
    query_lat = jnp.dot(normed_low, qdown, preferred_element_type=wide)
    query_norm, norm_q_back = jax.vjp(rms_scale, query_lat, gain_q)
    query_low = query_norm.astype(low)
    query_proj = jnp.dot(query_low, qup, preferred_element_type=wide)
    keyvals = jnp.dot(latent_low, lup, preferred_element_type=wide).astype(low)
    rope_tile = jnp.pad(all_rope, ((0, 0), (ND, 128 - head_dim)))
    queries, mixed_low, logs = attend(scale, query_proj, keyvals, rope_tile, bias, turns)
    branch = jnp.dot(mixed_low, aout, preferred_element_type=wide)
    residual = inputs + residual_scale * branch
    normed_ffn, norm_f_back = jax.vjp(rms_scale, residual, gain_f)
    ffn_low = normed_ffn.astype(low)

    ffn_all, up_w, grad_hidden = ffn_gather(1, ffn_low, up_quarter, gd_all, down_w)
    gate_pre = jnp.dot(ffn_all, gate_w, preferred_element_type=wide)
    up_pre = jnp.dot(ffn_all, up_w, preferred_element_type=wide)
    hidden, act_back = jax.vjp(swiglu, gate_pre, up_pre)
    hidden_low = hidden.astype(low)
    grad_gate_f, grad_up_f = act_back(grad_hidden)
    grad_gate = grad_gate_f.astype(low)
    grad_up = grad_up_f.astype(low)
    down_part = inner_rows(hidden_low, gd_all).astype(low)
    grad_ffn_in, down_own, gate_own, up_part = back_sums(
        2, down_part, ffn_all, grad_gate, grad_up, gate_w, up_w, slice_ff
    )

    grad_res_norm, grad_gain_ffn = norm_f_back(grad_ffn_in)
    grad_resid = grad_out + grad_res_norm
    grad_branch = (residual_scale * grad_resid).astype(low)
    cols = jnp.stack([mixed_low, normed_low]).reshape(2, rows, 8, width // 8).transpose(2, 0, 1, 3)
    (
        branch_all,
        cols_all,
        down_all,
        up_own,
        grad_q_proj,
        grad_kv,
        grad_rope,
        qup_part,
        lup_part,
    ) = middle_exchange(
        3,
        scale,
        grad_branch,
        cols,
        down_own,
        up_part,
        aout,
        query_low,
        latent_low,
        (queries, keyvals, rope_tile, bias, turns, logs),
    )
    down_grad = down_all.astype(wide)
    rope_sum = grad_rope[:, ND:head_dim]
    grad_lat_part = jnp.concatenate([outer_cols(grad_kv, lup), rope_sum], axis=1).astype(low)
    grad_lat_own = grad_lat_part[:rows].astype(wide)
    for j in range(1, 4):
        grad_lat_own = grad_lat_own + plane_swap(
            grad_lat_part[j * rows : (j + 1) * rows], j
        ).astype(wide)
    grad_q_lat_f, grad_gain_query = norm_q_back(outer_cols(grad_q_proj, qup))
    grad_q_lat = grad_q_lat_f.astype(low)
    grad_lat_c, grad_gain_latent = norm_l_back(grad_lat_own[:, :KR])
    grad_lat_r = key_back(grad_lat_own[:, KR:])[0]
    grad_lat = jnp.concatenate([grad_lat_c, grad_lat_r], axis=1).astype(low)
    grad_normed = outer_cols(grad_q_lat, qdown) + outer_cols(grad_lat, ldown)
    grad_in_norm, grad_gain_attn = norm_in_back(grad_normed)
    tokens_grad = (grad_resid + grad_in_norm).astype(low)

    grad_lats = jnp.concatenate([grad_q_lat, grad_lat], axis=1)
    lat_all, qup_own, lup_sum, out_part = latent_sums(
        4,
        grad_lats,
        qup_part.reshape(8, -1, qup_part.shape[1]),
        lup_part.reshape(8, -1, lup_part.shape[1]),
        hidden_low,
        down_w,
    )
    mixed_cols = cols_all[:, 0].reshape(8 * rows, width // 8)
    normed_cols = cols_all[:, 1].reshape(8 * rows, width // 8)
    aout_part = inner_rows(mixed_cols, branch_all).astype(low)
    lat_part = inner_rows(normed_cols, lat_all).astype(low)
    gains = jnp.concatenate(
        [
            v.reshape(8, -1)
            for v in (grad_gain_attn, grad_gain_ffn, grad_gain_query, grad_gain_latent)
        ]
        + [jnp.zeros((8, 1024 - 768), wide)],
        axis=1,
    ).reshape(8, 8, 128)
    gate_all, up_all, out_sum, aout_own, lat_own, lup_own, qup_own, gain_own = last_sums(
        5,
        gate_own,
        up_own,
        out_part,
        aout_part,
        lat_part.reshape(4, 80, -1),
        lup_sum.astype(low),
        qup_own,
        gains,
    )
    layer_out = (residual + residual_scale * out_sum).astype(low)
    gate_grad, up_grad = widen((gate_all, up_all), FF)
    aout_own = aout_own.astype(wide)
    lat_own = lat_own.reshape(320, -1).astype(wide)
    lup_own = lup_own.astype(wide)
    qup_own = unpack(qup_own, H)
    gain_own = gain_own.reshape(1024)

    return (
        layer_out[None],
        tokens_grad[None],
        gain_own[:320],
        lat_own[:, : query_down.shape[1]],
        gain_own[640:736],
        qup_own,
        lat_own[:, query_down.shape[1] :],
        gain_own[736:768],
        lup_own,
        aout_own,
        gain_own[320:640],
        gate_grad,
        up_grad,
        down_grad,
    )


def body(
    tokens,
    cotangent,
    doc_lengths,
    gain_attn,
    query_down,
    gain_query,
    query_up,
    latent_down,
    gain_latent,
    latent_up,
    attn_out,
    gain_ffn,
    w_gate,
    w_up,
    w_down,
):
    low_type = jnp.bfloat16
    wide_type = jnp.float32
    tok_rows = tokens.shape[1]
    seq_len = tok_rows * lax.axis_size("rep")
    head_dim = ND + RD
    group_size = math.gcd(H, 8)
    group_count = H // group_size
    softmax_scale = head_dim ** (-0.5)
    local_pos = lax.axis_index("rep") * tok_rows + jnp.arange(tok_rows, dtype=jnp.int32)
    key_pos = jnp.arange(seq_len, dtype=jnp.int32)
    query_seg, query_off = segment_of(doc_lengths[0], local_pos)
    key_seg = segment_of(doc_lengths[0], key_pos)[0]
    allowed = (query_seg[:, None] == key_seg[None, :]) & (key_pos[None, :] <= local_pos[:, None])
    cos_part, sin_part = rope_tables(query_off, RD)
    (
        gain_in_full,
        qdown_full,
        gain_q_full,
        qup_full,
        ldown_full,
        gain_l_full,
        lup_full,
        aout_full,
        gain_f_full,
    ) = (
        lax.all_gather(gain_attn, "shard", axis=0, tiled=True),
        lax.all_gather(query_down, "shard", axis=0, tiled=True),
        lax.all_gather(gain_query, "shard", axis=0, tiled=True),
        lax.all_gather(query_up, "shard", axis=0, tiled=True),
        lax.all_gather(latent_down, "shard", axis=0, tiled=True),
        lax.all_gather(gain_latent, "shard", axis=0, tiled=True),
        lax.all_gather(latent_up, "shard", axis=0, tiled=True),
        lax.all_gather(attn_out, "shard", axis=0, tiled=True),
        lax.all_gather(gain_ffn, "shard", axis=0, tiled=True),
    )
    inputs = tokens[0].astype(wide_type)
    normed, norm_in_back = jax.vjp(rms_scale, inputs, gain_in_full.astype(wide_type))
    normed_low = normed.astype(low_type)
    query_lat = jnp.dot(normed_low, qdown_full, preferred_element_type=wide_type)
    query_norm, norm_q_back = jax.vjp(rms_scale, query_lat, gain_q_full.astype(wide_type))
    query_low = query_norm.astype(low_type)
    query_proj = jnp.dot(query_low, qup_full, preferred_element_type=wide_type).reshape(
        tok_rows, H, head_dim
    )

    def query_rope(values):
        return jnp.concatenate(
            [
                values[..., :ND],
                rotate(values[..., ND:], cos_part[:, None, :], sin_part[:, None, :]),
            ],
            axis=-1,
        )

    query_rot, query_back = jax.vjp(query_rope, query_proj)
    query_used = query_rot.astype(low_type)
    latent_proj = jnp.dot(normed_low, ldown_full, preferred_element_type=wide_type)
    latent_norm, norm_l_back = jax.vjp(
        rms_scale, latent_proj[:, :KR], gain_l_full.astype(wide_type)
    )
    latent_low = latent_norm.astype(low_type)

    def key_rotate(values):
        return rotate(values, cos_part, sin_part)

    key_rot, key_back = jax.vjp(key_rotate, latent_proj[:, KR:])
    key_rope = key_rot.astype(low_type)
    keyvals = jnp.dot(latent_low, lup_full, preferred_element_type=wide_type).astype(low_type)
    all_keyvals, all_rope = (
        lax.all_gather(keyvals, "rep", axis=0, tiled=True),
        lax.all_gather(key_rope, "rep", axis=0, tiled=True),
    )
    queries = query_used.reshape(tok_rows, group_count, group_size, head_dim).transpose(1, 0, 2, 3)
    key_groups = all_keyvals.reshape(seq_len, group_count, group_size, ND + VD).transpose(
        1, 0, 2, 3
    )

    def scores_of(query_blk, key_blk):
        nope_part = jnp.einsum(
            "thd,shd->hts", query_blk[..., :ND], key_blk[..., :ND], preferred_element_type=wide_type
        )
        rope_part = jnp.einsum(
            "thd,sd->hts", query_blk[..., ND:], all_rope, preferred_element_type=wide_type
        )
        return jnp.where(allowed[None], (nope_part + rope_part) * softmax_scale, masked_score)

    def forward_group(carry, blocks):
        query_blk, key_blk = blocks
        scores = scores_of(query_blk, key_blk)
        row_max = jnp.max(scores, axis=-1, keepdims=True)
        exp_scores = jnp.exp(scores - row_max)
        totals = jnp.sum(exp_scores, axis=-1, keepdims=True)
        probs = (exp_scores / totals).astype(low_type)
        mixed = jnp.einsum(
            "hts,shd->thd", probs, key_blk[..., ND:], preferred_element_type=wide_type
        )
        return (carry, (mixed, row_max + jnp.log(totals)))

    start_carry = jnp.zeros((), wide_type)
    final_carry, (mixed_groups, log_totals) = lax.scan(
        forward_group, start_carry, (queries, key_groups)
    )
    mixed_low = mixed_groups.transpose(1, 0, 2, 3).reshape(tok_rows, H * VD).astype(low_type)
    branch = jnp.dot(mixed_low, aout_full, preferred_element_type=wide_type)
    residual = inputs + residual_scale * branch
    normed_ffn, norm_f_back = jax.vjp(rms_scale, residual, gain_f_full.astype(wide_type))
    ffn_low = normed_ffn.astype(low_type)
    gate_full, up_full, down_full = (
        lax.all_gather(w_gate, "shard", axis=0, tiled=True),
        lax.all_gather(w_up, "shard", axis=0, tiled=True),
        lax.all_gather(w_down, "shard", axis=0, tiled=True),
    )
    gate_pre = jnp.dot(ffn_low, gate_full, preferred_element_type=wide_type)
    up_pre = jnp.dot(ffn_low, up_full, preferred_element_type=wide_type)
    hidden, act_back = jax.vjp(swiglu, gate_pre, up_pre)
    hidden_low = hidden.astype(low_type)
    ffn_branch = jnp.dot(hidden_low, down_full, preferred_element_type=wide_type)
    layer_out = residual + residual_scale * ffn_branch
    grad_out = cotangent[0].astype(wide_type)
    grad_down_in = (residual_scale * grad_out).astype(low_type)
    gate_back_w, up_back_w, down_back_w = (
        lax.all_gather(w_gate, "shard", axis=0, tiled=True),
        lax.all_gather(w_up, "shard", axis=0, tiled=True),
        lax.all_gather(w_down, "shard", axis=0, tiled=True),
    )
    grad_hidden = outer_cols(grad_down_in, down_back_w)
    grad_gate_f, grad_up_f = act_back(grad_hidden)
    grad_gate = grad_gate_f.astype(low_type)
    grad_up = grad_up_f.astype(low_type)
    grad_ffn_in = outer_cols(grad_gate, gate_back_w) + outer_cols(grad_up, up_back_w)
    down_grad = lax.psum_scatter(
        inner_rows(hidden_low, grad_down_in).astype(jnp.bfloat16),
        "shard",
        scatter_dimension=0,
        tiled=True,
    )
    gate_up_in = jnp.concatenate([grad_gate, grad_up], axis=1)
    gate_up_grad = lax.psum_scatter(
        inner_rows(ffn_low, gate_up_in).astype(jnp.bfloat16),
        "shard",
        scatter_dimension=0,
        tiled=True,
    ).astype(jnp.float32)
    gate_grad = gate_up_grad[:, :FF]
    up_grad = gate_up_grad[:, FF:]
    grad_res_norm, grad_gain_ffn = norm_f_back(grad_ffn_in)
    grad_resid = grad_out + grad_res_norm
    qdown_back, qup_back, ldown_back, lup_back, aout_back = (
        lax.all_gather(query_down, "shard", axis=0, tiled=True),
        lax.all_gather(query_up, "shard", axis=0, tiled=True),
        lax.all_gather(latent_down, "shard", axis=0, tiled=True),
        lax.all_gather(latent_up, "shard", axis=0, tiled=True),
        lax.all_gather(attn_out, "shard", axis=0, tiled=True),
    )
    grad_branch = (residual_scale * grad_resid).astype(low_type)
    aout_grad = inner_rows(mixed_low, grad_branch)
    grad_mixed = outer_cols(grad_branch, aout_back).astype(low_type)
    grad_groups = grad_mixed.reshape(tok_rows, group_count, group_size, VD).transpose(1, 0, 2, 3)

    def backward_group(rope_acc, blocks):
        query_blk, key_blk, grad_blk, log_blk = blocks
        scores = scores_of(query_blk, key_blk)
        probs = jnp.exp(scores - log_blk)
        grad_probs = jnp.einsum(
            "thd,shd->hts", grad_blk, key_blk[..., ND:], preferred_element_type=wide_type
        )
        delta = jnp.sum(probs * grad_probs, axis=-1, keepdims=True)
        grad_scores = (probs * (grad_probs - delta)).astype(low_type)
        grad_query = (
            jnp.concatenate(
                [
                    jnp.einsum(
                        "hts,shd->thd",
                        grad_scores,
                        key_blk[..., :ND],
                        preferred_element_type=wide_type,
                    ),
                    jnp.einsum(
                        "hts,sd->thd", grad_scores, all_rope, preferred_element_type=wide_type
                    ),
                ],
                axis=-1,
            )
            * softmax_scale
        )
        grad_key = (
            jnp.einsum(
                "hts,thd->shd", grad_scores, query_blk[..., :ND], preferred_element_type=wide_type
            )
            * softmax_scale
        )
        grad_value = jnp.einsum(
            "hts,thd->shd", probs.astype(low_type), grad_blk, preferred_element_type=wide_type
        )
        rope_acc = (
            rope_acc
            + jnp.einsum(
                "hts,thd->sd", grad_scores, query_blk[..., ND:], preferred_element_type=wide_type
            )
            * softmax_scale
        )
        return (rope_acc, (grad_query, jnp.concatenate([grad_key, grad_value], axis=-1)))

    rope_start = jnp.zeros((seq_len, RD), wide_type)
    rope_sum, (grad_q_groups, grad_kv_groups) = lax.scan(
        backward_group, rope_start, (queries, key_groups, grad_groups, log_totals)
    )
    grad_kv_all = grad_kv_groups.transpose(1, 0, 2, 3).reshape(seq_len, H * (ND + VD))
    grad_kv_own, grad_rope_own = (
        lax.psum_scatter(
            grad_kv_all.astype(jnp.bfloat16), "rep", scatter_dimension=0, tiled=True
        ).astype(jnp.float32),
        lax.psum_scatter(
            rope_sum.astype(jnp.bfloat16), "rep", scatter_dimension=0, tiled=True
        ).astype(jnp.float32),
    )
    grad_q_full = grad_q_groups.transpose(1, 0, 2, 3).reshape(tok_rows, H, head_dim)
    grad_q_proj = query_back(grad_q_full)[0].reshape(tok_rows, H * head_dim).astype(low_type)
    qup_grad = inner_rows(query_low, grad_q_proj)
    grad_q_lat_f, grad_gain_query = norm_q_back(outer_cols(grad_q_proj, qup_back))
    grad_q_lat = grad_q_lat_f.astype(low_type)
    grad_kv_low = grad_kv_own.astype(low_type)
    lup_grad = inner_rows(latent_low, grad_kv_low)
    grad_lat_c, grad_gain_latent = norm_l_back(outer_cols(grad_kv_low, lup_back))
    grad_lat_r = key_back(grad_rope_own)[0]
    grad_lat = jnp.concatenate([grad_lat_c, grad_lat_r], axis=1).astype(low_type)
    qdown_grad = inner_rows(normed_low, grad_q_lat)
    ldown_grad = inner_rows(normed_low, grad_lat)
    grad_normed = outer_cols(grad_q_lat, qdown_back) + outer_cols(grad_lat, ldown_back)
    grad_in_norm, grad_gain_attn = norm_in_back(grad_normed)
    tokens_grad = (grad_resid + grad_in_norm).astype(low_type)
    (
        owned_gain_attn,
        owned_qdown,
        owned_gain_query,
        owned_qup,
        owned_ldown,
        owned_gain_latent,
        owned_lup,
        owned_aout,
        owned_gain_ffn,
    ) = (
        lax.psum_scatter(
            grad_gain_attn.astype(jnp.bfloat16), "shard", scatter_dimension=0, tiled=True
        ).astype(jnp.float32),
        lax.psum_scatter(
            qdown_grad.astype(jnp.bfloat16), "shard", scatter_dimension=0, tiled=True
        ).astype(jnp.float32),
        lax.psum_scatter(
            grad_gain_query.astype(jnp.bfloat16), "shard", scatter_dimension=0, tiled=True
        ).astype(jnp.float32),
        lax.psum_scatter(
            qup_grad.astype(jnp.bfloat16), "shard", scatter_dimension=0, tiled=True
        ).astype(jnp.float32),
        lax.psum_scatter(
            ldown_grad.astype(jnp.bfloat16), "shard", scatter_dimension=0, tiled=True
        ).astype(jnp.float32),
        lax.psum_scatter(
            grad_gain_latent.astype(jnp.bfloat16), "shard", scatter_dimension=0, tiled=True
        ).astype(jnp.float32),
        lax.psum_scatter(
            lup_grad.astype(jnp.bfloat16), "shard", scatter_dimension=0, tiled=True
        ).astype(jnp.float32),
        lax.psum_scatter(
            aout_grad.astype(jnp.bfloat16), "shard", scatter_dimension=0, tiled=True
        ).astype(jnp.float32),
        lax.psum_scatter(
            grad_gain_ffn.astype(jnp.bfloat16), "shard", scatter_dimension=0, tiled=True
        ).astype(jnp.float32),
    )
    summed = (
        lax.psum(owned_gain_attn.astype(jnp.bfloat16), "rep").astype(jnp.float32),
        lax.psum(owned_qdown.astype(jnp.bfloat16), "rep").astype(jnp.float32),
        lax.psum(owned_gain_query.astype(jnp.bfloat16), "rep").astype(jnp.float32),
        lax.psum(owned_qup.astype(jnp.bfloat16), "rep").astype(jnp.float32),
        lax.psum(owned_ldown.astype(jnp.bfloat16), "rep").astype(jnp.float32),
        lax.psum(owned_gain_latent.astype(jnp.bfloat16), "rep").astype(jnp.float32),
        lax.psum(owned_lup.astype(jnp.bfloat16), "rep").astype(jnp.float32),
        lax.psum(owned_aout.astype(jnp.bfloat16), "rep").astype(jnp.float32),
        lax.psum(owned_gain_ffn.astype(jnp.bfloat16), "rep").astype(jnp.float32),
        lax.psum(gate_grad.astype(jnp.bfloat16), "rep").astype(jnp.float32),
        lax.psum(up_grad.astype(jnp.bfloat16), "rep").astype(jnp.float32),
        lax.psum(down_grad, "rep").astype(jnp.float32),
    )
    return (
        layer_out.astype(low_type)[None],
        tokens_grad[None],
        summed[0],
        summed[1],
        summed[2],
        summed[3],
        summed[4],
        summed[5],
        summed[6],
        summed[7],
        summed[8],
        summed[9],
        summed[10],
        summed[11],
    )


def solution(mesh):
    placed = (
        P("shard", "rep", None),
        P("shard", "rep", None),
        P("shard", None),
        P("shard"),
        P("shard", None),
        P("shard"),
        P("shard", None),
        P("shard", None),
        P("shard"),
        P("shard", None),
        P("shard", None),
        P("shard"),
        P("shard", None),
        P("shard", None),
        P("shard", None),
    )
    fits = mesh.shape["rep"] == 4 and mesh.shape["shard"] == 8
    return jax.shard_map(
        column_body if fits else body,
        mesh=mesh,
        in_specs=placed,
        out_specs=(
            P("shard", "rep", None),
            P("shard", "rep", None),
            P("shard"),
            P("shard", None),
            P("shard"),
            P("shard", None),
            P("shard", None),
            P("shard"),
            P("shard", None),
            P("shard", None),
            P("shard"),
            P("shard", None),
            P("shard", None),
            P("shard", None),
        ),
        check_vma=False,
    )
```

```python
import functools
import math

import jax
import jax.numpy as jnp
from jax import lax
from jax.experimental import pallas as pl
from jax.experimental.pallas import tpu as pltpu
from jax.sharding import PartitionSpec as P

KR = 256
H = 40
ND = 64
RD = 32
VD = 64
FF = 6400


epsilon = 1e-05
residual_scale = 1.4 / math.sqrt(62.0)
rope_base = 10000.0
masked_score = -1e30


def rms_scale(values, gain):
    return values * lax.rsqrt(jnp.mean(values * values, axis=-1, keepdims=True) + epsilon) * gain


def rotate(values, cos_part, sin_part):
    midpoint = values.shape[-1] // 2
    former = values[..., :midpoint]
    latter = values[..., midpoint:]
    return jnp.concatenate(
        [former * cos_part - latter * sin_part, latter * cos_part + former * sin_part], axis=-1
    )


def segment_of(lengths, positions):
    doc_ends = jnp.cumsum(lengths)
    doc_starts = doc_ends - lengths
    segment = jnp.sum((positions[:, None] >= doc_ends[None, :]).astype(jnp.int32), axis=1)
    chosen = segment[:, None] == jnp.arange(lengths.shape[0], dtype=jnp.int32)[None, :]
    offsets = positions - jnp.sum(jnp.where(chosen, doc_starts[None, :], 0), axis=1)
    return (segment, offsets)


def rope_tables(offsets, rope_width):
    exponents = jnp.arange(0, rope_width, 2, dtype=jnp.float32) / rope_width
    angles = offsets.astype(jnp.float32)[:, None] * (rope_base ** (-exponents))[None, :]
    return (jnp.cos(angles), jnp.sin(angles))


def swiglu(gate_vals, up_vals):
    return jax.nn.silu(gate_vals) * up_vals


def inner_rows(leading, trailing):
    return lax.dot_general(
        leading, trailing, (((0,), (0,)), ((), ())), preferred_element_type=jnp.float32
    )


def outer_cols(leading, trailing):
    return lax.dot_general(
        leading, trailing, (((1,), (1,)), ((), ())), preferred_element_type=jnp.float32
    )


MESH = pl.DeviceIdType.MESH
ANY = pl.BlockSpec(memory_space=pl.ANY)

def place():
    rep = lax.axis_index("rep")
    shard = lax.axis_index("shard")
    zpos, core = shard // 2, shard % 2
    return rep, zpos, core

def mult(value, by):
    return pl.multiple_of(value, by)

def greet(rep, zpos, core, plane=0, column=False):
    barrier = pltpu.get_barrier_semaphore()
    shard = zpos * 2 + core

    def signal(r, s):
        pl.semaphore_signal(barrier, inc=1, device_id=(r, s), device_id_type=MESH)

    if column:
        for m in range(1, 8):
            signal(rep, column_place(zpos, core, m))
        count = 7
    else:
        signal(rep, zpos * 2 + 1 - core)

        @pl.when(zpos > 0)
        def _():
            signal(rep, shard - 2)

        @pl.when(zpos < 3)
        def _():
            signal(rep, shard + 2)

        count = 1 + jnp.minimum(zpos, 1) + jnp.minimum(3 - zpos, 1)
    if plane:
        for other in plane_places(rep)[:plane]:
            signal(other, shard)
        count = count + plane
    pl.semaphore_wait(barrier, count)


def plane_places(rep):
    return rep + 1 - 2 * (rep % 2), (rep + 2) % 4, 3 - rep


def column_place(zpos, core, m, back=False):
    step = 4 - m // 2 if back else m // 2
    return ((zpos + step) % 4) * 2 + (core + m) % 2


def remote(src, dst, ssem, rsem, r, s):
    return pltpu.make_async_remote_copy(
        src_ref=src, dst_ref=dst, send_sem=ssem, recv_sem=rsem, device_id=(r, s), device_id_type=MESH
    )


def dma_sems(*dims):
    return pltpu.SemaphoreType.DMA(dims)


def head_tile(h):
    return pl.ds(pl.multiple_of(h * 128, 128), 128)


def turn(values, tables, back=False):
    keep, high, low_part = tables
    if back:
        return values * keep + pltpu.roll(values * high, 112, 1) + pltpu.roll(values * low_part, 16, 1)
    return values * keep + pltpu.roll(values, 16, 1) * high + pltpu.roll(values, 112, 1) * low_part


def dot_nt(a, b):
    return lax.dot_general(a, b, (((1,), (1,)), ((), ())), preferred_element_type=jnp.float32)


def dot_tn(a, b):
    return lax.dot_general(a, b, (((0,), (0,)), ((), ())), preferred_element_type=jnp.float32)


def attend_heads(scale, proj, kv, rope, bias, turns, query, mixed, logs):
    low = jnp.bfloat16
    lane = lax.broadcasted_iota(jnp.int32, (1, 128), 1)
    first = lane < 64

    def group(i, carry):
        heads_here = [4 * i + j for j in range(4)]
        queries = [turn(proj[:, head_tile(h)], (turns[0], turns[1], turns[2])).astype(low) for h in heads_here]
        keyvals = [kv[:, head_tile(h)] for h in heads_here]
        scores = [dot_nt(q, jnp.where(first, keyval, rope[...])) * scale + bias[...] for q, keyval in zip(queries, keyvals)]
        tops = [jnp.max(s, axis=1, keepdims=True) for s in scores]
        grown = [jnp.exp(s - top) for s, top in zip(scores, tops)]
        totals = [jnp.sum(g, axis=1, keepdims=True) for g in grown]
        outs = [jnp.dot((g / total).astype(low), keyval, preferred_element_type=jnp.float32)
                for g, total, keyval in zip(grown, totals, keyvals)]
        for h, q, top, total in zip(heads_here, queries, tops, totals):
            query[:, head_tile(h)] = q
            logs[...] = jnp.where(lane == h, top + jnp.log(total), logs[...])
        for j in range(2):
            mixed[:, head_tile(2 * i + j)] = jnp.where(first, pltpu.roll(outs[2 * j], 64, 1), outs[2 * j + 1]).astype(low)
        return carry

    return group


def attend_back_heads(scale, query, kv, rope, bias, turns, logs, grad, grad_query, grad_packed, grad_kv, grad_rope, left):
    low = jnp.bfloat16
    rows = query.shape[0]
    lane = lax.broadcasted_iota(jnp.int32, (1, 128), 1)
    first = lane < 64

    def one(h, grad_value):
        q = query[:, head_tile(h)]
        keyval = kv[:, head_tile(h)]
        key = jnp.where(first, keyval, rope[...])
        left[0:rows, 0:128] = q
        left[rows:, 128:256] = grad_value
        both = dot_nt(left[...], jnp.concatenate([key, keyval], axis=1))
        log = jnp.sum(jnp.where(lane == h, logs[...], 0.0), axis=1, keepdims=True)
        probs = jnp.exp(both[:rows] * scale + bias[...] - log)
        weighed = probs * both[rows:]
        delta = jnp.sum(weighed, axis=1, keepdims=True)
        grad_scores = (weighed - probs * delta).astype(low)
        grad_q = jnp.dot(grad_scores, key, preferred_element_type=jnp.float32) * scale
        grad_q = turn(grad_q, (turns[0], turns[1], turns[2]), True)
        grad_query[:, head_tile(h)] = grad_q.astype(low)
        out = dot_tn(jnp.concatenate([grad_scores, probs.astype(low)], axis=0), left[...])
        grad_key = out[:, :128] * scale
        grad_rope[...] += grad_key
        grad_kv[:, head_tile(h)] = jnp.where(first, grad_key, out[:, 128:]).astype(low)
        return grad_q

    def quarter(i, carry):
        rotary = jnp.zeros((rows, 128), jnp.float32)
        for j in range(5):
            both = grad[:, head_tile(5 * i + j)].astype(jnp.float32)
            even = one(10 * i + 2 * j, jnp.where(first, 0.0, pltpu.roll(both, 64, 1)).astype(low))
            odd = one(10 * i + 2 * j + 1, jnp.where(first, 0.0, both).astype(low))
            grad_packed[:, head_tile(8 * i + j)] = jnp.where(first, even, pltpu.roll(odd, 64, 1)).astype(low)
            for k, got in ((2 * j, even), (2 * j + 1, odd)):
                at = 32 * (k % 4)
                moved = got if at == 64 else pltpu.roll(got, (at + 64) % 128, 1)
                rotary = jnp.where((lane >= at) & (lane < at + 32), moved, rotary)
                if k % 4 == 3 or k == 9:
                    grad_packed[:, head_tile(8 * i + 5 + k // 4)] = rotary.astype(low)
                    rotary = jnp.zeros((rows, 128), jnp.float32)
        return carry

    return quarter


def widen_kernel(*refs):
    n = len(refs) // 2
    for strips, out in zip(refs[:n], refs[n:]):
        each = out.shape[1] // 8
        for s in range(8):
            first, last = s * each // 128, (s + 1) * each // 128
            tiles = strips[s, 0].astype(jnp.float32)
            if s * each % 128:
                shared = strips[s - 1, 0, :, (first - (s - 1) * each // 128) * 128 :][:, :128]
                out[:, first * 128 : first * 128 + 128] = tiles[:, :128] + shared.astype(jnp.float32)
                first_full = first + 1
            else:
                first_full = first
            base = s * each // 128
            out[:, first_full * 128 : last * 128] = tiles[:, (first_full - base) * 128 : (last - base) * 128]


def unpack_kernel(heads, packed, out):
    pieces = []
    for h in range(heads):
        first, k = h // 10 * 1024, h % 10
        pieces.append(packed[:, first + 64 * k : first + 64 * k + 64])
        pieces.append(packed[:, first + 640 + 32 * k : first + 672 + 32 * k])
    out[...] = jnp.concatenate(pieces, axis=1).astype(jnp.float32)


def unpack(packed, heads):
    return pl.pallas_call(
        functools.partial(unpack_kernel, heads),
        out_shape=jax.ShapeDtypeStruct((packed.shape[0], heads * 96), jnp.float32), in_specs=[VMEM], out_specs=VMEM,
    )(packed)


def widen(arrays, cols):
    _, quarters, rows, strip = arrays[0].shape
    n = len(arrays)
    return pl.pallas_call(
        widen_kernel, grid=(quarters,),
        out_shape=[jax.ShapeDtypeStruct((quarters * rows, cols), jnp.float32)] * n,
        in_specs=[pl.BlockSpec((8, 1, rows, strip), lambda q: (0, q, 0, 0))] * n,
        out_specs=[pl.BlockSpec((rows, cols), lambda q: (q, 0))] * n,
        compiler_params=pltpu.CompilerParams(vmem_limit_bytes=56 * 2**20),
    )(*arrays)


class Gather:
    def __init__(self, ins, outs, sems):
        self.ins, self.outs = ins, outs
        self.zsend, self.zrecv, self.csend, self.crecv, self.own = sems
        self.rep, self.zpos, self.core = place()
        self.held = None

    @staticmethod
    def scratch(n):
        return [dma_sems(2, 3, n), dma_sems(2, 3, n), dma_sems(7, n), dma_sems(7, n), dma_sems(2, n)]

    def at(self, a, z, c):
        rows = self.ins[a].shape[0]
        return self.outs[a].at[pl.ds(mult((z * 2 + c) * rows, rows), rows)]

    def hop_copy(self, a, way, hop, z, src=None):
        dst = self.at(a, z, self.core)
        return remote(dst if src is None else src, dst, self.zsend.at[way, hop, a], self.zrecv.at[way, hop, a],
                      self.rep, (self.zpos + (1 - 2 * way)) * 2 + self.core)

    def core_copy(self, a, slot, z, c, src=None):
        dst = self.at(a, z, c)
        return remote(dst if src is None else src, dst, self.csend.at[slot, a], self.crecv.at[slot, a],
                      self.rep, self.zpos * 2 + 1 - self.core)

    def keep(self, a):
        return pltpu.make_async_copy(self.ins[a], self.at(a, self.zpos, self.core), self.own.at[0, a])

    def onward(self, way):
        return self.zpos < 3 if way == 0 else self.zpos > 0

    def source(self, way, hop):
        z = self.zpos - hop if way == 0 else self.zpos + hop
        return z, (z >= 0 if way == 0 else z <= 3)

    def start(self, which=None):
        which = range(len(self.ins)) if which is None else which
        for way in range(2):
            @pl.when(self.onward(way))
            def _():
                for a in which:
                    self.hop_copy(a, way, 0, self.zpos, src=self.ins[a]).start()
        for a in which:
            self.core_copy(a, 0, self.zpos, self.core, src=self.ins[a]).start()
            self.keep(a).start()

    def hop(self, hop, which=None):
        which = range(len(self.ins)) if which is None else which
        for way in range(2):
            z, there = self.source(way, hop)

            @pl.when(there)
            def _():
                for a in which:
                    self.hop_copy(a, way, hop - 1, z).wait_recv()
                    if hop < 3:
                        @pl.when(self.onward(way))
                        def _():
                            self.hop_copy(a, way, hop, z).start()
                    self.core_copy(a, way * 3 + hop, z, self.core).start()

    def finish(self):
        arrays = range(len(self.ins))
        for way in range(2):
            for hop in range(3):
                z, there = self.source(way, hop)

                @pl.when(there & self.onward(way))
                def _():
                    for a in arrays:
                        self.hop_copy(a, way, hop, z).wait_send()
        for a in arrays:
            self.keep(a).wait()
            self.core_copy(a, 0, self.zpos, self.core, src=self.ins[a]).wait_send()
            self.core_copy(a, 0, self.zpos, 1 - self.core).wait_recv()
        for way in range(2):
            for hop in range(1, 4):
                z, there = self.source(way, hop)

                @pl.when(there)
                def _():
                    for a in arrays:
                        self.core_copy(a, way * 3 + hop, z, self.core).wait_send()
                        self.core_copy(a, way * 3 + hop, z, 1 - self.core).wait_recv()


class Total:
    def __init__(self, term, out, bufs, sems):
        self.term, self.out = term, out
        self.theirs, self.landed = bufs
        self.zsend, self.zrecv, self.csend, self.crecv = sems
        self.rep, self.zpos, self.core = place()

    @staticmethod
    def scratch(term):
        return [pltpu.VMEM((4,) + term.shape[1:], term.dtype), pltpu.VMEM((5,) + term.shape[1:], term.dtype),
                dma_sems(2, 4), dma_sems(2, 4), dma_sems(4), dma_sems(4)]

    @staticmethod
    def split(term, out, refs):
        return Total(term, out, refs[:2], refs[2:6]), refs[6:]

    def pair_copy(self, z):
        return remote(self.term.at[z * 2 + 1 - self.core], self.theirs.at[z], self.csend.at[z], self.crecv.at[z],
                      self.rep, self.zpos * 2 + 1 - self.core)

    def hop_copy(self, way, z):
        return remote(self.theirs.at[z], self.landed.at[z + 1 - way], self.zsend.at[way, z], self.zrecv.at[way, z],
                      self.rep, (self.zpos + (1 - 2 * way)) * 2 + self.core)

    def each(self, step):
        for way in range(2):
            behind = self.zpos if way == 0 else 3 - self.zpos
            target = self.zpos + 3 - step if way == 0 else self.zpos - 3 + step
            yield way, behind, target, (behind <= step) & (behind < 3)

    def start(self):
        for z in (3, 0, 2, 1):
            self.pair_copy(z).start()

    def pair(self):
        for z in (3, 0, 2, 1):
            self.pair_copy(z).wait_recv()

    def both(self, z):
        return self.term[z * 2 + self.core].astype(jnp.float32) + self.theirs[z].astype(jnp.float32)

    def step(self, step):
        for way, behind, target, there in self.each(step):
            @pl.when(there)
            def _():
                total = self.both(target)

                @pl.when(behind == 0)
                def _():
                    self.theirs[target] = total.astype(self.theirs.dtype)

                @pl.when(behind > 0)
                def _():
                    self.hop_copy(way, target).wait_recv()
                    self.theirs[target] = (total + self.landed[target + 1 - way].astype(jnp.float32)).astype(self.theirs.dtype)
                self.hop_copy(way, target).start()

    def finish(self):
        self.out[...] = self.both(self.zpos)
        for way in range(2):
            @pl.when(self.zpos > 0 if way == 0 else self.zpos < 3)
            def _():
                self.hop_copy(way, self.zpos).wait_recv()
                self.out[...] += self.landed[self.zpos + 1 - way].astype(jnp.float32)
        for step in range(3):
            for way, behind, target, there in self.each(step):
                @pl.when(there)
                def _():
                    self.hop_copy(way, target).wait_send()
        for z in range(4):
            self.pair_copy(z).wait_send()


def kernel_params(cid):
    return pltpu.CompilerParams(collective_id=cid, has_side_effects=True, vmem_limit_bytes=56 * 2**20)


VMEM = pl.BlockSpec(memory_space=pltpu.VMEM)


class PlaneSum:
    def __init__(self, items, bufs, sems):
        self.items = items
        self.landed, self.stage, self.last = bufs
        self.asend, self.arecv, self.bsend, self.brecv = sems
        self.rep, self.zpos, self.core = place()
        self.shard = self.zpos * 2 + self.core

    @staticmethod
    def scratch(shapes, dtype):
        n = len(shapes)
        return ([pltpu.VMEM((2,) + s, dtype) for s in shapes] + [pltpu.VMEM(s, dtype) for s in shapes] * 2
                + [dma_sems(n, 2), dma_sems(n, 2), dma_sems(n), dma_sems(n)])

    @staticmethod
    def split(refs, n):
        return (refs[:n], refs[n : 2 * n], refs[2 * n : 3 * n]), refs[3 * n : 3 * n + 4], refs[3 * n + 4 :]

    def ways(self, i):
        xrep, yrep, drep = plane_places(self.rep)
        return (xrep, yrep, drep) if self.items[i][2] == 0 else (yrep, xrep, drep)

    def out(self, i, k):
        near, _, far = self.ways(i)
        return remote(self.items[i][0](far if k else near), self.landed[i].at[k], self.asend.at[i, k], self.arecv.at[i, k],
                      near, self.shard)

    def on(self, i):
        return remote(self.stage[i], self.last[i], self.bsend.at[i], self.brecv.at[i], self.ways(i)[1], self.shard)

    def start(self, which=None):
        for i in range(len(self.items)) if which is None else which:
            for k in (1, 0):
                self.out(i, k).start()

    def middle(self, i):
        wide = jnp.float32
        self.out(i, 1).wait_recv()
        term = self.items[i][0](self.ways(i)[1])
        self.stage[i][...] = (term[...].astype(wide) + self.landed[i][1].astype(wide)).astype(self.stage[i].dtype)
        self.on(i).start()

    def end(self, i):
        wide = jnp.float32
        self.out(i, 0).wait_recv()
        self.on(i).wait_recv()
        total = self.items[i][0](self.rep)[...].astype(wide) + self.landed[i][0].astype(wide)
        own = self.items[i][1]
        own[...] = (total + self.last[i][...].astype(wide)).astype(own.dtype)

    def finish(self):
        for i in range(len(self.items)):
            for k in range(2):
                self.out(i, k).wait_send()
            self.on(i).wait_send()


class PlaneGather:
    def __init__(self, items, sems):
        self.items = items
        self.send, self.recv, self.own = sems
        self.rep, self.zpos, self.core = place()
        self.shard = self.zpos * 2 + self.core

    @staticmethod
    def scratch(n):
        return [dma_sems(3, n), dma_sems(3, n), dma_sems(n)]

    def copy(self, i, kind, quarter, to):
        own, part, _ = self.items[i]
        dst = part(quarter)
        return remote(dst if kind == 2 or own is None else own, dst, self.send.at[kind, i], self.recv.at[kind, i], to, self.shard)

    def keep(self, i):
        return pltpu.make_async_copy(self.items[i][0], self.items[i][1](self.rep), self.own.at[i])

    def start(self, which=None):
        xrep, yrep, _ = plane_places(self.rep)
        for i in range(len(self.items)) if which is None else which:
            self.copy(i, 0, self.rep, xrep).start()
            self.copy(i, 1, self.rep, yrep).start()
            if self.items[i][0] is not None:
                self.keep(i).start()

    def middle(self, i):
        xrep, yrep, _ = plane_places(self.rep)
        self.copy(i, 0, xrep, xrep).wait_recv()
        if self.items[i][2] == 0:
            self.copy(i, 2, xrep, yrep).start()
        self.copy(i, 1, yrep, yrep).wait_recv()
        if self.items[i][2] == 1:
            self.copy(i, 2, yrep, xrep).start()

    def finish(self):
        xrep, yrep, drep = plane_places(self.rep)
        for i, (own, _, first) in enumerate(self.items):
            self.copy(i, 0, self.rep, xrep).wait_send()
            self.copy(i, 1, self.rep, yrep).wait_send()
            self.copy(i, 2, *((xrep, yrep) if first == 0 else (yrep, xrep))).wait_send()
            self.copy(i, 2, drep, drep).wait_recv()
            if own is not None:
                self.keep(i).wait()


class ColumnSwap:
    def __init__(self, items, sems, keeps=True):
        self.items, self.keeps = items, keeps
        self.send, self.recv, self.own = sems
        self.rep, self.zpos, self.core = place()
        self.shard = self.zpos * 2 + self.core

    near = (1, 2, 6, 3, 7, 4, 5)

    @staticmethod
    def scratch(n):
        return [dma_sems(7, n), dma_sems(7, n), dma_sems(n)]

    def copy(self, i, m, back=False):
        s2 = column_place(self.zpos, self.core, m, back)
        block, there = self.items[i]
        return remote(block(s2), there(s2 if back else self.shard), self.send.at[m - 1, i], self.recv.at[m - 1, i], self.rep, s2)

    def keep(self, i):
        return pltpu.make_async_copy(self.items[i][0](self.shard), self.items[i][1](self.shard), self.own.at[i])

    def start(self):
        for m in self.near:
            for i in range(len(self.items)):
                self.copy(i, m).start()
        for i in range(len(self.items) if self.keeps else 0):
            self.keep(i).start()

    def arrive(self, m):
        for i in range(len(self.items)):
            self.copy(i, m, True).wait_recv()

    def finish(self, arrive=True):
        for i in range(len(self.items)):
            if self.keeps:
                self.keep(i).wait()
            for m in self.near:
                self.copy(i, m).wait_send()
                if arrive:
                    self.copy(i, m, True).wait_recv()


def quarter_cols(ref, first, rows, p):
    width = ref.shape[1] // 4
    return ref.at[pl.ds(first, rows), pl.ds(mult(p * width, 128), width)]


def back_kernel(shift_unit, *refs):
    down, tokens, grad_gate, grad_up, gate_w, up_w, out, down_own, gate_own, up = refs[:10]
    term, gate, strips, strip_sems = refs[10:14]
    rep, zpos, core = place()
    total, rest = Total.split(term, out, refs[14:])
    bufs, sems, _ = PlaneSum.split(rest, 4)
    half = down_own.shape[0] // 2
    shift = mult((zpos * 2 + core) % 4 * shift_unit, 16)
    wide = jnp.float32

    def down_item(h):
        return (lambda p: quarter_cols(down, mult(shift + h * half, 16), half, p), down_own.at[pl.ds(h * half, half)], h)

    def gate_item(h):
        return (lambda p: gate.at[pl.ds(4 * h, 4), p], gate_own.at[pl.ds(4 * h, 4)], h)

    sums = PlaneSum([down_item(0), down_item(1), gate_item(0), gate_item(1)], bufs, sems)
    chunk = strips.shape[2]
    chunks = gate_w.shape[0] // chunk

    def strip(i, which):
        return pltpu.make_async_copy(
            (gate_w, up_w)[which].at[pl.ds(mult(i * chunk, 128), chunk)], strips.at[i % 2, which], strip_sems.at[i % 2, which])

    for which in range(2):
        strip(0, which).start()
    greet(rep, zpos, core, plane=2)
    sums.start((0, 1))

    def back(i, carry):
        for which in range(2):
            strip(i, which).wait()

        @pl.when(i < chunks - 1)
        def _():
            for which in range(2):
                strip(i + 1, which).start()

        part = dot_nt(grad_gate[...], strips[i % 2, 0]) + dot_nt(grad_up[...], strips[i % 2, 1])
        term[:, :, pl.ds(mult(i * chunk, 128), chunk)] = part.astype(term.dtype).reshape(8, -1, chunk)
        return carry

    lax.fori_loop(0, chunks, back, 0)
    total.start()
    wide_rows = tokens.shape[1] // 4

    def weight(grad, to, i):
        got = dot_tn(tokens[:, pl.ds(mult(i * wide_rows, 128), wide_rows)], grad[...])
        to[pl.ds(2 * i, 2)] = got.astype(to.dtype).reshape((2,) + to.shape[1:])

    def gate_step(i, carry):
        weight(grad_gate, gate, i)

        @pl.when(i == 2)
        def _():
            total.pair()
            total.step(0)
        return carry

    lax.fori_loop(0, 4, gate_step, 0)
    sums.start((2, 3))

    def up_step(i, carry):
        weight(grad_up, up, i)

        @pl.when(i == 1)
        def _():
            sums.middle(0)
            sums.middle(1)
            total.step(1)
        return carry

    lax.fori_loop(0, 4, up_step, 0)
    sums.end(0)
    sums.end(1)
    total.step(2)
    sums.middle(2)
    sums.middle(3)
    total.finish()
    sums.end(2)
    sums.end(3)
    sums.finish()


def back_sums(cid, down, tokens, grad_gate, grad_up, gate_w, up_w, rows):
    width = down.shape[1] // 4
    kind = down.dtype
    strip = gate_w.shape[1]
    parts = (8, 4, gate_w.shape[0] // 32, strip)
    term = jax.ShapeDtypeStruct((8, tokens.shape[0] // 8, tokens.shape[1]), kind)
    return pl.pallas_call(
        functools.partial(back_kernel, rows % 128),
        out_shape=[jax.ShapeDtypeStruct(term.shape[1:], jnp.float32), jax.ShapeDtypeStruct((rows, width), kind),
                   jax.ShapeDtypeStruct((8,) + parts[2:], kind), jax.ShapeDtypeStruct(parts, kind)],
        in_specs=[VMEM] * 4 + [ANY] * 2, out_specs=[VMEM] * 4,
        scratch_shapes=[pltpu.VMEM(term.shape, kind), pltpu.VMEM(parts, kind),
                        pltpu.VMEM((2, 2, gate_w.shape[0] // 5, strip), kind), dma_sems(2, 2)]
        + Total.scratch(term) + PlaneSum.scratch([(rows // 2, width)] * 2 + [(4,) + parts[2:]] * 2, kind),
        compiler_params=kernel_params(cid),
    )(down, tokens, grad_gate, grad_up, gate_w, up_w)


def middle_kernel(scale, *refs):
    branch, cols, down, up, attn_out, query_low, latent_low = refs[:7]
    query, kv, rope, bias, turns, logs = refs[7:13]
    branch_all, cols_all, down_all, up_own = refs[13:17]
    grad_query, grad_kv, grad_rope, query_up, latent_up = refs[17:22]
    scratch = list(refs[22:])
    left, mixed, packed, strips, strip_sems = scratch[:5]
    scratch = scratch[5:]
    rep, zpos, core = place()
    shard = zpos * 2 + core
    gather = Gather((branch,), (branch_all,), scratch[:5])
    swap = ColumnSwap([(lambda s: cols.at[s], lambda s: cols_all.at[s])], scratch[5:8])
    half = down.shape[0] // 2
    downs = PlaneGather(
        [(down.at[pl.ds(h * half, half)], functools.partial(quarter_cols, down_all, h * half, half), h) for h in range(2)],
        scratch[8:11])
    bufs, sems, _ = PlaneSum.split(scratch[11:], 2)
    sums = PlaneSum([(lambda p, h=h: up.at[pl.ds(4 * h, 4), p], up_own.at[pl.ds(4 * h, 4)], h) for h in range(2)], bufs, sems)
    rows = attn_out.shape[0] // 4

    def strip(i):
        return pltpu.make_async_copy(
            attn_out.at[pl.ds(mult(i * rows, 128), rows)], strips.at[i % 2], strip_sems.at[i % 2])

    strip(0).start()
    greet(rep, zpos, core, plane=2, column=True)
    gather.start()
    sums.start()
    downs.start()
    swap.start()
    left[...] = jnp.zeros_like(left)
    grad_rope[...] = jnp.zeros_like(grad_rope)
    quarter = attend_back_heads(
        scale, query, kv, rope, bias, turns, logs, mixed, grad_query, packed, grad_kv, grad_rope, left)

    def after_second():
        gather.hop(1)
        sums.middle(0)
        sums.middle(1)

    def after_fourth():
        gather.hop(2)
        downs.middle(0)
        downs.middle(1)

    def step(i, carry):
        strip(i).wait()

        @pl.when(i < 3)
        def _():
            strip(i + 1).start()

        mixed[:, pl.ds(mult(i * rows, 128), rows)] = dot_nt(branch[...], strips[i % 2]).astype(mixed.dtype)
        quarter(i, carry)
        pl.when(i == 1)(after_second)
        pl.when(i == 3)(after_fourth)
        return carry

    lax.fori_loop(0, 4, step, 0)

    def terms(i, carry):
        at = pl.ds(mult(i * 1024, 128), 1024)
        query_up[:, at] = dot_tn(query_low[...], packed[:, at]).astype(query_up.dtype)
        width = latent_up.shape[1] // 4
        at = pl.ds(mult(i * width, 128), width)
        latent_up[:, at] = dot_tn(latent_low[...], grad_kv[:, at]).astype(latent_up.dtype)
        return carry

    lax.fori_loop(0, 4, terms, 0)
    sums.end(0)
    sums.end(1)
    gather.hop(3)
    gather.finish()
    swap.finish()
    downs.finish()
    sums.finish()


def middle_exchange(cid, scale, branch, cols, down, up, attn_out, query_low, latent_low, attend_in):
    kind = branch.dtype
    query, kv, rope = attend_in[:3]
    rows = query.shape[0]
    return pl.pallas_call(
        functools.partial(middle_kernel, scale),
        out_shape=[jax.ShapeDtypeStruct((8 * branch.shape[0], branch.shape[1]), kind), jax.ShapeDtypeStruct(cols.shape, kind),
                   jax.ShapeDtypeStruct((down.shape[0], 4 * down.shape[1]), kind), jax.ShapeDtypeStruct((8,) + up.shape[2:], kind),
                   jax.ShapeDtypeStruct(query.shape, kind),
                   jax.ShapeDtypeStruct(kv.shape, kind), jax.ShapeDtypeStruct(rope.shape, jnp.float32),
                   jax.ShapeDtypeStruct((query_low.shape[1], 4096), kind),
                   jax.ShapeDtypeStruct((latent_low.shape[1], kv.shape[1]), kind)],
        in_specs=[VMEM] + [ANY] * 2 + [VMEM, ANY] + [VMEM] * 8, out_specs=[ANY] * 3 + [VMEM] * 6,
        scratch_shapes=[pltpu.VMEM((2 * rows, 256), kind), pltpu.VMEM(branch.shape, kind), pltpu.VMEM((rows, 4096), kind),
                        pltpu.VMEM((2, attn_out.shape[0] // 4, attn_out.shape[1]), kind), dma_sems(2)]
        + Gather.scratch(1) + ColumnSwap.scratch(1) + PlaneGather.scratch(2)
        + PlaneSum.scratch([(4,) + up.shape[2:]] * 2, kind),
        compiler_params=kernel_params(cid),
    )(branch, cols, down, up, attn_out, query_low, latent_low, *attend_in)


def last_kernel(*refs):
    gate, up, lat, query_up, latent_up, hidden, down, attn_out, cols, gain = refs[:10]
    gate_all, up_all, out, attn_sum, lat_sum, latent_sum, query_sum, gain_out = refs[10:18]
    scratch = list(refs[18:])
    rep, zpos, core = place()
    shard = zpos * 2 + core
    places = plane_places(rep)

    def take(n):
        nonlocal scratch
        got, scratch = scratch[:n], scratch[n:]
        return got

    swap = ColumnSwap([(lambda s, a=a: a.at[s], lambda s, b=b: b.at[s, rep]) for a, b in ((gate, gate_all), (up, up_all))],
                      take(2) + [None], keeps=False)
    spread_sems = take(3)
    lat_all, out_term, lat_term, query_part, latent_own, query_own = take(6)
    gather = Gather((lat,), (lat_all,), take(5))
    owns = take(5)
    gain_landed, gain_sum, gain_plane, gsend, grecv, hsend, hrecv = take(7)
    total, scratch = Total.split(out_term, out, scratch)
    query_total, scratch = Total.split(query_part, query_own, scratch)
    latent_total, scratch = Total.split(latent_up, latent_own, scratch)
    bufs, sems, _ = PlaneSum.split(scratch, 6)
    width = query_up.shape[2] // 4
    half = attn_out.shape[0] // 2

    def part(m, b):
        return lambda p: b.at[shard if m == 0 else column_place(zpos, core, m, True), p]

    def query_item(h):
        return (lambda p: query_up.at[pl.ds(4 * h, 4), :, pl.ds(mult(p * width, 128), width)], query_part.at[pl.ds(4 * h, 4)], h)

    latent_low = scratch[-1]
    sums = PlaneSum(
        [query_item(0), query_item(1)]
        + [(functools.partial(quarter_cols, attn_out, h * half, half), owns[h], h) for h in range(2)]
        + [(lambda p: lat_term.at[p], owns[2], 0),
           (functools.partial(quarter_cols, latent_low, 0, latent_low.shape[0]), owns[3], 1)],
        bufs, sems)
    spread = PlaneGather(
        [(a.at[shard] if m == 0 else None, part(m, b), h) for m in range(8) for h, (a, b) in enumerate(((gate, gate_all), (up, up_all)))]
        + [(owns[h], functools.partial(quarter_cols, attn_sum, h * half, half), h) for h in range(2)]
        + [(owns[2], lambda p: lat_sum.at[p], 0),
           (owns[3], functools.partial(quarter_cols, latent_sum, 0, latent_low.shape[0]), 1),
           (owns[4], functools.partial(quarter_cols, query_sum, 0, query_up.shape[1]), 0)], spread_sems)

    def gain_copy(m):
        s2 = column_place(zpos, core, m)
        return remote(gain.at[s2], gain_landed.at[m - 1], gsend.at[m - 1], grecv.at[m - 1], rep, s2)

    def gain_on(k):
        return remote(gain_sum, gain_plane.at[k], hsend.at[k], hrecv.at[k], places[k], shard)

    greet(rep, zpos, core, plane=3, column=True)
    for m in range(1, 8):
        gain_copy(m).start()
    swap.start()
    sums.start((0, 1))
    spread.start((0, 1))
    latent_total.start()
    gather.start()
    sums.start((2, 3))
    rows = lat.shape[0]

    def term(i, carry):
        out_term[i] = jnp.dot(hidden[pl.ds(mult(i * rows, rows), rows)], down[...],
                              preferred_element_type=jnp.float32).astype(out_term.dtype)
        return carry

    def arrive(m):
        swap.arrive(m)
        spread.start((2 * m, 2 * m + 1))

    def onward(*ms):
        for m in ms:
            spread.middle(2 * m)
            spread.middle(2 * m + 1)

    lax.fori_loop(0, 3, term, 0)
    arrive(1)
    latent_total.pair()
    latent_total.step(0)
    lax.fori_loop(3, 6, term, 0)
    onward(0)
    gather.hop(1)
    arrive(2)
    arrive(6)
    lax.fori_loop(6, 8, term, 0)
    latent_total.step(1)
    gain_sum[...] = gain[shard]
    for m in range(1, 8):
        gain_copy(m).wait_recv()
        gain_sum[...] += gain_landed[m - 1]
    for k in range(3):
        gain_on(k).start()
    total.start()
    onward(1)
    arrive(3)
    arrive(7)
    gather.hop(2)
    sums.middle(0)
    sums.middle(1)
    latent_total.step(2)
    onward(2, 6)
    arrive(4)
    arrive(5)
    gather.hop(3)
    total.pair()
    total.step(0)
    sums.middle(2)
    sums.middle(3)
    latent_total.finish()
    latent_low[...] = latent_own[...].astype(latent_low.dtype)
    sums.start((5,))
    sums.end(0)
    sums.end(1)
    query_total.start()
    gather.finish()
    lat_term[...] = dot_tn(cols[...], lat_all[...]).astype(lat_term.dtype).reshape(lat_term.shape)
    sums.start((4,))
    query_total.pair()
    query_total.step(0)
    onward(3, 7)
    total.step(1)
    sums.end(2)
    sums.end(3)
    spread.start((16, 17))
    query_total.step(1)
    onward(4, 5)
    sums.middle(5)
    sums.middle(4)
    query_total.step(2)
    total.step(2)
    query_total.finish()
    owns[4][...] = query_own[...].astype(owns[4].dtype)
    spread.start((20,))
    sums.end(5)
    spread.start((19,))
    sums.end(4)
    spread.start((18,))
    for i in (16, 17, 20, 19, 18):
        spread.middle(i)
    gain_out[...] = gain_sum[...]
    for k in range(3):
        gain_on(k).wait_recv()
        gain_out[...] += gain_plane[k]
    total.finish()
    for k in range(3):
        gain_on(k).wait_send()
    for m in range(1, 8):
        gain_copy(m).wait_send()
    swap.finish(arrive=False)
    sums.finish()
    spread.finish()


def last_sums(cid, gate, up, lat, query_up, latent_up, hidden, down, attn_out, cols, gain):
    kind = gate.dtype
    wide = jnp.float32
    rows = lat.shape[0]
    lat_shape = (4, cols.shape[1] // 4, lat.shape[1])
    query_shape = (query_up.shape[1], query_up.shape[2] // 4)
    shapes = [(attn_out.shape[0] // 2, attn_out.shape[1] // 4)] * 2 + [
        lat_shape[1:], (latent_up.shape[1], latent_up.shape[2] // 4)]
    out_term = jax.ShapeDtypeStruct((8, rows, down.shape[1]), kind)
    query_part = jax.ShapeDtypeStruct((8,) + query_shape, kind)
    return pl.pallas_call(
        last_kernel,
        out_shape=[jax.ShapeDtypeStruct((8, 4) + gate.shape[1:], kind)] * 2
        + [jax.ShapeDtypeStruct(out_term.shape[1:], wide)]
        + [jax.ShapeDtypeStruct(s, kind) for s in (attn_out.shape, lat_shape, latent_up.shape[1:])]
        + [jax.ShapeDtypeStruct((query_up.shape[1], query_up.shape[2]), kind), jax.ShapeDtypeStruct(gain.shape[1:], gain.dtype)],
        in_specs=[ANY] * 3 + [VMEM] * 7, out_specs=[ANY] * 2 + [VMEM] + [ANY] * 4 + [VMEM],
        scratch_shapes=[dma_sems(7, 2), dma_sems(7, 2)] + PlaneGather.scratch(21)
        + [pltpu.VMEM((8 * rows, lat.shape[1]), kind), pltpu.VMEM(out_term.shape, kind), pltpu.VMEM(lat_shape, kind),
           pltpu.VMEM(query_part.shape, kind), pltpu.VMEM(latent_up.shape[1:], wide), pltpu.VMEM(query_shape, wide)]
        + Gather.scratch(1) + [pltpu.VMEM(s, kind) for s in shapes + [query_shape]]
        + [pltpu.VMEM((7,) + gain.shape[1:], wide), pltpu.VMEM(gain.shape[1:], wide), pltpu.VMEM((3,) + gain.shape[1:], wide)]
        + [dma_sems(7)] * 2 + [dma_sems(3)] * 2
        + Total.scratch(out_term) + Total.scratch(query_part) + Total.scratch(latent_up)
        + PlaneSum.scratch([(4,) + query_shape] * 2 + shapes, kind) + [pltpu.VMEM(latent_up.shape[1:], kind)],
        compiler_params=kernel_params(cid),
    )(gate, up, lat, query_up, latent_up, hidden, down, attn_out, cols, gain)


def start_kernel(scale, *refs):
    ins, (gate, up), (tokens, bias, turns, down) = refs[:7], refs[7:9], refs[9:13]
    outs, cols, refs = refs[13:20], refs[20:22], refs[22:]
    (normed, query_low, latent, rope, kv, query, mixed, logs, query_lat, latent_proj, residual, ffn_all,
     grad_hidden) = refs[:13]
    refs = refs[13:]
    (zsend, zrecv, xsend, xrecv, ysend, yrecv, dsend, drecv, csend, crecv, own, gsend, grecv, psend, precv) = refs[:15]
    held, strips = refs[15:22], refs[22:24]
    (small, gains, w_query, w_latent, w_query_up, w_latent_up, w_out, proj, ffn, lsend, lrecv, load_sems,
     grad_sems) = refs[24:37]
    gather = Gather((ffn,), (ffn_all,), refs[37:])
    rep, zpos, core = place()
    xrep, yrep, drep = plane_places(rep)
    shard = zpos * 2 + core

    def whole(a, z, c):
        rows = ins[a].shape[0]
        return outs[a].at[pl.ds(mult((z * 2 + c) * rows, rows), rows)]

    def pieces(a, z, c, quarter, act, own_ref=False):
        def part(b, first, rows):
            full = ins[b].shape[0]
            if own_ref:
                return ins[b].at[pl.ds(mult(first, 16), rows)]
            return outs[b].at[pl.ds(mult((z * 2 + c) * full + first, 16), rows)]

        if a < 3:
            rows = ins[a].shape[0] // 4
            act(part(a, quarter * rows, rows))
        elif a == 3:
            @pl.when(quarter < 3)
            def _():
                act(part(3, jnp.minimum(quarter, 2) * 32, 32))

            @pl.when(quarter == 3)
            def _():
                act(part(4, 0, 32))
        else:
            act(ins[a + 1] if own_ref else whole(a + 1, z, c))

    copy = remote

    def hop(a, way, h, z, what):
        def act(ref):
            c = copy(ref, ref, zsend.at[way, h, a], zrecv.at[way, h, a], rep, (zpos + 1 - 2 * way) * 2 + core)
            getattr(c, what)()
        pieces(a, z, core, rep, act)

    def to_plane(a, k, z, quarter, what, sems, r):
        def act(ref):
            getattr(copy(ref, ref, sems[0].at[k, a], sems[1].at[k, a], r, shard), what)()
        pieces(a, z, core, quarter, act)

    def to_core(a, slot, z, c, what, src=None):
        ref = whole(a, z, c)
        getattr(copy(ref if src is None else src, ref, csend.at[slot, a], crecv.at[slot, a], rep, zpos * 2 + 1 - core), what)()

    greet(rep, zpos, core, plane=3, column=True)
    def send_own(a):
        def first(way):
            def go(src):
                def act(ref):
                    copy(src, ref, zsend.at[way, 0, a], zrecv.at[way, 0, a], rep, (zpos + 1 - 2 * way) * 2 + core).start()
                return act
            return go
        for way in range(2):
            @pl.when(zpos < 3 if way == 0 else zpos > 0)
            def _():
                if a < 3:
                    rows = ins[a].shape[0] // 4
                    src = ins[a].at[pl.ds(mult(rep * rows, 16), rows)]
                    pieces(a, zpos, core, rep, first(way)(src))
                elif a == 3:
                    @pl.when(rep < 3)
                    def _():
                        start = mult(jnp.minimum(rep, 2) * 32, 16)
                        src = ins[3].at[pl.ds(start, 32)]
                        dst = outs[3].at[pl.ds(mult(shard * 96 + start, 16), 32)]
                        first(way)(src)(dst)

                    @pl.when(rep == 3)
                    def _():
                        first(way)(ins[4])(whole(4, zpos, core))
                else:
                    first(way)(ins[a + 1])(whole(a + 1, zpos, core))

    def keep(a, half):
        if half == 0:
            return pltpu.make_async_copy(ins[a], held[a], own.at[0, a])
        return pltpu.make_async_copy(held[a], whole(a, zpos, core), own.at[1, a])

    for a in (5, 1, 2, 3, 0):
        send_own(a)

    strip = cols[0].shape[1]
    quarter_rows = gate.shape[0] // 4

    def slice_of(which, s, first, rows):
        start = mult((s * 25 // 4) * 128, 128)
        return (gate, up)[which].at[pl.ds(mult(first, 16), rows), pl.ds(start, strip)]

    def rows_of(which, s, quarter):
        return cols[which].at[pl.ds(mult(s * gate.shape[0] + quarter * quarter_rows, 16), quarter_rows)]

    def slice_copy(m, which):
        s2 = column_place(zpos, core, m)
        return remote(slice_of(which, s2, rep * quarter_rows, quarter_rows), rows_of(which, shard, rep),
                      gsend.at[m - 1, which], grecv.at[m - 1, which], rep, s2)

    def slice_plane(m, which, quarter, kind, r):
        ref = rows_of(which, column_place(zpos, core, m, back=True), quarter)
        return remote(ref, ref, psend.at[kind, m - 1, which], precv.at[kind, m - 1, which], r, shard)

    def own_slice(which, half):
        if half == 0:
            return pltpu.make_async_copy(slice_of(which, shard, 0, gate.shape[0]), strips[which], own.at[0, 7 + which])
        rows = gate.shape[0]
        return pltpu.make_async_copy(strips[which], cols[which].at[pl.ds(mult(shard * rows, rows), rows)], own.at[1, 7 + which])

    near = (1, 2, 6, 3, 7, 4, 5)
    for a in range(7):
        to_core(a, 0, zpos, core, "start", src=ins[a])
        keep(a, 0).start()
    for which in range(2):
        own_slice(which, 0).start()
    for a in range(7):
        keep(a, 0).wait()
        keep(a, 1).start()
    for which in range(2):
        own_slice(which, 0).wait()
        own_slice(which, 1).start()

    def slices_from_column(m):
        for which in range(2):
            s2 = column_place(zpos, core, m, back=True)
            ref = rows_of(which, s2, rep)
            remote(ref, ref, gsend.at[m - 1, which], grecv.at[m - 1, which], rep, s2).wait_recv()
        slices_to_plane(m, 0)

    def slices_to_plane(m, which):
        slice_plane(m, which, rep, 0, xrep).start()
        slice_plane(m, which, rep, 1, yrep).start()

    def slices_from_plane(m, which=0):
        slice_plane(m, which, xrep, 0, xrep).wait_recv()
        slice_plane(m, which, yrep, 1, yrep).wait_recv()
        slice_plane(m, which, *onward(m)).start()

    def onward(m):
        return (yrep, 2, xrep) if m % 2 else (xrep, 2, yrep)

    def from_column(h, way, z, slots):
        for a in slots:
            hop(a, way, h - 1, z, "wait_recv")
            if h < 3:
                @pl.when(zpos < 3 if way == 0 else zpos > 0)
                def _():
                    hop(a, way, h, z, "start")
            if a < 4:
                to_plane(a, way * 3 + h - 1, z, rep, "start", (xsend, xrecv), xrep)
                to_plane(a, way * 3 + h - 1, z, rep, "start", (ysend, yrecv), yrep)
            else:
                to_core(a + 1, way * 3 + h, z, core, "start")

    def from_plane(h, way, z, slots):
        k = way * 3 + h - 1
        for a in slots:
            to_plane(a, k, z, xrep, "wait_recv", (xsend, xrecv), xrep)
            if a == 0:
                to_plane(a, k, z, xrep, "start", (dsend, drecv), yrep)
            to_plane(a, k, z, yrep, "wait_recv", (ysend, yrecv), yrep)
            if a > 0:
                to_plane(a, k, z, yrep, "start", (dsend, drecv), xrep)

    def from_corner(h, way, z, slots):
        k = way * 3 + h - 1
        for a in slots:
            to_plane(a, k, z, drep, "wait_recv", (dsend, drecv), drep)
            for b in (a,) if a < 3 else (3, 4):
                to_core(b, k + 1, z, core, "start")

    def by_hop(stage, h, *more):
        for way in range(2):
            z = zpos - h if way == 0 else zpos + h

            @pl.when(z >= 0 if way == 0 else z <= 3)
            def _():
                stage(h, way, z, *more)

    def arrived(arrays):
        for b in arrays:
            keep(b, 1).wait()
            to_core(b, 0, zpos, 1 - core, "wait_recv")

            def theirs(h, way, z):
                to_core(b, way * 3 + h, z, 1 - core, "wait_recv")

            for h in range(1, 4):
                by_hop(theirs, h)

    wide, low = jnp.float32, jnp.bfloat16

    def tile(t):
        return slice(128 * t, 128 * t + 128)

    def normalize(src, dst, tiles, first):
        square = sum(jnp.sum(jnp.square(src(t)), axis=1, keepdims=True) for t in range(tiles))
        factor = lax.rsqrt(square / (128 * tiles) + epsilon)
        for t in range(tiles):
            dst[:, tile(t)] = (src(t) * factor * gains[first + t : first + t + 1, :]).astype(low)

    def load(b, to, i):
        return pltpu.make_async_copy(outs[b], to, load_sems.at[i])

    def share(k, what):
        rows = tokens.shape[0]
        for i, ref in enumerate((latent, rope)):
            copy_ = remote(ref.at[pl.ds(0, rows)], ref.at[pl.ds((k + 1) * rows, rows)], lsend.at[k, i], lrecv.at[k, i],
                           plane_places(rep)[k], shard)
            getattr(copy_, what)()

    def down_products():
        arrived((1, 2))
        load(1, w_query, 1).start()
        load(2, w_latent, 2).start()
        load(2, w_latent, 2).wait()
        latent_proj[...] = jnp.dot(normed[...], w_latent[...], preferred_element_type=wide)
        normalize(lambda t: latent_proj[:, tile(t)], latent.at[pl.ds(0, tokens.shape[0])], 2, 46)
        edge = jnp.zeros((tokens.shape[0], 64), wide)
        key = jnp.concatenate([edge, latent_proj[:, 256:288], edge[:, :32]], axis=1)
        rope[0 : tokens.shape[0]] = turn(key, (turns[0], turns[1], turns[2])).astype(low)
        for k in range(3):
            share(k, "start")
        load(1, w_query, 1).wait()
        query_lat[...] = jnp.dot(normed[...], w_query[...], preferred_element_type=wide)
        normalize(lambda t: query_lat[:, tile(t)], query_low, 6, 40)

    def chunk_loop(count, body):
        lax.fori_loop(0, count, lambda i, c: (body(i), c)[1], 0)

    def query_chunk(i):
        at = pl.ds(mult(i * 1024, 128), 1024)
        proj[:, at] = jnp.dot(query_low[...], w_query_up[:, at], preferred_element_type=wide)

    def key_chunk(i):
        at = pl.ds(mult(i * 1024, 128), 1024)
        kv[:, at] = jnp.dot(latent[...], w_latent_up[:, at], preferred_element_type=wide).astype(low)

    out_rows = w_out.shape[1]

    def out_strip(i):
        return pltpu.make_async_copy(outs[0].at[pl.ds(mult(i * out_rows, 128), out_rows)], w_out.at[i % 2], load_sems.at[4 + i % 2])

    by_hop(from_column, 1, (5, 1, 2))
    by_hop(from_column, 1, (3, 0))
    by_hop(from_column, 2, (5, 1, 2))
    by_hop(from_plane, 1, (1, 2))
    by_hop(from_column, 2, (3, 0))
    by_hop(from_plane, 1, (3, 0))
    by_hop(from_column, 3, (5, 1, 2))
    by_hop(from_plane, 2, (1, 2))
    by_hop(from_corner, 1, (1, 2))
    by_hop(from_column, 3, (3, 0))
    for m in near:
        for which in range(2):
            slice_copy(m, which).start()
    by_hop(from_plane, 3, (1, 2))
    by_hop(from_corner, 2, (1, 2))
    by_hop(from_plane, 2, (3, 0))
    arrived((6,))
    load(6, small, 0).start()
    load(6, small, 0).wait()
    gains[...] = sum(small[48 * s : 48 * s + 48, :] for s in range(8))
    normalize(lambda t: tokens[:, tile(t)].astype(wide), normed, 20, 0)
    by_hop(from_corner, 3, (1, 2))
    by_hop(from_corner, 1, (3, 0))
    down_products()
    by_hop(from_plane, 3, (3, 0))
    by_hop(from_corner, 2, (3, 0))
    for m in near[:3]:
        slices_from_column(m)
    send_own(4)
    by_hop(from_corner, 3, (3, 0))
    arrived((3, 4))
    load(3, w_query_up, 3).start()
    load(4, w_latent_up, 0).start()
    for m in near[3:]:
        slices_from_column(m)
    load(3, w_query_up, 3).wait()
    chunk_loop(5, query_chunk)
    for m in near[:3]:
        slices_from_plane(m)
    for k in range(3):
        share(k, "wait_recv")
    load(4, w_latent_up, 0).wait()
    chunk_loop(5, key_chunk)
    logs[...] = jnp.zeros_like(logs)
    group = attend_heads(scale, proj, kv, rope, bias, turns, query, mixed, logs)

    def attend_step(i, carry):
        group(i, carry)

        @pl.when(i == 3)
        def _():
            by_hop(from_column, 1, (4,))

        @pl.when(i == 8)
        def _():
            by_hop(from_column, 2, (4,))
        return carry

    lax.fori_loop(0, kv.shape[1] // 512, attend_step, 0)
    arrived((0,))
    out_strip(0).start()
    residual[...] = tokens[...].astype(wide)

    def out_step(i, carry):
        out_strip(i).wait()

        @pl.when(i < 3)
        def _():
            out_strip(i + 1).start()

        residual[...] += residual_scale * jnp.dot(
            mixed[:, pl.ds(mult(i * out_rows, 128), out_rows)], w_out[i % 2], preferred_element_type=wide)
        return carry

    lax.fori_loop(0, 4, out_step, 0)
    normalize(lambda t: residual[:, tile(t)], ffn, 20, 20)
    gather.start()
    for m in near:
        slices_to_plane(m, 1)
    by_hop(from_column, 3, (4,))
    for m in near[3:]:
        slices_from_plane(m)
    gather.hop(1)
    arrived((5,))
    chunk = 2 * tokens.shape[0]

    def grad_chunk(i):
        return pltpu.make_async_copy(
            outs[5].at[pl.ds(mult(i * chunk, chunk), chunk)], w_out.at[i % 2, pl.ds(0, chunk)], grad_sems.at[i % 2])

    def hidden_step(i, carry):
        grad_chunk(i).wait()

        @pl.when(i < 3)
        def _():
            grad_chunk(i + 1).start()

        grad_hidden[pl.ds(mult(i * chunk, chunk), chunk)] = dot_nt(w_out[i % 2, :chunk], down[...])

        @pl.when(i == 2)
        def _():
            gather.hop(2)
        return carry

    grad_chunk(0).start()
    lax.fori_loop(0, 4, hidden_step, 0)
    for m in near:
        slices_from_plane(m, 1)
    for k in range(3):
        share(k, "wait_send")
    gather.hop(3)
    gather.finish()
    for a in range(7):
        to_core(a, 0, zpos, core, "wait_send", src=ins[a])
    for which in range(2):
        own_slice(which, 1).wait()
        for m in near:
            slice_copy(m, which).wait_send()
    for m in near:
        for which in range(2):
            slice_plane(m, which, rep, 0, xrep).wait_send()
            slice_plane(m, which, rep, 1, yrep).wait_send()
            slice_plane(m, which, *onward(m)).wait_send()
            slice_plane(m, which, drep, 2, drep).wait_recv()
    for way in range(2):
        for h in range(3):
            z = zpos - h if way == 0 else zpos + h

            @pl.when((z >= 0) & (zpos < 3) if way == 0 else (z <= 3) & (zpos > 0))
            def _():
                for a in range(6):
                    hop(a, way, h, z, "wait_send")
    for h in range(1, 4):
        for way in range(2):
            z = zpos - h if way == 0 else zpos + h
            k = way * 3 + h - 1

            @pl.when(z >= 0 if way == 0 else z <= 3)
            def _():
                for a in range(4):
                    to_plane(a, k, z, rep, "wait_send", (xsend, xrecv), xrep)
                    to_plane(a, k, z, rep, "wait_send", (ysend, yrecv), yrep)
                    to_plane(a, k, z, xrep if a == 0 else yrep, "wait_send", (dsend, drecv), yrep)
                for a in range(7):
                    to_core(a, k + 1, z, core, "wait_send")

def start_gather(cid, scale, weights, gate, up, tokens, bias, turns, down):
    low, wide = jnp.bfloat16, jnp.float32
    rows, width = tokens.shape
    strip = down.shape[0]
    attn_out, query_down, latent_down, query_up, latent_up = weights[:5]
    tiles = query_up.shape[1]
    keys = bias.shape[1]
    out = [jax.ShapeDtypeStruct((a.shape[0] * 8,) + a.shape[1:], a.dtype) for a in weights]
    out += [jax.ShapeDtypeStruct((gate.shape[0] * 8, strip), gate.dtype)] * 2
    latent_rank = 8 * latent_up.shape[0]
    found = [((rows, width), low), ((rows, query_down.shape[1]), low), ((keys, latent_rank), low), ((keys, 128), low),
             ((keys, tiles), low), ((rows, tiles), low), ((rows, tiles // 2), low), ((rows, 128), wide),
             ((rows, query_down.shape[1]), wide), ((rows, latent_down.shape[1]), wide), ((rows, width), wide),
             ((8 * rows, width), low), ((8 * rows, strip), wide)]
    out += [jax.ShapeDtypeStruct(s, d) for s, d in found]
    whole = [pltpu.VMEM((a.shape[0] * 8, a.shape[1]), a.dtype) for a in (query_down, latent_down, query_up, latent_up)]
    return pl.pallas_call(
        functools.partial(start_kernel, scale), out_shape=out,
        in_specs=[ANY] * 9 + [VMEM] * 4, out_specs=[ANY] * 9 + [VMEM] * 11 + [ANY, VMEM],
        scratch_shapes=[dma_sems(2, 3, 6), dma_sems(2, 3, 6)] + [dma_sems(6, 4)] * 6
        + [dma_sems(7, 7), dma_sems(7, 7), dma_sems(2, 9), dma_sems(7, 2), dma_sems(7, 2), dma_sems(3, 7, 2), dma_sems(3, 7, 2)]
        + [pltpu.VMEM(a.shape, a.dtype) for a in weights] + [pltpu.VMEM((gate.shape[0], strip), gate.dtype)] * 2
        + [pltpu.VMEM((8 * weights[6].shape[0], 128), wide), pltpu.VMEM(weights[6].shape, wide)] + whole
        + [pltpu.VMEM((2, 2 * attn_out.shape[0], width), low), pltpu.VMEM((rows, tiles), wide),
           pltpu.VMEM((rows, width), low), dma_sems(3, 2), dma_sems(3, 2), dma_sems(6), dma_sems(2)] + Gather.scratch(1),
        compiler_params=kernel_params(cid),
    )(*weights, gate, up, tokens, bias, turns, down)

def plane_swap(values, j):
    return lax.ppermute(values, "rep", [(i, i ^ j) for i in range(4)])


def column_body(
    tokens,
    cotangent,
    doc_lengths,
    gain_attn,
    query_down,
    gain_query,
    query_up,
    latent_down,
    gain_latent,
    latent_up,
    attn_out,
    gain_ffn,
    w_gate,
    w_up,
    w_down,
):
    low = jnp.bfloat16
    wide = jnp.float32
    rows, width = tokens.shape[1], tokens.shape[2]
    seq_len = rows * 4
    head_dim = ND + RD
    scale = head_dim ** (-0.5)
    rep, shard = lax.axis_index("rep"), lax.axis_index("shard")
    slice_ff = FF // 8
    strip = 896
    shift = (slice_ff * shard) % 128

    gain_list = (gain_attn, gain_ffn, gain_query, gain_latent)
    small = jnp.concatenate(
        [
            lax.dynamic_update_slice(
                jnp.zeros((8 * v.shape[0],), wide), v.astype(wide), (shard * v.shape[0],)
            )
            for v in gain_list
        ]
    ).reshape(-1, 128)
    tile_up = jnp.pad(
        query_up.reshape(-1, H, head_dim), ((0, 0), (0, 0), (0, 128 - head_dim))
    ).reshape(-1, H * 128)
    grad_out = cotangent[0].astype(wide)
    grad_down_in = (residual_scale * grad_out).astype(low)
    down_w = lax.dynamic_update_slice(jnp.zeros((strip, width), low), w_down, (shift, 0))

    local_pos = rep * rows + jnp.arange(rows, dtype=jnp.int32)
    key_pos = jnp.concatenate(
        [(rep ^ j) * rows + jnp.arange(rows, dtype=jnp.int32) for j in range(4)]
    )
    query_seg, query_off = segment_of(doc_lengths[0], local_pos)
    key_seg = segment_of(doc_lengths[0], key_pos)[0]
    allowed = (query_seg[:, None] == key_seg[None, :]) & (key_pos[None, :] <= local_pos[:, None])
    bias = jnp.where(allowed, 0.0, masked_score).astype(wide)
    cos_part, sin_part = rope_tables(query_off, RD)
    none = jnp.zeros((rows, RD // 2), wide)
    edge = jnp.zeros((rows, ND), wide)
    tail = jnp.zeros((rows, 128 - head_dim), wide)
    turns = jnp.stack(
        [
            jnp.concatenate([edge + 1.0, cos_part, cos_part, tail], axis=1),
            jnp.concatenate([edge, none, sin_part, tail], axis=1),
            jnp.concatenate([edge, -sin_part, none, tail], axis=1),
        ]
    )
    (
        aout,
        qdown,
        ldown,
        qup,
        lup,
        gd_all,
        small_all,
        gate_w,
        up_w,
        normed_low,
        query_low,
        latent_low,
        rope_tile,
        keyvals,
        queries,
        mixed_low,
        logs,
        query_lat,
        latent_proj,
        residual,
        ffn_all,
        grad_hidden,
    ) = start_gather(
        0,
        scale,
        (attn_out, query_down, latent_down, tile_up, latent_up, grad_down_in, small),
        w_gate,
        w_up,
        tokens[0],
        bias,
        turns,
        down_w,
    )
    gains_all = jnp.sum(small_all.reshape(8, -1), axis=0)
    gain_in, gain_f = gains_all[:width], gains_all[width : 2 * width]
    gain_q = gains_all[2 * width : 2 * width + query_down.shape[1]]
    gain_l = gains_all[2 * width + query_down.shape[1] :]

    def key_rotate(values):
        return rotate(values, cos_part, sin_part)

    inputs = tokens[0].astype(wide)
    norm_in_back = jax.vjp(rms_scale, inputs, gain_in)[1]
    norm_q_back = jax.vjp(rms_scale, query_lat, gain_q)[1]
    norm_l_back = jax.vjp(rms_scale, latent_proj[:, :KR], gain_l)[1]
    key_back = jax.vjp(key_rotate, latent_proj[:, KR:])[1]
    norm_f_back = jax.vjp(rms_scale, residual, gain_f)[1]

    gate_pre = jnp.dot(ffn_all, gate_w, preferred_element_type=wide)
    up_pre = jnp.dot(ffn_all, up_w, preferred_element_type=wide)
    hidden, act_back = jax.vjp(swiglu, gate_pre, up_pre)
    hidden_low = hidden.astype(low)
    grad_gate_f, grad_up_f = act_back(grad_hidden)
    grad_gate = grad_gate_f.astype(low)
    grad_up = grad_up_f.astype(low)
    down_part = inner_rows(hidden_low, gd_all).astype(low)
    grad_ffn_in, down_own, gate_own, up_part = back_sums(
        2, down_part, ffn_all, grad_gate, grad_up, gate_w, up_w, slice_ff
    )

    grad_res_norm, grad_gain_ffn = norm_f_back(grad_ffn_in)
    grad_resid = grad_out + grad_res_norm
    grad_branch = (residual_scale * grad_resid).astype(low)
    cols = jnp.stack([mixed_low, normed_low]).reshape(2, rows, 8, width // 8).transpose(2, 0, 1, 3)
    (
        branch_all,
        cols_all,
        down_all,
        up_own,
        grad_q_proj,
        grad_kv,
        grad_rope,
        qup_part,
        lup_part,
    ) = middle_exchange(
        3,
        scale,
        grad_branch,
        cols,
        down_own,
        up_part,
        aout,
        query_low,
        latent_low,
        (queries, keyvals, rope_tile, bias, turns, logs),
    )
    down_grad = down_all.astype(wide)
    rope_sum = grad_rope[:, ND:head_dim]
    grad_lat_part = jnp.concatenate([outer_cols(grad_kv, lup), rope_sum], axis=1).astype(low)
    grad_lat_own = grad_lat_part[:rows].astype(wide)
    for j in range(1, 4):
        grad_lat_own = grad_lat_own + plane_swap(
            grad_lat_part[j * rows : (j + 1) * rows], j
        ).astype(wide)
    grad_q_lat_f, grad_gain_query = norm_q_back(outer_cols(grad_q_proj, qup))
    grad_q_lat = grad_q_lat_f.astype(low)
    grad_lat_c, grad_gain_latent = norm_l_back(grad_lat_own[:, :KR])
    grad_lat_r = key_back(grad_lat_own[:, KR:])[0]
    grad_lat = jnp.concatenate([grad_lat_c, grad_lat_r], axis=1).astype(low)
    grad_normed = outer_cols(grad_q_lat, qdown) + outer_cols(grad_lat, ldown)
    grad_in_norm, grad_gain_attn = norm_in_back(grad_normed)
    tokens_grad = (grad_resid + grad_in_norm).astype(low)

    grad_lats = jnp.concatenate([grad_q_lat, grad_lat], axis=1)
    mixed_cols = cols_all[:, 0].reshape(8 * rows, width // 8)
    normed_cols = cols_all[:, 1].reshape(8 * rows, width // 8)
    aout_part = inner_rows(mixed_cols, branch_all).astype(low)
    gains = jnp.concatenate(
        [
            v.reshape(8, -1)
            for v in (grad_gain_attn, grad_gain_ffn, grad_gain_query, grad_gain_latent)
        ]
        + [jnp.zeros((8, 1024 - 768), wide)],
        axis=1,
    ).reshape(8, 8, 128)
    gate_all, up_all, out_sum, aout_own, lat_own, lup_own, qup_own, gain_own = last_sums(
        4,
        gate_own,
        up_own,
        grad_lats,
        qup_part.reshape(8, -1, qup_part.shape[1]),
        lup_part.reshape(8, -1, lup_part.shape[1]),
        hidden_low,
        down_w,
        aout_part,
        normed_cols,
        gains,
    )
    layer_out = (residual + residual_scale * out_sum).astype(low)
    gate_grad, up_grad = widen((gate_all, up_all), FF)
    aout_own = aout_own.astype(wide)
    lat_own = lat_own.reshape(320, -1).astype(wide)
    lup_own = lup_own.astype(wide)
    qup_own = unpack(qup_own, H)
    gain_own = gain_own.reshape(1024)

    return (
        layer_out[None],
        tokens_grad[None],
        gain_own[:320],
        lat_own[:, : query_down.shape[1]],
        gain_own[640:736],
        qup_own,
        lat_own[:, query_down.shape[1] :],
        gain_own[736:768],
        lup_own,
        aout_own,
        gain_own[320:640],
        gate_grad,
        up_grad,
        down_grad,
    )


def body(
    tokens,
    cotangent,
    doc_lengths,
    gain_attn,
    query_down,
    gain_query,
    query_up,
    latent_down,
    gain_latent,
    latent_up,
    attn_out,
    gain_ffn,
    w_gate,
    w_up,
    w_down,
):
    low_type = jnp.bfloat16
    wide_type = jnp.float32
    tok_rows = tokens.shape[1]
    seq_len = tok_rows * lax.axis_size("rep")
    head_dim = ND + RD
    group_size = math.gcd(H, 8)
    group_count = H // group_size
    softmax_scale = head_dim ** (-0.5)
    local_pos = lax.axis_index("rep") * tok_rows + jnp.arange(tok_rows, dtype=jnp.int32)
    key_pos = jnp.arange(seq_len, dtype=jnp.int32)
    query_seg, query_off = segment_of(doc_lengths[0], local_pos)
    key_seg = segment_of(doc_lengths[0], key_pos)[0]
    allowed = (query_seg[:, None] == key_seg[None, :]) & (key_pos[None, :] <= local_pos[:, None])
    cos_part, sin_part = rope_tables(query_off, RD)
    (
        gain_in_full,
        qdown_full,
        gain_q_full,
        qup_full,
        ldown_full,
        gain_l_full,
        lup_full,
        aout_full,
        gain_f_full,
    ) = (
        lax.all_gather(gain_attn, "shard", axis=0, tiled=True),
        lax.all_gather(query_down, "shard", axis=0, tiled=True),
        lax.all_gather(gain_query, "shard", axis=0, tiled=True),
        lax.all_gather(query_up, "shard", axis=0, tiled=True),
        lax.all_gather(latent_down, "shard", axis=0, tiled=True),
        lax.all_gather(gain_latent, "shard", axis=0, tiled=True),
        lax.all_gather(latent_up, "shard", axis=0, tiled=True),
        lax.all_gather(attn_out, "shard", axis=0, tiled=True),
        lax.all_gather(gain_ffn, "shard", axis=0, tiled=True),
    )
    inputs = tokens[0].astype(wide_type)
    normed, norm_in_back = jax.vjp(rms_scale, inputs, gain_in_full.astype(wide_type))
    normed_low = normed.astype(low_type)
    query_lat = jnp.dot(normed_low, qdown_full, preferred_element_type=wide_type)
    query_norm, norm_q_back = jax.vjp(rms_scale, query_lat, gain_q_full.astype(wide_type))
    query_low = query_norm.astype(low_type)
    query_proj = jnp.dot(query_low, qup_full, preferred_element_type=wide_type).reshape(
        tok_rows, H, head_dim
    )

    def query_rope(values):
        return jnp.concatenate(
            [
                values[..., :ND],
                rotate(values[..., ND:], cos_part[:, None, :], sin_part[:, None, :]),
            ],
            axis=-1,
        )

    query_rot, query_back = jax.vjp(query_rope, query_proj)
    query_used = query_rot.astype(low_type)
    latent_proj = jnp.dot(normed_low, ldown_full, preferred_element_type=wide_type)
    latent_norm, norm_l_back = jax.vjp(
        rms_scale, latent_proj[:, :KR], gain_l_full.astype(wide_type)
    )
    latent_low = latent_norm.astype(low_type)

    def key_rotate(values):
        return rotate(values, cos_part, sin_part)

    key_rot, key_back = jax.vjp(key_rotate, latent_proj[:, KR:])
    key_rope = key_rot.astype(low_type)
    keyvals = jnp.dot(latent_low, lup_full, preferred_element_type=wide_type).astype(low_type)
    all_keyvals, all_rope = (
        lax.all_gather(keyvals, "rep", axis=0, tiled=True),
        lax.all_gather(key_rope, "rep", axis=0, tiled=True),
    )
    queries = query_used.reshape(tok_rows, group_count, group_size, head_dim).transpose(1, 0, 2, 3)
    key_groups = all_keyvals.reshape(seq_len, group_count, group_size, ND + VD).transpose(
        1, 0, 2, 3
    )

    def scores_of(query_blk, key_blk):
        nope_part = jnp.einsum(
            "thd,shd->hts", query_blk[..., :ND], key_blk[..., :ND], preferred_element_type=wide_type
        )
        rope_part = jnp.einsum(
            "thd,sd->hts", query_blk[..., ND:], all_rope, preferred_element_type=wide_type
        )
        return jnp.where(allowed[None], (nope_part + rope_part) * softmax_scale, masked_score)

    def forward_group(carry, blocks):
        query_blk, key_blk = blocks
        scores = scores_of(query_blk, key_blk)
        row_max = jnp.max(scores, axis=-1, keepdims=True)
        exp_scores = jnp.exp(scores - row_max)
        totals = jnp.sum(exp_scores, axis=-1, keepdims=True)
        probs = (exp_scores / totals).astype(low_type)
        mixed = jnp.einsum(
            "hts,shd->thd", probs, key_blk[..., ND:], preferred_element_type=wide_type
        )
        return (carry, (mixed, row_max + jnp.log(totals)))

    start_carry = jnp.zeros((), wide_type)
    final_carry, (mixed_groups, log_totals) = lax.scan(
        forward_group, start_carry, (queries, key_groups)
    )
    mixed_low = mixed_groups.transpose(1, 0, 2, 3).reshape(tok_rows, H * VD).astype(low_type)
    branch = jnp.dot(mixed_low, aout_full, preferred_element_type=wide_type)
    residual = inputs + residual_scale * branch
    normed_ffn, norm_f_back = jax.vjp(rms_scale, residual, gain_f_full.astype(wide_type))
    ffn_low = normed_ffn.astype(low_type)
    gate_full, up_full, down_full = (
        lax.all_gather(w_gate, "shard", axis=0, tiled=True),
        lax.all_gather(w_up, "shard", axis=0, tiled=True),
        lax.all_gather(w_down, "shard", axis=0, tiled=True),
    )
    gate_pre = jnp.dot(ffn_low, gate_full, preferred_element_type=wide_type)
    up_pre = jnp.dot(ffn_low, up_full, preferred_element_type=wide_type)
    hidden, act_back = jax.vjp(swiglu, gate_pre, up_pre)
    hidden_low = hidden.astype(low_type)
    ffn_branch = jnp.dot(hidden_low, down_full, preferred_element_type=wide_type)
    layer_out = residual + residual_scale * ffn_branch
    grad_out = cotangent[0].astype(wide_type)
    grad_down_in = (residual_scale * grad_out).astype(low_type)
    gate_back_w, up_back_w, down_back_w = (
        lax.all_gather(w_gate, "shard", axis=0, tiled=True),
        lax.all_gather(w_up, "shard", axis=0, tiled=True),
        lax.all_gather(w_down, "shard", axis=0, tiled=True),
    )
    grad_hidden = outer_cols(grad_down_in, down_back_w)
    grad_gate_f, grad_up_f = act_back(grad_hidden)
    grad_gate = grad_gate_f.astype(low_type)
    grad_up = grad_up_f.astype(low_type)
    grad_ffn_in = outer_cols(grad_gate, gate_back_w) + outer_cols(grad_up, up_back_w)
    down_grad = lax.psum_scatter(
        inner_rows(hidden_low, grad_down_in).astype(jnp.bfloat16),
        "shard",
        scatter_dimension=0,
        tiled=True,
    )
    gate_up_in = jnp.concatenate([grad_gate, grad_up], axis=1)
    gate_up_grad = lax.psum_scatter(
        inner_rows(ffn_low, gate_up_in).astype(jnp.bfloat16),
        "shard",
        scatter_dimension=0,
        tiled=True,
    ).astype(jnp.float32)
    gate_grad = gate_up_grad[:, :FF]
    up_grad = gate_up_grad[:, FF:]
    grad_res_norm, grad_gain_ffn = norm_f_back(grad_ffn_in)
    grad_resid = grad_out + grad_res_norm
    qdown_back, qup_back, ldown_back, lup_back, aout_back = (
        lax.all_gather(query_down, "shard", axis=0, tiled=True),
        lax.all_gather(query_up, "shard", axis=0, tiled=True),
        lax.all_gather(latent_down, "shard", axis=0, tiled=True),
        lax.all_gather(latent_up, "shard", axis=0, tiled=True),
        lax.all_gather(attn_out, "shard", axis=0, tiled=True),
    )
    grad_branch = (residual_scale * grad_resid).astype(low_type)
    aout_grad = inner_rows(mixed_low, grad_branch)
    grad_mixed = outer_cols(grad_branch, aout_back).astype(low_type)
    grad_groups = grad_mixed.reshape(tok_rows, group_count, group_size, VD).transpose(1, 0, 2, 3)

    def backward_group(rope_acc, blocks):
        query_blk, key_blk, grad_blk, log_blk = blocks
        scores = scores_of(query_blk, key_blk)
        probs = jnp.exp(scores - log_blk)
        grad_probs = jnp.einsum(
            "thd,shd->hts", grad_blk, key_blk[..., ND:], preferred_element_type=wide_type
        )
        delta = jnp.sum(probs * grad_probs, axis=-1, keepdims=True)
        grad_scores = (probs * (grad_probs - delta)).astype(low_type)
        grad_query = (
            jnp.concatenate(
                [
                    jnp.einsum(
                        "hts,shd->thd",
                        grad_scores,
                        key_blk[..., :ND],
                        preferred_element_type=wide_type,
                    ),
                    jnp.einsum(
                        "hts,sd->thd", grad_scores, all_rope, preferred_element_type=wide_type
                    ),
                ],
                axis=-1,
            )
            * softmax_scale
        )
        grad_key = (
            jnp.einsum(
                "hts,thd->shd", grad_scores, query_blk[..., :ND], preferred_element_type=wide_type
            )
            * softmax_scale
        )
        grad_value = jnp.einsum(
            "hts,thd->shd", probs.astype(low_type), grad_blk, preferred_element_type=wide_type
        )
        rope_acc = (
            rope_acc
            + jnp.einsum(
                "hts,thd->sd", grad_scores, query_blk[..., ND:], preferred_element_type=wide_type
            )
            * softmax_scale
        )
        return (rope_acc, (grad_query, jnp.concatenate([grad_key, grad_value], axis=-1)))

    rope_start = jnp.zeros((seq_len, RD), wide_type)
    rope_sum, (grad_q_groups, grad_kv_groups) = lax.scan(
        backward_group, rope_start, (queries, key_groups, grad_groups, log_totals)
    )
    grad_kv_all = grad_kv_groups.transpose(1, 0, 2, 3).reshape(seq_len, H * (ND + VD))
    grad_kv_own, grad_rope_own = (
        lax.psum_scatter(
            grad_kv_all.astype(jnp.bfloat16), "rep", scatter_dimension=0, tiled=True
        ).astype(jnp.float32),
        lax.psum_scatter(
            rope_sum.astype(jnp.bfloat16), "rep", scatter_dimension=0, tiled=True
        ).astype(jnp.float32),
    )
    grad_q_full = grad_q_groups.transpose(1, 0, 2, 3).reshape(tok_rows, H, head_dim)
    grad_q_proj = query_back(grad_q_full)[0].reshape(tok_rows, H * head_dim).astype(low_type)
    qup_grad = inner_rows(query_low, grad_q_proj)
    grad_q_lat_f, grad_gain_query = norm_q_back(outer_cols(grad_q_proj, qup_back))
    grad_q_lat = grad_q_lat_f.astype(low_type)
    grad_kv_low = grad_kv_own.astype(low_type)
    lup_grad = inner_rows(latent_low, grad_kv_low)
    grad_lat_c, grad_gain_latent = norm_l_back(outer_cols(grad_kv_low, lup_back))
    grad_lat_r = key_back(grad_rope_own)[0]
    grad_lat = jnp.concatenate([grad_lat_c, grad_lat_r], axis=1).astype(low_type)
    qdown_grad = inner_rows(normed_low, grad_q_lat)
    ldown_grad = inner_rows(normed_low, grad_lat)
    grad_normed = outer_cols(grad_q_lat, qdown_back) + outer_cols(grad_lat, ldown_back)
    grad_in_norm, grad_gain_attn = norm_in_back(grad_normed)
    tokens_grad = (grad_resid + grad_in_norm).astype(low_type)
    (
        owned_gain_attn,
        owned_qdown,
        owned_gain_query,
        owned_qup,
        owned_ldown,
        owned_gain_latent,
        owned_lup,
        owned_aout,
        owned_gain_ffn,
    ) = (
        lax.psum_scatter(
            grad_gain_attn.astype(jnp.bfloat16), "shard", scatter_dimension=0, tiled=True
        ).astype(jnp.float32),
        lax.psum_scatter(
            qdown_grad.astype(jnp.bfloat16), "shard", scatter_dimension=0, tiled=True
        ).astype(jnp.float32),
        lax.psum_scatter(
            grad_gain_query.astype(jnp.bfloat16), "shard", scatter_dimension=0, tiled=True
        ).astype(jnp.float32),
        lax.psum_scatter(
            qup_grad.astype(jnp.bfloat16), "shard", scatter_dimension=0, tiled=True
        ).astype(jnp.float32),
        lax.psum_scatter(
            ldown_grad.astype(jnp.bfloat16), "shard", scatter_dimension=0, tiled=True
        ).astype(jnp.float32),
        lax.psum_scatter(
            grad_gain_latent.astype(jnp.bfloat16), "shard", scatter_dimension=0, tiled=True
        ).astype(jnp.float32),
        lax.psum_scatter(
            lup_grad.astype(jnp.bfloat16), "shard", scatter_dimension=0, tiled=True
        ).astype(jnp.float32),
        lax.psum_scatter(
            aout_grad.astype(jnp.bfloat16), "shard", scatter_dimension=0, tiled=True
        ).astype(jnp.float32),
        lax.psum_scatter(
            grad_gain_ffn.astype(jnp.bfloat16), "shard", scatter_dimension=0, tiled=True
        ).astype(jnp.float32),
    )
    summed = (
        lax.psum(owned_gain_attn.astype(jnp.bfloat16), "rep").astype(jnp.float32),
        lax.psum(owned_qdown.astype(jnp.bfloat16), "rep").astype(jnp.float32),
        lax.psum(owned_gain_query.astype(jnp.bfloat16), "rep").astype(jnp.float32),
        lax.psum(owned_qup.astype(jnp.bfloat16), "rep").astype(jnp.float32),
        lax.psum(owned_ldown.astype(jnp.bfloat16), "rep").astype(jnp.float32),
        lax.psum(owned_gain_latent.astype(jnp.bfloat16), "rep").astype(jnp.float32),
        lax.psum(owned_lup.astype(jnp.bfloat16), "rep").astype(jnp.float32),
        lax.psum(owned_aout.astype(jnp.bfloat16), "rep").astype(jnp.float32),
        lax.psum(owned_gain_ffn.astype(jnp.bfloat16), "rep").astype(jnp.float32),
        lax.psum(gate_grad.astype(jnp.bfloat16), "rep").astype(jnp.float32),
        lax.psum(up_grad.astype(jnp.bfloat16), "rep").astype(jnp.float32),
        lax.psum(down_grad, "rep").astype(jnp.float32),
    )
    return (
        layer_out.astype(low_type)[None],
        tokens_grad[None],
        summed[0],
        summed[1],
        summed[2],
        summed[3],
        summed[4],
        summed[5],
        summed[6],
        summed[7],
        summed[8],
        summed[9],
        summed[10],
        summed[11],
    )


def solution(mesh):
    placed = (
        P("shard", "rep", None),
        P("shard", "rep", None),
        P("shard", None),
        P("shard"),
        P("shard", None),
        P("shard"),
        P("shard", None),
        P("shard", None),
        P("shard"),
        P("shard", None),
        P("shard", None),
        P("shard"),
        P("shard", None),
        P("shard", None),
        P("shard", None),
    )
    fits = mesh.shape["rep"] == 4 and mesh.shape["shard"] == 8
    return jax.shard_map(
        column_body if fits else body,
        mesh=mesh,
        in_specs=placed,
        out_specs=(
            P("shard", "rep", None),
            P("shard", "rep", None),
            P("shard"),
            P("shard", None),
            P("shard"),
            P("shard", None),
            P("shard", None),
            P("shard"),
            P("shard", None),
            P("shard", None),
            P("shard"),
            P("shard", None),
            P("shard", None),
            P("shard", None),
        ),
        check_vma=False,
    )
```

```python
import functools
import math

import jax
import jax.numpy as jnp
from jax import lax
from jax.experimental import pallas as pl
from jax.experimental.pallas import tpu as pltpu
from jax.sharding import PartitionSpec as P

KR = 256
H = 40
ND = 64
RD = 32
VD = 64
FF = 6400


epsilon = 1e-05
residual_scale = 1.4 / math.sqrt(62.0)
rope_base = 10000.0
masked_score = -1e30


def rms_scale(values, gain):
    return values * lax.rsqrt(jnp.mean(values * values, axis=-1, keepdims=True) + epsilon) * gain


def rotate(values, cos_part, sin_part):
    midpoint = values.shape[-1] // 2
    former = values[..., :midpoint]
    latter = values[..., midpoint:]
    return jnp.concatenate(
        [former * cos_part - latter * sin_part, latter * cos_part + former * sin_part], axis=-1
    )


def segment_of(lengths, positions):
    doc_ends = jnp.cumsum(lengths)
    doc_starts = doc_ends - lengths
    segment = jnp.sum((positions[:, None] >= doc_ends[None, :]).astype(jnp.int32), axis=1)
    chosen = segment[:, None] == jnp.arange(lengths.shape[0], dtype=jnp.int32)[None, :]
    offsets = positions - jnp.sum(jnp.where(chosen, doc_starts[None, :], 0), axis=1)
    return (segment, offsets)


def rope_tables(offsets, rope_width):
    exponents = jnp.arange(0, rope_width, 2, dtype=jnp.float32) / rope_width
    angles = offsets.astype(jnp.float32)[:, None] * (rope_base ** (-exponents))[None, :]
    return (jnp.cos(angles), jnp.sin(angles))


def swiglu(gate_vals, up_vals):
    return jax.nn.silu(gate_vals) * up_vals


def inner_rows(leading, trailing):
    return lax.dot_general(
        leading, trailing, (((0,), (0,)), ((), ())), preferred_element_type=jnp.float32
    )


def outer_cols(leading, trailing):
    return lax.dot_general(
        leading, trailing, (((1,), (1,)), ((), ())), preferred_element_type=jnp.float32
    )


MESH = pl.DeviceIdType.MESH
ANY = pl.BlockSpec(memory_space=pl.ANY)

def place():
    rep = lax.axis_index("rep")
    shard = lax.axis_index("shard")
    zpos, core = shard // 2, shard % 2
    return rep, zpos, core

def mult(value, by):
    return pl.multiple_of(value, by)

def greet(rep, zpos, core, plane=0, column=False):
    barrier = pltpu.get_barrier_semaphore()
    shard = zpos * 2 + core

    def signal(r, s):
        pl.semaphore_signal(barrier, inc=1, device_id=(r, s), device_id_type=MESH)

    if column:
        for m in range(1, 8):
            signal(rep, column_place(zpos, core, m))
        count = 7
    else:
        signal(rep, zpos * 2 + 1 - core)

        @pl.when(zpos > 0)
        def _():
            signal(rep, shard - 2)

        @pl.when(zpos < 3)
        def _():
            signal(rep, shard + 2)

        count = 1 + jnp.minimum(zpos, 1) + jnp.minimum(3 - zpos, 1)
    if plane:
        for other in plane_places(rep)[:plane]:
            signal(other, shard)
        count = count + plane
    pl.semaphore_wait(barrier, count)


def plane_places(rep):
    return rep + 1 - 2 * (rep % 2), (rep + 2) % 4, 3 - rep


def column_place(zpos, core, m, back=False):
    step = 4 - m // 2 if back else m // 2
    return ((zpos + step) % 4) * 2 + (core + m) % 2


def remote(src, dst, ssem, rsem, r, s):
    return pltpu.make_async_remote_copy(
        src_ref=src, dst_ref=dst, send_sem=ssem, recv_sem=rsem, device_id=(r, s), device_id_type=MESH
    )


def dma_sems(*dims):
    return pltpu.SemaphoreType.DMA(dims)


def head_tile(h):
    return pl.ds(pl.multiple_of(h * 128, 128), 128)


def turn(values, tables, back=False):
    keep, high, low_part = tables
    if back:
        return values * keep + pltpu.roll(values * high, 112, 1) + pltpu.roll(values * low_part, 16, 1)
    return values * keep + pltpu.roll(values, 16, 1) * high + pltpu.roll(values, 112, 1) * low_part


def dot_nt(a, b):
    return lax.dot_general(a, b, (((1,), (1,)), ((), ())), preferred_element_type=jnp.float32)


def dot_tn(a, b):
    return lax.dot_general(a, b, (((0,), (0,)), ((), ())), preferred_element_type=jnp.float32)


def attend_heads(scale, proj, kv, rope, bias, turns, query, mixed, logs):
    low = jnp.bfloat16
    lane = lax.broadcasted_iota(jnp.int32, (1, 128), 1)
    first = lane < 64

    def group(i, carry):
        heads_here = [4 * i + j for j in range(4)]
        queries = [turn(proj[:, head_tile(h)], (turns[0], turns[1], turns[2])).astype(low) for h in heads_here]
        keyvals = [kv[:, head_tile(h)] for h in heads_here]
        scores = [dot_nt(q, jnp.where(first, keyval, rope[...])) * scale + bias[...] for q, keyval in zip(queries, keyvals)]
        tops = [jnp.max(s, axis=1, keepdims=True) for s in scores]
        grown = [jnp.exp(s - top) for s, top in zip(scores, tops)]
        totals = [jnp.sum(g, axis=1, keepdims=True) for g in grown]
        outs = [jnp.dot((g / total).astype(low), keyval, preferred_element_type=jnp.float32)
                for g, total, keyval in zip(grown, totals, keyvals)]
        for h, q, top, total in zip(heads_here, queries, tops, totals):
            query[:, head_tile(h)] = q
            logs[...] = jnp.where(lane == h, top + jnp.log(total), logs[...])
        for j in range(2):
            mixed[:, head_tile(2 * i + j)] = jnp.where(first, pltpu.roll(outs[2 * j], 64, 1), outs[2 * j + 1]).astype(low)
        return carry

    return group


def attend_back_heads(scale, query, kv, rope, bias, turns, logs, grad, grad_query, grad_packed, grad_kv, grad_rope, left):
    low = jnp.bfloat16
    rows = query.shape[0]
    lane = lax.broadcasted_iota(jnp.int32, (1, 128), 1)
    first = lane < 64

    def one(h, grad_value):
        q = query[:, head_tile(h)]
        keyval = kv[:, head_tile(h)]
        key = jnp.where(first, keyval, rope[...])
        left[0:rows, 0:128] = q
        left[rows:, 128:256] = grad_value
        both = dot_nt(left[...], jnp.concatenate([key, keyval], axis=1))
        log = jnp.sum(jnp.where(lane == h, logs[...], 0.0), axis=1, keepdims=True)
        probs = jnp.exp(both[:rows] * scale + bias[...] - log)
        weighed = probs * both[rows:]
        delta = jnp.sum(weighed, axis=1, keepdims=True)
        grad_scores = (weighed - probs * delta).astype(low)
        grad_q = jnp.dot(grad_scores, key, preferred_element_type=jnp.float32) * scale
        grad_q = turn(grad_q, (turns[0], turns[1], turns[2]), True)
        grad_query[:, head_tile(h)] = grad_q.astype(low)
        out = dot_tn(jnp.concatenate([grad_scores, probs.astype(low)], axis=0), left[...])
        grad_key = out[:, :128] * scale
        grad_rope[...] += grad_key
        grad_kv[:, head_tile(h)] = jnp.where(first, grad_key, out[:, 128:]).astype(low)
        return grad_q

    def quarter(i, carry):
        rotary = jnp.zeros((rows, 128), jnp.float32)
        for j in range(5):
            both = grad[:, head_tile(5 * i + j)].astype(jnp.float32)
            even = one(10 * i + 2 * j, jnp.where(first, 0.0, pltpu.roll(both, 64, 1)).astype(low))
            odd = one(10 * i + 2 * j + 1, jnp.where(first, 0.0, both).astype(low))
            grad_packed[:, head_tile(8 * i + j)] = jnp.where(first, even, pltpu.roll(odd, 64, 1)).astype(low)
            for k, got in ((2 * j, even), (2 * j + 1, odd)):
                at = 32 * (k % 4)
                moved = got if at == 64 else pltpu.roll(got, (at + 64) % 128, 1)
                rotary = jnp.where((lane >= at) & (lane < at + 32), moved, rotary)
                if k % 4 == 3 or k == 9:
                    grad_packed[:, head_tile(8 * i + 5 + k // 4)] = rotary.astype(low)
                    rotary = jnp.zeros((rows, 128), jnp.float32)
        return carry

    return quarter


def unpacked(packed, heads):
    pieces = []
    for h in range(heads):
        first, k = h // 10 * 1024, h % 10
        pieces.append(packed[:, first + 64 * k : first + 64 * k + 64])
        pieces.append(packed[:, first + 640 + 32 * k : first + 672 + 32 * k])
    return jnp.concatenate(pieces, axis=1)


def widen_kernel(heads, gate, up, down, attn_out, lat, latent_up, query_up, *outs):
    wide = jnp.float32
    for strips, out in zip((gate, up), outs[:2]):
        each = out.shape[1] // 8
        for s in range(8):
            first, last = s * each // 128, (s + 1) * each // 128
            tiles = strips[s, 0].astype(wide)
            if s * each % 128:
                shared = strips[s - 1, 0, :, (first - (s - 1) * each // 128) * 128 :][:, :128]
                out[:, first * 128 : first * 128 + 128] = tiles[:, :128] + shared.astype(wide)
                first_full = first + 1
            else:
                first_full = first
            out[:, first_full * 128 : last * 128] = tiles[:, (first_full - first) * 128 : (last - first) * 128]
    down_out, attn_out_out, query_down_out, latent_down_out, latent_up_out, query_up_out = outs[2:]
    down_out[...] = down[...].astype(wide)
    attn_out_out[...] = attn_out[...].astype(wide)
    rank = query_down_out.shape[1]
    query_down_out[...] = lat[0, :, :rank].astype(wide)
    latent_down_out[...] = lat[0, :, rank:].astype(wide)

    @pl.when(pl.program_id(0) == 0)
    def _():
        latent_up_out[...] = latent_up[...].astype(wide)
        query_up_out[...] = unpacked(query_up[...], heads).astype(wide)


def widen(gate, up, down, attn_out, lat, latent_up, query_up, cols, rank, heads):
    _, quarters, rows, strip = gate.shape
    width = attn_out.shape[1]
    whole = lambda a: pl.BlockSpec(a, lambda q: (0, 0))
    by_rows = lambda c: pl.BlockSpec((rows, c), lambda q: (q, 0))
    by_cols = pl.BlockSpec((down.shape[0], width // quarters), lambda q: (0, q))
    strips = pl.BlockSpec((8, 1, rows, strip), lambda q: (0, q, 0, 0))
    shapes = [(quarters * rows, cols)] * 2 + [down.shape, attn_out.shape, (quarters * rows, rank),
                                              (quarters * rows, lat.shape[2] - rank), latent_up.shape, (query_up.shape[0], heads * 96)]
    return pl.pallas_call(
        functools.partial(widen_kernel, heads), grid=(quarters,),
        out_shape=[jax.ShapeDtypeStruct(s, jnp.float32) for s in shapes],
        in_specs=[strips, strips, by_cols, by_rows(width), pl.BlockSpec((1,) + lat.shape[1:], lambda q: (q, 0, 0)),
                  whole(latent_up.shape), whole(query_up.shape)],
        out_specs=[by_rows(cols)] * 2 + [by_cols, by_rows(width), by_rows(rank), by_rows(lat.shape[2] - rank),
                                         whole(latent_up.shape), whole(shapes[-1])],
        compiler_params=pltpu.CompilerParams(vmem_limit_bytes=56 * 2**20),
    )(gate, up, down, attn_out, lat, latent_up, query_up)


class Gather:
    def __init__(self, ins, outs, sems):
        self.ins, self.outs = ins, outs
        self.zsend, self.zrecv, self.csend, self.crecv, self.own = sems
        self.rep, self.zpos, self.core = place()
        self.held = None

    @staticmethod
    def scratch(n):
        return [dma_sems(2, 3, n), dma_sems(2, 3, n), dma_sems(7, n), dma_sems(7, n), dma_sems(2, n)]

    def at(self, a, z, c):
        rows = self.ins[a].shape[0]
        return self.outs[a].at[pl.ds(mult((z * 2 + c) * rows, rows), rows)]

    def hop_copy(self, a, way, hop, z, src=None):
        dst = self.at(a, z, self.core)
        return remote(dst if src is None else src, dst, self.zsend.at[way, hop, a], self.zrecv.at[way, hop, a],
                      self.rep, (self.zpos + (1 - 2 * way)) * 2 + self.core)

    def core_copy(self, a, slot, z, c, src=None):
        dst = self.at(a, z, c)
        return remote(dst if src is None else src, dst, self.csend.at[slot, a], self.crecv.at[slot, a],
                      self.rep, self.zpos * 2 + 1 - self.core)

    def keep(self, a):
        return pltpu.make_async_copy(self.ins[a], self.at(a, self.zpos, self.core), self.own.at[0, a])

    def onward(self, way):
        return self.zpos < 3 if way == 0 else self.zpos > 0

    def source(self, way, hop):
        z = self.zpos - hop if way == 0 else self.zpos + hop
        return z, (z >= 0 if way == 0 else z <= 3)

    def start(self, which=None):
        which = range(len(self.ins)) if which is None else which
        for way in range(2):
            @pl.when(self.onward(way))
            def _():
                for a in which:
                    self.hop_copy(a, way, 0, self.zpos, src=self.ins[a]).start()
        for a in which:
            self.core_copy(a, 0, self.zpos, self.core, src=self.ins[a]).start()
            self.keep(a).start()

    def hop(self, hop, which=None):
        which = range(len(self.ins)) if which is None else which
        for way in range(2):
            z, there = self.source(way, hop)

            @pl.when(there)
            def _():
                for a in which:
                    self.hop_copy(a, way, hop - 1, z).wait_recv()
                    if hop < 3:
                        @pl.when(self.onward(way))
                        def _():
                            self.hop_copy(a, way, hop, z).start()
                    self.core_copy(a, way * 3 + hop, z, self.core).start()

    def finish(self):
        arrays = range(len(self.ins))
        for way in range(2):
            for hop in range(3):
                z, there = self.source(way, hop)

                @pl.when(there & self.onward(way))
                def _():
                    for a in arrays:
                        self.hop_copy(a, way, hop, z).wait_send()
        for a in arrays:
            self.keep(a).wait()
            self.core_copy(a, 0, self.zpos, self.core, src=self.ins[a]).wait_send()
            self.core_copy(a, 0, self.zpos, 1 - self.core).wait_recv()
        for way in range(2):
            for hop in range(1, 4):
                z, there = self.source(way, hop)

                @pl.when(there)
                def _():
                    for a in arrays:
                        self.core_copy(a, way * 3 + hop, z, self.core).wait_send()
                        self.core_copy(a, way * 3 + hop, z, 1 - self.core).wait_recv()


class Total:
    def __init__(self, term, out, bufs, sems):
        self.term, self.out = term, out
        self.theirs, self.landed = bufs
        self.zsend, self.zrecv, self.csend, self.crecv = sems
        self.rep, self.zpos, self.core = place()

    @staticmethod
    def scratch(term):
        return [pltpu.VMEM((4,) + term.shape[1:], term.dtype), pltpu.VMEM((5,) + term.shape[1:], term.dtype),
                dma_sems(2, 4), dma_sems(2, 4), dma_sems(4), dma_sems(4)]

    @staticmethod
    def split(term, out, refs):
        return Total(term, out, refs[:2], refs[2:6]), refs[6:]

    def pair_copy(self, z):
        return remote(self.term.at[z * 2 + 1 - self.core], self.theirs.at[z], self.csend.at[z], self.crecv.at[z],
                      self.rep, self.zpos * 2 + 1 - self.core)

    def hop_copy(self, way, z):
        return remote(self.theirs.at[z], self.landed.at[z + 1 - way], self.zsend.at[way, z], self.zrecv.at[way, z],
                      self.rep, (self.zpos + (1 - 2 * way)) * 2 + self.core)

    def each(self, step):
        for way in range(2):
            behind = self.zpos if way == 0 else 3 - self.zpos
            target = self.zpos + 3 - step if way == 0 else self.zpos - 3 + step
            yield way, behind, target, (behind <= step) & (behind < 3)

    def start(self):
        for z in (3, 0, 2, 1):
            self.pair_copy(z).start()

    def pair(self):
        for z in (3, 0, 2, 1):
            self.pair_copy(z).wait_recv()

    def both(self, z):
        return self.term[z * 2 + self.core].astype(jnp.float32) + self.theirs[z].astype(jnp.float32)

    def step(self, step):
        for way, behind, target, there in self.each(step):
            @pl.when(there)
            def _():
                total = self.both(target)

                @pl.when(behind == 0)
                def _():
                    self.theirs[target] = total.astype(self.theirs.dtype)

                @pl.when(behind > 0)
                def _():
                    self.hop_copy(way, target).wait_recv()
                    self.theirs[target] = (total + self.landed[target + 1 - way].astype(jnp.float32)).astype(self.theirs.dtype)
                self.hop_copy(way, target).start()

    def finish(self):
        self.out[...] = self.both(self.zpos)
        for way in range(2):
            @pl.when(self.zpos > 0 if way == 0 else self.zpos < 3)
            def _():
                self.hop_copy(way, self.zpos).wait_recv()
                self.out[...] += self.landed[self.zpos + 1 - way].astype(jnp.float32)
        for step in range(3):
            for way, behind, target, there in self.each(step):
                @pl.when(there)
                def _():
                    self.hop_copy(way, target).wait_send()
        for z in range(4):
            self.pair_copy(z).wait_send()


def kernel_params(cid):
    return pltpu.CompilerParams(collective_id=cid, has_side_effects=True, vmem_limit_bytes=58 * 2**20)


VMEM = pl.BlockSpec(memory_space=pltpu.VMEM)


class PlaneSum:
    def __init__(self, items, bufs, sems):
        self.items = items
        self.landed, self.stage, self.last = bufs
        self.asend, self.arecv, self.bsend, self.brecv = sems
        self.rep, self.zpos, self.core = place()
        self.shard = self.zpos * 2 + self.core

    @staticmethod
    def scratch(shapes, dtype):
        n = len(shapes)
        return ([pltpu.VMEM((2,) + s, dtype) for s in shapes] + [pltpu.VMEM(s, dtype) for s in shapes] * 2
                + [dma_sems(n, 2), dma_sems(n, 2), dma_sems(n), dma_sems(n)])

    @staticmethod
    def split(refs, n):
        return (refs[:n], refs[n : 2 * n], refs[2 * n : 3 * n]), refs[3 * n : 3 * n + 4], refs[3 * n + 4 :]

    def ways(self, i):
        xrep, yrep, drep = plane_places(self.rep)
        return (xrep, yrep, drep) if self.items[i][2] == 0 else (yrep, xrep, drep)

    def out(self, i, k):
        near, _, far = self.ways(i)
        return remote(self.items[i][0](far if k else near), self.landed[i].at[k], self.asend.at[i, k], self.arecv.at[i, k],
                      near, self.shard)

    def on(self, i):
        return remote(self.stage[i], self.last[i], self.bsend.at[i], self.brecv.at[i], self.ways(i)[1], self.shard)

    def start(self, which=None):
        for i in range(len(self.items)) if which is None else which:
            for k in (1, 0):
                self.out(i, k).start()

    def middle(self, i):
        wide = jnp.float32
        self.out(i, 1).wait_recv()
        term = self.items[i][0](self.ways(i)[1])
        self.stage[i][...] = (term[...].astype(wide) + self.landed[i][1].astype(wide)).astype(self.stage[i].dtype)
        self.on(i).start()

    def end(self, i):
        wide = jnp.float32
        self.out(i, 0).wait_recv()
        self.on(i).wait_recv()
        total = self.items[i][0](self.rep)[...].astype(wide) + self.landed[i][0].astype(wide)
        own = self.items[i][1]
        own[...] = (total + self.last[i][...].astype(wide)).astype(own.dtype)

    def finish(self):
        for i in range(len(self.items)):
            for k in range(2):
                self.out(i, k).wait_send()
            self.on(i).wait_send()


class PlaneGather:
    def __init__(self, items, sems):
        self.items = items
        self.send, self.recv, self.own = sems
        self.rep, self.zpos, self.core = place()
        self.shard = self.zpos * 2 + self.core

    @staticmethod
    def scratch(n):
        return [dma_sems(3, n), dma_sems(3, n), dma_sems(n)]

    def copy(self, i, kind, quarter, to):
        own, part, _ = self.items[i]
        dst = part(quarter)
        return remote(dst if kind == 2 or own is None else own, dst, self.send.at[kind, i], self.recv.at[kind, i], to, self.shard)

    def keep(self, i):
        return pltpu.make_async_copy(self.items[i][0], self.items[i][1](self.rep), self.own.at[i])

    def start(self, which=None):
        xrep, yrep, _ = plane_places(self.rep)
        for i in range(len(self.items)) if which is None else which:
            self.copy(i, 0, self.rep, xrep).start()
            self.copy(i, 1, self.rep, yrep).start()
            if self.items[i][0] is not None:
                self.keep(i).start()

    def middle(self, i):
        xrep, yrep, _ = plane_places(self.rep)
        self.copy(i, 0, xrep, xrep).wait_recv()
        if self.items[i][2] == 0:
            self.copy(i, 2, xrep, yrep).start()
        self.copy(i, 1, yrep, yrep).wait_recv()
        if self.items[i][2] == 1:
            self.copy(i, 2, yrep, xrep).start()

    def finish(self):
        xrep, yrep, drep = plane_places(self.rep)
        for i, (own, _, first) in enumerate(self.items):
            self.copy(i, 0, self.rep, xrep).wait_send()
            self.copy(i, 1, self.rep, yrep).wait_send()
            self.copy(i, 2, *((xrep, yrep) if first == 0 else (yrep, xrep))).wait_send()
            self.copy(i, 2, drep, drep).wait_recv()
            if own is not None:
                self.keep(i).wait()


class ColumnSwap:
    def __init__(self, items, sems, keeps=True):
        self.items, self.keeps = items, keeps
        self.send, self.recv, self.own = sems
        self.rep, self.zpos, self.core = place()
        self.shard = self.zpos * 2 + self.core

    near = (1, 2, 6, 3, 7, 4, 5)

    @staticmethod
    def scratch(n):
        return [dma_sems(7, n), dma_sems(7, n), dma_sems(n)]

    def copy(self, i, m, back=False):
        s2 = column_place(self.zpos, self.core, m, back)
        block, there = self.items[i]
        return remote(block(s2), there(s2 if back else self.shard), self.send.at[m - 1, i], self.recv.at[m - 1, i], self.rep, s2)

    def keep(self, i):
        return pltpu.make_async_copy(self.items[i][0](self.shard), self.items[i][1](self.shard), self.own.at[i])

    def start(self):
        for m in self.near:
            for i in range(len(self.items)):
                self.copy(i, m).start()
        for i in range(len(self.items) if self.keeps else 0):
            self.keep(i).start()

    def arrive(self, m):
        for i in range(len(self.items)):
            self.copy(i, m, True).wait_recv()

    def finish(self, arrive=True):
        for i in range(len(self.items)):
            if self.keeps:
                self.keep(i).wait()
            for m in self.near:
                self.copy(i, m).wait_send()
                if arrive:
                    self.copy(i, m, True).wait_recv()


class Strips:
    def __init__(self, own, whole, sems):
        rep, zpos, core = place()
        shard = zpos * 2 + core
        self.swap = ColumnSwap([(lambda s: own.at[s], lambda s: whole.at[s, rep])], sems[:2] + [None], keeps=False)

        def part(m):
            return lambda p: whole.at[shard if m == 0 else column_place(zpos, core, m, True), p]

        self.spread = PlaneGather([(None if m else own.at[shard], part(m), m % 2) for m in range(8)], sems[2:5])

    @staticmethod
    def scratch():
        return [dma_sems(7, 1), dma_sems(7, 1)] + PlaneGather.scratch(8)

    def start(self):
        self.swap.start()
        self.spread.start((0,))

    def arrive(self, *places):
        for m in places:
            self.swap.arrive(m)
            self.spread.start((m,))

    def onward(self, *places):
        for m in places:
            self.spread.middle(m)

    def finish(self):
        self.swap.finish(arrive=False)
        self.spread.finish()


def quarter_cols(ref, first, rows, p):
    width = ref.shape[1] // 4
    return ref.at[pl.ds(first, rows), pl.ds(mult(p * width, 128), width)]


def back_kernel(shift_unit, *refs):
    down, tokens, grad_gate, grad_up, gate_w, up_w, out, down_own, gate_own, up = refs[:10]
    term, gate, strips, strip_sems = refs[10:14]
    rep, zpos, core = place()
    total, rest = Total.split(term, out, refs[14:])
    bufs, sems, _ = PlaneSum.split(rest, 4)
    half = down_own.shape[0] // 2
    shift = mult((zpos * 2 + core) % 4 * shift_unit, 16)
    wide = jnp.float32

    def down_item(h):
        return (lambda p: quarter_cols(down, mult(shift + h * half, 16), half, p), down_own.at[pl.ds(h * half, half)], h)

    def gate_item(h):
        return (lambda p: gate.at[pl.ds(4 * h, 4), p], gate_own.at[pl.ds(4 * h, 4)], h)

    sums = PlaneSum([down_item(0), down_item(1), gate_item(0), gate_item(1)], bufs, sems)
    chunk = strips.shape[2]
    chunks = gate_w.shape[0] // chunk

    def strip(i, which):
        return pltpu.make_async_copy(
            (gate_w, up_w)[which].at[pl.ds(mult(i * chunk, 128), chunk)], strips.at[i % 2, which], strip_sems.at[i % 2, which])

    for which in range(2):
        strip(0, which).start()
    greet(rep, zpos, core, plane=2)
    sums.start((0, 1))

    def back(i, carry):
        for which in range(2):
            strip(i, which).wait()

        @pl.when(i < chunks - 1)
        def _():
            for which in range(2):
                strip(i + 1, which).start()

        part = dot_nt(grad_gate[...], strips[i % 2, 0]) + dot_nt(grad_up[...], strips[i % 2, 1])
        term[:, :, pl.ds(mult(i * chunk, 128), chunk)] = part.astype(term.dtype).reshape(8, -1, chunk)
        return carry

    lax.fori_loop(0, chunks, back, 0)
    total.start()
    wide_rows = tokens.shape[1] // 4

    def weight(grad, to, i):
        got = dot_tn(tokens[:, pl.ds(mult(i * wide_rows, 128), wide_rows)], grad[...])
        to[pl.ds(2 * i, 2)] = got.astype(to.dtype).reshape((2,) + to.shape[1:])

    def gate_step(i, carry):
        weight(grad_gate, gate, i)

        @pl.when(i == 2)
        def _():
            total.pair()
            total.step(0)
        return carry

    lax.fori_loop(0, 4, gate_step, 0)
    sums.start((2, 3))

    def up_step(i, carry):
        weight(grad_up, up, i)

        @pl.when(i == 1)
        def _():
            sums.middle(0)
            sums.middle(1)
            total.step(1)
        return carry

    lax.fori_loop(0, 4, up_step, 0)
    sums.end(0)
    sums.end(1)
    total.step(2)
    sums.middle(2)
    sums.middle(3)
    total.finish()
    sums.end(2)
    sums.end(3)
    sums.finish()


def back_sums(cid, down, tokens, grad_gate, grad_up, gate_w, up_w, rows):
    width = down.shape[1] // 4
    kind = down.dtype
    strip = gate_w.shape[1]
    parts = (8, 4, gate_w.shape[0] // 32, strip)
    term = jax.ShapeDtypeStruct((8, tokens.shape[0] // 8, tokens.shape[1]), kind)
    return pl.pallas_call(
        functools.partial(back_kernel, rows % 128),
        out_shape=[jax.ShapeDtypeStruct(term.shape[1:], jnp.float32), jax.ShapeDtypeStruct((rows, width), kind),
                   jax.ShapeDtypeStruct((8,) + parts[2:], kind), jax.ShapeDtypeStruct(parts, kind)],
        in_specs=[VMEM] * 4 + [ANY] * 2, out_specs=[VMEM] * 4,
        scratch_shapes=[pltpu.VMEM(term.shape, kind), pltpu.VMEM(parts, kind),
                        pltpu.VMEM((2, 2, gate_w.shape[0] // 5, strip), kind), dma_sems(2, 2)]
        + Total.scratch(term) + PlaneSum.scratch([(rows // 2, width)] * 2 + [(4,) + parts[2:]] * 2, kind),
        compiler_params=kernel_params(cid),
    )(down, tokens, grad_gate, grad_up, gate_w, up_w)


def middle_kernel(scale, *refs):
    gate, refs = refs[0], refs[1:]
    branch, cols, down, up, attn_out, w_query_up, w_latent_up, query_low, latent_low = refs[:9]
    query, kv, rope, bias, turns, logs = refs[9:15]
    w_query, w_latent, tokens, query_lat, latent_proj, gains, grad_residual, gain_ffn = refs[15:23]
    branch_all, cols_all, down_all, gate_all, up_own, query_up, latent_up, tokens_grad, lats, gain_terms = refs[23:33]
    scratch = list(refs[33:])
    (left, mixed, packed, grad_query, grad_kv, grad_rope, strips, query_strips, latent_strips, strip_sems, grad_low,
     grad_latent, grad_normed, latent_send, rope_send, latent_land, rope_land, lsend, lrecv, query_rows, latent_rows,
     row_sems) = scratch[:22]
    scratch = scratch[22:]
    rep, zpos, core = place()
    shard = zpos * 2 + core
    gather = Gather((branch,), (branch_all,), scratch[:5])
    swap = ColumnSwap([(lambda s: cols.at[s], lambda s: cols_all.at[s])], scratch[5:8])
    half = down.shape[0] // 2
    downs = PlaneGather(
        [(down.at[pl.ds(h * half, half)], functools.partial(quarter_cols, down_all, h * half, half), h) for h in range(2)],
        scratch[8:11])
    strips_out = Strips(gate, gate_all, scratch[11:16])
    bufs, sems, _ = PlaneSum.split(scratch[16:], 2)
    sums = PlaneSum([(lambda p, h=h: up.at[pl.ds(4 * h, 4), p], up_own.at[pl.ds(4 * h, 4)], h) for h in range(2)], bufs, sems)
    rows = tokens.shape[0]
    out_rows = attn_out.shape[0] // 4
    quarter_width = kv.shape[1] // 4
    wide, low = jnp.float32, jnp.bfloat16

    def strip(i, k):
        at = pl.ds(mult(i * quarter_width, 128), quarter_width)
        src = (attn_out.at[pl.ds(mult(i * out_rows, 128), out_rows)], w_query_up.at[:, at], w_latent_up.at[:, at])[k]
        return pltpu.make_async_copy(src, (strips, query_strips, latent_strips)[k].at[i % 2], strip_sems.at[i % 2, k])

    def share(k, what):
        for i, (src, dst) in enumerate(((latent_send, latent_land), (rope_send, rope_land))):
            getattr(remote(src.at[pl.ds((k + 1) * rows, rows)], dst.at[k], lsend.at[k, i], lrecv.at[k, i],
                           plane_places(rep)[k], shard), what)()

    for k in range(3):
        strip(0, k).start()
    greet(rep, zpos, core, plane=3, column=True)
    strips_out.start()
    sums.start()
    downs.start()
    left[...] = jnp.zeros_like(left)
    grad_rope[...] = jnp.zeros_like(grad_rope)
    grad_low[...] = jnp.zeros_like(grad_low)
    grad_latent[...] = jnp.zeros_like(grad_latent)
    quarter = attend_back_heads(
        scale, query, kv, rope, bias, turns, logs, mixed, grad_query, packed, grad_kv, grad_rope, left)

    def after_first():
        gather.start()
        swap.start()
        strips_out.arrive(1, 2, 6)

    def after_second():
        strips_out.arrive(3, 7, 4, 5)
        sums.middle(0)
        sums.middle(1)

    def after_third():
        gather.hop(1)
        downs.middle(0)
        downs.middle(1)
        strips_out.onward(0, 1, 2)

    def after_fourth():
        gather.hop(2)
        strips_out.onward(6, 3)

    def step(i, carry):
        for k in range(3):
            strip(i, k).wait()

        @pl.when(i < 3)
        def _():
            for k in range(3):
                strip(i + 1, k).start()

        mixed[:, pl.ds(mult(i * out_rows, 128), out_rows)] = dot_nt(branch[...], strips[i % 2]).astype(mixed.dtype)
        quarter(i, carry)
        at = pl.ds(mult(i * quarter_width, 128), quarter_width)
        grad_low[...] += dot_nt(grad_query[:, at], query_strips[i % 2])
        grad_latent[...] += dot_nt(grad_kv[:, at], latent_strips[i % 2])
        for k, service in enumerate((after_first, after_second, after_third, after_fourth)):
            pl.when(i == k)(service)
        return carry

    lax.fori_loop(0, 4, step, 0)
    latent_send[...] = grad_latent[...].astype(low)
    rope_send[...] = grad_rope[...].astype(low)
    for k in range(3):
        share(k, "start")

    def terms(i, carry):
        at = pl.ds(mult(i * 1024, 128), 1024)
        query_up[:, at] = dot_tn(query_low[...], packed[:, at]).astype(query_up.dtype)
        at = pl.ds(mult(i * quarter_width, 128), quarter_width)
        latent_up[:, at] = dot_tn(latent_low[...], grad_kv[:, at]).astype(latent_up.dtype)
        return carry

    lax.fori_loop(0, 4, terms, 0)
    strips_out.onward(7, 4, 5)
    sums.end(0)
    sums.end(1)

    def tile(t):
        return slice(128 * t, 128 * t + 128)

    def norm_back(src, grad, tiles, first, put):
        square = sum(jnp.sum(jnp.square(src(t)), axis=1, keepdims=True) for t in range(tiles))
        factor = lax.rsqrt(square / (128 * tiles) + epsilon)
        along = jnp.zeros_like(factor)
        for t in range(tiles):
            unit = src(t) * factor
            weighed = grad(t) * unit
            gain_terms[first + t : first + t + 1, :] = jnp.sum(weighed, axis=0, keepdims=True)
            along = along + jnp.sum(weighed * gains[first + t : first + t + 1, :], axis=1, keepdims=True)
        along = along / (128 * tiles)
        for t in range(tiles):
            put(t, factor * (grad(t) * gains[first + t : first + t + 1, :] - src(t) * factor * along))

    def put_query(t, value):
        lats[:, tile(t)] = value.astype(low)

    def put_latent(t, value):
        lats[:, tile(6 + t)] = value.astype(low)

    def put_tokens(t, value):
        tokens_grad[:, tile(t)] = (grad_residual[:, tile(t)] + value).astype(low)

    norm_back(lambda t: query_lat[:, tile(t)], lambda t: grad_low[:, tile(t)], 6, 40, put_query)
    own = grad_latent[0:rows].astype(low).astype(wide)
    own_rope = grad_rope[0:rows].astype(low).astype(wide)
    for k in range(3):
        share(k, "wait_recv")
        own = own + latent_land[k].astype(wide)
        own_rope = own_rope + rope_land[k].astype(wide)
    grad_latent[0:rows] = own
    norm_back(lambda t: latent_proj[:, tile(t)], lambda t: grad_latent[0:rows, tile(t)], 2, 46, put_latent)
    turned = turn(own_rope, (turns[0], turns[1], turns[2]), True)
    lats[:, 1024:1056] = turned[:, 64:96].astype(low)
    chunk = query_rows.shape[1]
    chunks = w_query.shape[0] // chunk

    def row_copy(i, k):
        at = pl.ds(mult(i * chunk, chunk), chunk)
        return pltpu.make_async_copy((w_query, w_latent)[k].at[at], (query_rows, latent_rows)[k].at[i % 2], row_sems.at[i % 2, k])

    def normed_step(i, carry):
        for k in range(2):
            row_copy(i, k).wait()

        @pl.when(i < chunks - 1)
        def _():
            for k in range(2):
                row_copy(i + 1, k).start()

        grad_normed[:, pl.ds(mult(i * chunk, chunk), chunk)] = (
            dot_nt(lats[:, :768], query_rows[i % 2]) + dot_nt(lats[:, 768:1056], latent_rows[i % 2]))
        return carry

    for k in range(2):
        row_copy(0, k).start()
    lax.fori_loop(0, chunks, normed_step, 0)
    norm_back(lambda t: tokens[:, tile(t)].astype(wide), lambda t: grad_normed[:, tile(t)], 20, 0, put_tokens)
    gain_terms[20:40, :] = gain_ffn[...]
    gather.hop(3)
    for k in range(3):
        share(k, "wait_send")
    gather.finish()
    swap.finish()
    downs.finish()
    sums.finish()
    strips_out.finish()


def middle_exchange(cid, scale, gate, branch, cols, down, up, weights, query_low, latent_low, attend_in, norm_in):
    kind = branch.dtype
    wide = jnp.float32
    query, kv, rope = attend_in[:3]
    rows, width = branch.shape
    attn_out, w_query_up, w_latent_up, w_query, w_latent = weights
    keys, latent_rank = latent_low.shape
    query_rank = query_low.shape[1]
    quarter = kv.shape[1] // 4
    gains = norm_in[3]
    return pl.pallas_call(
        functools.partial(middle_kernel, scale),
        out_shape=[jax.ShapeDtypeStruct((8 * rows, width), kind), jax.ShapeDtypeStruct(cols.shape, kind),
                   jax.ShapeDtypeStruct((down.shape[0], 4 * down.shape[1]), kind),
                   jax.ShapeDtypeStruct((8, 4) + gate.shape[1:], kind), jax.ShapeDtypeStruct((8,) + up.shape[2:], kind),
                   jax.ShapeDtypeStruct((query_rank, 4096), kind), jax.ShapeDtypeStruct((latent_rank, kv.shape[1]), kind),
                   jax.ShapeDtypeStruct((rows, width), kind),
                   jax.ShapeDtypeStruct((rows, query_rank + w_latent.shape[1]), kind), jax.ShapeDtypeStruct(gains.shape, wide)],
        in_specs=[ANY, VMEM] + [ANY] * 2 + [VMEM] + [ANY] * 3 + [VMEM] * 8 + [ANY] * 2 + [VMEM] * 6,
        out_specs=[ANY] * 4 + [VMEM] * 6,
        scratch_shapes=[pltpu.VMEM((2 * rows, 256), kind), pltpu.VMEM(branch.shape, kind), pltpu.VMEM((rows, 4096), kind),
                        pltpu.VMEM(query.shape, kind), pltpu.VMEM(kv.shape, kind), pltpu.VMEM(rope.shape, wide),
                        pltpu.VMEM((2, attn_out.shape[0] // 4, width), kind), pltpu.VMEM((2, query_rank, quarter), kind),
                        pltpu.VMEM((2, latent_rank, quarter), kind), dma_sems(2, 3),
                        pltpu.VMEM((rows, query_rank), wide), pltpu.VMEM((keys, latent_rank), wide), pltpu.VMEM((rows, width), wide),
                        pltpu.VMEM((keys, latent_rank), kind), pltpu.VMEM((keys, 128), kind),
                        pltpu.VMEM((3, rows, latent_rank), kind), pltpu.VMEM((3, rows, 128), kind), dma_sems(3, 2), dma_sems(3, 2),
                        pltpu.VMEM((2, width // 5, query_rank), kind), pltpu.VMEM((2, width // 5, w_latent.shape[1]), kind), dma_sems(2, 2)]
        + Gather.scratch(1) + ColumnSwap.scratch(1) + PlaneGather.scratch(2) + Strips.scratch()
        + PlaneSum.scratch([(4,) + up.shape[2:]] * 2, kind),
        compiler_params=kernel_params(cid),
    )(gate, branch, cols, down, up, attn_out, w_query_up, w_latent_up, query_low, latent_low, *attend_in, w_query, w_latent, *norm_in)


def last_kernel(*refs):
    up, lat, query_up, latent_up, hidden, down, attn_out, cols, gain = refs[:9]
    up_all, out, attn_sum, lat_sum, latent_sum, query_sum, gain_out = refs[9:16]
    scratch = list(refs[16:])
    rep, zpos, core = place()
    shard = zpos * 2 + core
    places = plane_places(rep)

    def take(n):
        nonlocal scratch
        got, scratch = scratch[:n], scratch[n:]
        return got

    strips_out = Strips(up, up_all, take(5))
    spread_sems = take(3)
    lat_all, out_term, lat_term, query_part, latent_own, query_own = take(6)
    gather = Gather((lat,), (lat_all,), take(5))
    owns = take(5)
    gain_landed, gain_sum, gain_plane, gsend, grecv, hsend, hrecv = take(7)
    total, scratch = Total.split(out_term, out, scratch)
    query_total, scratch = Total.split(query_part, query_own, scratch)
    latent_total, scratch = Total.split(latent_up, latent_own, scratch)
    bufs, sems, _ = PlaneSum.split(scratch, 6)
    width = query_up.shape[2] // 4
    half = attn_out.shape[0] // 2

    def query_item(h):
        return (lambda p: query_up.at[pl.ds(4 * h, 4), :, pl.ds(mult(p * width, 128), width)], query_part.at[pl.ds(4 * h, 4)], h)

    latent_low = scratch[-1]
    sums = PlaneSum(
        [query_item(0), query_item(1)]
        + [(functools.partial(quarter_cols, attn_out, h * half, half), owns[h], h) for h in range(2)]
        + [(lambda p: lat_term.at[p], owns[2], 0),
           (functools.partial(quarter_cols, latent_low, 0, latent_low.shape[0]), owns[3], 1)],
        bufs, sems)
    spread = PlaneGather(
        [(owns[h], functools.partial(quarter_cols, attn_sum, h * half, half), h) for h in range(2)]
        + [(owns[2], lambda p: lat_sum.at[p], 0),
           (owns[3], functools.partial(quarter_cols, latent_sum, 0, latent_low.shape[0]), 1),
           (owns[4], functools.partial(quarter_cols, query_sum, 0, query_up.shape[1]), 0)], spread_sems)

    def gain_copy(m):
        s2 = column_place(zpos, core, m)
        return remote(gain, gain_landed.at[m - 1], gsend.at[m - 1], grecv.at[m - 1], rep, s2)

    def gain_on(k):
        return remote(gain_sum, gain_plane.at[k], hsend.at[k], hrecv.at[k], places[k], shard)

    greet(rep, zpos, core, plane=3, column=True)
    for m in range(1, 8):
        gain_copy(m).start()
    strips_out.start()
    sums.start((0, 1))
    latent_total.start()
    gather.start()
    sums.start((2, 3))
    rows = lat.shape[0]

    def term(i, carry):
        out_term[i] = jnp.dot(hidden[pl.ds(mult(i * rows, rows), rows)], down[...],
                              preferred_element_type=jnp.float32).astype(out_term.dtype)
        return carry

    arrive, onward = strips_out.arrive, strips_out.onward
    lax.fori_loop(0, 3, term, 0)
    arrive(1)
    latent_total.pair()
    latent_total.step(0)
    lax.fori_loop(3, 6, term, 0)
    onward(0)
    gather.hop(1)
    arrive(2)
    arrive(6)
    lax.fori_loop(6, 8, term, 0)
    latent_total.step(1)
    gain_sum[...] = gain[...]
    for m in range(1, 8):
        gain_copy(m).wait_recv()
        gain_sum[...] += gain_landed[m - 1]
    for k in range(3):
        gain_on(k).start()
    total.start()
    onward(1)
    arrive(3)
    arrive(7)
    gather.hop(2)
    sums.middle(0)
    sums.middle(1)
    latent_total.step(2)
    onward(2, 6)
    arrive(4)
    arrive(5)
    gather.hop(3)
    total.pair()
    total.step(0)
    sums.middle(2)
    sums.middle(3)
    latent_total.finish()
    latent_low[...] = latent_own[...].astype(latent_low.dtype)
    sums.start((5,))
    sums.end(0)
    sums.end(1)
    query_total.start()
    gather.finish()
    lat_term[...] = dot_tn(cols[...], lat_all[...]).astype(lat_term.dtype).reshape(lat_term.shape)
    sums.start((4,))
    query_total.pair()
    query_total.step(0)
    onward(3, 7)
    total.step(1)
    sums.end(2)
    sums.end(3)
    spread.start((0, 1))
    query_total.step(1)
    onward(4, 5)
    sums.middle(5)
    sums.middle(4)
    query_total.step(2)
    total.step(2)
    query_total.finish()
    owns[4][...] = query_own[...].astype(owns[4].dtype)
    spread.start((4,))
    sums.end(5)
    spread.start((3,))
    sums.end(4)
    spread.start((2,))
    for i in (0, 1, 4, 3, 2):
        spread.middle(i)
    gain_out[...] = gain_sum[...]
    for k in range(3):
        gain_on(k).wait_recv()
        gain_out[...] += gain_plane[k]
    total.finish()
    for k in range(3):
        gain_on(k).wait_send()
    for m in range(1, 8):
        gain_copy(m).wait_send()
    strips_out.finish()
    sums.finish()
    spread.finish()


def last_sums(cid, up, lat, query_up, latent_up, hidden, down, attn_out, cols, gain):
    kind = up.dtype
    wide = jnp.float32
    rows = lat.shape[0]
    lat_shape = (4, cols.shape[1] // 4, lat.shape[1])
    query_shape = (query_up.shape[1], query_up.shape[2] // 4)
    shapes = [(attn_out.shape[0] // 2, attn_out.shape[1] // 4)] * 2 + [
        lat_shape[1:], (latent_up.shape[1], latent_up.shape[2] // 4)]
    out_term = jax.ShapeDtypeStruct((8, rows, down.shape[1]), kind)
    query_part = jax.ShapeDtypeStruct((8,) + query_shape, kind)
    return pl.pallas_call(
        last_kernel,
        out_shape=[jax.ShapeDtypeStruct((8, 4) + up.shape[1:], kind)]
        + [jax.ShapeDtypeStruct(out_term.shape[1:], wide)]
        + [jax.ShapeDtypeStruct(s, kind) for s in (attn_out.shape, lat_shape, latent_up.shape[1:])]
        + [jax.ShapeDtypeStruct((query_up.shape[1], query_up.shape[2]), kind), jax.ShapeDtypeStruct(gain.shape, gain.dtype)],
        in_specs=[ANY] * 2 + [VMEM] * 7, out_specs=[ANY, VMEM] + [ANY] * 4 + [VMEM],
        scratch_shapes=Strips.scratch() + PlaneGather.scratch(5)
        + [pltpu.VMEM((8 * rows, lat.shape[1]), kind), pltpu.VMEM(out_term.shape, kind), pltpu.VMEM(lat_shape, kind),
           pltpu.VMEM(query_part.shape, kind), pltpu.VMEM(latent_up.shape[1:], wide), pltpu.VMEM(query_shape, wide)]
        + Gather.scratch(1) + [pltpu.VMEM(s, kind) for s in shapes + [query_shape]]
        + [pltpu.VMEM((7,) + gain.shape, wide), pltpu.VMEM(gain.shape, wide), pltpu.VMEM((3,) + gain.shape, wide)]
        + [dma_sems(7)] * 2 + [dma_sems(3)] * 2
        + Total.scratch(out_term) + Total.scratch(query_part) + Total.scratch(latent_up)
        + PlaneSum.scratch([(4,) + query_shape] * 2 + shapes, kind) + [pltpu.VMEM(latent_up.shape[1:], kind)],
        compiler_params=kernel_params(cid),
    )(up, lat, query_up, latent_up, hidden, down, attn_out, cols, gain)


def start_kernel(scale, *refs):
    ins, (gate, up), (tokens, bias, turns, down) = refs[:7], refs[7:9], refs[9:13]
    outs, cols, refs = refs[13:20], refs[20:22], refs[22:]
    (normed, query_low, latent, rope, kv, query, mixed, logs, query_lat, latent_proj, residual, ffn_all,
     grad_hidden) = refs[:13]
    refs = refs[13:]
    (zsend, zrecv, xsend, xrecv, ysend, yrecv, dsend, drecv, csend, crecv, own, gsend, grecv, psend, precv) = refs[:15]
    held, strips = refs[15:22], refs[22:24]
    (small, gains, w_query, w_latent, w_query_up, w_latent_up, w_out, proj, ffn, lsend, lrecv, load_sems,
     grad_sems) = refs[24:37]
    gather = Gather((ffn,), (ffn_all,), refs[37:])
    rep, zpos, core = place()
    xrep, yrep, drep = plane_places(rep)
    shard = zpos * 2 + core

    def whole(a, z, c):
        rows = ins[a].shape[0]
        return outs[a].at[pl.ds(mult((z * 2 + c) * rows, rows), rows)]

    def pieces(a, z, c, quarter, act, own_ref=False):
        def part(b, first, rows):
            full = ins[b].shape[0]
            if own_ref:
                return ins[b].at[pl.ds(mult(first, 16), rows)]
            return outs[b].at[pl.ds(mult((z * 2 + c) * full + first, 16), rows)]

        if a < 3:
            rows = ins[a].shape[0] // 4
            act(part(a, quarter * rows, rows))
        elif a == 3:
            @pl.when(quarter < 3)
            def _():
                act(part(3, jnp.minimum(quarter, 2) * 32, 32))

            @pl.when(quarter == 3)
            def _():
                act(part(4, 0, 32))
        else:
            act(ins[a + 1] if own_ref else whole(a + 1, z, c))

    copy = remote

    def hop(a, way, h, z, what):
        def act(ref):
            c = copy(ref, ref, zsend.at[way, h, a], zrecv.at[way, h, a], rep, (zpos + 1 - 2 * way) * 2 + core)
            getattr(c, what)()
        pieces(a, z, core, rep, act)

    def to_plane(a, k, z, quarter, what, sems, r):
        def act(ref):
            getattr(copy(ref, ref, sems[0].at[k, a], sems[1].at[k, a], r, shard), what)()
        pieces(a, z, core, quarter, act)

    def to_core(a, slot, z, c, what, src=None):
        ref = whole(a, z, c)
        getattr(copy(ref if src is None else src, ref, csend.at[slot, a], crecv.at[slot, a], rep, zpos * 2 + 1 - core), what)()

    greet(rep, zpos, core, plane=3, column=True)
    def send_own(a):
        def first(way):
            def go(src):
                def act(ref):
                    copy(src, ref, zsend.at[way, 0, a], zrecv.at[way, 0, a], rep, (zpos + 1 - 2 * way) * 2 + core).start()
                return act
            return go
        for way in range(2):
            @pl.when(zpos < 3 if way == 0 else zpos > 0)
            def _():
                if a < 3:
                    rows = ins[a].shape[0] // 4
                    src = ins[a].at[pl.ds(mult(rep * rows, 16), rows)]
                    pieces(a, zpos, core, rep, first(way)(src))
                elif a == 3:
                    @pl.when(rep < 3)
                    def _():
                        start = mult(jnp.minimum(rep, 2) * 32, 16)
                        src = ins[3].at[pl.ds(start, 32)]
                        dst = outs[3].at[pl.ds(mult(shard * 96 + start, 16), 32)]
                        first(way)(src)(dst)

                    @pl.when(rep == 3)
                    def _():
                        first(way)(ins[4])(whole(4, zpos, core))
                else:
                    first(way)(ins[a + 1])(whole(a + 1, zpos, core))

    def keep(a, half):
        if half == 0:
            return pltpu.make_async_copy(ins[a], held[a], own.at[0, a])
        return pltpu.make_async_copy(held[a], whole(a, zpos, core), own.at[1, a])

    for a in (5, 1, 2, 3, 0):
        send_own(a)

    strip = cols[0].shape[1]
    quarter_rows = gate.shape[0] // 4

    def slice_of(which, s, first, rows):
        start = mult((s * 25 // 4) * 128, 128)
        return (gate, up)[which].at[pl.ds(mult(first, 16), rows), pl.ds(start, strip)]

    def rows_of(which, s, quarter):
        return cols[which].at[pl.ds(mult(s * gate.shape[0] + quarter * quarter_rows, 16), quarter_rows)]

    def slice_copy(m, which):
        s2 = column_place(zpos, core, m)
        return remote(slice_of(which, s2, rep * quarter_rows, quarter_rows), rows_of(which, shard, rep),
                      gsend.at[m - 1, which], grecv.at[m - 1, which], rep, s2)

    def slice_plane(m, which, quarter, kind, r):
        ref = rows_of(which, column_place(zpos, core, m, back=True), quarter)
        return remote(ref, ref, psend.at[kind, m - 1, which], precv.at[kind, m - 1, which], r, shard)

    def own_slice(which, half):
        if half == 0:
            return pltpu.make_async_copy(slice_of(which, shard, 0, gate.shape[0]), strips[which], own.at[0, 7 + which])
        rows = gate.shape[0]
        return pltpu.make_async_copy(strips[which], cols[which].at[pl.ds(mult(shard * rows, rows), rows)], own.at[1, 7 + which])

    near = (1, 2, 6, 3, 7, 4, 5)
    for a in range(7):
        to_core(a, 0, zpos, core, "start", src=ins[a])
        keep(a, 0).start()
    for which in range(2):
        own_slice(which, 0).start()
    for a in range(7):
        keep(a, 0).wait()
        keep(a, 1).start()
    for which in range(2):
        own_slice(which, 0).wait()
        own_slice(which, 1).start()

    def slices_from_column(m):
        for which in range(2):
            s2 = column_place(zpos, core, m, back=True)
            ref = rows_of(which, s2, rep)
            remote(ref, ref, gsend.at[m - 1, which], grecv.at[m - 1, which], rep, s2).wait_recv()
        slices_to_plane(m, 0)

    def slices_to_plane(m, which):
        slice_plane(m, which, rep, 0, xrep).start()
        slice_plane(m, which, rep, 1, yrep).start()

    def slices_from_plane(m, which=0):
        slice_plane(m, which, xrep, 0, xrep).wait_recv()
        slice_plane(m, which, yrep, 1, yrep).wait_recv()
        slice_plane(m, which, *onward(m)).start()

    def onward(m):
        return (yrep, 2, xrep) if m % 2 else (xrep, 2, yrep)

    def from_column(h, way, z, slots):
        for a in slots:
            hop(a, way, h - 1, z, "wait_recv")
            if h < 3:
                @pl.when(zpos < 3 if way == 0 else zpos > 0)
                def _():
                    hop(a, way, h, z, "start")
            if a < 4:
                to_plane(a, way * 3 + h - 1, z, rep, "start", (xsend, xrecv), xrep)
                to_plane(a, way * 3 + h - 1, z, rep, "start", (ysend, yrecv), yrep)
            else:
                to_core(a + 1, way * 3 + h, z, core, "start")

    def from_plane(h, way, z, slots):
        k = way * 3 + h - 1
        for a in slots:
            to_plane(a, k, z, xrep, "wait_recv", (xsend, xrecv), xrep)
            if a == 0:
                to_plane(a, k, z, xrep, "start", (dsend, drecv), yrep)
            to_plane(a, k, z, yrep, "wait_recv", (ysend, yrecv), yrep)
            if a > 0:
                to_plane(a, k, z, yrep, "start", (dsend, drecv), xrep)

    def from_corner(h, way, z, slots):
        k = way * 3 + h - 1
        for a in slots:
            to_plane(a, k, z, drep, "wait_recv", (dsend, drecv), drep)
            for b in (a,) if a < 3 else (3, 4):
                to_core(b, k + 1, z, core, "start")

    def by_hop(stage, h, *more):
        for way in range(2):
            z = zpos - h if way == 0 else zpos + h

            @pl.when(z >= 0 if way == 0 else z <= 3)
            def _():
                stage(h, way, z, *more)

    def arrived(arrays):
        for b in arrays:
            keep(b, 1).wait()
            to_core(b, 0, zpos, 1 - core, "wait_recv")

            def theirs(h, way, z):
                to_core(b, way * 3 + h, z, 1 - core, "wait_recv")

            for h in range(1, 4):
                by_hop(theirs, h)

    wide, low = jnp.float32, jnp.bfloat16

    def tile(t):
        return slice(128 * t, 128 * t + 128)

    def normalize(src, dst, tiles, first):
        square = sum(jnp.sum(jnp.square(src(t)), axis=1, keepdims=True) for t in range(tiles))
        factor = lax.rsqrt(square / (128 * tiles) + epsilon)
        for t in range(tiles):
            dst[:, tile(t)] = (src(t) * factor * gains[first + t : first + t + 1, :]).astype(low)

    def load(b, to, i):
        return pltpu.make_async_copy(outs[b], to, load_sems.at[i])

    def share(k, what):
        rows = tokens.shape[0]
        for i, ref in enumerate((latent, rope)):
            copy_ = remote(ref.at[pl.ds(0, rows)], ref.at[pl.ds((k + 1) * rows, rows)], lsend.at[k, i], lrecv.at[k, i],
                           plane_places(rep)[k], shard)
            getattr(copy_, what)()

    def down_products():
        arrived((1, 2))
        load(1, w_query, 1).start()
        load(2, w_latent, 2).start()
        load(2, w_latent, 2).wait()
        latent_proj[...] = jnp.dot(normed[...], w_latent[...], preferred_element_type=wide)
        normalize(lambda t: latent_proj[:, tile(t)], latent.at[pl.ds(0, tokens.shape[0])], 2, 46)
        edge = jnp.zeros((tokens.shape[0], 64), wide)
        key = jnp.concatenate([edge, latent_proj[:, 256:288], edge[:, :32]], axis=1)
        rope[0 : tokens.shape[0]] = turn(key, (turns[0], turns[1], turns[2])).astype(low)
        for k in range(3):
            share(k, "start")
        load(1, w_query, 1).wait()
        query_lat[...] = jnp.dot(normed[...], w_query[...], preferred_element_type=wide)
        normalize(lambda t: query_lat[:, tile(t)], query_low, 6, 40)

    def chunk_loop(count, body):
        lax.fori_loop(0, count, lambda i, c: (body(i), c)[1], 0)

    def query_chunk(i):
        at = pl.ds(mult(i * 1024, 128), 1024)
        proj[:, at] = jnp.dot(query_low[...], w_query_up[:, at], preferred_element_type=wide)

    def key_chunk(i):
        at = pl.ds(mult(i * 1024, 128), 1024)
        kv[:, at] = jnp.dot(latent[...], w_latent_up[:, at], preferred_element_type=wide).astype(low)

    out_rows = w_out.shape[1]

    def out_strip(i):
        return pltpu.make_async_copy(outs[0].at[pl.ds(mult(i * out_rows, 128), out_rows)], w_out.at[i % 2], load_sems.at[4 + i % 2])

    by_hop(from_column, 1, (5, 1, 2))
    by_hop(from_column, 1, (3, 0))
    by_hop(from_column, 2, (5, 1, 2))
    by_hop(from_plane, 1, (1, 2))
    by_hop(from_column, 2, (3, 0))
    by_hop(from_plane, 1, (3, 0))
    by_hop(from_column, 3, (5, 1, 2))
    by_hop(from_plane, 2, (1, 2))
    by_hop(from_corner, 1, (1, 2))
    by_hop(from_column, 3, (3, 0))
    for m in near:
        for which in range(2):
            slice_copy(m, which).start()
    by_hop(from_plane, 3, (1, 2))
    by_hop(from_corner, 2, (1, 2))
    by_hop(from_plane, 2, (3, 0))
    arrived((6,))
    load(6, small, 0).start()
    load(6, small, 0).wait()
    gains[...] = sum(small[48 * s : 48 * s + 48, :] for s in range(8))
    normalize(lambda t: tokens[:, tile(t)].astype(wide), normed, 20, 0)
    by_hop(from_corner, 3, (1, 2))
    by_hop(from_corner, 1, (3, 0))
    down_products()
    by_hop(from_plane, 3, (3, 0))
    by_hop(from_corner, 2, (3, 0))
    for m in near[:3]:
        slices_from_column(m)
    send_own(4)
    by_hop(from_corner, 3, (3, 0))
    arrived((3, 4))
    load(3, w_query_up, 3).start()
    load(4, w_latent_up, 0).start()
    for m in near[3:]:
        slices_from_column(m)
    load(3, w_query_up, 3).wait()
    chunk_loop(5, query_chunk)
    for m in near[:3]:
        slices_from_plane(m)
    for k in range(3):
        share(k, "wait_recv")
    load(4, w_latent_up, 0).wait()
    chunk_loop(5, key_chunk)
    logs[...] = jnp.zeros_like(logs)
    group = attend_heads(scale, proj, kv, rope, bias, turns, query, mixed, logs)

    def attend_step(i, carry):
        group(i, carry)

        @pl.when(i == 3)
        def _():
            by_hop(from_column, 1, (4,))

        @pl.when(i == 8)
        def _():
            by_hop(from_column, 2, (4,))
        return carry

    lax.fori_loop(0, kv.shape[1] // 512, attend_step, 0)
    arrived((0,))
    out_strip(0).start()
    residual[...] = tokens[...].astype(wide)

    def out_step(i, carry):
        out_strip(i).wait()

        @pl.when(i < 3)
        def _():
            out_strip(i + 1).start()

        residual[...] += residual_scale * jnp.dot(
            mixed[:, pl.ds(mult(i * out_rows, 128), out_rows)], w_out[i % 2], preferred_element_type=wide)
        return carry

    lax.fori_loop(0, 4, out_step, 0)
    normalize(lambda t: residual[:, tile(t)], ffn, 20, 20)
    gather.start()
    for m in near:
        slices_to_plane(m, 1)
    by_hop(from_column, 3, (4,))
    for m in near[3:]:
        slices_from_plane(m)
    gather.hop(1)
    arrived((5,))
    chunk = 2 * tokens.shape[0]

    def grad_chunk(i):
        return pltpu.make_async_copy(
            outs[5].at[pl.ds(mult(i * chunk, chunk), chunk)], w_out.at[i % 2, pl.ds(0, chunk)], grad_sems.at[i % 2])

    def hidden_step(i, carry):
        grad_chunk(i).wait()

        @pl.when(i < 3)
        def _():
            grad_chunk(i + 1).start()

        grad_hidden[pl.ds(mult(i * chunk, chunk), chunk)] = dot_nt(w_out[i % 2, :chunk], down[...])

        @pl.when(i == 2)
        def _():
            gather.hop(2)
        return carry

    grad_chunk(0).start()
    lax.fori_loop(0, 4, hidden_step, 0)
    for m in near:
        slices_from_plane(m, 1)
    for k in range(3):
        share(k, "wait_send")
    gather.hop(3)
    gather.finish()
    for a in range(7):
        to_core(a, 0, zpos, core, "wait_send", src=ins[a])
    for which in range(2):
        own_slice(which, 1).wait()
        for m in near:
            slice_copy(m, which).wait_send()
    for m in near:
        for which in range(2):
            slice_plane(m, which, rep, 0, xrep).wait_send()
            slice_plane(m, which, rep, 1, yrep).wait_send()
            slice_plane(m, which, *onward(m)).wait_send()
            slice_plane(m, which, drep, 2, drep).wait_recv()
    for way in range(2):
        for h in range(3):
            z = zpos - h if way == 0 else zpos + h

            @pl.when((z >= 0) & (zpos < 3) if way == 0 else (z <= 3) & (zpos > 0))
            def _():
                for a in range(6):
                    hop(a, way, h, z, "wait_send")
    for h in range(1, 4):
        for way in range(2):
            z = zpos - h if way == 0 else zpos + h
            k = way * 3 + h - 1

            @pl.when(z >= 0 if way == 0 else z <= 3)
            def _():
                for a in range(4):
                    to_plane(a, k, z, rep, "wait_send", (xsend, xrecv), xrep)
                    to_plane(a, k, z, rep, "wait_send", (ysend, yrecv), yrep)
                    to_plane(a, k, z, xrep if a == 0 else yrep, "wait_send", (dsend, drecv), yrep)
                for a in range(7):
                    to_core(a, k + 1, z, core, "wait_send")

def start_gather(cid, scale, weights, gate, up, tokens, bias, turns, down):
    low, wide = jnp.bfloat16, jnp.float32
    rows, width = tokens.shape
    strip = down.shape[0]
    attn_out, query_down, latent_down, query_up, latent_up = weights[:5]
    tiles = query_up.shape[1]
    keys = bias.shape[1]
    out = [jax.ShapeDtypeStruct((a.shape[0] * 8,) + a.shape[1:], a.dtype) for a in weights]
    out += [jax.ShapeDtypeStruct((gate.shape[0] * 8, strip), gate.dtype)] * 2
    latent_rank = 8 * latent_up.shape[0]
    found = [((rows, width), low), ((rows, query_down.shape[1]), low), ((keys, latent_rank), low), ((keys, 128), low),
             ((keys, tiles), low), ((rows, tiles), low), ((rows, tiles // 2), low), ((rows, 128), wide),
             ((rows, query_down.shape[1]), wide), ((rows, latent_down.shape[1]), wide), ((rows, width), wide),
             ((8 * rows, width), low), ((8 * rows, strip), wide)]
    out += [jax.ShapeDtypeStruct(s, d) for s, d in found]
    whole = [pltpu.VMEM((a.shape[0] * 8, a.shape[1]), a.dtype) for a in (query_down, latent_down, query_up, latent_up)]
    return pl.pallas_call(
        functools.partial(start_kernel, scale), out_shape=out,
        in_specs=[ANY] * 9 + [VMEM] * 4, out_specs=[ANY] * 9 + [VMEM] * 11 + [ANY, VMEM],
        scratch_shapes=[dma_sems(2, 3, 6), dma_sems(2, 3, 6)] + [dma_sems(6, 4)] * 6
        + [dma_sems(7, 7), dma_sems(7, 7), dma_sems(2, 9), dma_sems(7, 2), dma_sems(7, 2), dma_sems(3, 7, 2), dma_sems(3, 7, 2)]
        + [pltpu.VMEM(a.shape, a.dtype) for a in weights] + [pltpu.VMEM((gate.shape[0], strip), gate.dtype)] * 2
        + [pltpu.VMEM((8 * weights[6].shape[0], 128), wide), pltpu.VMEM(weights[6].shape, wide)] + whole
        + [pltpu.VMEM((2, 2 * attn_out.shape[0], width), low), pltpu.VMEM((rows, tiles), wide),
           pltpu.VMEM((rows, width), low), dma_sems(3, 2), dma_sems(3, 2), dma_sems(6), dma_sems(2)] + Gather.scratch(1),
        compiler_params=kernel_params(cid),
    )(*weights, gate, up, tokens, bias, turns, down)

def plane_swap(values, j):
    return lax.ppermute(values, "rep", [(i, i ^ j) for i in range(4)])


def column_body(
    tokens,
    cotangent,
    doc_lengths,
    gain_attn,
    query_down,
    gain_query,
    query_up,
    latent_down,
    gain_latent,
    latent_up,
    attn_out,
    gain_ffn,
    w_gate,
    w_up,
    w_down,
):
    low = jnp.bfloat16
    wide = jnp.float32
    rows, width = tokens.shape[1], tokens.shape[2]
    seq_len = rows * 4
    head_dim = ND + RD
    scale = head_dim ** (-0.5)
    rep, shard = lax.axis_index("rep"), lax.axis_index("shard")
    slice_ff = FF // 8
    strip = 896
    shift = (slice_ff * shard) % 128

    gain_list = (gain_attn, gain_ffn, gain_query, gain_latent)
    small = jnp.concatenate(
        [
            lax.dynamic_update_slice(
                jnp.zeros((8 * v.shape[0],), wide), v.astype(wide), (shard * v.shape[0],)
            )
            for v in gain_list
        ]
    ).reshape(-1, 128)
    tile_up = jnp.pad(
        query_up.reshape(-1, H, head_dim), ((0, 0), (0, 0), (0, 128 - head_dim))
    ).reshape(-1, H * 128)
    grad_out = cotangent[0].astype(wide)
    grad_down_in = (residual_scale * grad_out).astype(low)
    down_w = lax.dynamic_update_slice(jnp.zeros((strip, width), low), w_down, (shift, 0))

    local_pos = rep * rows + jnp.arange(rows, dtype=jnp.int32)
    key_pos = jnp.concatenate(
        [(rep ^ j) * rows + jnp.arange(rows, dtype=jnp.int32) for j in range(4)]
    )
    query_seg, query_off = segment_of(doc_lengths[0], local_pos)
    key_seg = segment_of(doc_lengths[0], key_pos)[0]
    allowed = (query_seg[:, None] == key_seg[None, :]) & (key_pos[None, :] <= local_pos[:, None])
    bias = jnp.where(allowed, 0.0, masked_score).astype(wide)
    cos_part, sin_part = rope_tables(query_off, RD)
    none = jnp.zeros((rows, RD // 2), wide)
    edge = jnp.zeros((rows, ND), wide)
    tail = jnp.zeros((rows, 128 - head_dim), wide)
    turns = jnp.stack(
        [
            jnp.concatenate([edge + 1.0, cos_part, cos_part, tail], axis=1),
            jnp.concatenate([edge, none, sin_part, tail], axis=1),
            jnp.concatenate([edge, -sin_part, none, tail], axis=1),
        ]
    )
    (
        aout,
        qdown,
        ldown,
        qup,
        lup,
        gd_all,
        small_all,
        gate_w,
        up_w,
        normed_low,
        query_low,
        latent_low,
        rope_tile,
        keyvals,
        queries,
        mixed_low,
        logs,
        query_lat,
        latent_proj,
        residual,
        ffn_all,
        grad_hidden,
    ) = start_gather(
        0,
        scale,
        (attn_out, query_down, latent_down, tile_up, latent_up, grad_down_in, small),
        w_gate,
        w_up,
        tokens[0],
        bias,
        turns,
        down_w,
    )
    gains_all = jnp.sum(small_all.reshape((8,) + small.shape), axis=0)
    gain_f = gains_all[width // 128 : 2 * width // 128].reshape(-1)
    norm_f_back = jax.vjp(rms_scale, residual, gain_f)[1]

    gate_pre = jnp.dot(ffn_all, gate_w, preferred_element_type=wide)
    up_pre = jnp.dot(ffn_all, up_w, preferred_element_type=wide)
    hidden, act_back = jax.vjp(swiglu, gate_pre, up_pre)
    hidden_low = hidden.astype(low)
    grad_gate_f, grad_up_f = act_back(grad_hidden)
    grad_gate = grad_gate_f.astype(low)
    grad_up = grad_up_f.astype(low)
    down_part = inner_rows(hidden_low, gd_all).astype(low)
    grad_ffn_in, down_own, gate_own, up_part = back_sums(
        2, down_part, ffn_all, grad_gate, grad_up, gate_w, up_w, slice_ff
    )

    grad_res_norm, grad_gain_ffn = norm_f_back(grad_ffn_in)
    grad_resid = grad_out + grad_res_norm
    grad_branch = (residual_scale * grad_resid).astype(low)
    cols = jnp.stack([mixed_low, normed_low]).reshape(2, rows, 8, width // 8).transpose(2, 0, 1, 3)
    (
        branch_all,
        cols_all,
        down_all,
        gate_all,
        up_own,
        qup_part,
        lup_part,
        tokens_grad,
        grad_lats,
        gain_terms,
    ) = middle_exchange(
        3,
        scale,
        gate_own,
        grad_branch,
        cols,
        down_own,
        up_part,
        (aout, qup, lup, qdown, ldown),
        query_low,
        latent_low,
        (queries, keyvals, rope_tile, bias, turns, logs),
        (
            tokens[0],
            query_lat,
            latent_proj,
            gains_all,
            grad_resid,
            grad_gain_ffn.reshape(-1, 128),
        ),
    )

    mixed_cols = cols_all[:, 0].reshape(8 * rows, width // 8)
    normed_cols = cols_all[:, 1].reshape(8 * rows, width // 8)
    aout_part = inner_rows(mixed_cols, branch_all).astype(low)
    up_all, out_sum, aout_own, lat_own, lup_own, qup_own, gain_own = last_sums(
        4,
        up_own,
        grad_lats,
        qup_part.reshape(8, -1, qup_part.shape[1]),
        lup_part.reshape(8, -1, lup_part.shape[1]),
        hidden_low,
        down_w,
        aout_part,
        normed_cols,
        gain_terms,
    )
    layer_out = (residual + residual_scale * out_sum).astype(low)
    query_rank = query_down.shape[1]
    gate_grad, up_grad, down_grad, aout_own, qdown_own, ldown_own, lup_own, qup_own = widen(
        gate_all, up_all, down_all, aout_own, lat_own, lup_own, qup_own, FF, query_rank, H
    )
    gain_own = gain_own.reshape(-1)
    owned, first = [], 0
    for v in gain_list:
        owned.append(lax.dynamic_slice(gain_own, (first + shard * v.shape[0],), (v.shape[0],)))
        first += 8 * v.shape[0]

    return (
        layer_out[None],
        tokens_grad[None],
        owned[0],
        qdown_own,
        owned[2],
        qup_own,
        ldown_own,
        owned[3],
        lup_own,
        aout_own,
        owned[1],
        gate_grad,
        up_grad,
        down_grad,
    )


def body(
    tokens,
    cotangent,
    doc_lengths,
    gain_attn,
    query_down,
    gain_query,
    query_up,
    latent_down,
    gain_latent,
    latent_up,
    attn_out,
    gain_ffn,
    w_gate,
    w_up,
    w_down,
):
    low_type = jnp.bfloat16
    wide_type = jnp.float32
    tok_rows = tokens.shape[1]
    seq_len = tok_rows * lax.axis_size("rep")
    head_dim = ND + RD
    group_size = math.gcd(H, 8)
    group_count = H // group_size
    softmax_scale = head_dim ** (-0.5)
    local_pos = lax.axis_index("rep") * tok_rows + jnp.arange(tok_rows, dtype=jnp.int32)
    key_pos = jnp.arange(seq_len, dtype=jnp.int32)
    query_seg, query_off = segment_of(doc_lengths[0], local_pos)
    key_seg = segment_of(doc_lengths[0], key_pos)[0]
    allowed = (query_seg[:, None] == key_seg[None, :]) & (key_pos[None, :] <= local_pos[:, None])
    cos_part, sin_part = rope_tables(query_off, RD)
    (
        gain_in_full,
        qdown_full,
        gain_q_full,
        qup_full,
        ldown_full,
        gain_l_full,
        lup_full,
        aout_full,
        gain_f_full,
    ) = (
        lax.all_gather(gain_attn, "shard", axis=0, tiled=True),
        lax.all_gather(query_down, "shard", axis=0, tiled=True),
        lax.all_gather(gain_query, "shard", axis=0, tiled=True),
        lax.all_gather(query_up, "shard", axis=0, tiled=True),
        lax.all_gather(latent_down, "shard", axis=0, tiled=True),
        lax.all_gather(gain_latent, "shard", axis=0, tiled=True),
        lax.all_gather(latent_up, "shard", axis=0, tiled=True),
        lax.all_gather(attn_out, "shard", axis=0, tiled=True),
        lax.all_gather(gain_ffn, "shard", axis=0, tiled=True),
    )
    inputs = tokens[0].astype(wide_type)
    normed, norm_in_back = jax.vjp(rms_scale, inputs, gain_in_full.astype(wide_type))
    normed_low = normed.astype(low_type)
    query_lat = jnp.dot(normed_low, qdown_full, preferred_element_type=wide_type)
    query_norm, norm_q_back = jax.vjp(rms_scale, query_lat, gain_q_full.astype(wide_type))
    query_low = query_norm.astype(low_type)
    query_proj = jnp.dot(query_low, qup_full, preferred_element_type=wide_type).reshape(
        tok_rows, H, head_dim
    )

    def query_rope(values):
        return jnp.concatenate(
            [
                values[..., :ND],
                rotate(values[..., ND:], cos_part[:, None, :], sin_part[:, None, :]),
            ],
            axis=-1,
        )

    query_rot, query_back = jax.vjp(query_rope, query_proj)
    query_used = query_rot.astype(low_type)
    latent_proj = jnp.dot(normed_low, ldown_full, preferred_element_type=wide_type)
    latent_norm, norm_l_back = jax.vjp(
        rms_scale, latent_proj[:, :KR], gain_l_full.astype(wide_type)
    )
    latent_low = latent_norm.astype(low_type)

    def key_rotate(values):
        return rotate(values, cos_part, sin_part)

    key_rot, key_back = jax.vjp(key_rotate, latent_proj[:, KR:])
    key_rope = key_rot.astype(low_type)
    keyvals = jnp.dot(latent_low, lup_full, preferred_element_type=wide_type).astype(low_type)
    all_keyvals, all_rope = (
        lax.all_gather(keyvals, "rep", axis=0, tiled=True),
        lax.all_gather(key_rope, "rep", axis=0, tiled=True),
    )
    queries = query_used.reshape(tok_rows, group_count, group_size, head_dim).transpose(1, 0, 2, 3)
    key_groups = all_keyvals.reshape(seq_len, group_count, group_size, ND + VD).transpose(
        1, 0, 2, 3
    )

    def scores_of(query_blk, key_blk):
        nope_part = jnp.einsum(
            "thd,shd->hts", query_blk[..., :ND], key_blk[..., :ND], preferred_element_type=wide_type
        )
        rope_part = jnp.einsum(
            "thd,sd->hts", query_blk[..., ND:], all_rope, preferred_element_type=wide_type
        )
        return jnp.where(allowed[None], (nope_part + rope_part) * softmax_scale, masked_score)

    def forward_group(carry, blocks):
        query_blk, key_blk = blocks
        scores = scores_of(query_blk, key_blk)
        row_max = jnp.max(scores, axis=-1, keepdims=True)
        exp_scores = jnp.exp(scores - row_max)
        totals = jnp.sum(exp_scores, axis=-1, keepdims=True)
        probs = (exp_scores / totals).astype(low_type)
        mixed = jnp.einsum(
            "hts,shd->thd", probs, key_blk[..., ND:], preferred_element_type=wide_type
        )
        return (carry, (mixed, row_max + jnp.log(totals)))

    start_carry = jnp.zeros((), wide_type)
    final_carry, (mixed_groups, log_totals) = lax.scan(
        forward_group, start_carry, (queries, key_groups)
    )
    mixed_low = mixed_groups.transpose(1, 0, 2, 3).reshape(tok_rows, H * VD).astype(low_type)
    branch = jnp.dot(mixed_low, aout_full, preferred_element_type=wide_type)
    residual = inputs + residual_scale * branch
    normed_ffn, norm_f_back = jax.vjp(rms_scale, residual, gain_f_full.astype(wide_type))
    ffn_low = normed_ffn.astype(low_type)
    gate_full, up_full, down_full = (
        lax.all_gather(w_gate, "shard", axis=0, tiled=True),
        lax.all_gather(w_up, "shard", axis=0, tiled=True),
        lax.all_gather(w_down, "shard", axis=0, tiled=True),
    )
    gate_pre = jnp.dot(ffn_low, gate_full, preferred_element_type=wide_type)
    up_pre = jnp.dot(ffn_low, up_full, preferred_element_type=wide_type)
    hidden, act_back = jax.vjp(swiglu, gate_pre, up_pre)
    hidden_low = hidden.astype(low_type)
    ffn_branch = jnp.dot(hidden_low, down_full, preferred_element_type=wide_type)
    layer_out = residual + residual_scale * ffn_branch
    grad_out = cotangent[0].astype(wide_type)
    grad_down_in = (residual_scale * grad_out).astype(low_type)
    gate_back_w, up_back_w, down_back_w = (
        lax.all_gather(w_gate, "shard", axis=0, tiled=True),
        lax.all_gather(w_up, "shard", axis=0, tiled=True),
        lax.all_gather(w_down, "shard", axis=0, tiled=True),
    )
    grad_hidden = outer_cols(grad_down_in, down_back_w)
    grad_gate_f, grad_up_f = act_back(grad_hidden)
    grad_gate = grad_gate_f.astype(low_type)
    grad_up = grad_up_f.astype(low_type)
    grad_ffn_in = outer_cols(grad_gate, gate_back_w) + outer_cols(grad_up, up_back_w)
    down_grad = lax.psum_scatter(
        inner_rows(hidden_low, grad_down_in).astype(jnp.bfloat16),
        "shard",
        scatter_dimension=0,
        tiled=True,
    )
    gate_up_in = jnp.concatenate([grad_gate, grad_up], axis=1)
    gate_up_grad = lax.psum_scatter(
        inner_rows(ffn_low, gate_up_in).astype(jnp.bfloat16),
        "shard",
        scatter_dimension=0,
        tiled=True,
    ).astype(jnp.float32)
    gate_grad = gate_up_grad[:, :FF]
    up_grad = gate_up_grad[:, FF:]
    grad_res_norm, grad_gain_ffn = norm_f_back(grad_ffn_in)
    grad_resid = grad_out + grad_res_norm
    qdown_back, qup_back, ldown_back, lup_back, aout_back = (
        lax.all_gather(query_down, "shard", axis=0, tiled=True),
        lax.all_gather(query_up, "shard", axis=0, tiled=True),
        lax.all_gather(latent_down, "shard", axis=0, tiled=True),
        lax.all_gather(latent_up, "shard", axis=0, tiled=True),
        lax.all_gather(attn_out, "shard", axis=0, tiled=True),
    )
    grad_branch = (residual_scale * grad_resid).astype(low_type)
    aout_grad = inner_rows(mixed_low, grad_branch)
    grad_mixed = outer_cols(grad_branch, aout_back).astype(low_type)
    grad_groups = grad_mixed.reshape(tok_rows, group_count, group_size, VD).transpose(1, 0, 2, 3)

    def backward_group(rope_acc, blocks):
        query_blk, key_blk, grad_blk, log_blk = blocks
        scores = scores_of(query_blk, key_blk)
        probs = jnp.exp(scores - log_blk)
        grad_probs = jnp.einsum(
            "thd,shd->hts", grad_blk, key_blk[..., ND:], preferred_element_type=wide_type
        )
        delta = jnp.sum(probs * grad_probs, axis=-1, keepdims=True)
        grad_scores = (probs * (grad_probs - delta)).astype(low_type)
        grad_query = (
            jnp.concatenate(
                [
                    jnp.einsum(
                        "hts,shd->thd",
                        grad_scores,
                        key_blk[..., :ND],
                        preferred_element_type=wide_type,
                    ),
                    jnp.einsum(
                        "hts,sd->thd", grad_scores, all_rope, preferred_element_type=wide_type
                    ),
                ],
                axis=-1,
            )
            * softmax_scale
        )
        grad_key = (
            jnp.einsum(
                "hts,thd->shd", grad_scores, query_blk[..., :ND], preferred_element_type=wide_type
            )
            * softmax_scale
        )
        grad_value = jnp.einsum(
            "hts,thd->shd", probs.astype(low_type), grad_blk, preferred_element_type=wide_type
        )
        rope_acc = (
            rope_acc
            + jnp.einsum(
                "hts,thd->sd", grad_scores, query_blk[..., ND:], preferred_element_type=wide_type
            )
            * softmax_scale
        )
        return (rope_acc, (grad_query, jnp.concatenate([grad_key, grad_value], axis=-1)))

    rope_start = jnp.zeros((seq_len, RD), wide_type)
    rope_sum, (grad_q_groups, grad_kv_groups) = lax.scan(
        backward_group, rope_start, (queries, key_groups, grad_groups, log_totals)
    )
    grad_kv_all = grad_kv_groups.transpose(1, 0, 2, 3).reshape(seq_len, H * (ND + VD))
    grad_kv_own, grad_rope_own = (
        lax.psum_scatter(
            grad_kv_all.astype(jnp.bfloat16), "rep", scatter_dimension=0, tiled=True
        ).astype(jnp.float32),
        lax.psum_scatter(
            rope_sum.astype(jnp.bfloat16), "rep", scatter_dimension=0, tiled=True
        ).astype(jnp.float32),
    )
    grad_q_full = grad_q_groups.transpose(1, 0, 2, 3).reshape(tok_rows, H, head_dim)
    grad_q_proj = query_back(grad_q_full)[0].reshape(tok_rows, H * head_dim).astype(low_type)
    qup_grad = inner_rows(query_low, grad_q_proj)
    grad_q_lat_f, grad_gain_query = norm_q_back(outer_cols(grad_q_proj, qup_back))
    grad_q_lat = grad_q_lat_f.astype(low_type)
    grad_kv_low = grad_kv_own.astype(low_type)
    lup_grad = inner_rows(latent_low, grad_kv_low)
    grad_lat_c, grad_gain_latent = norm_l_back(outer_cols(grad_kv_low, lup_back))
    grad_lat_r = key_back(grad_rope_own)[0]
    grad_lat = jnp.concatenate([grad_lat_c, grad_lat_r], axis=1).astype(low_type)
    qdown_grad = inner_rows(normed_low, grad_q_lat)
    ldown_grad = inner_rows(normed_low, grad_lat)
    grad_normed = outer_cols(grad_q_lat, qdown_back) + outer_cols(grad_lat, ldown_back)
    grad_in_norm, grad_gain_attn = norm_in_back(grad_normed)
    tokens_grad = (grad_resid + grad_in_norm).astype(low_type)
    (
        owned_gain_attn,
        owned_qdown,
        owned_gain_query,
        owned_qup,
        owned_ldown,
        owned_gain_latent,
        owned_lup,
        owned_aout,
        owned_gain_ffn,
    ) = (
        lax.psum_scatter(
            grad_gain_attn.astype(jnp.bfloat16), "shard", scatter_dimension=0, tiled=True
        ).astype(jnp.float32),
        lax.psum_scatter(
            qdown_grad.astype(jnp.bfloat16), "shard", scatter_dimension=0, tiled=True
        ).astype(jnp.float32),
        lax.psum_scatter(
            grad_gain_query.astype(jnp.bfloat16), "shard", scatter_dimension=0, tiled=True
        ).astype(jnp.float32),
        lax.psum_scatter(
            qup_grad.astype(jnp.bfloat16), "shard", scatter_dimension=0, tiled=True
        ).astype(jnp.float32),
        lax.psum_scatter(
            ldown_grad.astype(jnp.bfloat16), "shard", scatter_dimension=0, tiled=True
        ).astype(jnp.float32),
        lax.psum_scatter(
            grad_gain_latent.astype(jnp.bfloat16), "shard", scatter_dimension=0, tiled=True
        ).astype(jnp.float32),
        lax.psum_scatter(
            lup_grad.astype(jnp.bfloat16), "shard", scatter_dimension=0, tiled=True
        ).astype(jnp.float32),
        lax.psum_scatter(
            aout_grad.astype(jnp.bfloat16), "shard", scatter_dimension=0, tiled=True
        ).astype(jnp.float32),
        lax.psum_scatter(
            grad_gain_ffn.astype(jnp.bfloat16), "shard", scatter_dimension=0, tiled=True
        ).astype(jnp.float32),
    )
    summed = (
        lax.psum(owned_gain_attn.astype(jnp.bfloat16), "rep").astype(jnp.float32),
        lax.psum(owned_qdown.astype(jnp.bfloat16), "rep").astype(jnp.float32),
        lax.psum(owned_gain_query.astype(jnp.bfloat16), "rep").astype(jnp.float32),
        lax.psum(owned_qup.astype(jnp.bfloat16), "rep").astype(jnp.float32),
        lax.psum(owned_ldown.astype(jnp.bfloat16), "rep").astype(jnp.float32),
        lax.psum(owned_gain_latent.astype(jnp.bfloat16), "rep").astype(jnp.float32),
        lax.psum(owned_lup.astype(jnp.bfloat16), "rep").astype(jnp.float32),
        lax.psum(owned_aout.astype(jnp.bfloat16), "rep").astype(jnp.float32),
        lax.psum(owned_gain_ffn.astype(jnp.bfloat16), "rep").astype(jnp.float32),
        lax.psum(gate_grad.astype(jnp.bfloat16), "rep").astype(jnp.float32),
        lax.psum(up_grad.astype(jnp.bfloat16), "rep").astype(jnp.float32),
        lax.psum(down_grad, "rep").astype(jnp.float32),
    )
    return (
        layer_out.astype(low_type)[None],
        tokens_grad[None],
        summed[0],
        summed[1],
        summed[2],
        summed[3],
        summed[4],
        summed[5],
        summed[6],
        summed[7],
        summed[8],
        summed[9],
        summed[10],
        summed[11],
    )


def solution(mesh):
    placed = (
        P("shard", "rep", None),
        P("shard", "rep", None),
        P("shard", None),
        P("shard"),
        P("shard", None),
        P("shard"),
        P("shard", None),
        P("shard", None),
        P("shard"),
        P("shard", None),
        P("shard", None),
        P("shard"),
        P("shard", None),
        P("shard", None),
        P("shard", None),
    )
    fits = mesh.shape["rep"] == 4 and mesh.shape["shard"] == 8
    return jax.shard_map(
        column_body if fits else body,
        mesh=mesh,
        in_specs=placed,
        out_specs=(
            P("shard", "rep", None),
            P("shard", "rep", None),
            P("shard"),
            P("shard", None),
            P("shard"),
            P("shard", None),
            P("shard", None),
            P("shard"),
            P("shard", None),
            P("shard", None),
            P("shard"),
            P("shard", None),
            P("shard", None),
            P("shard", None),
        ),
        check_vma=False,
    )
```

```python
import functools
import math

import jax
import jax.numpy as jnp
from jax import lax
from jax.experimental import pallas as pl
from jax.experimental.pallas import tpu as pltpu
from jax.sharding import PartitionSpec as P

KR = 256
H = 40
ND = 64
RD = 32
VD = 64
FF = 6400


epsilon = 1e-05
residual_scale = 1.4 / math.sqrt(62.0)
rope_base = 10000.0
masked_score = -1e30


def rms_scale(values, gain):
    return values * lax.rsqrt(jnp.mean(values * values, axis=-1, keepdims=True) + epsilon) * gain


def rotate(values, cos_part, sin_part):
    midpoint = values.shape[-1] // 2
    former = values[..., :midpoint]
    latter = values[..., midpoint:]
    return jnp.concatenate(
        [former * cos_part - latter * sin_part, latter * cos_part + former * sin_part], axis=-1
    )


def segment_of(lengths, positions):
    doc_ends = jnp.cumsum(lengths)
    doc_starts = doc_ends - lengths
    segment = jnp.sum((positions[:, None] >= doc_ends[None, :]).astype(jnp.int32), axis=1)
    chosen = segment[:, None] == jnp.arange(lengths.shape[0], dtype=jnp.int32)[None, :]
    offsets = positions - jnp.sum(jnp.where(chosen, doc_starts[None, :], 0), axis=1)
    return (segment, offsets)


def rope_tables(offsets, rope_width):
    exponents = jnp.arange(0, rope_width, 2, dtype=jnp.float32) / rope_width
    angles = offsets.astype(jnp.float32)[:, None] * (rope_base ** (-exponents))[None, :]
    return (jnp.cos(angles), jnp.sin(angles))


def swiglu(gate_vals, up_vals):
    return jax.nn.silu(gate_vals) * up_vals


def inner_rows(leading, trailing):
    return lax.dot_general(
        leading, trailing, (((0,), (0,)), ((), ())), preferred_element_type=jnp.float32
    )


def outer_cols(leading, trailing):
    return lax.dot_general(
        leading, trailing, (((1,), (1,)), ((), ())), preferred_element_type=jnp.float32
    )


MESH = pl.DeviceIdType.MESH
ANY = pl.BlockSpec(memory_space=pl.ANY)

def place():
    rep = lax.axis_index("rep")
    shard = lax.axis_index("shard")
    zpos, core = shard // 2, shard % 2
    return rep, zpos, core

def mult(value, by):
    return pl.multiple_of(value, by)

def greet(rep, zpos, core, plane=0, column=False):
    barrier = pltpu.get_barrier_semaphore()
    shard = zpos * 2 + core

    def signal(r, s):
        pl.semaphore_signal(barrier, inc=1, device_id=(r, s), device_id_type=MESH)

    if column:
        for m in range(1, 8):
            signal(rep, column_place(zpos, core, m))
        count = 7
    else:
        signal(rep, zpos * 2 + 1 - core)

        @pl.when(zpos > 0)
        def _():
            signal(rep, shard - 2)

        @pl.when(zpos < 3)
        def _():
            signal(rep, shard + 2)

        count = 1 + jnp.minimum(zpos, 1) + jnp.minimum(3 - zpos, 1)
    if plane:
        for other in plane_places(rep)[:plane]:
            signal(other, shard)
        count = count + plane
    pl.semaphore_wait(barrier, count)


def plane_places(rep):
    return rep + 1 - 2 * (rep % 2), (rep + 2) % 4, 3 - rep


def column_place(zpos, core, m, back=False):
    step = 4 - m // 2 if back else m // 2
    return ((zpos + step) % 4) * 2 + (core + m) % 2


def remote(src, dst, ssem, rsem, r, s):
    return pltpu.make_async_remote_copy(
        src_ref=src, dst_ref=dst, send_sem=ssem, recv_sem=rsem, device_id=(r, s), device_id_type=MESH
    )


def dma_sems(*dims):
    return pltpu.SemaphoreType.DMA(dims)


def head_tile(h):
    return pl.ds(pl.multiple_of(h * 128, 128), 128)


def turn(values, tables, back=False):
    keep, high, low_part = tables
    if back:
        return values * keep + pltpu.roll(values * high, 112, 1) + pltpu.roll(values * low_part, 16, 1)
    return values * keep + pltpu.roll(values, 16, 1) * high + pltpu.roll(values, 112, 1) * low_part


def dot_nt(a, b):
    return lax.dot_general(a, b, (((1,), (1,)), ((), ())), preferred_element_type=jnp.float32)


def dot_tn(a, b):
    return lax.dot_general(a, b, (((0,), (0,)), ((), ())), preferred_element_type=jnp.float32)


def attend_heads(scale, proj, kv, rope, bias, turns, query, mixed, logs):
    low = jnp.bfloat16
    lane = lax.broadcasted_iota(jnp.int32, (1, 128), 1)
    first = lane < 64

    def group(i, carry):
        heads_here = [4 * i + j for j in range(4)]
        queries = [turn(proj[:, head_tile(h)], (turns[0], turns[1], turns[2])).astype(low) for h in heads_here]
        keyvals = [kv[:, head_tile(h)] for h in heads_here]
        scores = [dot_nt(q, jnp.where(first, keyval, rope[...])) * scale + bias[...] for q, keyval in zip(queries, keyvals)]
        tops = [jnp.max(s, axis=1, keepdims=True) for s in scores]
        grown = [jnp.exp(s - top) for s, top in zip(scores, tops)]
        totals = [jnp.sum(g, axis=1, keepdims=True) for g in grown]
        outs = [jnp.dot((g / total).astype(low), keyval, preferred_element_type=jnp.float32)
                for g, total, keyval in zip(grown, totals, keyvals)]
        for h, q, top, total in zip(heads_here, queries, tops, totals):
            query[:, head_tile(h)] = q
            logs[...] = jnp.where(lane == h, top + jnp.log(total), logs[...])
        for j in range(2):
            mixed[:, head_tile(2 * i + j)] = jnp.where(first, pltpu.roll(outs[2 * j], 64, 1), outs[2 * j + 1]).astype(low)
        return carry

    return group


def attend_back_heads(scale, query, kv, rope, bias, turns, logs, grad, grad_query, grad_packed, grad_kv, grad_rope, left):
    low = jnp.bfloat16
    rows = query.shape[0]
    lane = lax.broadcasted_iota(jnp.int32, (1, 128), 1)
    first = lane < 64

    def one(h, grad_value):
        q = query[:, head_tile(h)]
        keyval = kv[:, head_tile(h)]
        key = jnp.where(first, keyval, rope[...])
        left[0:rows, 0:128] = q
        left[rows:, 128:256] = grad_value
        both = dot_nt(left[...], jnp.concatenate([key, keyval], axis=1))
        log = jnp.sum(jnp.where(lane == h, logs[...], 0.0), axis=1, keepdims=True)
        probs = jnp.exp(both[:rows] * scale + bias[...] - log)
        weighed = probs * both[rows:]
        delta = jnp.sum(weighed, axis=1, keepdims=True)
        grad_scores = (weighed - probs * delta).astype(low)
        grad_q = jnp.dot(grad_scores, key, preferred_element_type=jnp.float32) * scale
        grad_q = turn(grad_q, (turns[0], turns[1], turns[2]), True)
        grad_query[:, head_tile(h)] = grad_q.astype(low)
        out = dot_tn(jnp.concatenate([grad_scores, probs.astype(low)], axis=0), left[...])
        grad_key = out[:, :128] * scale
        grad_rope[...] += grad_key
        grad_kv[:, head_tile(h)] = jnp.where(first, grad_key, out[:, 128:]).astype(low)
        return grad_q

    def quarter(i, carry):
        rotary = jnp.zeros((rows, 128), jnp.float32)
        for j in range(5):
            both = grad[:, head_tile(5 * i + j)].astype(jnp.float32)
            even = one(10 * i + 2 * j, jnp.where(first, 0.0, pltpu.roll(both, 64, 1)).astype(low))
            odd = one(10 * i + 2 * j + 1, jnp.where(first, 0.0, both).astype(low))
            grad_packed[:, head_tile(8 * i + j)] = jnp.where(first, even, pltpu.roll(odd, 64, 1)).astype(low)
            for k, got in ((2 * j, even), (2 * j + 1, odd)):
                at = 32 * (k % 4)
                moved = got if at == 64 else pltpu.roll(got, (at + 64) % 128, 1)
                rotary = jnp.where((lane >= at) & (lane < at + 32), moved, rotary)
                if k % 4 == 3 or k == 9:
                    grad_packed[:, head_tile(8 * i + 5 + k // 4)] = rotary.astype(low)
                    rotary = jnp.zeros((rows, 128), jnp.float32)
        return carry

    return quarter


def unpacked(packed, heads):
    pieces = []
    for h in range(heads):
        first, k = h // 10 * 1024, h % 10
        pieces.append(packed[:, first + 64 * k : first + 64 * k + 64])
        pieces.append(packed[:, first + 640 + 32 * k : first + 672 + 32 * k])
    return jnp.concatenate(pieces, axis=1)


def widen_kernel(heads, gate, up, down, attn_out, lat, latent_up, query_up, *outs):
    wide = jnp.float32
    for strips, out in zip((gate, up), outs[:2]):
        each = out.shape[1] // 8
        for s in range(8):
            first, last = s * each // 128, (s + 1) * each // 128
            tiles = strips[s, 0].astype(wide)
            if s * each % 128:
                shared = strips[s - 1, 0, :, (first - (s - 1) * each // 128) * 128 :][:, :128]
                out[:, first * 128 : first * 128 + 128] = tiles[:, :128] + shared.astype(wide)
                first_full = first + 1
            else:
                first_full = first
            out[:, first_full * 128 : last * 128] = tiles[:, (first_full - first) * 128 : (last - first) * 128]
    down_out, attn_out_out, query_down_out, latent_down_out, latent_up_out, query_up_out = outs[2:]
    down_out[...] = down[...].astype(wide)
    attn_out_out[...] = attn_out[...].astype(wide)
    rank = query_down_out.shape[1]
    query_down_out[...] = lat[0, :, :rank].astype(wide)
    latent_down_out[...] = lat[0, :, rank:].astype(wide)

    @pl.when(pl.program_id(0) == 0)
    def _():
        latent_up_out[...] = latent_up[...].astype(wide)
        query_up_out[...] = unpacked(query_up[...], heads).astype(wide)


def widen(gate, up, down, attn_out, lat, latent_up, query_up, cols, rank, heads):
    _, quarters, rows, strip = gate.shape
    width = attn_out.shape[1]
    whole = lambda a: pl.BlockSpec(a, lambda q: (0, 0))
    by_rows = lambda c: pl.BlockSpec((rows, c), lambda q: (q, 0))
    by_cols = pl.BlockSpec((down.shape[0], width // quarters), lambda q: (0, q))
    strips = pl.BlockSpec((8, 1, rows, strip), lambda q: (0, q, 0, 0))
    shapes = [(quarters * rows, cols)] * 2 + [down.shape, attn_out.shape, (quarters * rows, rank),
                                              (quarters * rows, lat.shape[2] - rank), latent_up.shape, (query_up.shape[0], heads * 96)]
    return pl.pallas_call(
        functools.partial(widen_kernel, heads), grid=(quarters,),
        out_shape=[jax.ShapeDtypeStruct(s, jnp.float32) for s in shapes],
        in_specs=[strips, strips, by_cols, by_rows(width), pl.BlockSpec((1,) + lat.shape[1:], lambda q: (q, 0, 0)),
                  whole(latent_up.shape), whole(query_up.shape)],
        out_specs=[by_rows(cols)] * 2 + [by_cols, by_rows(width), by_rows(rank), by_rows(lat.shape[2] - rank),
                                         whole(latent_up.shape), whole(shapes[-1])],
        compiler_params=pltpu.CompilerParams(vmem_limit_bytes=56 * 2**20),
    )(gate, up, down, attn_out, lat, latent_up, query_up)


class Gather:
    def __init__(self, ins, outs, sems):
        self.ins, self.outs = ins, outs
        self.zsend, self.zrecv, self.csend, self.crecv, self.own = sems
        self.rep, self.zpos, self.core = place()
        self.held = None

    @staticmethod
    def scratch(n):
        return [dma_sems(2, 3, n), dma_sems(2, 3, n), dma_sems(7, n), dma_sems(7, n), dma_sems(2, n)]

    def at(self, a, z, c):
        rows = self.ins[a].shape[0]
        return self.outs[a].at[pl.ds(mult((z * 2 + c) * rows, rows), rows)]

    def hop_copy(self, a, way, hop, z, src=None):
        dst = self.at(a, z, self.core)
        return remote(dst if src is None else src, dst, self.zsend.at[way, hop, a], self.zrecv.at[way, hop, a],
                      self.rep, (self.zpos + (1 - 2 * way)) * 2 + self.core)

    def core_copy(self, a, slot, z, c, src=None):
        dst = self.at(a, z, c)
        return remote(dst if src is None else src, dst, self.csend.at[slot, a], self.crecv.at[slot, a],
                      self.rep, self.zpos * 2 + 1 - self.core)

    def keep(self, a):
        return pltpu.make_async_copy(self.ins[a], self.at(a, self.zpos, self.core), self.own.at[0, a])

    def onward(self, way):
        return self.zpos < 3 if way == 0 else self.zpos > 0

    def source(self, way, hop):
        z = self.zpos - hop if way == 0 else self.zpos + hop
        return z, (z >= 0 if way == 0 else z <= 3)

    def start(self, which=None):
        which = range(len(self.ins)) if which is None else which
        for way in range(2):
            @pl.when(self.onward(way))
            def _():
                for a in which:
                    self.hop_copy(a, way, 0, self.zpos, src=self.ins[a]).start()
        for a in which:
            self.core_copy(a, 0, self.zpos, self.core, src=self.ins[a]).start()
            self.keep(a).start()

    def hop(self, hop, which=None):
        which = range(len(self.ins)) if which is None else which
        for way in range(2):
            z, there = self.source(way, hop)

            @pl.when(there)
            def _():
                for a in which:
                    self.hop_copy(a, way, hop - 1, z).wait_recv()
                    if hop < 3:
                        @pl.when(self.onward(way))
                        def _():
                            self.hop_copy(a, way, hop, z).start()
                    self.core_copy(a, way * 3 + hop, z, self.core).start()

    def finish(self):
        arrays = range(len(self.ins))
        for way in range(2):
            for hop in range(3):
                z, there = self.source(way, hop)

                @pl.when(there & self.onward(way))
                def _():
                    for a in arrays:
                        self.hop_copy(a, way, hop, z).wait_send()
        for a in arrays:
            self.keep(a).wait()
            self.core_copy(a, 0, self.zpos, self.core, src=self.ins[a]).wait_send()
            self.core_copy(a, 0, self.zpos, 1 - self.core).wait_recv()
        for way in range(2):
            for hop in range(1, 4):
                z, there = self.source(way, hop)

                @pl.when(there)
                def _():
                    for a in arrays:
                        self.core_copy(a, way * 3 + hop, z, self.core).wait_send()
                        self.core_copy(a, way * 3 + hop, z, 1 - self.core).wait_recv()


class Total:
    def __init__(self, term, out, bufs, sems):
        self.term, self.out = term, out
        self.theirs, self.landed = bufs
        self.zsend, self.zrecv, self.csend, self.crecv = sems
        self.rep, self.zpos, self.core = place()

    @staticmethod
    def scratch(term):
        return [pltpu.VMEM((4,) + term.shape[1:], term.dtype), pltpu.VMEM((5,) + term.shape[1:], term.dtype),
                dma_sems(2, 4), dma_sems(2, 4), dma_sems(4), dma_sems(4)]

    @staticmethod
    def split(term, out, refs):
        return Total(term, out, refs[:2], refs[2:6]), refs[6:]

    def pair_copy(self, z):
        return remote(self.term.at[z * 2 + 1 - self.core], self.theirs.at[z], self.csend.at[z], self.crecv.at[z],
                      self.rep, self.zpos * 2 + 1 - self.core)

    def hop_copy(self, way, z):
        return remote(self.theirs.at[z], self.landed.at[z + 1 - way], self.zsend.at[way, z], self.zrecv.at[way, z],
                      self.rep, (self.zpos + (1 - 2 * way)) * 2 + self.core)

    def each(self, step):
        for way in range(2):
            behind = self.zpos if way == 0 else 3 - self.zpos
            target = self.zpos + 3 - step if way == 0 else self.zpos - 3 + step
            yield way, behind, target, (behind <= step) & (behind < 3)

    def start(self):
        for z in (3, 0, 2, 1):
            self.pair_copy(z).start()

    def pair(self):
        for z in (3, 0, 2, 1):
            self.pair_copy(z).wait_recv()

    def both(self, z):
        return self.term[z * 2 + self.core].astype(jnp.float32) + self.theirs[z].astype(jnp.float32)

    def step(self, step):
        for way, behind, target, there in self.each(step):
            @pl.when(there)
            def _():
                total = self.both(target)

                @pl.when(behind == 0)
                def _():
                    self.theirs[target] = total.astype(self.theirs.dtype)

                @pl.when(behind > 0)
                def _():
                    self.hop_copy(way, target).wait_recv()
                    self.theirs[target] = (total + self.landed[target + 1 - way].astype(jnp.float32)).astype(self.theirs.dtype)
                self.hop_copy(way, target).start()

    def finish(self):
        self.out[...] = self.both(self.zpos)
        for way in range(2):
            @pl.when(self.zpos > 0 if way == 0 else self.zpos < 3)
            def _():
                self.hop_copy(way, self.zpos).wait_recv()
                self.out[...] += self.landed[self.zpos + 1 - way].astype(jnp.float32)
        for step in range(3):
            for way, behind, target, there in self.each(step):
                @pl.when(there)
                def _():
                    self.hop_copy(way, target).wait_send()
        for z in range(4):
            self.pair_copy(z).wait_send()


def kernel_params(cid):
    return pltpu.CompilerParams(collective_id=cid, has_side_effects=True, vmem_limit_bytes=58 * 2**20)


VMEM = pl.BlockSpec(memory_space=pltpu.VMEM)


class PlaneSum:
    def __init__(self, items, bufs, sems):
        self.items = items
        self.landed, self.stage, self.last = bufs
        self.asend, self.arecv, self.bsend, self.brecv = sems
        self.rep, self.zpos, self.core = place()
        self.shard = self.zpos * 2 + self.core

    @staticmethod
    def scratch(shapes, dtype):
        n = len(shapes)
        return ([pltpu.VMEM((2,) + s, dtype) for s in shapes] + [pltpu.VMEM(s, dtype) for s in shapes] * 2
                + [dma_sems(n, 2), dma_sems(n, 2), dma_sems(n), dma_sems(n)])

    @staticmethod
    def split(refs, n):
        return (refs[:n], refs[n : 2 * n], refs[2 * n : 3 * n]), refs[3 * n : 3 * n + 4], refs[3 * n + 4 :]

    def ways(self, i):
        xrep, yrep, drep = plane_places(self.rep)
        return (xrep, yrep, drep) if self.items[i][2] == 0 else (yrep, xrep, drep)

    def out(self, i, k):
        near, _, far = self.ways(i)
        return remote(self.items[i][0](far if k else near), self.landed[i].at[k], self.asend.at[i, k], self.arecv.at[i, k],
                      near, self.shard)

    def on(self, i):
        return remote(self.stage[i], self.last[i], self.bsend.at[i], self.brecv.at[i], self.ways(i)[1], self.shard)

    def start(self, which=None):
        for i in range(len(self.items)) if which is None else which:
            for k in (1, 0):
                self.out(i, k).start()

    def middle(self, i):
        wide = jnp.float32
        self.out(i, 1).wait_recv()
        term = self.items[i][0](self.ways(i)[1])
        self.stage[i][...] = (term[...].astype(wide) + self.landed[i][1].astype(wide)).astype(self.stage[i].dtype)
        self.on(i).start()

    def end(self, i):
        wide = jnp.float32
        self.out(i, 0).wait_recv()
        self.on(i).wait_recv()
        total = self.items[i][0](self.rep)[...].astype(wide) + self.landed[i][0].astype(wide)
        own = self.items[i][1]
        own[...] = (total + self.last[i][...].astype(wide)).astype(own.dtype)

    def finish(self):
        for i in range(len(self.items)):
            for k in range(2):
                self.out(i, k).wait_send()
            self.on(i).wait_send()


class PlaneGather:
    def __init__(self, items, sems):
        self.items = items
        self.send, self.recv, self.own = sems
        self.rep, self.zpos, self.core = place()
        self.shard = self.zpos * 2 + self.core

    @staticmethod
    def scratch(n):
        return [dma_sems(3, n), dma_sems(3, n), dma_sems(n)]

    def copy(self, i, kind, quarter, to):
        own, part, _ = self.items[i]
        dst = part(quarter)
        return remote(dst if kind == 2 or own is None else own, dst, self.send.at[kind, i], self.recv.at[kind, i], to, self.shard)

    def keep(self, i):
        return pltpu.make_async_copy(self.items[i][0], self.items[i][1](self.rep), self.own.at[i])

    def start(self, which=None):
        xrep, yrep, _ = plane_places(self.rep)
        for i in range(len(self.items)) if which is None else which:
            self.copy(i, 0, self.rep, xrep).start()
            self.copy(i, 1, self.rep, yrep).start()
            if self.items[i][0] is not None:
                self.keep(i).start()

    def middle(self, i):
        xrep, yrep, _ = plane_places(self.rep)
        self.copy(i, 0, xrep, xrep).wait_recv()
        if self.items[i][2] == 0:
            self.copy(i, 2, xrep, yrep).start()
        self.copy(i, 1, yrep, yrep).wait_recv()
        if self.items[i][2] == 1:
            self.copy(i, 2, yrep, xrep).start()

    def finish(self):
        xrep, yrep, drep = plane_places(self.rep)
        for i, (own, _, first) in enumerate(self.items):
            self.copy(i, 0, self.rep, xrep).wait_send()
            self.copy(i, 1, self.rep, yrep).wait_send()
            self.copy(i, 2, *((xrep, yrep) if first == 0 else (yrep, xrep))).wait_send()
            self.copy(i, 2, drep, drep).wait_recv()
            if own is not None:
                self.keep(i).wait()


class ColumnSwap:
    def __init__(self, items, sems, keeps=True):
        self.items, self.keeps = items, keeps
        self.send, self.recv, self.own = sems
        self.rep, self.zpos, self.core = place()
        self.shard = self.zpos * 2 + self.core

    near = (1, 2, 6, 3, 7, 4, 5)

    @staticmethod
    def scratch(n):
        return [dma_sems(7, n), dma_sems(7, n), dma_sems(n)]

    def copy(self, i, m, back=False):
        s2 = column_place(self.zpos, self.core, m, back)
        block, there = self.items[i]
        return remote(block(s2), there(s2 if back else self.shard), self.send.at[m - 1, i], self.recv.at[m - 1, i], self.rep, s2)

    def keep(self, i):
        return pltpu.make_async_copy(self.items[i][0](self.shard), self.items[i][1](self.shard), self.own.at[i])

    def start(self):
        for m in self.near:
            for i in range(len(self.items)):
                self.copy(i, m).start()
        for i in range(len(self.items) if self.keeps else 0):
            self.keep(i).start()

    def arrive(self, m):
        for i in range(len(self.items)):
            self.copy(i, m, True).wait_recv()

    def finish(self, arrive=True):
        for i in range(len(self.items)):
            if self.keeps:
                self.keep(i).wait()
            for m in self.near:
                self.copy(i, m).wait_send()
                if arrive:
                    self.copy(i, m, True).wait_recv()


class Strips:
    def __init__(self, own, whole, sems):
        rep, zpos, core = place()
        shard = zpos * 2 + core
        self.swap = ColumnSwap([(lambda s: own.at[s], lambda s: whole.at[s, rep])], sems[:2] + [None], keeps=False)

        def part(m):
            return lambda p: whole.at[shard if m == 0 else column_place(zpos, core, m, True), p]

        self.spread = PlaneGather([(None if m else own.at[shard], part(m), m % 2) for m in range(8)], sems[2:5])

    @staticmethod
    def scratch():
        return [dma_sems(7, 1), dma_sems(7, 1)] + PlaneGather.scratch(8)

    def start(self):
        self.swap.start()
        self.spread.start((0,))

    def arrive(self, *places):
        for m in places:
            self.swap.arrive(m)
            self.spread.start((m,))

    def onward(self, *places):
        for m in places:
            self.spread.middle(m)

    def finish(self):
        self.swap.finish(arrive=False)
        self.spread.finish()


def quarter_cols(ref, first, rows, p):
    width = ref.shape[1] // 4
    return ref.at[pl.ds(first, rows), pl.ds(mult(p * width, 128), width)]


def back_kernel(shift_unit, *refs):
    down, tokens, grad_gate, grad_up, gate_w, up_w, out, down_own, gate_own, up = refs[:10]
    term, gate, strips, strip_sems = refs[10:14]
    rep, zpos, core = place()
    total, rest = Total.split(term, out, refs[14:])
    bufs, sems, _ = PlaneSum.split(rest, 4)
    half = down_own.shape[0] // 2
    shift = mult((zpos * 2 + core) % 4 * shift_unit, 16)
    wide = jnp.float32

    def down_item(h):
        return (lambda p: quarter_cols(down, mult(shift + h * half, 16), half, p), down_own.at[pl.ds(h * half, half)], h)

    def gate_item(h):
        return (lambda p: gate.at[pl.ds(4 * h, 4), p], gate_own.at[pl.ds(4 * h, 4)], h)

    sums = PlaneSum([down_item(0), down_item(1), gate_item(0), gate_item(1)], bufs, sems)
    chunk = strips.shape[2]
    chunks = gate_w.shape[0] // chunk

    def strip(i, which):
        return pltpu.make_async_copy(
            (gate_w, up_w)[which].at[pl.ds(mult(i * chunk, 128), chunk)], strips.at[i % 2, which], strip_sems.at[i % 2, which])

    for which in range(2):
        strip(0, which).start()
    greet(rep, zpos, core, plane=2)
    sums.start((0, 1))

    def back(i, carry):
        for which in range(2):
            strip(i, which).wait()

        @pl.when(i < chunks - 1)
        def _():
            for which in range(2):
                strip(i + 1, which).start()

        part = dot_nt(grad_gate[...], strips[i % 2, 0]) + dot_nt(grad_up[...], strips[i % 2, 1])
        term[:, :, pl.ds(mult(i * chunk, 128), chunk)] = part.astype(term.dtype).reshape(8, -1, chunk)
        return carry

    lax.fori_loop(0, chunks, back, 0)
    total.start()
    wide_rows = tokens.shape[1] // 4

    def weight(grad, to, i):
        got = dot_tn(tokens[:, pl.ds(mult(i * wide_rows, 128), wide_rows)], grad[...])
        to[pl.ds(2 * i, 2)] = got.astype(to.dtype).reshape((2,) + to.shape[1:])

    def gate_step(i, carry):
        weight(grad_gate, gate, i)

        @pl.when(i == 2)
        def _():
            total.pair()
            total.step(0)
        return carry

    lax.fori_loop(0, 4, gate_step, 0)
    sums.start((2, 3))

    def up_step(i, carry):
        weight(grad_up, up, i)

        @pl.when(i == 1)
        def _():
            sums.middle(0)
            sums.middle(1)
            total.step(1)
        return carry

    lax.fori_loop(0, 4, up_step, 0)
    sums.end(0)
    sums.end(1)
    total.step(2)
    sums.middle(2)
    sums.middle(3)
    total.finish()
    sums.end(2)
    sums.end(3)
    sums.finish()


def back_sums(cid, down, tokens, grad_gate, grad_up, gate_w, up_w, rows):
    width = down.shape[1] // 4
    kind = down.dtype
    strip = gate_w.shape[1]
    parts = (8, 4, gate_w.shape[0] // 32, strip)
    term = jax.ShapeDtypeStruct((8, tokens.shape[0] // 8, tokens.shape[1]), kind)
    return pl.pallas_call(
        functools.partial(back_kernel, rows % 128),
        out_shape=[jax.ShapeDtypeStruct(term.shape[1:], jnp.float32), jax.ShapeDtypeStruct((rows, width), kind),
                   jax.ShapeDtypeStruct((8,) + parts[2:], kind), jax.ShapeDtypeStruct(parts, kind)],
        in_specs=[VMEM] * 4 + [ANY] * 2, out_specs=[VMEM] * 4,
        scratch_shapes=[pltpu.VMEM(term.shape, kind), pltpu.VMEM(parts, kind),
                        pltpu.VMEM((2, 2, gate_w.shape[0] // 5, strip), kind), dma_sems(2, 2)]
        + Total.scratch(term) + PlaneSum.scratch([(rows // 2, width)] * 2 + [(4,) + parts[2:]] * 2, kind),
        compiler_params=kernel_params(cid),
    )(down, tokens, grad_gate, grad_up, gate_w, up_w)


def middle_kernel(scale, *refs):
    gate, refs = refs[0], refs[1:]
    branch, cols, down, up, attn_out, w_query_up, w_latent_up, query_low, latent_low = refs[:9]
    query, kv, rope, bias, turns, logs = refs[9:15]
    w_query, w_latent, tokens, query_lat, latent_proj, gains, grad_residual, gain_ffn = refs[15:23]
    branch_all, cols_all, down_all, gate_all, up_own, query_up, latent_up, tokens_grad, lats, gain_terms = refs[23:33]
    scratch = list(refs[33:])
    (left, mixed, packed, grad_query, grad_kv, grad_rope, strips, query_strips, latent_strips, strip_sems, grad_low,
     grad_latent, grad_normed, latent_send, rope_send, latent_land, rope_land, lsend, lrecv, query_rows, latent_rows,
     row_sems) = scratch[:22]
    scratch = scratch[22:]
    rep, zpos, core = place()
    shard = zpos * 2 + core
    gather = Gather((branch,), (branch_all,), scratch[:5])
    swap = ColumnSwap([(lambda s: cols.at[s], lambda s: cols_all.at[s])], scratch[5:8])
    half = down.shape[0] // 2
    downs = PlaneGather(
        [(down.at[pl.ds(h * half, half)], functools.partial(quarter_cols, down_all, h * half, half), h) for h in range(2)],
        scratch[8:11])
    strips_out = Strips(gate, gate_all, scratch[11:16])
    bufs, sems, _ = PlaneSum.split(scratch[16:], 2)
    sums = PlaneSum([(lambda p, h=h: up.at[pl.ds(4 * h, 4), p], up_own.at[pl.ds(4 * h, 4)], h) for h in range(2)], bufs, sems)
    rows = tokens.shape[0]
    out_rows = attn_out.shape[0] // 4
    quarter_width = kv.shape[1] // 4
    wide, low = jnp.float32, jnp.bfloat16

    def strip(i, k):
        at = pl.ds(mult(i * quarter_width, 128), quarter_width)
        src = (attn_out.at[pl.ds(mult(i * out_rows, 128), out_rows)], w_query_up.at[:, at], w_latent_up.at[:, at])[k]
        return pltpu.make_async_copy(src, (strips, query_strips, latent_strips)[k].at[i % 2], strip_sems.at[i % 2, k])

    def share(k, what):
        for i, (src, dst) in enumerate(((latent_send, latent_land), (rope_send, rope_land))):
            getattr(remote(src.at[pl.ds((k + 1) * rows, rows)], dst.at[k], lsend.at[k, i], lrecv.at[k, i],
                           plane_places(rep)[k], shard), what)()

    for k in range(3):
        strip(0, k).start()
    greet(rep, zpos, core, plane=3, column=True)
    strips_out.start()
    sums.start()
    downs.start()
    left[...] = jnp.zeros_like(left)
    grad_rope[...] = jnp.zeros_like(grad_rope)
    grad_low[...] = jnp.zeros_like(grad_low)
    grad_latent[...] = jnp.zeros_like(grad_latent)
    quarter = attend_back_heads(
        scale, query, kv, rope, bias, turns, logs, mixed, grad_query, packed, grad_kv, grad_rope, left)

    def after_first():
        gather.start()
        swap.start()
        strips_out.arrive(1, 2, 6)

    def after_second():
        strips_out.arrive(3, 7, 4, 5)
        sums.middle(0)
        sums.middle(1)

    def after_third():
        gather.hop(1)
        downs.middle(0)
        downs.middle(1)
        strips_out.onward(0, 1, 2)

    def after_fourth():
        gather.hop(2)
        strips_out.onward(6, 3)

    def step(i, carry):
        for k in range(3):
            strip(i, k).wait()

        @pl.when(i < 3)
        def _():
            for k in range(3):
                strip(i + 1, k).start()

        mixed[:, pl.ds(mult(i * out_rows, 128), out_rows)] = dot_nt(branch[...], strips[i % 2]).astype(mixed.dtype)
        quarter(i, carry)
        at = pl.ds(mult(i * quarter_width, 128), quarter_width)
        grad_low[...] += dot_nt(grad_query[:, at], query_strips[i % 2])
        grad_latent[...] += dot_nt(grad_kv[:, at], latent_strips[i % 2])
        for k, service in enumerate((after_first, after_second, after_third, after_fourth)):
            pl.when(i == k)(service)
        return carry

    lax.fori_loop(0, 4, step, 0)
    latent_send[...] = grad_latent[...].astype(low)
    rope_send[...] = grad_rope[...].astype(low)
    for k in range(3):
        share(k, "start")

    def terms(i, carry):
        at = pl.ds(mult(i * 1024, 128), 1024)
        query_up[:, at] = dot_tn(query_low[...], packed[:, at]).astype(query_up.dtype)
        at = pl.ds(mult(i * quarter_width, 128), quarter_width)
        latent_up[:, at] = dot_tn(latent_low[...], grad_kv[:, at]).astype(latent_up.dtype)
        return carry

    lax.fori_loop(0, 4, terms, 0)
    strips_out.onward(7, 4, 5)
    sums.end(0)
    sums.end(1)

    def tile(t):
        return slice(128 * t, 128 * t + 128)

    def norm_back(src, grad, tiles, first, put):
        square = sum(jnp.sum(jnp.square(src(t)), axis=1, keepdims=True) for t in range(tiles))
        factor = lax.rsqrt(square / (128 * tiles) + epsilon)
        along = jnp.zeros_like(factor)
        for t in range(tiles):
            unit = src(t) * factor
            weighed = grad(t) * unit
            gain_terms[first + t : first + t + 1, :] = jnp.sum(weighed, axis=0, keepdims=True)
            along = along + jnp.sum(weighed * gains[first + t : first + t + 1, :], axis=1, keepdims=True)
        along = along / (128 * tiles)
        for t in range(tiles):
            put(t, factor * (grad(t) * gains[first + t : first + t + 1, :] - src(t) * factor * along))

    def put_query(t, value):
        lats[:, tile(t)] = value.astype(low)

    def put_latent(t, value):
        lats[:, tile(6 + t)] = value.astype(low)

    def put_tokens(t, value):
        tokens_grad[:, tile(t)] = (grad_residual[:, tile(t)] + value).astype(low)

    norm_back(lambda t: query_lat[:, tile(t)], lambda t: grad_low[:, tile(t)], 6, 40, put_query)
    own = grad_latent[0:rows].astype(low).astype(wide)
    own_rope = grad_rope[0:rows].astype(low).astype(wide)
    for k in range(3):
        share(k, "wait_recv")
        own = own + latent_land[k].astype(wide)
        own_rope = own_rope + rope_land[k].astype(wide)
    grad_latent[0:rows] = own
    norm_back(lambda t: latent_proj[:, tile(t)], lambda t: grad_latent[0:rows, tile(t)], 2, 46, put_latent)
    turned = turn(own_rope, (turns[0], turns[1], turns[2]), True)
    lats[:, 1024:1056] = turned[:, 64:96].astype(low)
    chunk = query_rows.shape[1]
    chunks = w_query.shape[0] // chunk

    def row_copy(i, k):
        at = pl.ds(mult(i * chunk, chunk), chunk)
        return pltpu.make_async_copy((w_query, w_latent)[k].at[at], (query_rows, latent_rows)[k].at[i % 2], row_sems.at[i % 2, k])

    def normed_step(i, carry):
        for k in range(2):
            row_copy(i, k).wait()

        @pl.when(i < chunks - 1)
        def _():
            for k in range(2):
                row_copy(i + 1, k).start()

        grad_normed[:, pl.ds(mult(i * chunk, chunk), chunk)] = (
            dot_nt(lats[:, :768], query_rows[i % 2]) + dot_nt(lats[:, 768:1056], latent_rows[i % 2]))
        return carry

    for k in range(2):
        row_copy(0, k).start()
    lax.fori_loop(0, chunks, normed_step, 0)
    norm_back(lambda t: tokens[:, tile(t)].astype(wide), lambda t: grad_normed[:, tile(t)], 20, 0, put_tokens)
    gain_terms[20:40, :] = gain_ffn[...]
    gather.hop(3)
    for k in range(3):
        share(k, "wait_send")
    gather.finish()
    swap.finish()
    downs.finish()
    sums.finish()
    strips_out.finish()


def middle_exchange(cid, scale, gate, branch, cols, down, up, weights, query_low, latent_low, attend_in, norm_in):
    kind = branch.dtype
    wide = jnp.float32
    query, kv, rope = attend_in[:3]
    rows, width = branch.shape
    attn_out, w_query_up, w_latent_up, w_query, w_latent = weights
    keys, latent_rank = latent_low.shape
    query_rank = query_low.shape[1]
    quarter = kv.shape[1] // 4
    gains = norm_in[3]
    return pl.pallas_call(
        functools.partial(middle_kernel, scale),
        out_shape=[jax.ShapeDtypeStruct((8 * rows, width), kind), jax.ShapeDtypeStruct(cols.shape, kind),
                   jax.ShapeDtypeStruct((down.shape[0], 4 * down.shape[1]), kind),
                   jax.ShapeDtypeStruct((8, 4) + gate.shape[1:], kind), jax.ShapeDtypeStruct((8,) + up.shape[2:], kind),
                   jax.ShapeDtypeStruct((query_rank, 4096), kind), jax.ShapeDtypeStruct((latent_rank, kv.shape[1]), kind),
                   jax.ShapeDtypeStruct((rows, width), kind),
                   jax.ShapeDtypeStruct((rows, query_rank + w_latent.shape[1]), kind), jax.ShapeDtypeStruct(gains.shape, wide)],
        in_specs=[ANY, VMEM] + [ANY] * 2 + [VMEM] + [ANY] * 3 + [VMEM] * 8 + [ANY] * 2 + [VMEM] * 6,
        out_specs=[ANY] * 4 + [VMEM] * 6,
        scratch_shapes=[pltpu.VMEM((2 * rows, 256), kind), pltpu.VMEM(branch.shape, kind), pltpu.VMEM((rows, 4096), kind),
                        pltpu.VMEM(query.shape, kind), pltpu.VMEM(kv.shape, kind), pltpu.VMEM(rope.shape, wide),
                        pltpu.VMEM((2, attn_out.shape[0] // 4, width), kind), pltpu.VMEM((2, query_rank, quarter), kind),
                        pltpu.VMEM((2, latent_rank, quarter), kind), dma_sems(2, 3),
                        pltpu.VMEM((rows, query_rank), wide), pltpu.VMEM((keys, latent_rank), wide), pltpu.VMEM((rows, width), wide),
                        pltpu.VMEM((keys, latent_rank), kind), pltpu.VMEM((keys, 128), kind),
                        pltpu.VMEM((3, rows, latent_rank), kind), pltpu.VMEM((3, rows, 128), kind), dma_sems(3, 2), dma_sems(3, 2),
                        pltpu.VMEM((2, width // 5, query_rank), kind), pltpu.VMEM((2, width // 5, w_latent.shape[1]), kind), dma_sems(2, 2)]
        + Gather.scratch(1) + ColumnSwap.scratch(1) + PlaneGather.scratch(2) + Strips.scratch()
        + PlaneSum.scratch([(4,) + up.shape[2:]] * 2, kind),
        compiler_params=kernel_params(cid),
    )(gate, branch, cols, down, up, attn_out, w_query_up, w_latent_up, query_low, latent_low, *attend_in, w_query, w_latent, *norm_in)


def last_kernel(*refs):
    up, lat, query_up, latent_up, hidden, down, branch, cols, gain = refs[:9]
    up_all, out, attn_sum, lat_sum, latent_sum, query_sum, gain_out = refs[9:16]
    attn_out, branch_sem, scratch = refs[16], refs[17], list(refs[18:])
    rep, zpos, core = place()
    shard = zpos * 2 + core
    places = plane_places(rep)

    def take(n):
        nonlocal scratch
        got, scratch = scratch[:n], scratch[n:]
        return got

    strips_out = Strips(up, up_all, take(5))
    spread_sems = take(3)
    lat_all, out_term, lat_term, query_part, latent_own, query_own = take(6)
    gather = Gather((lat,), (lat_all,), take(5))
    owns = take(5)
    gain_landed, gain_sum, gain_plane, gsend, grecv, hsend, hrecv = take(7)
    total, scratch = Total.split(out_term, out, scratch)
    query_total, scratch = Total.split(query_part, query_own, scratch)
    latent_total, scratch = Total.split(latent_up, latent_own, scratch)
    bufs, sems, _ = PlaneSum.split(scratch, 6)
    width = query_up.shape[2] // 4
    half = attn_out.shape[0] // 2

    def query_item(h):
        return (lambda p: query_up.at[pl.ds(4 * h, 4), :, pl.ds(mult(p * width, 128), width)], query_part.at[pl.ds(4 * h, 4)], h)

    latent_low = scratch[-1]
    sums = PlaneSum(
        [query_item(0), query_item(1)]
        + [(functools.partial(quarter_cols, attn_out, h * half, half), owns[h], h) for h in range(2)]
        + [(lambda p: lat_term.at[p], owns[2], 0),
           (functools.partial(quarter_cols, latent_low, 0, latent_low.shape[0]), owns[3], 1)],
        bufs, sems)
    spread = PlaneGather(
        [(owns[h], functools.partial(quarter_cols, attn_sum, h * half, half), h) for h in range(2)]
        + [(owns[2], lambda p: lat_sum.at[p], 0),
           (owns[3], functools.partial(quarter_cols, latent_sum, 0, latent_low.shape[0]), 1),
           (owns[4], functools.partial(quarter_cols, query_sum, 0, query_up.shape[1]), 0)], spread_sems)

    def gain_copy(m):
        s2 = column_place(zpos, core, m)
        return remote(gain, gain_landed.at[m - 1], gsend.at[m - 1], grecv.at[m - 1], rep, s2)

    def gain_on(k):
        return remote(gain_sum, gain_plane.at[k], hsend.at[k], hrecv.at[k], places[k], shard)

    greet(rep, zpos, core, plane=3, column=True)
    for m in range(1, 8):
        gain_copy(m).start()
    strips_out.start()
    sums.start((0, 1))
    latent_total.start()
    branch_copy = pltpu.make_async_copy(branch, out_term, branch_sem.at[0])
    branch_copy.start()
    gather.start()
    rows = lat.shape[0]
    tokens = 8 * rows

    def attn_term(i, carry):
        at = pl.ds(mult(i * (attn_out.shape[1] // 4), 128), attn_out.shape[1] // 4)
        attn_out[:, at] = dot_tn(cols[:, 0].reshape(tokens, -1), out_term[:, :, at].reshape(tokens, -1)).astype(attn_out.dtype)
        return carry

    def term(i, carry):
        out_term[i] = jnp.dot(hidden[pl.ds(mult(i * rows, rows), rows)], down[...],
                              preferred_element_type=jnp.float32).astype(out_term.dtype)
        return carry

    arrive, onward = strips_out.arrive, strips_out.onward
    branch_copy.wait()
    lax.fori_loop(0, 4, attn_term, 0)
    sums.start((2, 3))
    lax.fori_loop(0, 3, term, 0)
    arrive(1)
    latent_total.pair()
    latent_total.step(0)
    lax.fori_loop(3, 6, term, 0)
    onward(0)
    gather.hop(1)
    arrive(2)
    arrive(6)
    lax.fori_loop(6, 8, term, 0)
    latent_total.step(1)
    gain_sum[...] = gain[...]
    for m in range(1, 8):
        gain_copy(m).wait_recv()
        gain_sum[...] += gain_landed[m - 1]
    for k in range(3):
        gain_on(k).start()
    total.start()
    onward(1)
    arrive(3)
    arrive(7)
    gather.hop(2)
    sums.middle(0)
    sums.middle(1)
    latent_total.step(2)
    onward(2, 6)
    arrive(4)
    arrive(5)
    gather.hop(3)
    total.pair()
    total.step(0)
    sums.middle(2)
    sums.middle(3)
    latent_total.finish()
    latent_low[...] = latent_own[...].astype(latent_low.dtype)
    sums.start((5,))
    sums.end(0)
    sums.end(1)
    query_total.start()
    gather.finish()
    lat_term[...] = dot_tn(cols[:, 1].reshape(tokens, -1), lat_all[...]).astype(lat_term.dtype).reshape(lat_term.shape)
    sums.start((4,))
    query_total.pair()
    query_total.step(0)
    onward(3, 7)
    total.step(1)
    sums.end(2)
    sums.end(3)
    spread.start((0, 1))
    query_total.step(1)
    onward(4, 5)
    sums.middle(5)
    sums.middle(4)
    query_total.step(2)
    total.step(2)
    query_total.finish()
    owns[4][...] = query_own[...].astype(owns[4].dtype)
    spread.start((4,))
    sums.end(5)
    spread.start((3,))
    sums.end(4)
    spread.start((2,))
    for i in (0, 1, 4, 3, 2):
        spread.middle(i)
    gain_out[...] = gain_sum[...]
    for k in range(3):
        gain_on(k).wait_recv()
        gain_out[...] += gain_plane[k]
    total.finish()
    for k in range(3):
        gain_on(k).wait_send()
    for m in range(1, 8):
        gain_copy(m).wait_send()
    strips_out.finish()
    sums.finish()
    spread.finish()


def last_sums(cid, up, lat, query_up, latent_up, hidden, down, branch, cols, gain):
    kind = up.dtype
    wide = jnp.float32
    rows = lat.shape[0]
    attn_out = jax.ShapeDtypeStruct((cols.shape[3], branch.shape[2]), kind)
    lat_shape = (4, cols.shape[3] // 4, lat.shape[1])
    query_shape = (query_up.shape[1], query_up.shape[2] // 4)
    shapes = [(attn_out.shape[0] // 2, attn_out.shape[1] // 4)] * 2 + [
        lat_shape[1:], (latent_up.shape[1], latent_up.shape[2] // 4)]
    out_term = jax.ShapeDtypeStruct((8, rows, down.shape[1]), kind)
    query_part = jax.ShapeDtypeStruct((8,) + query_shape, kind)
    return pl.pallas_call(
        last_kernel,
        out_shape=[jax.ShapeDtypeStruct((8, 4) + up.shape[1:], kind)]
        + [jax.ShapeDtypeStruct(out_term.shape[1:], wide)]
        + [jax.ShapeDtypeStruct(s, kind) for s in (attn_out.shape, lat_shape, latent_up.shape[1:])]
        + [jax.ShapeDtypeStruct((query_up.shape[1], query_up.shape[2]), kind), jax.ShapeDtypeStruct(gain.shape, gain.dtype)],
        in_specs=[ANY] * 2 + [VMEM] * 4 + [ANY] + [VMEM] * 2, out_specs=[ANY, VMEM] + [ANY] * 4 + [VMEM],
        scratch_shapes=[pltpu.VMEM(attn_out.shape, kind), dma_sems(1)] + Strips.scratch() + PlaneGather.scratch(5)
        + [pltpu.VMEM((8 * rows, lat.shape[1]), kind), pltpu.VMEM(out_term.shape, kind), pltpu.VMEM(lat_shape, kind),
           pltpu.VMEM(query_part.shape, kind), pltpu.VMEM(latent_up.shape[1:], wide), pltpu.VMEM(query_shape, wide)]
        + Gather.scratch(1) + [pltpu.VMEM(s, kind) for s in shapes + [query_shape]]
        + [pltpu.VMEM((7,) + gain.shape, wide), pltpu.VMEM(gain.shape, wide), pltpu.VMEM((3,) + gain.shape, wide)]
        + [dma_sems(7)] * 2 + [dma_sems(3)] * 2
        + Total.scratch(out_term) + Total.scratch(query_part) + Total.scratch(latent_up)
        + PlaneSum.scratch([(4,) + query_shape] * 2 + shapes, kind) + [pltpu.VMEM(latent_up.shape[1:], kind)],
        compiler_params=kernel_params(cid),
    )(up, lat, query_up, latent_up, hidden, down, branch, cols, gain)


def start_kernel(scale, *refs):
    ins, (gate, up), (tokens, bias, turns, w_down) = refs[:7], refs[7:9], refs[9:13]
    outs, cols, refs = refs[13:20], refs[20:22], refs[22:]
    (normed, query_low, latent, rope, kv, query, mixed, logs, query_lat, latent_proj, residual, ffn_all,
     grad_hidden, down) = refs[:14]
    refs = refs[14:]
    (zsend, zrecv, xsend, xrecv, ysend, yrecv, dsend, drecv, csend, crecv, own, gsend, grecv, psend, precv) = refs[:15]
    held, strips = refs[15:22], refs[22:24]
    (small, gains, w_query, w_latent, w_query_up, w_latent_up, w_out, proj, ffn, lsend, lrecv, load_sems,
     grad_sems, down_sem) = refs[24:38]
    gather = Gather((ffn,), (ffn_all,), refs[38:])
    rep, zpos, core = place()
    xrep, yrep, drep = plane_places(rep)
    shard = zpos * 2 + core

    def whole(a, z, c):
        rows = ins[a].shape[0]
        return outs[a].at[pl.ds(mult((z * 2 + c) * rows, rows), rows)]

    def pieces(a, z, c, quarter, act, own_ref=False):
        def part(b, first, rows):
            full = ins[b].shape[0]
            if own_ref:
                return ins[b].at[pl.ds(mult(first, 16), rows)]
            return outs[b].at[pl.ds(mult((z * 2 + c) * full + first, 16), rows)]

        if a < 3:
            rows = ins[a].shape[0] // 4
            act(part(a, quarter * rows, rows))
        elif a == 3:
            @pl.when(quarter < 3)
            def _():
                act(part(3, jnp.minimum(quarter, 2) * 32, 32))

            @pl.when(quarter == 3)
            def _():
                act(part(4, 0, 32))
        else:
            act(ins[a + 1] if own_ref else whole(a + 1, z, c))

    copy = remote

    def hop(a, way, h, z, what):
        def act(ref):
            c = copy(ref, ref, zsend.at[way, h, a], zrecv.at[way, h, a], rep, (zpos + 1 - 2 * way) * 2 + core)
            getattr(c, what)()
        pieces(a, z, core, rep, act)

    def to_plane(a, k, z, quarter, what, sems, r):
        def act(ref):
            getattr(copy(ref, ref, sems[0].at[k, a], sems[1].at[k, a], r, shard), what)()
        pieces(a, z, core, quarter, act)

    def to_core(a, slot, z, c, what, src=None):
        ref = whole(a, z, c)
        getattr(copy(ref if src is None else src, ref, csend.at[slot, a], crecv.at[slot, a], rep, zpos * 2 + 1 - core), what)()

    greet(rep, zpos, core, plane=3, column=True)
    def send_own(a):
        def first(way):
            def go(src):
                def act(ref):
                    copy(src, ref, zsend.at[way, 0, a], zrecv.at[way, 0, a], rep, (zpos + 1 - 2 * way) * 2 + core).start()
                return act
            return go
        for way in range(2):
            @pl.when(zpos < 3 if way == 0 else zpos > 0)
            def _():
                if a < 3:
                    rows = ins[a].shape[0] // 4
                    src = ins[a].at[pl.ds(mult(rep * rows, 16), rows)]
                    pieces(a, zpos, core, rep, first(way)(src))
                elif a == 3:
                    @pl.when(rep < 3)
                    def _():
                        start = mult(jnp.minimum(rep, 2) * 32, 16)
                        src = ins[3].at[pl.ds(start, 32)]
                        dst = outs[3].at[pl.ds(mult(shard * 96 + start, 16), 32)]
                        first(way)(src)(dst)

                    @pl.when(rep == 3)
                    def _():
                        first(way)(ins[4])(whole(4, zpos, core))
                else:
                    first(way)(ins[a + 1])(whole(a + 1, zpos, core))

    def keep(a, half):
        if half == 0:
            return pltpu.make_async_copy(ins[a], held[a], own.at[0, a])
        return pltpu.make_async_copy(held[a], whole(a, zpos, core), own.at[1, a])

    for a in (5, 1, 2, 3, 0):
        send_own(a)

    strip = cols[0].shape[1]
    quarter_rows = gate.shape[0] // 4

    def slice_of(which, s, first, rows):
        start = mult((s * 25 // 4) * 128, 128)
        return (gate, up)[which].at[pl.ds(mult(first, 16), rows), pl.ds(start, strip)]

    def rows_of(which, s, quarter):
        return cols[which].at[pl.ds(mult(s * gate.shape[0] + quarter * quarter_rows, 16), quarter_rows)]

    def slice_copy(m, which):
        s2 = column_place(zpos, core, m)
        return remote(slice_of(which, s2, rep * quarter_rows, quarter_rows), rows_of(which, shard, rep),
                      gsend.at[m - 1, which], grecv.at[m - 1, which], rep, s2)

    def slice_plane(m, which, quarter, kind, r):
        ref = rows_of(which, column_place(zpos, core, m, back=True), quarter)
        return remote(ref, ref, psend.at[kind, m - 1, which], precv.at[kind, m - 1, which], r, shard)

    def own_slice(which, half):
        if half == 0:
            return pltpu.make_async_copy(slice_of(which, shard, 0, gate.shape[0]), strips[which], own.at[0, 7 + which])
        rows = gate.shape[0]
        return pltpu.make_async_copy(strips[which], cols[which].at[pl.ds(mult(shard * rows, rows), rows)], own.at[1, 7 + which])

    near = (1, 2, 6, 3, 7, 4, 5)
    for a in range(7):
        to_core(a, 0, zpos, core, "start", src=ins[a])
        keep(a, 0).start()
    for which in range(2):
        own_slice(which, 0).start()
    for a in range(7):
        keep(a, 0).wait()
        keep(a, 1).start()
    for which in range(2):
        own_slice(which, 0).wait()
        own_slice(which, 1).start()

    def slices_from_column(m):
        for which in range(2):
            s2 = column_place(zpos, core, m, back=True)
            ref = rows_of(which, s2, rep)
            remote(ref, ref, gsend.at[m - 1, which], grecv.at[m - 1, which], rep, s2).wait_recv()
        slices_to_plane(m, 0)

    def slices_to_plane(m, which):
        slice_plane(m, which, rep, 0, xrep).start()
        slice_plane(m, which, rep, 1, yrep).start()

    def slices_from_plane(m, which=0):
        slice_plane(m, which, xrep, 0, xrep).wait_recv()
        slice_plane(m, which, yrep, 1, yrep).wait_recv()
        slice_plane(m, which, *onward(m)).start()

    def onward(m):
        return (yrep, 2, xrep) if m % 2 else (xrep, 2, yrep)

    def from_column(h, way, z, slots):
        for a in slots:
            hop(a, way, h - 1, z, "wait_recv")
            if h < 3:
                @pl.when(zpos < 3 if way == 0 else zpos > 0)
                def _():
                    hop(a, way, h, z, "start")
            if a < 4:
                to_plane(a, way * 3 + h - 1, z, rep, "start", (xsend, xrecv), xrep)
                to_plane(a, way * 3 + h - 1, z, rep, "start", (ysend, yrecv), yrep)
            else:
                to_core(a + 1, way * 3 + h, z, core, "start")

    def from_plane(h, way, z, slots):
        k = way * 3 + h - 1
        for a in slots:
            to_plane(a, k, z, xrep, "wait_recv", (xsend, xrecv), xrep)
            if a == 0:
                to_plane(a, k, z, xrep, "start", (dsend, drecv), yrep)
            to_plane(a, k, z, yrep, "wait_recv", (ysend, yrecv), yrep)
            if a > 0:
                to_plane(a, k, z, yrep, "start", (dsend, drecv), xrep)

    def from_corner(h, way, z, slots):
        k = way * 3 + h - 1
        for a in slots:
            to_plane(a, k, z, drep, "wait_recv", (dsend, drecv), drep)
            for b in (a,) if a < 3 else (3, 4):
                to_core(b, k + 1, z, core, "start")

    def by_hop(stage, h, *more):
        for way in range(2):
            z = zpos - h if way == 0 else zpos + h

            @pl.when(z >= 0 if way == 0 else z <= 3)
            def _():
                stage(h, way, z, *more)

    def arrived(arrays):
        for b in arrays:
            keep(b, 1).wait()
            to_core(b, 0, zpos, 1 - core, "wait_recv")

            def theirs(h, way, z):
                to_core(b, way * 3 + h, z, 1 - core, "wait_recv")

            for h in range(1, 4):
                by_hop(theirs, h)

    wide, low = jnp.float32, jnp.bfloat16

    def tile(t):
        return slice(128 * t, 128 * t + 128)

    def normalize(src, dst, tiles, first):
        square = sum(jnp.sum(jnp.square(src(t)), axis=1, keepdims=True) for t in range(tiles))
        factor = lax.rsqrt(square / (128 * tiles) + epsilon)
        for t in range(tiles):
            dst[:, tile(t)] = (src(t) * factor * gains[first + t : first + t + 1, :]).astype(low)

    def load(b, to, i):
        return pltpu.make_async_copy(outs[b], to, load_sems.at[i])

    def share(k, what):
        rows = tokens.shape[0]
        for i, ref in enumerate((latent, rope)):
            copy_ = remote(ref.at[pl.ds(0, rows)], ref.at[pl.ds((k + 1) * rows, rows)], lsend.at[k, i], lrecv.at[k, i],
                           plane_places(rep)[k], shard)
            getattr(copy_, what)()

    def down_products():
        arrived((1, 2))
        load(1, w_query, 1).start()
        load(2, w_latent, 2).start()
        load(2, w_latent, 2).wait()
        latent_proj[...] = jnp.dot(normed[...], w_latent[...], preferred_element_type=wide)
        normalize(lambda t: latent_proj[:, tile(t)], latent.at[pl.ds(0, tokens.shape[0])], 2, 46)
        edge = jnp.zeros((tokens.shape[0], 64), wide)
        key = jnp.concatenate([edge, latent_proj[:, 256:288], edge[:, :32]], axis=1)
        rope[0 : tokens.shape[0]] = turn(key, (turns[0], turns[1], turns[2])).astype(low)
        for k in range(3):
            share(k, "start")
        load(1, w_query, 1).wait()
        query_lat[...] = jnp.dot(normed[...], w_query[...], preferred_element_type=wide)
        normalize(lambda t: query_lat[:, tile(t)], query_low, 6, 40)

    def chunk_loop(count, body):
        lax.fori_loop(0, count, lambda i, c: (body(i), c)[1], 0)

    def query_chunk(i):
        at = pl.ds(mult(i * 1024, 128), 1024)
        proj[:, at] = jnp.dot(query_low[...], w_query_up[:, at], preferred_element_type=wide)

    def key_chunk(i):
        at = pl.ds(mult(i * 1024, 128), 1024)
        kv[:, at] = jnp.dot(latent[...], w_latent_up[:, at], preferred_element_type=wide).astype(low)

    out_rows = w_out.shape[1]

    def out_strip(i):
        return pltpu.make_async_copy(outs[0].at[pl.ds(mult(i * out_rows, 128), out_rows)], w_out.at[i % 2], load_sems.at[4 + i % 2])

    down_copy = pltpu.make_async_copy(
        w_down, down.at[pl.ds(mult(shard % 4 * (w_down.shape[0] % 128), 16), w_down.shape[0])], down_sem.at[0])
    down[...] = jnp.zeros_like(down)
    down_copy.start()
    by_hop(from_column, 1, (5, 1, 2))
    by_hop(from_column, 1, (3, 0))
    by_hop(from_column, 2, (5, 1, 2))
    by_hop(from_plane, 1, (1, 2))
    by_hop(from_column, 2, (3, 0))
    by_hop(from_plane, 1, (3, 0))
    by_hop(from_column, 3, (5, 1, 2))
    by_hop(from_plane, 2, (1, 2))
    by_hop(from_corner, 1, (1, 2))
    by_hop(from_column, 3, (3, 0))
    for m in near:
        for which in range(2):
            slice_copy(m, which).start()
    by_hop(from_plane, 3, (1, 2))
    by_hop(from_corner, 2, (1, 2))
    by_hop(from_plane, 2, (3, 0))
    arrived((6,))
    load(6, small, 0).start()
    load(6, small, 0).wait()
    gains[...] = sum(small[48 * s : 48 * s + 48, :] for s in range(8))
    normalize(lambda t: tokens[:, tile(t)].astype(wide), normed, 20, 0)
    by_hop(from_corner, 3, (1, 2))
    by_hop(from_corner, 1, (3, 0))
    down_products()
    by_hop(from_plane, 3, (3, 0))
    by_hop(from_corner, 2, (3, 0))
    for m in near[:3]:
        slices_from_column(m)
    send_own(4)
    by_hop(from_corner, 3, (3, 0))
    arrived((3, 4))
    load(3, w_query_up, 3).start()
    load(4, w_latent_up, 0).start()
    for m in near[3:]:
        slices_from_column(m)
    load(3, w_query_up, 3).wait()
    chunk_loop(5, query_chunk)
    for m in near[:3]:
        slices_from_plane(m)
    for k in range(3):
        share(k, "wait_recv")
    load(4, w_latent_up, 0).wait()
    chunk_loop(5, key_chunk)
    logs[...] = jnp.zeros_like(logs)
    group = attend_heads(scale, proj, kv, rope, bias, turns, query, mixed, logs)

    def attend_step(i, carry):
        group(i, carry)

        @pl.when(i == 3)
        def _():
            by_hop(from_column, 1, (4,))

        @pl.when(i == 8)
        def _():
            by_hop(from_column, 2, (4,))
        return carry

    lax.fori_loop(0, kv.shape[1] // 512, attend_step, 0)
    arrived((0,))
    out_strip(0).start()
    residual[...] = tokens[...].astype(wide)

    def out_step(i, carry):
        out_strip(i).wait()

        @pl.when(i < 3)
        def _():
            out_strip(i + 1).start()

        residual[...] += residual_scale * jnp.dot(
            mixed[:, pl.ds(mult(i * out_rows, 128), out_rows)], w_out[i % 2], preferred_element_type=wide)
        return carry

    lax.fori_loop(0, 4, out_step, 0)
    normalize(lambda t: residual[:, tile(t)], ffn, 20, 20)
    gather.start()
    for m in near:
        slices_to_plane(m, 1)
    by_hop(from_column, 3, (4,))
    for m in near[3:]:
        slices_from_plane(m)
    gather.hop(1)
    arrived((5,))
    down_copy.wait()
    chunk = 2 * tokens.shape[0]

    def grad_chunk(i):
        return pltpu.make_async_copy(
            outs[5].at[pl.ds(mult(i * chunk, chunk), chunk)], w_out.at[i % 2, pl.ds(0, chunk)], grad_sems.at[i % 2])

    def hidden_step(i, carry):
        grad_chunk(i).wait()

        @pl.when(i < 3)
        def _():
            grad_chunk(i + 1).start()

        grad_hidden[pl.ds(mult(i * chunk, chunk), chunk)] = dot_nt(w_out[i % 2, :chunk], down[...])

        @pl.when(i == 2)
        def _():
            gather.hop(2)
        return carry

    grad_chunk(0).start()
    lax.fori_loop(0, 4, hidden_step, 0)
    for m in near:
        slices_from_plane(m, 1)
    for k in range(3):
        share(k, "wait_send")
    gather.hop(3)
    gather.finish()
    for a in range(7):
        to_core(a, 0, zpos, core, "wait_send", src=ins[a])
    for which in range(2):
        own_slice(which, 1).wait()
        for m in near:
            slice_copy(m, which).wait_send()
    for m in near:
        for which in range(2):
            slice_plane(m, which, rep, 0, xrep).wait_send()
            slice_plane(m, which, rep, 1, yrep).wait_send()
            slice_plane(m, which, *onward(m)).wait_send()
            slice_plane(m, which, drep, 2, drep).wait_recv()
    for way in range(2):
        for h in range(3):
            z = zpos - h if way == 0 else zpos + h

            @pl.when((z >= 0) & (zpos < 3) if way == 0 else (z <= 3) & (zpos > 0))
            def _():
                for a in range(6):
                    hop(a, way, h, z, "wait_send")
    for h in range(1, 4):
        for way in range(2):
            z = zpos - h if way == 0 else zpos + h
            k = way * 3 + h - 1

            @pl.when(z >= 0 if way == 0 else z <= 3)
            def _():
                for a in range(4):
                    to_plane(a, k, z, rep, "wait_send", (xsend, xrecv), xrep)
                    to_plane(a, k, z, rep, "wait_send", (ysend, yrecv), yrep)
                    to_plane(a, k, z, xrep if a == 0 else yrep, "wait_send", (dsend, drecv), yrep)
                for a in range(7):
                    to_core(a, k + 1, z, core, "wait_send")

def start_gather(cid, scale, weights, gate, up, tokens, bias, turns, w_down):
    low, wide = jnp.bfloat16, jnp.float32
    rows, width = tokens.shape
    strip = (w_down.shape[0] // 128 + 1) * 128
    attn_out, query_down, latent_down, query_up, latent_up = weights[:5]
    tiles = query_up.shape[1]
    keys = bias.shape[1]
    out = [jax.ShapeDtypeStruct((a.shape[0] * 8,) + a.shape[1:], a.dtype) for a in weights]
    out += [jax.ShapeDtypeStruct((gate.shape[0] * 8, strip), gate.dtype)] * 2
    latent_rank = 8 * latent_up.shape[0]
    found = [((rows, width), low), ((rows, query_down.shape[1]), low), ((keys, latent_rank), low), ((keys, 128), low),
             ((keys, tiles), low), ((rows, tiles), low), ((rows, tiles // 2), low), ((rows, 128), wide),
             ((rows, query_down.shape[1]), wide), ((rows, latent_down.shape[1]), wide), ((rows, width), wide),
             ((8 * rows, width), low), ((8 * rows, strip), wide), ((strip, width), low)]
    out += [jax.ShapeDtypeStruct(s, d) for s, d in found]
    whole = [pltpu.VMEM((a.shape[0] * 8, a.shape[1]), a.dtype) for a in (query_down, latent_down, query_up, latent_up)]
    return pl.pallas_call(
        functools.partial(start_kernel, scale), out_shape=out,
        in_specs=[ANY] * 9 + [VMEM] * 3 + [ANY], out_specs=[ANY] * 9 + [VMEM] * 11 + [ANY, VMEM, VMEM],
        scratch_shapes=[dma_sems(2, 3, 6), dma_sems(2, 3, 6)] + [dma_sems(6, 4)] * 6
        + [dma_sems(7, 7), dma_sems(7, 7), dma_sems(2, 9), dma_sems(7, 2), dma_sems(7, 2), dma_sems(3, 7, 2), dma_sems(3, 7, 2)]
        + [pltpu.VMEM(a.shape, a.dtype) for a in weights] + [pltpu.VMEM((gate.shape[0], strip), gate.dtype)] * 2
        + [pltpu.VMEM((8 * weights[6].shape[0], 128), wide), pltpu.VMEM(weights[6].shape, wide)] + whole
        + [pltpu.VMEM((2, 2 * attn_out.shape[0], width), low), pltpu.VMEM((rows, tiles), wide),
           pltpu.VMEM((rows, width), low), dma_sems(3, 2), dma_sems(3, 2), dma_sems(6), dma_sems(2), dma_sems(1)] + Gather.scratch(1),
        compiler_params=kernel_params(cid),
    )(*weights, gate, up, tokens, bias, turns, w_down)

def plane_swap(values, j):
    return lax.ppermute(values, "rep", [(i, i ^ j) for i in range(4)])


def column_body(
    tokens,
    cotangent,
    doc_lengths,
    gain_attn,
    query_down,
    gain_query,
    query_up,
    latent_down,
    gain_latent,
    latent_up,
    attn_out,
    gain_ffn,
    w_gate,
    w_up,
    w_down,
):
    low = jnp.bfloat16
    wide = jnp.float32
    rows, width = tokens.shape[1], tokens.shape[2]
    seq_len = rows * 4
    head_dim = ND + RD
    scale = head_dim ** (-0.5)
    rep, shard = lax.axis_index("rep"), lax.axis_index("shard")
    slice_ff = FF // 8
    strip = 896
    shift = (slice_ff * shard) % 128

    gain_list = (gain_attn, gain_ffn, gain_query, gain_latent)
    small = jnp.concatenate(
        [
            jnp.where(
                jnp.arange(8 * v.shape[0], dtype=jnp.int32) // v.shape[0] == shard,
                jnp.tile(v.astype(wide), 8),
                0.0,
            )
            for v in gain_list
        ]
    ).reshape(-1, 128)
    tile_up = jnp.pad(
        query_up.reshape(-1, H, head_dim), ((0, 0), (0, 0), (0, 128 - head_dim))
    ).reshape(-1, H * 128)
    grad_out = cotangent[0].astype(wide)
    grad_down_in = (residual_scale * grad_out).astype(low)
    local_pos = rep * rows + jnp.arange(rows, dtype=jnp.int32)
    key_pos = jnp.concatenate(
        [(rep ^ j) * rows + jnp.arange(rows, dtype=jnp.int32) for j in range(4)]
    )
    query_seg, query_off = segment_of(doc_lengths[0], local_pos)
    key_seg = segment_of(doc_lengths[0], key_pos)[0]
    allowed = (query_seg[:, None] == key_seg[None, :]) & (key_pos[None, :] <= local_pos[:, None])
    bias = jnp.where(allowed, 0.0, masked_score).astype(wide)
    cos_part, sin_part = rope_tables(query_off, RD)
    none = jnp.zeros((rows, RD // 2), wide)
    edge = jnp.zeros((rows, ND), wide)
    tail = jnp.zeros((rows, 128 - head_dim), wide)
    turns = jnp.stack(
        [
            jnp.concatenate([edge + 1.0, cos_part, cos_part, tail], axis=1),
            jnp.concatenate([edge, none, sin_part, tail], axis=1),
            jnp.concatenate([edge, -sin_part, none, tail], axis=1),
        ]
    )
    (
        aout,
        qdown,
        ldown,
        qup,
        lup,
        gd_all,
        small_all,
        gate_w,
        up_w,
        normed_low,
        query_low,
        latent_low,
        rope_tile,
        keyvals,
        queries,
        mixed_low,
        logs,
        query_lat,
        latent_proj,
        residual,
        ffn_all,
        grad_hidden,
        down_w,
    ) = start_gather(
        0,
        scale,
        (attn_out, query_down, latent_down, tile_up, latent_up, grad_down_in, small),
        w_gate,
        w_up,
        tokens[0],
        bias,
        turns,
        w_down,
    )
    gains_all = jnp.sum(small_all.reshape((8,) + small.shape), axis=0)
    gain_f = gains_all[width // 128 : 2 * width // 128].reshape(-1)
    norm_f_back = jax.vjp(rms_scale, residual, gain_f)[1]

    gate_pre = jnp.dot(ffn_all, gate_w, preferred_element_type=wide)
    up_pre = jnp.dot(ffn_all, up_w, preferred_element_type=wide)
    hidden, act_back = jax.vjp(swiglu, gate_pre, up_pre)
    hidden_low = hidden.astype(low)
    grad_gate_f, grad_up_f = act_back(grad_hidden)
    grad_gate = grad_gate_f.astype(low)
    grad_up = grad_up_f.astype(low)
    down_part = inner_rows(hidden_low, gd_all).astype(low)
    grad_ffn_in, down_own, gate_own, up_part = back_sums(
        2, down_part, ffn_all, grad_gate, grad_up, gate_w, up_w, slice_ff
    )

    grad_res_norm, grad_gain_ffn = norm_f_back(grad_ffn_in)
    grad_resid = grad_out + grad_res_norm
    grad_branch = (residual_scale * grad_resid).astype(low)
    cols = jnp.stack([mixed_low, normed_low]).reshape(2, rows, 8, width // 8).transpose(2, 0, 1, 3)
    (
        branch_all,
        cols_all,
        down_all,
        gate_all,
        up_own,
        qup_part,
        lup_part,
        tokens_grad,
        grad_lats,
        gain_terms,
    ) = middle_exchange(
        3,
        scale,
        gate_own,
        grad_branch,
        cols,
        down_own,
        up_part,
        (aout, qup, lup, qdown, ldown),
        query_low,
        latent_low,
        (queries, keyvals, rope_tile, bias, turns, logs),
        (
            tokens[0],
            query_lat,
            latent_proj,
            gains_all,
            grad_resid,
            grad_gain_ffn.reshape(-1, 128),
        ),
    )

    up_all, out_sum, aout_own, lat_own, lup_own, qup_own, gain_own = last_sums(
        4,
        up_own,
        grad_lats,
        qup_part.reshape(8, -1, qup_part.shape[1]),
        lup_part.reshape(8, -1, lup_part.shape[1]),
        hidden_low,
        down_w,
        branch_all.reshape(8, rows, width),
        cols_all,
        gain_terms,
    )
    layer_out = (residual + residual_scale * out_sum).astype(low)
    query_rank = query_down.shape[1]
    gate_grad, up_grad, down_grad, aout_own, qdown_own, ldown_own, lup_own, qup_own = widen(
        gate_all, up_all, down_all, aout_own, lat_own, lup_own, qup_own, FF, query_rank, H
    )
    gain_own = gain_own.reshape(-1)
    owned, first = [], 0
    for v in gain_list:
        owned.append(lax.dynamic_slice(gain_own, (first + shard * v.shape[0],), (v.shape[0],)))
        first += 8 * v.shape[0]

    return (
        layer_out[None],
        tokens_grad[None],
        owned[0],
        qdown_own,
        owned[2],
        qup_own,
        ldown_own,
        owned[3],
        lup_own,
        aout_own,
        owned[1],
        gate_grad,
        up_grad,
        down_grad,
    )


def body(
    tokens,
    cotangent,
    doc_lengths,
    gain_attn,
    query_down,
    gain_query,
    query_up,
    latent_down,
    gain_latent,
    latent_up,
    attn_out,
    gain_ffn,
    w_gate,
    w_up,
    w_down,
):
    low_type = jnp.bfloat16
    wide_type = jnp.float32
    tok_rows = tokens.shape[1]
    seq_len = tok_rows * lax.axis_size("rep")
    head_dim = ND + RD
    group_size = math.gcd(H, 8)
    group_count = H // group_size
    softmax_scale = head_dim ** (-0.5)
    local_pos = lax.axis_index("rep") * tok_rows + jnp.arange(tok_rows, dtype=jnp.int32)
    key_pos = jnp.arange(seq_len, dtype=jnp.int32)
    query_seg, query_off = segment_of(doc_lengths[0], local_pos)
    key_seg = segment_of(doc_lengths[0], key_pos)[0]
    allowed = (query_seg[:, None] == key_seg[None, :]) & (key_pos[None, :] <= local_pos[:, None])
    cos_part, sin_part = rope_tables(query_off, RD)
    (
        gain_in_full,
        qdown_full,
        gain_q_full,
        qup_full,
        ldown_full,
        gain_l_full,
        lup_full,
        aout_full,
        gain_f_full,
    ) = (
        lax.all_gather(gain_attn, "shard", axis=0, tiled=True),
        lax.all_gather(query_down, "shard", axis=0, tiled=True),
        lax.all_gather(gain_query, "shard", axis=0, tiled=True),
        lax.all_gather(query_up, "shard", axis=0, tiled=True),
        lax.all_gather(latent_down, "shard", axis=0, tiled=True),
        lax.all_gather(gain_latent, "shard", axis=0, tiled=True),
        lax.all_gather(latent_up, "shard", axis=0, tiled=True),
        lax.all_gather(attn_out, "shard", axis=0, tiled=True),
        lax.all_gather(gain_ffn, "shard", axis=0, tiled=True),
    )
    inputs = tokens[0].astype(wide_type)
    normed, norm_in_back = jax.vjp(rms_scale, inputs, gain_in_full.astype(wide_type))
    normed_low = normed.astype(low_type)
    query_lat = jnp.dot(normed_low, qdown_full, preferred_element_type=wide_type)
    query_norm, norm_q_back = jax.vjp(rms_scale, query_lat, gain_q_full.astype(wide_type))
    query_low = query_norm.astype(low_type)
    query_proj = jnp.dot(query_low, qup_full, preferred_element_type=wide_type).reshape(
        tok_rows, H, head_dim
    )

    def query_rope(values):
        return jnp.concatenate(
            [
                values[..., :ND],
                rotate(values[..., ND:], cos_part[:, None, :], sin_part[:, None, :]),
            ],
            axis=-1,
        )

    query_rot, query_back = jax.vjp(query_rope, query_proj)
    query_used = query_rot.astype(low_type)
    latent_proj = jnp.dot(normed_low, ldown_full, preferred_element_type=wide_type)
    latent_norm, norm_l_back = jax.vjp(
        rms_scale, latent_proj[:, :KR], gain_l_full.astype(wide_type)
    )
    latent_low = latent_norm.astype(low_type)

    def key_rotate(values):
        return rotate(values, cos_part, sin_part)

    key_rot, key_back = jax.vjp(key_rotate, latent_proj[:, KR:])
    key_rope = key_rot.astype(low_type)
    keyvals = jnp.dot(latent_low, lup_full, preferred_element_type=wide_type).astype(low_type)
    all_keyvals, all_rope = (
        lax.all_gather(keyvals, "rep", axis=0, tiled=True),
        lax.all_gather(key_rope, "rep", axis=0, tiled=True),
    )
    queries = query_used.reshape(tok_rows, group_count, group_size, head_dim).transpose(1, 0, 2, 3)
    key_groups = all_keyvals.reshape(seq_len, group_count, group_size, ND + VD).transpose(
        1, 0, 2, 3
    )

    def scores_of(query_blk, key_blk):
        nope_part = jnp.einsum(
            "thd,shd->hts", query_blk[..., :ND], key_blk[..., :ND], preferred_element_type=wide_type
        )
        rope_part = jnp.einsum(
            "thd,sd->hts", query_blk[..., ND:], all_rope, preferred_element_type=wide_type
        )
        return jnp.where(allowed[None], (nope_part + rope_part) * softmax_scale, masked_score)

    def forward_group(carry, blocks):
        query_blk, key_blk = blocks
        scores = scores_of(query_blk, key_blk)
        row_max = jnp.max(scores, axis=-1, keepdims=True)
        exp_scores = jnp.exp(scores - row_max)
        totals = jnp.sum(exp_scores, axis=-1, keepdims=True)
        probs = (exp_scores / totals).astype(low_type)
        mixed = jnp.einsum(
            "hts,shd->thd", probs, key_blk[..., ND:], preferred_element_type=wide_type
        )
        return (carry, (mixed, row_max + jnp.log(totals)))

    start_carry = jnp.zeros((), wide_type)
    final_carry, (mixed_groups, log_totals) = lax.scan(
        forward_group, start_carry, (queries, key_groups)
    )
    mixed_low = mixed_groups.transpose(1, 0, 2, 3).reshape(tok_rows, H * VD).astype(low_type)
    branch = jnp.dot(mixed_low, aout_full, preferred_element_type=wide_type)
    residual = inputs + residual_scale * branch
    normed_ffn, norm_f_back = jax.vjp(rms_scale, residual, gain_f_full.astype(wide_type))
    ffn_low = normed_ffn.astype(low_type)
    gate_full, up_full, down_full = (
        lax.all_gather(w_gate, "shard", axis=0, tiled=True),
        lax.all_gather(w_up, "shard", axis=0, tiled=True),
        lax.all_gather(w_down, "shard", axis=0, tiled=True),
    )
    gate_pre = jnp.dot(ffn_low, gate_full, preferred_element_type=wide_type)
    up_pre = jnp.dot(ffn_low, up_full, preferred_element_type=wide_type)
    hidden, act_back = jax.vjp(swiglu, gate_pre, up_pre)
    hidden_low = hidden.astype(low_type)
    ffn_branch = jnp.dot(hidden_low, down_full, preferred_element_type=wide_type)
    layer_out = residual + residual_scale * ffn_branch
    grad_out = cotangent[0].astype(wide_type)
    grad_down_in = (residual_scale * grad_out).astype(low_type)
    gate_back_w, up_back_w, down_back_w = (
        lax.all_gather(w_gate, "shard", axis=0, tiled=True),
        lax.all_gather(w_up, "shard", axis=0, tiled=True),
        lax.all_gather(w_down, "shard", axis=0, tiled=True),
    )
    grad_hidden = outer_cols(grad_down_in, down_back_w)
    grad_gate_f, grad_up_f = act_back(grad_hidden)
    grad_gate = grad_gate_f.astype(low_type)
    grad_up = grad_up_f.astype(low_type)
    grad_ffn_in = outer_cols(grad_gate, gate_back_w) + outer_cols(grad_up, up_back_w)
    down_grad = lax.psum_scatter(
        inner_rows(hidden_low, grad_down_in).astype(jnp.bfloat16),
        "shard",
        scatter_dimension=0,
        tiled=True,
    )
    gate_up_in = jnp.concatenate([grad_gate, grad_up], axis=1)
    gate_up_grad = lax.psum_scatter(
        inner_rows(ffn_low, gate_up_in).astype(jnp.bfloat16),
        "shard",
        scatter_dimension=0,
        tiled=True,
    ).astype(jnp.float32)
    gate_grad = gate_up_grad[:, :FF]
    up_grad = gate_up_grad[:, FF:]
    grad_res_norm, grad_gain_ffn = norm_f_back(grad_ffn_in)
    grad_resid = grad_out + grad_res_norm
    qdown_back, qup_back, ldown_back, lup_back, aout_back = (
        lax.all_gather(query_down, "shard", axis=0, tiled=True),
        lax.all_gather(query_up, "shard", axis=0, tiled=True),
        lax.all_gather(latent_down, "shard", axis=0, tiled=True),
        lax.all_gather(latent_up, "shard", axis=0, tiled=True),
        lax.all_gather(attn_out, "shard", axis=0, tiled=True),
    )
    grad_branch = (residual_scale * grad_resid).astype(low_type)
    aout_grad = inner_rows(mixed_low, grad_branch)
    grad_mixed = outer_cols(grad_branch, aout_back).astype(low_type)
    grad_groups = grad_mixed.reshape(tok_rows, group_count, group_size, VD).transpose(1, 0, 2, 3)

    def backward_group(rope_acc, blocks):
        query_blk, key_blk, grad_blk, log_blk = blocks
        scores = scores_of(query_blk, key_blk)
        probs = jnp.exp(scores - log_blk)
        grad_probs = jnp.einsum(
            "thd,shd->hts", grad_blk, key_blk[..., ND:], preferred_element_type=wide_type
        )
        delta = jnp.sum(probs * grad_probs, axis=-1, keepdims=True)
        grad_scores = (probs * (grad_probs - delta)).astype(low_type)
        grad_query = (
            jnp.concatenate(
                [
                    jnp.einsum(
                        "hts,shd->thd",
                        grad_scores,
                        key_blk[..., :ND],
                        preferred_element_type=wide_type,
                    ),
                    jnp.einsum(
                        "hts,sd->thd", grad_scores, all_rope, preferred_element_type=wide_type
                    ),
                ],
                axis=-1,
            )
            * softmax_scale
        )
        grad_key = (
            jnp.einsum(
                "hts,thd->shd", grad_scores, query_blk[..., :ND], preferred_element_type=wide_type
            )
            * softmax_scale
        )
        grad_value = jnp.einsum(
            "hts,thd->shd", probs.astype(low_type), grad_blk, preferred_element_type=wide_type
        )
        rope_acc = (
            rope_acc
            + jnp.einsum(
                "hts,thd->sd", grad_scores, query_blk[..., ND:], preferred_element_type=wide_type
            )
            * softmax_scale
        )
        return (rope_acc, (grad_query, jnp.concatenate([grad_key, grad_value], axis=-1)))

    rope_start = jnp.zeros((seq_len, RD), wide_type)
    rope_sum, (grad_q_groups, grad_kv_groups) = lax.scan(
        backward_group, rope_start, (queries, key_groups, grad_groups, log_totals)
    )
    grad_kv_all = grad_kv_groups.transpose(1, 0, 2, 3).reshape(seq_len, H * (ND + VD))
    grad_kv_own, grad_rope_own = (
        lax.psum_scatter(
            grad_kv_all.astype(jnp.bfloat16), "rep", scatter_dimension=0, tiled=True
        ).astype(jnp.float32),
        lax.psum_scatter(
            rope_sum.astype(jnp.bfloat16), "rep", scatter_dimension=0, tiled=True
        ).astype(jnp.float32),
    )
    grad_q_full = grad_q_groups.transpose(1, 0, 2, 3).reshape(tok_rows, H, head_dim)
    grad_q_proj = query_back(grad_q_full)[0].reshape(tok_rows, H * head_dim).astype(low_type)
    qup_grad = inner_rows(query_low, grad_q_proj)
    grad_q_lat_f, grad_gain_query = norm_q_back(outer_cols(grad_q_proj, qup_back))
    grad_q_lat = grad_q_lat_f.astype(low_type)
    grad_kv_low = grad_kv_own.astype(low_type)
    lup_grad = inner_rows(latent_low, grad_kv_low)
    grad_lat_c, grad_gain_latent = norm_l_back(outer_cols(grad_kv_low, lup_back))
    grad_lat_r = key_back(grad_rope_own)[0]
    grad_lat = jnp.concatenate([grad_lat_c, grad_lat_r], axis=1).astype(low_type)
    qdown_grad = inner_rows(normed_low, grad_q_lat)
    ldown_grad = inner_rows(normed_low, grad_lat)
    grad_normed = outer_cols(grad_q_lat, qdown_back) + outer_cols(grad_lat, ldown_back)
    grad_in_norm, grad_gain_attn = norm_in_back(grad_normed)
    tokens_grad = (grad_resid + grad_in_norm).astype(low_type)
    (
        owned_gain_attn,
        owned_qdown,
        owned_gain_query,
        owned_qup,
        owned_ldown,
        owned_gain_latent,
        owned_lup,
        owned_aout,
        owned_gain_ffn,
    ) = (
        lax.psum_scatter(
            grad_gain_attn.astype(jnp.bfloat16), "shard", scatter_dimension=0, tiled=True
        ).astype(jnp.float32),
        lax.psum_scatter(
            qdown_grad.astype(jnp.bfloat16), "shard", scatter_dimension=0, tiled=True
        ).astype(jnp.float32),
        lax.psum_scatter(
            grad_gain_query.astype(jnp.bfloat16), "shard", scatter_dimension=0, tiled=True
        ).astype(jnp.float32),
        lax.psum_scatter(
            qup_grad.astype(jnp.bfloat16), "shard", scatter_dimension=0, tiled=True
        ).astype(jnp.float32),
        lax.psum_scatter(
            ldown_grad.astype(jnp.bfloat16), "shard", scatter_dimension=0, tiled=True
        ).astype(jnp.float32),
        lax.psum_scatter(
            grad_gain_latent.astype(jnp.bfloat16), "shard", scatter_dimension=0, tiled=True
        ).astype(jnp.float32),
        lax.psum_scatter(
            lup_grad.astype(jnp.bfloat16), "shard", scatter_dimension=0, tiled=True
        ).astype(jnp.float32),
        lax.psum_scatter(
            aout_grad.astype(jnp.bfloat16), "shard", scatter_dimension=0, tiled=True
        ).astype(jnp.float32),
        lax.psum_scatter(
            grad_gain_ffn.astype(jnp.bfloat16), "shard", scatter_dimension=0, tiled=True
        ).astype(jnp.float32),
    )
    summed = (
        lax.psum(owned_gain_attn.astype(jnp.bfloat16), "rep").astype(jnp.float32),
        lax.psum(owned_qdown.astype(jnp.bfloat16), "rep").astype(jnp.float32),
        lax.psum(owned_gain_query.astype(jnp.bfloat16), "rep").astype(jnp.float32),
        lax.psum(owned_qup.astype(jnp.bfloat16), "rep").astype(jnp.float32),
        lax.psum(owned_ldown.astype(jnp.bfloat16), "rep").astype(jnp.float32),
        lax.psum(owned_gain_latent.astype(jnp.bfloat16), "rep").astype(jnp.float32),
        lax.psum(owned_lup.astype(jnp.bfloat16), "rep").astype(jnp.float32),
        lax.psum(owned_aout.astype(jnp.bfloat16), "rep").astype(jnp.float32),
        lax.psum(owned_gain_ffn.astype(jnp.bfloat16), "rep").astype(jnp.float32),
        lax.psum(gate_grad.astype(jnp.bfloat16), "rep").astype(jnp.float32),
        lax.psum(up_grad.astype(jnp.bfloat16), "rep").astype(jnp.float32),
        lax.psum(down_grad, "rep").astype(jnp.float32),
    )
    return (
        layer_out.astype(low_type)[None],
        tokens_grad[None],
        summed[0],
        summed[1],
        summed[2],
        summed[3],
        summed[4],
        summed[5],
        summed[6],
        summed[7],
        summed[8],
        summed[9],
        summed[10],
        summed[11],
    )


def solution(mesh):
    placed = (
        P("shard", "rep", None),
        P("shard", "rep", None),
        P("shard", None),
        P("shard"),
        P("shard", None),
        P("shard"),
        P("shard", None),
        P("shard", None),
        P("shard"),
        P("shard", None),
        P("shard", None),
        P("shard"),
        P("shard", None),
        P("shard", None),
        P("shard", None),
    )
    fits = mesh.shape["rep"] == 4 and mesh.shape["shard"] == 8
    return jax.shard_map(
        column_body if fits else body,
        mesh=mesh,
        in_specs=placed,
        out_specs=(
            P("shard", "rep", None),
            P("shard", "rep", None),
            P("shard"),
            P("shard", None),
            P("shard"),
            P("shard", None),
            P("shard", None),
            P("shard"),
            P("shard", None),
            P("shard", None),
            P("shard"),
            P("shard", None),
            P("shard", None),
            P("shard", None),
        ),
        check_vma=False,
    )
```

```python
import functools
import math

import jax
import jax.numpy as jnp
from jax import lax
from jax.experimental import pallas as pl
from jax.experimental.pallas import tpu as pltpu
from jax.sharding import PartitionSpec as P

KR = 256
H = 40
ND = 64
RD = 32
VD = 64
FF = 6400


epsilon = 1e-05
residual_scale = 1.4 / math.sqrt(62.0)
rope_base = 10000.0
masked_score = -1e30


def rms_scale(values, gain):
    return values * lax.rsqrt(jnp.mean(values * values, axis=-1, keepdims=True) + epsilon) * gain


def rotate(values, cos_part, sin_part):
    midpoint = values.shape[-1] // 2
    former = values[..., :midpoint]
    latter = values[..., midpoint:]
    return jnp.concatenate(
        [former * cos_part - latter * sin_part, latter * cos_part + former * sin_part], axis=-1
    )


def segment_of(lengths, positions):
    doc_ends = jnp.cumsum(lengths)
    doc_starts = doc_ends - lengths
    segment = jnp.sum((positions[:, None] >= doc_ends[None, :]).astype(jnp.int32), axis=1)
    chosen = segment[:, None] == jnp.arange(lengths.shape[0], dtype=jnp.int32)[None, :]
    offsets = positions - jnp.sum(jnp.where(chosen, doc_starts[None, :], 0), axis=1)
    return (segment, offsets)


def rope_tables(offsets, rope_width):
    exponents = jnp.arange(0, rope_width, 2, dtype=jnp.float32) / rope_width
    angles = offsets.astype(jnp.float32)[:, None] * (rope_base ** (-exponents))[None, :]
    return (jnp.cos(angles), jnp.sin(angles))


def swiglu(gate_vals, up_vals):
    return jax.nn.silu(gate_vals) * up_vals


def inner_rows(leading, trailing):
    return lax.dot_general(
        leading, trailing, (((0,), (0,)), ((), ())), preferred_element_type=jnp.float32
    )


def outer_cols(leading, trailing):
    return lax.dot_general(
        leading, trailing, (((1,), (1,)), ((), ())), preferred_element_type=jnp.float32
    )


MESH = pl.DeviceIdType.MESH
ANY = pl.BlockSpec(memory_space=pl.ANY)

def place():
    rep = lax.axis_index("rep")
    shard = lax.axis_index("shard")
    zpos, core = shard // 2, shard % 2
    return rep, zpos, core

def mult(value, by):
    return pl.multiple_of(value, by)

def greet(rep, zpos, core, plane=0, column=False):
    barrier = pltpu.get_barrier_semaphore()
    shard = zpos * 2 + core

    def signal(r, s):
        pl.semaphore_signal(barrier, inc=1, device_id=(r, s), device_id_type=MESH)

    if column:
        for m in range(1, 8):
            signal(rep, column_place(zpos, core, m))
        count = 7
    else:
        signal(rep, zpos * 2 + 1 - core)

        @pl.when(zpos > 0)
        def _():
            signal(rep, shard - 2)

        @pl.when(zpos < 3)
        def _():
            signal(rep, shard + 2)

        count = 1 + jnp.minimum(zpos, 1) + jnp.minimum(3 - zpos, 1)
    if plane:
        for other in plane_places(rep)[:plane]:
            signal(other, shard)
        count = count + plane
    pl.semaphore_wait(barrier, count)


def plane_places(rep):
    return rep + 1 - 2 * (rep % 2), (rep + 2) % 4, 3 - rep


def column_place(zpos, core, m, back=False):
    step = 4 - m // 2 if back else m // 2
    return ((zpos + step) % 4) * 2 + (core + m) % 2


def remote(src, dst, ssem, rsem, r, s):
    return pltpu.make_async_remote_copy(
        src_ref=src, dst_ref=dst, send_sem=ssem, recv_sem=rsem, device_id=(r, s), device_id_type=MESH
    )


def dma_sems(*dims):
    return pltpu.SemaphoreType.DMA(dims)


def head_tile(h):
    return pl.ds(pl.multiple_of(h * 128, 128), 128)


def turn(values, tables, back=False):
    keep, high, low_part = tables
    if back:
        return values * keep + pltpu.roll(values * high, 112, 1) + pltpu.roll(values * low_part, 16, 1)
    return values * keep + pltpu.roll(values, 16, 1) * high + pltpu.roll(values, 112, 1) * low_part


def dot_nt(a, b):
    return lax.dot_general(a, b, (((1,), (1,)), ((), ())), preferred_element_type=jnp.float32)


def dot_tn(a, b):
    return lax.dot_general(a, b, (((0,), (0,)), ((), ())), preferred_element_type=jnp.float32)


def attend_heads(scale, proj, kv, rope, bias, turns, query, mixed, logs):
    low = jnp.bfloat16
    lane = lax.broadcasted_iota(jnp.int32, (1, 128), 1)
    first = lane < 64

    def group(i, carry):
        heads_here = [4 * i + j for j in range(4)]
        queries = [turn(proj[:, head_tile(h)], (turns[0], turns[1], turns[2])).astype(low) for h in heads_here]
        keyvals = [kv[:, head_tile(h)] for h in heads_here]
        scores = [dot_nt(q, jnp.where(first, keyval, rope[...])) * scale + bias[...] for q, keyval in zip(queries, keyvals)]
        tops = [jnp.max(s, axis=1, keepdims=True) for s in scores]
        grown = [jnp.exp(s - top) for s, top in zip(scores, tops)]
        totals = [jnp.sum(g, axis=1, keepdims=True) for g in grown]
        outs = [jnp.dot((g / total).astype(low), keyval, preferred_element_type=jnp.float32)
                for g, total, keyval in zip(grown, totals, keyvals)]
        for h, q, top, total in zip(heads_here, queries, tops, totals):
            query[:, head_tile(h)] = q
            logs[...] = jnp.where(lane == h, top + jnp.log(total), logs[...])
        for j in range(2):
            mixed[:, head_tile(2 * i + j)] = jnp.where(first, pltpu.roll(outs[2 * j], 64, 1), outs[2 * j + 1]).astype(low)
        return carry

    return group


def attend_back_heads(scale, query, kv, rope, bias, turns, logs, grad, grad_query, grad_packed, grad_kv, grad_rope, left):
    low = jnp.bfloat16
    rows = query.shape[0]
    lane = lax.broadcasted_iota(jnp.int32, (1, 128), 1)
    first = lane < 64

    def one(h, grad_value):
        q = query[:, head_tile(h)]
        keyval = kv[:, head_tile(h)]
        key = jnp.where(first, keyval, rope[...])
        left[0:rows, 0:128] = q
        left[rows:, 128:256] = grad_value
        both = dot_nt(left[...], jnp.concatenate([key, keyval], axis=1))
        log = jnp.sum(jnp.where(lane == h, logs[...], 0.0), axis=1, keepdims=True)
        probs = jnp.exp(both[:rows] * scale + bias[...] - log)
        weighed = probs * both[rows:]
        delta = jnp.sum(weighed, axis=1, keepdims=True)
        grad_scores = (weighed - probs * delta).astype(low)
        grad_q = jnp.dot(grad_scores, key, preferred_element_type=jnp.float32) * scale
        grad_q = turn(grad_q, (turns[0], turns[1], turns[2]), True)
        grad_query[:, head_tile(h)] = grad_q.astype(low)
        out = dot_tn(jnp.concatenate([grad_scores, probs.astype(low)], axis=0), left[...])
        grad_key = out[:, :128] * scale
        grad_rope[...] += grad_key
        grad_kv[:, head_tile(h)] = jnp.where(first, grad_key, out[:, 128:]).astype(low)
        return grad_q

    def quarter(i, carry):
        rotary = jnp.zeros((rows, 128), jnp.float32)
        for j in range(5):
            both = grad[:, head_tile(5 * i + j)].astype(jnp.float32)
            even = one(10 * i + 2 * j, jnp.where(first, 0.0, pltpu.roll(both, 64, 1)).astype(low))
            odd = one(10 * i + 2 * j + 1, jnp.where(first, 0.0, both).astype(low))
            grad_packed[:, head_tile(8 * i + j)] = jnp.where(first, even, pltpu.roll(odd, 64, 1)).astype(low)
            for k, got in ((2 * j, even), (2 * j + 1, odd)):
                at = 32 * (k % 4)
                moved = got if at == 64 else pltpu.roll(got, (at + 64) % 128, 1)
                rotary = jnp.where((lane >= at) & (lane < at + 32), moved, rotary)
                if k % 4 == 3 or k == 9:
                    grad_packed[:, head_tile(8 * i + 5 + k // 4)] = rotary.astype(low)
                    rotary = jnp.zeros((rows, 128), jnp.float32)
        return carry

    return quarter


def unpacked(packed, heads):
    pieces = []
    for h in range(heads):
        first, k = h // 10 * 1024, h % 10
        pieces.append(packed[:, first + 64 * k : first + 64 * k + 64])
        pieces.append(packed[:, first + 640 + 32 * k : first + 672 + 32 * k])
    return jnp.concatenate(pieces, axis=1)


def widen_kernel(heads, gate, up, down, attn_out, lat, latent_up, query_up, *outs):
    wide = jnp.float32
    for strips, out in zip((gate, up), outs[:2]):
        each = out.shape[1] // 8
        for s in range(8):
            first, last = s * each // 128, (s + 1) * each // 128
            tiles = strips[s, 0].astype(wide)
            if s * each % 128:
                shared = strips[s - 1, 0, :, (first - (s - 1) * each // 128) * 128 :][:, :128]
                out[:, first * 128 : first * 128 + 128] = tiles[:, :128] + shared.astype(wide)
                first_full = first + 1
            else:
                first_full = first
            out[:, first_full * 128 : last * 128] = tiles[:, (first_full - first) * 128 : (last - first) * 128]
    down_out, attn_out_out, query_down_out, latent_down_out, latent_up_out, query_up_out = outs[2:]
    down_out[...] = down[...].astype(wide)
    attn_out_out[...] = attn_out[...].astype(wide)
    rank = query_down_out.shape[1]
    query_down_out[...] = lat[0, :, :rank].astype(wide)
    latent_down_out[...] = lat[0, :, rank:].astype(wide)

    @pl.when(pl.program_id(0) == 0)
    def _():
        latent_up_out[...] = latent_up[...].astype(wide)
        query_up_out[...] = unpacked(query_up[...], heads).astype(wide)


def widen(gate, up, down, attn_out, lat, latent_up, query_up, cols, rank, heads):
    _, quarters, rows, strip = gate.shape
    width = attn_out.shape[1]
    whole = lambda a: pl.BlockSpec(a, lambda q: (0, 0))
    by_rows = lambda c: pl.BlockSpec((rows, c), lambda q: (q, 0))
    by_cols = pl.BlockSpec((down.shape[0], width // quarters), lambda q: (0, q))
    strips = pl.BlockSpec((8, 1, rows, strip), lambda q: (0, q, 0, 0))
    shapes = [(quarters * rows, cols)] * 2 + [down.shape, attn_out.shape, (quarters * rows, rank),
                                              (quarters * rows, lat.shape[2] - rank), latent_up.shape, (query_up.shape[0], heads * 96)]
    return pl.pallas_call(
        functools.partial(widen_kernel, heads), grid=(quarters,),
        out_shape=[jax.ShapeDtypeStruct(s, jnp.float32) for s in shapes],
        in_specs=[strips, strips, by_cols, by_rows(width), pl.BlockSpec((1,) + lat.shape[1:], lambda q: (q, 0, 0)),
                  whole(latent_up.shape), whole(query_up.shape)],
        out_specs=[by_rows(cols)] * 2 + [by_cols, by_rows(width), by_rows(rank), by_rows(lat.shape[2] - rank),
                                         whole(latent_up.shape), whole(shapes[-1])],
        compiler_params=pltpu.CompilerParams(vmem_limit_bytes=56 * 2**20),
    )(gate, up, down, attn_out, lat, latent_up, query_up)


class Gather:
    def __init__(self, ins, outs, sems):
        self.ins, self.outs = ins, outs
        self.zsend, self.zrecv, self.csend, self.crecv, self.own = sems
        self.rep, self.zpos, self.core = place()
        self.held = None

    @staticmethod
    def scratch(n):
        return [dma_sems(2, 3, n), dma_sems(2, 3, n), dma_sems(7, n), dma_sems(7, n), dma_sems(2, n)]

    def at(self, a, z, c):
        rows = self.ins[a].shape[0]
        return self.outs[a].at[pl.ds(mult((z * 2 + c) * rows, rows), rows)]

    def hop_copy(self, a, way, hop, z, src=None):
        dst = self.at(a, z, self.core)
        return remote(dst if src is None else src, dst, self.zsend.at[way, hop, a], self.zrecv.at[way, hop, a],
                      self.rep, (self.zpos + (1 - 2 * way)) * 2 + self.core)

    def core_copy(self, a, slot, z, c, src=None):
        dst = self.at(a, z, c)
        return remote(dst if src is None else src, dst, self.csend.at[slot, a], self.crecv.at[slot, a],
                      self.rep, self.zpos * 2 + 1 - self.core)

    def keep(self, a):
        return pltpu.make_async_copy(self.ins[a], self.at(a, self.zpos, self.core), self.own.at[0, a])

    def onward(self, way):
        return self.zpos < 3 if way == 0 else self.zpos > 0

    def source(self, way, hop):
        z = self.zpos - hop if way == 0 else self.zpos + hop
        return z, (z >= 0 if way == 0 else z <= 3)

    def start(self, which=None):
        which = range(len(self.ins)) if which is None else which
        for way in range(2):
            @pl.when(self.onward(way))
            def _():
                for a in which:
                    self.hop_copy(a, way, 0, self.zpos, src=self.ins[a]).start()
        for a in which:
            self.core_copy(a, 0, self.zpos, self.core, src=self.ins[a]).start()
            self.keep(a).start()

    def hop(self, hop, which=None):
        which = range(len(self.ins)) if which is None else which
        for way in range(2):
            z, there = self.source(way, hop)

            @pl.when(there)
            def _():
                for a in which:
                    self.hop_copy(a, way, hop - 1, z).wait_recv()
                    if hop < 3:
                        @pl.when(self.onward(way))
                        def _():
                            self.hop_copy(a, way, hop, z).start()
                    self.core_copy(a, way * 3 + hop, z, self.core).start()

    def finish(self):
        arrays = range(len(self.ins))
        for way in range(2):
            for hop in range(3):
                z, there = self.source(way, hop)

                @pl.when(there & self.onward(way))
                def _():
                    for a in arrays:
                        self.hop_copy(a, way, hop, z).wait_send()
        for a in arrays:
            self.keep(a).wait()
            self.core_copy(a, 0, self.zpos, self.core, src=self.ins[a]).wait_send()
            self.core_copy(a, 0, self.zpos, 1 - self.core).wait_recv()
        for way in range(2):
            for hop in range(1, 4):
                z, there = self.source(way, hop)

                @pl.when(there)
                def _():
                    for a in arrays:
                        self.core_copy(a, way * 3 + hop, z, self.core).wait_send()
                        self.core_copy(a, way * 3 + hop, z, 1 - self.core).wait_recv()


class Total:
    def __init__(self, term, out, bufs, sems):
        self.term, self.out = term, out
        self.theirs, self.landed = bufs
        self.zsend, self.zrecv, self.csend, self.crecv = sems
        self.rep, self.zpos, self.core = place()

    @staticmethod
    def scratch(term):
        return [pltpu.VMEM((4,) + term.shape[1:], term.dtype), pltpu.VMEM((5,) + term.shape[1:], term.dtype),
                dma_sems(2, 4), dma_sems(2, 4), dma_sems(4), dma_sems(4)]

    @staticmethod
    def split(term, out, refs):
        return Total(term, out, refs[:2], refs[2:6]), refs[6:]

    def pair_copy(self, z):
        return remote(self.term.at[z * 2 + 1 - self.core], self.theirs.at[z], self.csend.at[z], self.crecv.at[z],
                      self.rep, self.zpos * 2 + 1 - self.core)

    def hop_copy(self, way, z):
        return remote(self.theirs.at[z], self.landed.at[z + 1 - way], self.zsend.at[way, z], self.zrecv.at[way, z],
                      self.rep, (self.zpos + (1 - 2 * way)) * 2 + self.core)

    def each(self, step):
        for way in range(2):
            behind = self.zpos if way == 0 else 3 - self.zpos
            target = self.zpos + 3 - step if way == 0 else self.zpos - 3 + step
            yield way, behind, target, (behind <= step) & (behind < 3)

    def start(self):
        for z in (3, 0, 2, 1):
            self.pair_copy(z).start()

    def pair(self):
        for z in (3, 0, 2, 1):
            self.pair_copy(z).wait_recv()

    def both(self, z):
        return self.term[z * 2 + self.core].astype(jnp.float32) + self.theirs[z].astype(jnp.float32)

    def step(self, step):
        for way, behind, target, there in self.each(step):
            @pl.when(there)
            def _():
                total = self.both(target)

                @pl.when(behind == 0)
                def _():
                    self.theirs[target] = total.astype(self.theirs.dtype)

                @pl.when(behind > 0)
                def _():
                    self.hop_copy(way, target).wait_recv()
                    self.theirs[target] = (total + self.landed[target + 1 - way].astype(jnp.float32)).astype(self.theirs.dtype)
                self.hop_copy(way, target).start()

    def finish(self):
        self.out[...] = self.both(self.zpos)
        for way in range(2):
            @pl.when(self.zpos > 0 if way == 0 else self.zpos < 3)
            def _():
                self.hop_copy(way, self.zpos).wait_recv()
                self.out[...] += self.landed[self.zpos + 1 - way].astype(jnp.float32)
        for step in range(3):
            for way, behind, target, there in self.each(step):
                @pl.when(there)
                def _():
                    self.hop_copy(way, target).wait_send()
        for z in range(4):
            self.pair_copy(z).wait_send()


def kernel_params(cid):
    return pltpu.CompilerParams(collective_id=cid, has_side_effects=True, vmem_limit_bytes=58 * 2**20)


VMEM = pl.BlockSpec(memory_space=pltpu.VMEM)


class PlaneSum:
    def __init__(self, items, bufs, sems):
        self.items = items
        self.landed, self.stage, self.last = bufs
        self.asend, self.arecv, self.bsend, self.brecv = sems
        self.rep, self.zpos, self.core = place()
        self.shard = self.zpos * 2 + self.core

    @staticmethod
    def scratch(shapes, dtype):
        n = len(shapes)
        return ([pltpu.VMEM((2,) + s, dtype) for s in shapes] + [pltpu.VMEM(s, dtype) for s in shapes] * 2
                + [dma_sems(n, 2), dma_sems(n, 2), dma_sems(n), dma_sems(n)])

    @staticmethod
    def split(refs, n):
        return (refs[:n], refs[n : 2 * n], refs[2 * n : 3 * n]), refs[3 * n : 3 * n + 4], refs[3 * n + 4 :]

    def ways(self, i):
        xrep, yrep, drep = plane_places(self.rep)
        return (xrep, yrep, drep) if self.items[i][2] == 0 else (yrep, xrep, drep)

    def out(self, i, k):
        near, _, far = self.ways(i)
        return remote(self.items[i][0](far if k else near), self.landed[i].at[k], self.asend.at[i, k], self.arecv.at[i, k],
                      near, self.shard)

    def on(self, i):
        return remote(self.stage[i], self.last[i], self.bsend.at[i], self.brecv.at[i], self.ways(i)[1], self.shard)

    def start(self, which=None):
        for i in range(len(self.items)) if which is None else which:
            for k in (1, 0):
                self.out(i, k).start()

    def middle(self, i):
        wide = jnp.float32
        self.out(i, 1).wait_recv()
        term = self.items[i][0](self.ways(i)[1])
        self.stage[i][...] = (term[...].astype(wide) + self.landed[i][1].astype(wide)).astype(self.stage[i].dtype)
        self.on(i).start()

    def end(self, i):
        wide = jnp.float32
        self.out(i, 0).wait_recv()
        self.on(i).wait_recv()
        total = self.items[i][0](self.rep)[...].astype(wide) + self.landed[i][0].astype(wide)
        own = self.items[i][1]
        own[...] = (total + self.last[i][...].astype(wide)).astype(own.dtype)

    def finish(self):
        for i in range(len(self.items)):
            for k in range(2):
                self.out(i, k).wait_send()
            self.on(i).wait_send()


class PlaneGather:
    def __init__(self, items, sems):
        self.items = items
        self.send, self.recv, self.own = sems
        self.rep, self.zpos, self.core = place()
        self.shard = self.zpos * 2 + self.core

    @staticmethod
    def scratch(n):
        return [dma_sems(3, n), dma_sems(3, n), dma_sems(n)]

    def copy(self, i, kind, quarter, to):
        own, part, _ = self.items[i]
        dst = part(quarter)
        return remote(dst if kind == 2 or own is None else own, dst, self.send.at[kind, i], self.recv.at[kind, i], to, self.shard)

    def keep(self, i):
        return pltpu.make_async_copy(self.items[i][0], self.items[i][1](self.rep), self.own.at[i])

    def start(self, which=None):
        xrep, yrep, _ = plane_places(self.rep)
        for i in range(len(self.items)) if which is None else which:
            self.copy(i, 0, self.rep, xrep).start()
            self.copy(i, 1, self.rep, yrep).start()
            if self.items[i][0] is not None:
                self.keep(i).start()

    def middle(self, i):
        xrep, yrep, _ = plane_places(self.rep)
        self.copy(i, 0, xrep, xrep).wait_recv()
        if self.items[i][2] == 0:
            self.copy(i, 2, xrep, yrep).start()
        self.copy(i, 1, yrep, yrep).wait_recv()
        if self.items[i][2] == 1:
            self.copy(i, 2, yrep, xrep).start()

    def finish(self):
        xrep, yrep, drep = plane_places(self.rep)
        for i, (own, _, first) in enumerate(self.items):
            self.copy(i, 0, self.rep, xrep).wait_send()
            self.copy(i, 1, self.rep, yrep).wait_send()
            self.copy(i, 2, *((xrep, yrep) if first == 0 else (yrep, xrep))).wait_send()
            self.copy(i, 2, drep, drep).wait_recv()
            if own is not None:
                self.keep(i).wait()


class ColumnSwap:
    def __init__(self, items, sems, keeps=True):
        self.items, self.keeps = items, keeps
        self.send, self.recv, self.own = sems
        self.rep, self.zpos, self.core = place()
        self.shard = self.zpos * 2 + self.core

    near = (1, 2, 6, 3, 7, 4, 5)

    @staticmethod
    def scratch(n):
        return [dma_sems(7, n), dma_sems(7, n), dma_sems(n)]

    def copy(self, i, m, back=False):
        s2 = column_place(self.zpos, self.core, m, back)
        block, there = self.items[i]
        return remote(block(s2), there(s2 if back else self.shard), self.send.at[m - 1, i], self.recv.at[m - 1, i], self.rep, s2)

    def keep(self, i):
        return pltpu.make_async_copy(self.items[i][0](self.shard), self.items[i][1](self.shard), self.own.at[i])

    def start(self):
        for m in self.near:
            for i in range(len(self.items)):
                self.copy(i, m).start()
        for i in range(len(self.items) if self.keeps else 0):
            self.keep(i).start()

    def arrive(self, m):
        for i in range(len(self.items)):
            self.copy(i, m, True).wait_recv()

    def finish(self, arrive=True):
        for i in range(len(self.items)):
            if self.keeps:
                self.keep(i).wait()
            for m in self.near:
                self.copy(i, m).wait_send()
                if arrive:
                    self.copy(i, m, True).wait_recv()


class Strips:
    def __init__(self, own, whole, sems):
        rep, zpos, core = place()
        shard = zpos * 2 + core
        self.swap = ColumnSwap([(lambda s: own.at[s], lambda s: whole.at[s, rep])], sems[:2] + [None], keeps=False)

        def part(m):
            return lambda p: whole.at[shard if m == 0 else column_place(zpos, core, m, True), p]

        self.spread = PlaneGather([(None if m else own.at[shard], part(m), m % 2) for m in range(8)], sems[2:5])

    @staticmethod
    def scratch():
        return [dma_sems(7, 1), dma_sems(7, 1)] + PlaneGather.scratch(8)

    def start(self):
        self.swap.start()
        self.spread.start((0,))

    def arrive(self, *places):
        for m in places:
            self.swap.arrive(m)
            self.spread.start((m,))

    def onward(self, *places):
        for m in places:
            self.spread.middle(m)

    def finish(self):
        self.swap.finish(arrive=False)
        self.spread.finish()


def quarter_cols(ref, first, rows, p):
    width = ref.shape[1] // 4
    return ref.at[pl.ds(first, rows), pl.ds(mult(p * width, 128), width)]


def back_kernel(shift_unit, *refs):
    down, tokens, grad_gate, grad_up, gate_w, up_w, out, down_own, gate_own, up = refs[:10]
    term, gate, strips, strip_sems = refs[10:14]
    rep, zpos, core = place()
    total, rest = Total.split(term, out, refs[14:])
    bufs, sems, _ = PlaneSum.split(rest, 4)
    half = down_own.shape[0] // 2
    shift = mult((zpos * 2 + core) % 4 * shift_unit, 16)
    wide = jnp.float32

    def down_item(h):
        return (lambda p: quarter_cols(down, mult(shift + h * half, 16), half, p), down_own.at[pl.ds(h * half, half)], h)

    def gate_item(h):
        return (lambda p: gate.at[pl.ds(4 * h, 4), p], gate_own.at[pl.ds(4 * h, 4)], h)

    sums = PlaneSum([down_item(0), down_item(1), gate_item(0), gate_item(1)], bufs, sems)
    chunk = strips.shape[2]
    chunks = gate_w.shape[0] // chunk

    def strip(i, which):
        return pltpu.make_async_copy(
            (gate_w, up_w)[which].at[pl.ds(mult(i * chunk, 128), chunk)], strips.at[i % 2, which], strip_sems.at[i % 2, which])

    for which in range(2):
        strip(0, which).start()
    greet(rep, zpos, core, plane=2)
    sums.start((0, 1))

    def back(i, carry):
        for which in range(2):
            strip(i, which).wait()

        @pl.when(i < chunks - 1)
        def _():
            for which in range(2):
                strip(i + 1, which).start()

        part = dot_nt(grad_gate[...], strips[i % 2, 0]) + dot_nt(grad_up[...], strips[i % 2, 1])
        term[:, :, pl.ds(mult(i * chunk, 128), chunk)] = part.astype(term.dtype).reshape(8, -1, chunk)
        return carry

    lax.fori_loop(0, chunks, back, 0)
    total.start()
    wide_rows = tokens.shape[1] // 4

    def weight(grad, to, i):
        got = dot_tn(tokens[:, pl.ds(mult(i * wide_rows, 128), wide_rows)], grad[...])
        to[pl.ds(2 * i, 2)] = got.astype(to.dtype).reshape((2,) + to.shape[1:])

    def gate_step(i, carry):
        weight(grad_gate, gate, i)

        @pl.when(i == 2)
        def _():
            total.pair()
            total.step(0)
        return carry

    lax.fori_loop(0, 4, gate_step, 0)
    sums.start((2, 3))

    def up_step(i, carry):
        weight(grad_up, up, i)

        @pl.when(i == 1)
        def _():
            sums.middle(0)
            sums.middle(1)
            total.step(1)
        return carry

    lax.fori_loop(0, 4, up_step, 0)
    sums.end(0)
    sums.end(1)
    total.step(2)
    sums.middle(2)
    sums.middle(3)
    total.finish()
    sums.end(2)
    sums.end(3)
    sums.finish()


def back_sums(cid, down, tokens, grad_gate, grad_up, gate_w, up_w, rows):
    width = down.shape[1] // 4
    kind = down.dtype
    strip = gate_w.shape[1]
    parts = (8, 4, gate_w.shape[0] // 32, strip)
    term = jax.ShapeDtypeStruct((8, tokens.shape[0] // 8, tokens.shape[1]), kind)
    return pl.pallas_call(
        functools.partial(back_kernel, rows % 128),
        out_shape=[jax.ShapeDtypeStruct(term.shape[1:], jnp.float32), jax.ShapeDtypeStruct((rows, width), kind),
                   jax.ShapeDtypeStruct((8,) + parts[2:], kind), jax.ShapeDtypeStruct(parts, kind)],
        in_specs=[VMEM] * 4 + [ANY] * 2, out_specs=[VMEM] * 4,
        scratch_shapes=[pltpu.VMEM(term.shape, kind), pltpu.VMEM(parts, kind),
                        pltpu.VMEM((2, 2, gate_w.shape[0] // 5, strip), kind), dma_sems(2, 2)]
        + Total.scratch(term) + PlaneSum.scratch([(rows // 2, width)] * 2 + [(4,) + parts[2:]] * 2, kind),
        compiler_params=kernel_params(cid),
    )(down, tokens, grad_gate, grad_up, gate_w, up_w)


def middle_kernel(scale, *refs):
    gate, refs = refs[0], refs[1:]
    branch, cols, down, up, attn_out, w_query_up, w_latent_up, query_low, latent_low = refs[:9]
    query, kv, rope, bias, turns, logs = refs[9:15]
    w_query, w_latent, tokens, query_lat, latent_proj, gains, grad_residual, gain_ffn = refs[15:23]
    branch_all, cols_all, down_all, gate_all, up_own, query_up, latent_up, tokens_grad, lats, gain_terms = refs[23:33]
    scratch = list(refs[33:])
    (left, mixed, packed, grad_query, grad_kv, grad_rope, strips, query_strips, latent_strips, strip_sems, grad_low,
     grad_latent, grad_normed, latent_send, rope_send, latent_land, rope_land, lsend, lrecv, query_rows, latent_rows,
     row_sems) = scratch[:22]
    scratch = scratch[22:]
    rep, zpos, core = place()
    shard = zpos * 2 + core
    gather = Gather((branch,), (branch_all,), scratch[:5])
    swap = ColumnSwap([(lambda s: cols.at[s], lambda s: cols_all.at[s])], scratch[5:8])
    half = down.shape[0] // 2
    downs = PlaneGather(
        [(down.at[pl.ds(h * half, half)], functools.partial(quarter_cols, down_all, h * half, half), h) for h in range(2)],
        scratch[8:11])
    strips_out = Strips(gate, gate_all, scratch[11:16])
    bufs, sems, _ = PlaneSum.split(scratch[16:], 2)
    sums = PlaneSum([(lambda p, h=h: up.at[pl.ds(4 * h, 4), p], up_own.at[pl.ds(4 * h, 4)], h) for h in range(2)], bufs, sems)
    rows = tokens.shape[0]
    out_rows = attn_out.shape[0] // 4
    quarter_width = kv.shape[1] // 4
    wide, low = jnp.float32, jnp.bfloat16

    def strip(i, k):
        at = pl.ds(mult(i * quarter_width, 128), quarter_width)
        src = (attn_out.at[pl.ds(mult(i * out_rows, 128), out_rows)], w_query_up.at[:, at], w_latent_up.at[:, at])[k]
        return pltpu.make_async_copy(src, (strips, query_strips, latent_strips)[k].at[i % 2], strip_sems.at[i % 2, k])

    def share(k, what):
        for i, (src, dst) in enumerate(((latent_send, latent_land), (rope_send, rope_land))):
            getattr(remote(src.at[pl.ds((k + 1) * rows, rows)], dst.at[k], lsend.at[k, i], lrecv.at[k, i],
                           plane_places(rep)[k], shard), what)()

    for k in range(3):
        strip(0, k).start()
    greet(rep, zpos, core, plane=3, column=True)
    strips_out.start()
    sums.start()
    downs.start()
    left[...] = jnp.zeros_like(left)
    grad_rope[...] = jnp.zeros_like(grad_rope)
    grad_low[...] = jnp.zeros_like(grad_low)
    grad_latent[...] = jnp.zeros_like(grad_latent)
    quarter = attend_back_heads(
        scale, query, kv, rope, bias, turns, logs, mixed, grad_query, packed, grad_kv, grad_rope, left)

    def after_first():
        gather.start()
        swap.start()
        strips_out.arrive(1, 2, 6)

    def after_second():
        strips_out.arrive(3, 7, 4, 5)
        sums.middle(0)
        sums.middle(1)

    def after_third():
        gather.hop(1)
        downs.middle(0)
        downs.middle(1)
        strips_out.onward(0, 1, 2)

    def after_fourth():
        gather.hop(2)
        strips_out.onward(6, 3)

    def step(i, carry):
        for k in range(3):
            strip(i, k).wait()

        @pl.when(i < 3)
        def _():
            for k in range(3):
                strip(i + 1, k).start()

        mixed[:, pl.ds(mult(i * out_rows, 128), out_rows)] = dot_nt(branch[...], strips[i % 2]).astype(mixed.dtype)
        quarter(i, carry)
        at = pl.ds(mult(i * quarter_width, 128), quarter_width)
        grad_low[...] += dot_nt(grad_query[:, at], query_strips[i % 2])
        grad_latent[...] += dot_nt(grad_kv[:, at], latent_strips[i % 2])
        for k, service in enumerate((after_first, after_second, after_third, after_fourth)):
            pl.when(i == k)(service)
        return carry

    lax.fori_loop(0, 4, step, 0)
    latent_send[...] = grad_latent[...].astype(low)
    rope_send[...] = grad_rope[...].astype(low)
    for k in range(3):
        share(k, "start")

    def terms(i, carry):
        at = pl.ds(mult(i * 1024, 128), 1024)
        query_up[:, at] = dot_tn(query_low[...], packed[:, at]).astype(query_up.dtype)
        at = pl.ds(mult(i * quarter_width, 128), quarter_width)
        latent_up[:, at] = dot_tn(latent_low[...], grad_kv[:, at]).astype(latent_up.dtype)
        return carry

    lax.fori_loop(0, 4, terms, 0)
    strips_out.onward(7, 4, 5)
    sums.end(0)
    sums.end(1)

    def tile(t):
        return slice(128 * t, 128 * t + 128)

    def norm_back(src, grad, tiles, first, put):
        square = sum(jnp.sum(jnp.square(src(t)), axis=1, keepdims=True) for t in range(tiles))
        factor = lax.rsqrt(square / (128 * tiles) + epsilon)
        along = jnp.zeros_like(factor)
        for t in range(tiles):
            unit = src(t) * factor
            weighed = grad(t) * unit
            gain_terms[first + t : first + t + 1, :] = jnp.sum(weighed, axis=0, keepdims=True)
            along = along + jnp.sum(weighed * gains[first + t : first + t + 1, :], axis=1, keepdims=True)
        along = along / (128 * tiles)
        for t in range(tiles):
            put(t, factor * (grad(t) * gains[first + t : first + t + 1, :] - src(t) * factor * along))

    def put_query(t, value):
        lats[:, tile(t)] = value.astype(low)

    def put_latent(t, value):
        lats[:, tile(6 + t)] = value.astype(low)

    def put_tokens(t, value):
        tokens_grad[:, tile(t)] = (grad_residual[:, tile(t)] + value).astype(low)

    norm_back(lambda t: query_lat[:, tile(t)], lambda t: grad_low[:, tile(t)], 6, 40, put_query)
    own = grad_latent[0:rows].astype(low).astype(wide)
    own_rope = grad_rope[0:rows].astype(low).astype(wide)
    for k in range(3):
        share(k, "wait_recv")
        own = own + latent_land[k].astype(wide)
        own_rope = own_rope + rope_land[k].astype(wide)
    grad_latent[0:rows] = own
    norm_back(lambda t: latent_proj[:, tile(t)], lambda t: grad_latent[0:rows, tile(t)], 2, 46, put_latent)
    turned = turn(own_rope, (turns[0], turns[1], turns[2]), True)
    lats[:, 1024:1056] = turned[:, 64:96].astype(low)
    chunk = query_rows.shape[1]
    chunks = w_query.shape[0] // chunk

    def row_copy(i, k):
        at = pl.ds(mult(i * chunk, chunk), chunk)
        return pltpu.make_async_copy((w_query, w_latent)[k].at[at], (query_rows, latent_rows)[k].at[i % 2], row_sems.at[i % 2, k])

    def normed_step(i, carry):
        for k in range(2):
            row_copy(i, k).wait()

        @pl.when(i < chunks - 1)
        def _():
            for k in range(2):
                row_copy(i + 1, k).start()

        grad_normed[:, pl.ds(mult(i * chunk, chunk), chunk)] = (
            dot_nt(lats[:, :768], query_rows[i % 2]) + dot_nt(lats[:, 768:1056], latent_rows[i % 2]))
        return carry

    for k in range(2):
        row_copy(0, k).start()
    lax.fori_loop(0, chunks, normed_step, 0)
    norm_back(lambda t: tokens[:, tile(t)].astype(wide), lambda t: grad_normed[:, tile(t)], 20, 0, put_tokens)
    gain_terms[20:40, :] = gain_ffn[...]
    gather.hop(3)
    for k in range(3):
        share(k, "wait_send")
    gather.finish()
    swap.finish()
    downs.finish()
    sums.finish()
    strips_out.finish()


def middle_exchange(cid, scale, gate, branch, cols, down, up, weights, query_low, latent_low, attend_in, norm_in):
    kind = branch.dtype
    wide = jnp.float32
    query, kv, rope = attend_in[:3]
    rows, width = branch.shape
    attn_out, w_query_up, w_latent_up, w_query, w_latent = weights
    keys, latent_rank = latent_low.shape
    query_rank = query_low.shape[1]
    quarter = kv.shape[1] // 4
    gains = norm_in[3]
    return pl.pallas_call(
        functools.partial(middle_kernel, scale),
        out_shape=[jax.ShapeDtypeStruct((8 * rows, width), kind), jax.ShapeDtypeStruct(cols.shape, kind),
                   jax.ShapeDtypeStruct((down.shape[0], 4 * down.shape[1]), kind),
                   jax.ShapeDtypeStruct((8, 4) + gate.shape[1:], kind), jax.ShapeDtypeStruct((8,) + up.shape[2:], kind),
                   jax.ShapeDtypeStruct((query_rank, 4096), kind), jax.ShapeDtypeStruct((latent_rank, kv.shape[1]), kind),
                   jax.ShapeDtypeStruct((rows, width), kind),
                   jax.ShapeDtypeStruct((rows, query_rank + w_latent.shape[1]), kind), jax.ShapeDtypeStruct(gains.shape, wide)],
        in_specs=[ANY, VMEM] + [ANY] * 2 + [VMEM] + [ANY] * 3 + [VMEM] * 8 + [ANY] * 2 + [VMEM] * 6,
        out_specs=[ANY] * 4 + [VMEM] * 6,
        scratch_shapes=[pltpu.VMEM((2 * rows, 256), kind), pltpu.VMEM(branch.shape, kind), pltpu.VMEM((rows, 4096), kind),
                        pltpu.VMEM(query.shape, kind), pltpu.VMEM(kv.shape, kind), pltpu.VMEM(rope.shape, wide),
                        pltpu.VMEM((2, attn_out.shape[0] // 4, width), kind), pltpu.VMEM((2, query_rank, quarter), kind),
                        pltpu.VMEM((2, latent_rank, quarter), kind), dma_sems(2, 3),
                        pltpu.VMEM((rows, query_rank), wide), pltpu.VMEM((keys, latent_rank), wide), pltpu.VMEM((rows, width), wide),
                        pltpu.VMEM((keys, latent_rank), kind), pltpu.VMEM((keys, 128), kind),
                        pltpu.VMEM((3, rows, latent_rank), kind), pltpu.VMEM((3, rows, 128), kind), dma_sems(3, 2), dma_sems(3, 2),
                        pltpu.VMEM((2, width // 5, query_rank), kind), pltpu.VMEM((2, width // 5, w_latent.shape[1]), kind), dma_sems(2, 2)]
        + Gather.scratch(1) + ColumnSwap.scratch(1) + PlaneGather.scratch(2) + Strips.scratch()
        + PlaneSum.scratch([(4,) + up.shape[2:]] * 2, kind),
        compiler_params=kernel_params(cid),
    )(gate, branch, cols, down, up, attn_out, w_query_up, w_latent_up, query_low, latent_low, *attend_in, w_query, w_latent, *norm_in)


def last_kernel(*refs):
    up, lat, query_up, latent_up, hidden, down, branch, cols, gain = refs[:9]
    up_all, out, attn_sum, lat_sum, latent_sum, query_sum, gain_out = refs[9:16]
    attn_out, branch_sem, scratch = refs[16], refs[17], list(refs[18:])
    rep, zpos, core = place()
    shard = zpos * 2 + core
    places = plane_places(rep)

    def take(n):
        nonlocal scratch
        got, scratch = scratch[:n], scratch[n:]
        return got

    strips_out = Strips(up, up_all, take(5))
    spread_sems = take(3)
    lat_all, out_term, lat_term, query_part, latent_own, query_own = take(6)
    gather = Gather((lat,), (lat_all,), take(5))
    owns = take(5)
    gain_landed, gain_sum, gain_plane, gsend, grecv, hsend, hrecv = take(7)
    total, scratch = Total.split(out_term, out, scratch)
    query_total, scratch = Total.split(query_part, query_own, scratch)
    latent_total, scratch = Total.split(latent_up, latent_own, scratch)
    bufs, sems, _ = PlaneSum.split(scratch, 6)
    width = query_up.shape[2] // 4
    half = attn_out.shape[0] // 2

    def query_item(h):
        return (lambda p: query_up.at[pl.ds(4 * h, 4), :, pl.ds(mult(p * width, 128), width)], query_part.at[pl.ds(4 * h, 4)], h)

    latent_low = scratch[-1]
    sums = PlaneSum(
        [query_item(0), query_item(1)]
        + [(functools.partial(quarter_cols, attn_out, h * half, half), owns[h], h) for h in range(2)]
        + [(lambda p: lat_term.at[p], owns[2], 0),
           (functools.partial(quarter_cols, latent_low, 0, latent_low.shape[0]), owns[3], 1)],
        bufs, sems)
    spread = PlaneGather(
        [(owns[h], functools.partial(quarter_cols, attn_sum, h * half, half), h) for h in range(2)]
        + [(owns[2], lambda p: lat_sum.at[p], 0),
           (owns[3], functools.partial(quarter_cols, latent_sum, 0, latent_low.shape[0]), 1),
           (owns[4], functools.partial(quarter_cols, query_sum, 0, query_up.shape[1]), 0)], spread_sems)

    def gain_copy(m):
        s2 = column_place(zpos, core, m)
        return remote(gain, gain_landed.at[m - 1], gsend.at[m - 1], grecv.at[m - 1], rep, s2)

    def gain_on(k):
        return remote(gain_sum, gain_plane.at[k], hsend.at[k], hrecv.at[k], places[k], shard)

    greet(rep, zpos, core, plane=3, column=True)
    for m in range(1, 8):
        gain_copy(m).start()
    strips_out.start()
    sums.start((0, 1))
    latent_total.start()
    branch_copy = pltpu.make_async_copy(branch, out_term, branch_sem.at[0])
    branch_copy.start()
    gather.start()
    rows = lat.shape[0]
    tokens = 8 * rows

    def attn_term(i, carry):
        at = pl.ds(mult(i * (attn_out.shape[1] // 4), 128), attn_out.shape[1] // 4)
        attn_out[:, at] = dot_tn(cols[:, 0].reshape(tokens, -1), out_term[:, :, at].reshape(tokens, -1)).astype(attn_out.dtype)
        return carry

    def term(i, carry):
        out_term[i] = jnp.dot(hidden[pl.ds(mult(i * rows, rows), rows)], down[...],
                              preferred_element_type=jnp.float32).astype(out_term.dtype)
        return carry

    arrive, onward = strips_out.arrive, strips_out.onward
    branch_copy.wait()
    lax.fori_loop(0, 4, attn_term, 0)
    sums.start((2, 3))
    lax.fori_loop(0, 3, term, 0)
    arrive(1)
    latent_total.pair()
    latent_total.step(0)
    lax.fori_loop(3, 6, term, 0)
    onward(0)
    gather.hop(1)
    arrive(2)
    arrive(6)
    lax.fori_loop(6, 8, term, 0)
    latent_total.step(1)
    gain_sum[...] = gain[...]
    for m in range(1, 8):
        gain_copy(m).wait_recv()
        gain_sum[...] += gain_landed[m - 1]
    for k in range(3):
        gain_on(k).start()
    total.start()
    onward(1)
    arrive(3)
    arrive(7)
    gather.hop(2)
    sums.middle(0)
    sums.middle(1)
    latent_total.step(2)
    onward(2, 6)
    arrive(4)
    arrive(5)
    gather.hop(3)
    total.pair()
    total.step(0)
    sums.middle(2)
    sums.middle(3)
    latent_total.finish()
    latent_low[...] = latent_own[...].astype(latent_low.dtype)
    sums.start((5,))
    sums.end(0)
    sums.end(1)
    query_total.start()
    gather.finish()
    lat_term[...] = dot_tn(cols[:, 1].reshape(tokens, -1), lat_all[...]).astype(lat_term.dtype).reshape(lat_term.shape)
    sums.start((4,))
    query_total.pair()
    query_total.step(0)
    onward(3, 7)
    total.step(1)
    sums.end(2)
    sums.end(3)
    spread.start((0, 1))
    query_total.step(1)
    onward(4, 5)
    sums.middle(5)
    sums.middle(4)
    query_total.step(2)
    total.step(2)
    query_total.finish()
    owns[4][...] = query_own[...].astype(owns[4].dtype)
    spread.start((4,))
    sums.end(5)
    spread.start((3,))
    sums.end(4)
    spread.start((2,))
    for i in (0, 1, 4, 3, 2):
        spread.middle(i)
    gain_out[...] = gain_sum[...]
    for k in range(3):
        gain_on(k).wait_recv()
        gain_out[...] += gain_plane[k]
    total.finish()
    for k in range(3):
        gain_on(k).wait_send()
    for m in range(1, 8):
        gain_copy(m).wait_send()
    strips_out.finish()
    sums.finish()
    spread.finish()


def last_sums(cid, up, lat, query_up, latent_up, hidden, down, branch, cols, gain):
    kind = up.dtype
    wide = jnp.float32
    rows = lat.shape[0]
    attn_out = jax.ShapeDtypeStruct((cols.shape[3], branch.shape[2]), kind)
    lat_shape = (4, cols.shape[3] // 4, lat.shape[1])
    query_shape = (query_up.shape[1], query_up.shape[2] // 4)
    shapes = [(attn_out.shape[0] // 2, attn_out.shape[1] // 4)] * 2 + [
        lat_shape[1:], (latent_up.shape[1], latent_up.shape[2] // 4)]
    out_term = jax.ShapeDtypeStruct((8, rows, down.shape[1]), kind)
    query_part = jax.ShapeDtypeStruct((8,) + query_shape, kind)
    return pl.pallas_call(
        last_kernel,
        out_shape=[jax.ShapeDtypeStruct((8, 4) + up.shape[1:], kind)]
        + [jax.ShapeDtypeStruct(out_term.shape[1:], wide)]
        + [jax.ShapeDtypeStruct(s, kind) for s in (attn_out.shape, lat_shape, latent_up.shape[1:])]
        + [jax.ShapeDtypeStruct((query_up.shape[1], query_up.shape[2]), kind), jax.ShapeDtypeStruct(gain.shape, gain.dtype)],
        in_specs=[ANY] * 2 + [VMEM] * 4 + [ANY] + [VMEM] * 2, out_specs=[ANY, VMEM] + [ANY] * 4 + [VMEM],
        scratch_shapes=[pltpu.VMEM(attn_out.shape, kind), dma_sems(1)] + Strips.scratch() + PlaneGather.scratch(5)
        + [pltpu.VMEM((8 * rows, lat.shape[1]), kind), pltpu.VMEM(out_term.shape, kind), pltpu.VMEM(lat_shape, kind),
           pltpu.VMEM(query_part.shape, kind), pltpu.VMEM(latent_up.shape[1:], wide), pltpu.VMEM(query_shape, wide)]
        + Gather.scratch(1) + [pltpu.VMEM(s, kind) for s in shapes + [query_shape]]
        + [pltpu.VMEM((7,) + gain.shape, wide), pltpu.VMEM(gain.shape, wide), pltpu.VMEM((3,) + gain.shape, wide)]
        + [dma_sems(7)] * 2 + [dma_sems(3)] * 2
        + Total.scratch(out_term) + Total.scratch(query_part) + Total.scratch(latent_up)
        + PlaneSum.scratch([(4,) + query_shape] * 2 + shapes, kind) + [pltpu.VMEM(latent_up.shape[1:], kind)],
        compiler_params=kernel_params(cid),
    )(up, lat, query_up, latent_up, hidden, down, branch, cols, gain)


def start_kernel(scale, *refs):
    ins, (gate, up), (tokens, bias, turns, w_down) = list(refs[:7]), refs[7:9], refs[9:13]
    outs, cols, refs = refs[13:20], refs[20:22], refs[22:]
    (normed, query_low, latent, rope, kv, query, mixed, logs, query_lat, latent_proj, residual, ffn_all,
     grad_hidden, down) = refs[:14]
    refs = refs[14:]
    (zsend, zrecv, xsend, xrecv, ysend, yrecv, dsend, drecv, csend, crecv, own, gsend, grecv, psend, precv) = refs[:15]
    held, strips = refs[15:22], refs[22:24]
    cotangent, ins[5] = ins[5], held[5]
    (small, gains, w_query, w_latent, w_query_up, w_latent_up, w_out, proj, ffn, lsend, lrecv, load_sems,
     grad_sems, down_sem) = refs[24:38]
    gather = Gather((ffn,), (ffn_all,), refs[38:])
    rep, zpos, core = place()
    xrep, yrep, drep = plane_places(rep)
    shard = zpos * 2 + core

    def whole(a, z, c):
        rows = ins[a].shape[0]
        return outs[a].at[pl.ds(mult((z * 2 + c) * rows, rows), rows)]

    def pieces(a, z, c, quarter, act, own_ref=False):
        def part(b, first, rows):
            full = ins[b].shape[0]
            if own_ref:
                return ins[b].at[pl.ds(mult(first, 16), rows)]
            return outs[b].at[pl.ds(mult((z * 2 + c) * full + first, 16), rows)]

        if a < 3:
            rows = ins[a].shape[0] // 4
            act(part(a, quarter * rows, rows))
        elif a == 3:
            @pl.when(quarter < 3)
            def _():
                act(part(3, jnp.minimum(quarter, 2) * 32, 32))

            @pl.when(quarter == 3)
            def _():
                act(part(4, 0, 32))
        else:
            act(ins[a + 1] if own_ref else whole(a + 1, z, c))

    copy = remote

    def hop(a, way, h, z, what):
        def act(ref):
            c = copy(ref, ref, zsend.at[way, h, a], zrecv.at[way, h, a], rep, (zpos + 1 - 2 * way) * 2 + core)
            getattr(c, what)()
        pieces(a, z, core, rep, act)

    def to_plane(a, k, z, quarter, what, sems, r):
        def act(ref):
            getattr(copy(ref, ref, sems[0].at[k, a], sems[1].at[k, a], r, shard), what)()
        pieces(a, z, core, quarter, act)

    def to_core(a, slot, z, c, what, src=None):
        ref = whole(a, z, c)
        getattr(copy(ref if src is None else src, ref, csend.at[slot, a], crecv.at[slot, a], rep, zpos * 2 + 1 - core), what)()

    greet(rep, zpos, core, plane=3, column=True)
    def send_own(a):
        def first(way):
            def go(src):
                def act(ref):
                    copy(src, ref, zsend.at[way, 0, a], zrecv.at[way, 0, a], rep, (zpos + 1 - 2 * way) * 2 + core).start()
                return act
            return go
        for way in range(2):
            @pl.when(zpos < 3 if way == 0 else zpos > 0)
            def _():
                if a < 3:
                    rows = ins[a].shape[0] // 4
                    src = ins[a].at[pl.ds(mult(rep * rows, 16), rows)]
                    pieces(a, zpos, core, rep, first(way)(src))
                elif a == 3:
                    @pl.when(rep < 3)
                    def _():
                        start = mult(jnp.minimum(rep, 2) * 32, 16)
                        src = ins[3].at[pl.ds(start, 32)]
                        dst = outs[3].at[pl.ds(mult(shard * 96 + start, 16), 32)]
                        first(way)(src)(dst)

                    @pl.when(rep == 3)
                    def _():
                        first(way)(ins[4])(whole(4, zpos, core))
                else:
                    first(way)(ins[a + 1])(whole(a + 1, zpos, core))

    def keep(a, half):
        if half == 0:
            return pltpu.make_async_copy(ins[a], held[a], own.at[0, a])
        return pltpu.make_async_copy(held[a], whole(a, zpos, core), own.at[1, a])

    for a in (5, 1, 2, 3, 0):
        send_own(a)

    strip = cols[0].shape[1]
    quarter_rows = gate.shape[0] // 4

    def slice_of(which, s, first, rows):
        start = mult((s * 25 // 4) * 128, 128)
        return (gate, up)[which].at[pl.ds(mult(first, 16), rows), pl.ds(start, strip)]

    def rows_of(which, s, quarter):
        return cols[which].at[pl.ds(mult(s * gate.shape[0] + quarter * quarter_rows, 16), quarter_rows)]

    def slice_copy(m, which):
        s2 = column_place(zpos, core, m)
        return remote(slice_of(which, s2, rep * quarter_rows, quarter_rows), rows_of(which, shard, rep),
                      gsend.at[m - 1, which], grecv.at[m - 1, which], rep, s2)

    def slice_plane(m, which, quarter, kind, r):
        ref = rows_of(which, column_place(zpos, core, m, back=True), quarter)
        return remote(ref, ref, psend.at[kind, m - 1, which], precv.at[kind, m - 1, which], r, shard)

    def own_slice(which, half):
        if half == 0:
            return pltpu.make_async_copy(slice_of(which, shard, 0, gate.shape[0]), strips[which], own.at[0, 7 + which])
        rows = gate.shape[0]
        return pltpu.make_async_copy(strips[which], cols[which].at[pl.ds(mult(shard * rows, rows), rows)], own.at[1, 7 + which])

    near = (1, 2, 6, 3, 7, 4, 5)
    held[5][...] = (residual_scale * cotangent[...].astype(jnp.float32)).astype(held[5].dtype)
    for a in range(7):
        to_core(a, 0, zpos, core, "start", src=ins[a])
        if a != 5:
            keep(a, 0).start()
    for which in range(2):
        own_slice(which, 0).start()
    for a in range(7):
        if a != 5:
            keep(a, 0).wait()
        keep(a, 1).start()
    for which in range(2):
        own_slice(which, 0).wait()
        own_slice(which, 1).start()

    def slices_from_column(m):
        for which in range(2):
            s2 = column_place(zpos, core, m, back=True)
            ref = rows_of(which, s2, rep)
            remote(ref, ref, gsend.at[m - 1, which], grecv.at[m - 1, which], rep, s2).wait_recv()
        slices_to_plane(m, 0)

    def slices_to_plane(m, which):
        slice_plane(m, which, rep, 0, xrep).start()
        slice_plane(m, which, rep, 1, yrep).start()

    def slices_from_plane(m, which=0):
        slice_plane(m, which, xrep, 0, xrep).wait_recv()
        slice_plane(m, which, yrep, 1, yrep).wait_recv()
        slice_plane(m, which, *onward(m)).start()

    def onward(m):
        return (yrep, 2, xrep) if m % 2 else (xrep, 2, yrep)

    def from_column(h, way, z, slots):
        for a in slots:
            hop(a, way, h - 1, z, "wait_recv")
            if h < 3:
                @pl.when(zpos < 3 if way == 0 else zpos > 0)
                def _():
                    hop(a, way, h, z, "start")
            if a < 4:
                to_plane(a, way * 3 + h - 1, z, rep, "start", (xsend, xrecv), xrep)
                to_plane(a, way * 3 + h - 1, z, rep, "start", (ysend, yrecv), yrep)
            else:
                to_core(a + 1, way * 3 + h, z, core, "start")

    def from_plane(h, way, z, slots):
        k = way * 3 + h - 1
        for a in slots:
            to_plane(a, k, z, xrep, "wait_recv", (xsend, xrecv), xrep)
            if a == 0:
                to_plane(a, k, z, xrep, "start", (dsend, drecv), yrep)
            to_plane(a, k, z, yrep, "wait_recv", (ysend, yrecv), yrep)
            if a > 0:
                to_plane(a, k, z, yrep, "start", (dsend, drecv), xrep)

    def from_corner(h, way, z, slots):
        k = way * 3 + h - 1
        for a in slots:
            to_plane(a, k, z, drep, "wait_recv", (dsend, drecv), drep)
            for b in (a,) if a < 3 else (3, 4):
                to_core(b, k + 1, z, core, "start")

    def by_hop(stage, h, *more):
        for way in range(2):
            z = zpos - h if way == 0 else zpos + h

            @pl.when(z >= 0 if way == 0 else z <= 3)
            def _():
                stage(h, way, z, *more)

    def arrived(arrays):
        for b in arrays:
            keep(b, 1).wait()
            to_core(b, 0, zpos, 1 - core, "wait_recv")

            def theirs(h, way, z):
                to_core(b, way * 3 + h, z, 1 - core, "wait_recv")

            for h in range(1, 4):
                by_hop(theirs, h)

    wide, low = jnp.float32, jnp.bfloat16

    def tile(t):
        return slice(128 * t, 128 * t + 128)

    def normalize(src, dst, tiles, first):
        square = sum(jnp.sum(jnp.square(src(t)), axis=1, keepdims=True) for t in range(tiles))
        factor = lax.rsqrt(square / (128 * tiles) + epsilon)
        for t in range(tiles):
            dst[:, tile(t)] = (src(t) * factor * gains[first + t : first + t + 1, :]).astype(low)

    def load(b, to, i):
        return pltpu.make_async_copy(outs[b], to, load_sems.at[i])

    def share(k, what):
        rows = tokens.shape[0]
        for i, ref in enumerate((latent, rope)):
            copy_ = remote(ref.at[pl.ds(0, rows)], ref.at[pl.ds((k + 1) * rows, rows)], lsend.at[k, i], lrecv.at[k, i],
                           plane_places(rep)[k], shard)
            getattr(copy_, what)()

    def down_products():
        arrived((1, 2))
        load(1, w_query, 1).start()
        load(2, w_latent, 2).start()
        load(2, w_latent, 2).wait()
        latent_proj[...] = jnp.dot(normed[...], w_latent[...], preferred_element_type=wide)
        normalize(lambda t: latent_proj[:, tile(t)], latent.at[pl.ds(0, tokens.shape[0])], 2, 46)
        edge = jnp.zeros((tokens.shape[0], 64), wide)
        key = jnp.concatenate([edge, latent_proj[:, 256:288], edge[:, :32]], axis=1)
        rope[0 : tokens.shape[0]] = turn(key, (turns[0], turns[1], turns[2])).astype(low)
        for k in range(3):
            share(k, "start")
        load(1, w_query, 1).wait()
        query_lat[...] = jnp.dot(normed[...], w_query[...], preferred_element_type=wide)
        normalize(lambda t: query_lat[:, tile(t)], query_low, 6, 40)

    def chunk_loop(count, body):
        lax.fori_loop(0, count, lambda i, c: (body(i), c)[1], 0)

    def query_chunk(i):
        at = pl.ds(mult(i * 1024, 128), 1024)
        proj[:, at] = jnp.dot(query_low[...], w_query_up[:, at], preferred_element_type=wide)

    def key_chunk(i):
        at = pl.ds(mult(i * 1024, 128), 1024)
        kv[:, at] = jnp.dot(latent[...], w_latent_up[:, at], preferred_element_type=wide).astype(low)

    out_rows = w_out.shape[1]

    def out_strip(i):
        return pltpu.make_async_copy(outs[0].at[pl.ds(mult(i * out_rows, 128), out_rows)], w_out.at[i % 2], load_sems.at[4 + i % 2])

    down_copy = pltpu.make_async_copy(
        w_down, down.at[pl.ds(mult(shard % 4 * (w_down.shape[0] % 128), 16), w_down.shape[0])], down_sem.at[0])
    down[...] = jnp.zeros_like(down)
    down_copy.start()
    by_hop(from_column, 1, (5, 1, 2))
    by_hop(from_column, 1, (3, 0))
    by_hop(from_column, 2, (5, 1, 2))
    by_hop(from_plane, 1, (1, 2))
    by_hop(from_column, 2, (3, 0))
    by_hop(from_plane, 1, (3, 0))
    by_hop(from_column, 3, (5, 1, 2))
    by_hop(from_plane, 2, (1, 2))
    by_hop(from_corner, 1, (1, 2))
    by_hop(from_column, 3, (3, 0))
    for m in near:
        for which in range(2):
            slice_copy(m, which).start()
    by_hop(from_plane, 3, (1, 2))
    by_hop(from_corner, 2, (1, 2))
    by_hop(from_plane, 2, (3, 0))
    arrived((6,))
    load(6, small, 0).start()
    load(6, small, 0).wait()
    gains[...] = sum(small[48 * s : 48 * s + 48, :] for s in range(8))
    normalize(lambda t: tokens[:, tile(t)].astype(wide), normed, 20, 0)
    by_hop(from_corner, 3, (1, 2))
    by_hop(from_corner, 1, (3, 0))
    send_own(4)
    down_products()
    by_hop(from_plane, 3, (3, 0))
    by_hop(from_corner, 2, (3, 0))
    by_hop(from_corner, 3, (3, 0))
    arrived((3, 4))
    load(3, w_query_up, 3).start()
    load(4, w_latent_up, 0).start()
    load(3, w_query_up, 3).wait()
    chunk_loop(5, query_chunk)
    for k in range(3):
        share(k, "wait_recv")
    load(4, w_latent_up, 0).wait()
    chunk_loop(5, key_chunk)
    for m in near:
        slices_from_column(m)
    logs[...] = jnp.zeros_like(logs)
    group = attend_heads(scale, proj, kv, rope, bias, turns, query, mixed, logs)

    def attend_step(i, carry):
        group(i, carry)

        @pl.when(i == 3)
        def _():
            by_hop(from_column, 1, (4,))

        @pl.when(i == 8)
        def _():
            by_hop(from_column, 2, (4,))
        return carry

    lax.fori_loop(0, kv.shape[1] // 512, attend_step, 0)
    for m in near[:3]:
        slices_from_plane(m)
    arrived((0,))
    out_strip(0).start()
    residual[...] = tokens[...].astype(wide)

    def out_step(i, carry):
        out_strip(i).wait()

        @pl.when(i < 3)
        def _():
            out_strip(i + 1).start()

        residual[...] += residual_scale * jnp.dot(
            mixed[:, pl.ds(mult(i * out_rows, 128), out_rows)], w_out[i % 2], preferred_element_type=wide)
        return carry

    lax.fori_loop(0, 4, out_step, 0)
    normalize(lambda t: residual[:, tile(t)], ffn, 20, 20)
    gather.start()
    for m in near:
        slices_to_plane(m, 1)
    by_hop(from_column, 3, (4,))
    for m in near[3:]:
        slices_from_plane(m)
    gather.hop(1)
    arrived((5,))
    down_copy.wait()
    chunk = 2 * tokens.shape[0]

    def grad_chunk(i):
        return pltpu.make_async_copy(
            outs[5].at[pl.ds(mult(i * chunk, chunk), chunk)], w_out.at[i % 2, pl.ds(0, chunk)], grad_sems.at[i % 2])

    def hidden_step(i, carry):
        grad_chunk(i).wait()

        @pl.when(i < 3)
        def _():
            grad_chunk(i + 1).start()

        grad_hidden[pl.ds(mult(i * chunk, chunk), chunk)] = dot_nt(w_out[i % 2, :chunk], down[...])

        @pl.when(i == 2)
        def _():
            gather.hop(2)
        return carry

    grad_chunk(0).start()
    lax.fori_loop(0, 4, hidden_step, 0)
    for m in near:
        slices_from_plane(m, 1)
    for k in range(3):
        share(k, "wait_send")
    gather.hop(3)
    gather.finish()
    for a in range(7):
        to_core(a, 0, zpos, core, "wait_send", src=ins[a])
    for which in range(2):
        own_slice(which, 1).wait()
        for m in near:
            slice_copy(m, which).wait_send()
    for m in near:
        for which in range(2):
            slice_plane(m, which, rep, 0, xrep).wait_send()
            slice_plane(m, which, rep, 1, yrep).wait_send()
            slice_plane(m, which, *onward(m)).wait_send()
            slice_plane(m, which, drep, 2, drep).wait_recv()
    for way in range(2):
        for h in range(3):
            z = zpos - h if way == 0 else zpos + h

            @pl.when((z >= 0) & (zpos < 3) if way == 0 else (z <= 3) & (zpos > 0))
            def _():
                for a in range(6):
                    hop(a, way, h, z, "wait_send")
    for h in range(1, 4):
        for way in range(2):
            z = zpos - h if way == 0 else zpos + h
            k = way * 3 + h - 1

            @pl.when(z >= 0 if way == 0 else z <= 3)
            def _():
                for a in range(4):
                    to_plane(a, k, z, rep, "wait_send", (xsend, xrecv), xrep)
                    to_plane(a, k, z, rep, "wait_send", (ysend, yrecv), yrep)
                    to_plane(a, k, z, xrep if a == 0 else yrep, "wait_send", (dsend, drecv), yrep)
                for a in range(7):
                    to_core(a, k + 1, z, core, "wait_send")

def start_gather(cid, scale, weights, gate, up, tokens, bias, turns, w_down):
    low, wide = jnp.bfloat16, jnp.float32
    rows, width = tokens.shape
    strip = (w_down.shape[0] // 128 + 1) * 128
    attn_out, query_down, latent_down, query_up, latent_up = weights[:5]
    tiles = query_up.shape[1]
    keys = bias.shape[1]
    out = [jax.ShapeDtypeStruct((a.shape[0] * 8,) + a.shape[1:], a.dtype) for a in weights]
    out += [jax.ShapeDtypeStruct((gate.shape[0] * 8, strip), gate.dtype)] * 2
    latent_rank = 8 * latent_up.shape[0]
    found = [((rows, width), low), ((rows, query_down.shape[1]), low), ((keys, latent_rank), low), ((keys, 128), low),
             ((keys, tiles), low), ((rows, tiles), low), ((rows, tiles // 2), low), ((rows, 128), wide),
             ((rows, query_down.shape[1]), wide), ((rows, latent_down.shape[1]), wide), ((rows, width), wide),
             ((8 * rows, width), low), ((8 * rows, strip), wide), ((strip, width), low)]
    out += [jax.ShapeDtypeStruct(s, d) for s, d in found]
    whole = [pltpu.VMEM((a.shape[0] * 8, a.shape[1]), a.dtype) for a in (query_down, latent_down, query_up, latent_up)]
    return pl.pallas_call(
        functools.partial(start_kernel, scale), out_shape=out,
        in_specs=[ANY] * 5 + [VMEM] + [ANY] * 3 + [VMEM] * 3 + [ANY], out_specs=[ANY] * 9 + [VMEM] * 11 + [ANY, VMEM, VMEM],
        scratch_shapes=[dma_sems(2, 3, 6), dma_sems(2, 3, 6)] + [dma_sems(6, 4)] * 6
        + [dma_sems(7, 7), dma_sems(7, 7), dma_sems(2, 9), dma_sems(7, 2), dma_sems(7, 2), dma_sems(3, 7, 2), dma_sems(3, 7, 2)]
        + [pltpu.VMEM(a.shape, a.dtype) for a in weights] + [pltpu.VMEM((gate.shape[0], strip), gate.dtype)] * 2
        + [pltpu.VMEM((8 * weights[6].shape[0], 128), wide), pltpu.VMEM(weights[6].shape, wide)] + whole
        + [pltpu.VMEM((2, 2 * attn_out.shape[0], width), low), pltpu.VMEM((rows, tiles), wide),
           pltpu.VMEM((rows, width), low), dma_sems(3, 2), dma_sems(3, 2), dma_sems(6), dma_sems(2), dma_sems(1)] + Gather.scratch(1),
        compiler_params=kernel_params(cid),
    )(*weights, gate, up, tokens, bias, turns, w_down)

def plane_swap(values, j):
    return lax.ppermute(values, "rep", [(i, i ^ j) for i in range(4)])


def column_body(
    tokens,
    cotangent,
    doc_lengths,
    gain_attn,
    query_down,
    gain_query,
    query_up,
    latent_down,
    gain_latent,
    latent_up,
    attn_out,
    gain_ffn,
    w_gate,
    w_up,
    w_down,
):
    low = jnp.bfloat16
    wide = jnp.float32
    rows, width = tokens.shape[1], tokens.shape[2]
    seq_len = rows * 4
    head_dim = ND + RD
    scale = head_dim ** (-0.5)
    rep, shard = lax.axis_index("rep"), lax.axis_index("shard")
    slice_ff = FF // 8
    strip = 896
    shift = (slice_ff * shard) % 128

    gain_list = (gain_attn, gain_ffn, gain_query, gain_latent)
    small = jnp.concatenate(
        [
            jnp.where(
                jnp.arange(8 * v.shape[0], dtype=jnp.int32) // v.shape[0] == shard,
                jnp.tile(v.astype(wide), 8),
                0.0,
            )
            for v in gain_list
        ]
    ).reshape(-1, 128)
    tile_up = jnp.pad(
        query_up.reshape(-1, H, head_dim), ((0, 0), (0, 0), (0, 128 - head_dim))
    ).reshape(-1, H * 128)
    grad_out = cotangent[0].astype(wide)
    local_pos = rep * rows + jnp.arange(rows, dtype=jnp.int32)
    key_pos = jnp.concatenate(
        [(rep ^ j) * rows + jnp.arange(rows, dtype=jnp.int32) for j in range(4)]
    )
    query_seg, query_off = segment_of(doc_lengths[0], local_pos)
    key_seg = segment_of(doc_lengths[0], key_pos)[0]
    allowed = (query_seg[:, None] == key_seg[None, :]) & (key_pos[None, :] <= local_pos[:, None])
    bias = jnp.where(allowed, 0.0, masked_score).astype(wide)
    cos_part, sin_part = rope_tables(query_off, RD)
    none = jnp.zeros((rows, RD // 2), wide)
    edge = jnp.zeros((rows, ND), wide)
    tail = jnp.zeros((rows, 128 - head_dim), wide)
    turns = jnp.stack(
        [
            jnp.concatenate([edge + 1.0, cos_part, cos_part, tail], axis=1),
            jnp.concatenate([edge, none, sin_part, tail], axis=1),
            jnp.concatenate([edge, -sin_part, none, tail], axis=1),
        ]
    )
    (
        aout,
        qdown,
        ldown,
        qup,
        lup,
        gd_all,
        small_all,
        gate_w,
        up_w,
        normed_low,
        query_low,
        latent_low,
        rope_tile,
        keyvals,
        queries,
        mixed_low,
        logs,
        query_lat,
        latent_proj,
        residual,
        ffn_all,
        grad_hidden,
        down_w,
    ) = start_gather(
        0,
        scale,
        (attn_out, query_down, latent_down, tile_up, latent_up, cotangent[0], small),
        w_gate,
        w_up,
        tokens[0],
        bias,
        turns,
        w_down,
    )
    gains_all = jnp.sum(small_all.reshape((8,) + small.shape), axis=0)
    gain_f = gains_all[width // 128 : 2 * width // 128].reshape(-1)
    norm_f_back = jax.vjp(rms_scale, residual, gain_f)[1]

    gate_pre = jnp.dot(ffn_all, gate_w, preferred_element_type=wide)
    up_pre = jnp.dot(ffn_all, up_w, preferred_element_type=wide)
    hidden, act_back = jax.vjp(swiglu, gate_pre, up_pre)
    hidden_low = hidden.astype(low)
    grad_gate_f, grad_up_f = act_back(grad_hidden)
    grad_gate = grad_gate_f.astype(low)
    grad_up = grad_up_f.astype(low)
    down_part = inner_rows(hidden_low, gd_all).astype(low)
    grad_ffn_in, down_own, gate_own, up_part = back_sums(
        2, down_part, ffn_all, grad_gate, grad_up, gate_w, up_w, slice_ff
    )

    grad_res_norm, grad_gain_ffn = norm_f_back(grad_ffn_in)
    grad_resid = grad_out + grad_res_norm
    grad_branch = (residual_scale * grad_resid).astype(low)
    cols = jnp.stack([mixed_low, normed_low]).reshape(2, rows, 8, width // 8).transpose(2, 0, 1, 3)
    (
        branch_all,
        cols_all,
        down_all,
        gate_all,
        up_own,
        qup_part,
        lup_part,
        tokens_grad,
        grad_lats,
        gain_terms,
    ) = middle_exchange(
        3,
        scale,
        gate_own,
        grad_branch,
        cols,
        down_own,
        up_part,
        (aout, qup, lup, qdown, ldown),
        query_low,
        latent_low,
        (queries, keyvals, rope_tile, bias, turns, logs),
        (
            tokens[0],
            query_lat,
            latent_proj,
            gains_all,
            grad_resid,
            grad_gain_ffn.reshape(-1, 128),
        ),
    )

    up_all, out_sum, aout_own, lat_own, lup_own, qup_own, gain_own = last_sums(
        4,
        up_own,
        grad_lats,
        qup_part.reshape(8, -1, qup_part.shape[1]),
        lup_part.reshape(8, -1, lup_part.shape[1]),
        hidden_low,
        down_w,
        branch_all.reshape(8, rows, width),
        cols_all,
        gain_terms,
    )
    layer_out = (residual + residual_scale * out_sum).astype(low)
    query_rank = query_down.shape[1]
    gate_grad, up_grad, down_grad, aout_own, qdown_own, ldown_own, lup_own, qup_own = widen(
        gate_all, up_all, down_all, aout_own, lat_own, lup_own, qup_own, FF, query_rank, H
    )
    gain_own = gain_own.reshape(-1)
    owned, first = [], 0
    for v in gain_list:
        owned.append(lax.dynamic_slice(gain_own, (first + shard * v.shape[0],), (v.shape[0],)))
        first += 8 * v.shape[0]

    return (
        layer_out[None],
        tokens_grad[None],
        owned[0],
        qdown_own,
        owned[2],
        qup_own,
        ldown_own,
        owned[3],
        lup_own,
        aout_own,
        owned[1],
        gate_grad,
        up_grad,
        down_grad,
    )


def body(
    tokens,
    cotangent,
    doc_lengths,
    gain_attn,
    query_down,
    gain_query,
    query_up,
    latent_down,
    gain_latent,
    latent_up,
    attn_out,
    gain_ffn,
    w_gate,
    w_up,
    w_down,
):
    low_type = jnp.bfloat16
    wide_type = jnp.float32
    tok_rows = tokens.shape[1]
    seq_len = tok_rows * lax.axis_size("rep")
    head_dim = ND + RD
    group_size = math.gcd(H, 8)
    group_count = H // group_size
    softmax_scale = head_dim ** (-0.5)
    local_pos = lax.axis_index("rep") * tok_rows + jnp.arange(tok_rows, dtype=jnp.int32)
    key_pos = jnp.arange(seq_len, dtype=jnp.int32)
    query_seg, query_off = segment_of(doc_lengths[0], local_pos)
    key_seg = segment_of(doc_lengths[0], key_pos)[0]
    allowed = (query_seg[:, None] == key_seg[None, :]) & (key_pos[None, :] <= local_pos[:, None])
    cos_part, sin_part = rope_tables(query_off, RD)
    (
        gain_in_full,
        qdown_full,
        gain_q_full,
        qup_full,
        ldown_full,
        gain_l_full,
        lup_full,
        aout_full,
        gain_f_full,
    ) = (
        lax.all_gather(gain_attn, "shard", axis=0, tiled=True),
        lax.all_gather(query_down, "shard", axis=0, tiled=True),
        lax.all_gather(gain_query, "shard", axis=0, tiled=True),
        lax.all_gather(query_up, "shard", axis=0, tiled=True),
        lax.all_gather(latent_down, "shard", axis=0, tiled=True),
        lax.all_gather(gain_latent, "shard", axis=0, tiled=True),
        lax.all_gather(latent_up, "shard", axis=0, tiled=True),
        lax.all_gather(attn_out, "shard", axis=0, tiled=True),
        lax.all_gather(gain_ffn, "shard", axis=0, tiled=True),
    )
    inputs = tokens[0].astype(wide_type)
    normed, norm_in_back = jax.vjp(rms_scale, inputs, gain_in_full.astype(wide_type))
    normed_low = normed.astype(low_type)
    query_lat = jnp.dot(normed_low, qdown_full, preferred_element_type=wide_type)
    query_norm, norm_q_back = jax.vjp(rms_scale, query_lat, gain_q_full.astype(wide_type))
    query_low = query_norm.astype(low_type)
    query_proj = jnp.dot(query_low, qup_full, preferred_element_type=wide_type).reshape(
        tok_rows, H, head_dim
    )

    def query_rope(values):
        return jnp.concatenate(
            [
                values[..., :ND],
                rotate(values[..., ND:], cos_part[:, None, :], sin_part[:, None, :]),
            ],
            axis=-1,
        )

    query_rot, query_back = jax.vjp(query_rope, query_proj)
    query_used = query_rot.astype(low_type)
    latent_proj = jnp.dot(normed_low, ldown_full, preferred_element_type=wide_type)
    latent_norm, norm_l_back = jax.vjp(
        rms_scale, latent_proj[:, :KR], gain_l_full.astype(wide_type)
    )
    latent_low = latent_norm.astype(low_type)

    def key_rotate(values):
        return rotate(values, cos_part, sin_part)

    key_rot, key_back = jax.vjp(key_rotate, latent_proj[:, KR:])
    key_rope = key_rot.astype(low_type)
    keyvals = jnp.dot(latent_low, lup_full, preferred_element_type=wide_type).astype(low_type)
    all_keyvals, all_rope = (
        lax.all_gather(keyvals, "rep", axis=0, tiled=True),
        lax.all_gather(key_rope, "rep", axis=0, tiled=True),
    )
    queries = query_used.reshape(tok_rows, group_count, group_size, head_dim).transpose(1, 0, 2, 3)
    key_groups = all_keyvals.reshape(seq_len, group_count, group_size, ND + VD).transpose(
        1, 0, 2, 3
    )

    def scores_of(query_blk, key_blk):
        nope_part = jnp.einsum(
            "thd,shd->hts", query_blk[..., :ND], key_blk[..., :ND], preferred_element_type=wide_type
        )
        rope_part = jnp.einsum(
            "thd,sd->hts", query_blk[..., ND:], all_rope, preferred_element_type=wide_type
        )
        return jnp.where(allowed[None], (nope_part + rope_part) * softmax_scale, masked_score)

    def forward_group(carry, blocks):
        query_blk, key_blk = blocks
        scores = scores_of(query_blk, key_blk)
        row_max = jnp.max(scores, axis=-1, keepdims=True)
        exp_scores = jnp.exp(scores - row_max)
        totals = jnp.sum(exp_scores, axis=-1, keepdims=True)
        probs = (exp_scores / totals).astype(low_type)
        mixed = jnp.einsum(
            "hts,shd->thd", probs, key_blk[..., ND:], preferred_element_type=wide_type
        )
        return (carry, (mixed, row_max + jnp.log(totals)))

    start_carry = jnp.zeros((), wide_type)
    final_carry, (mixed_groups, log_totals) = lax.scan(
        forward_group, start_carry, (queries, key_groups)
    )
    mixed_low = mixed_groups.transpose(1, 0, 2, 3).reshape(tok_rows, H * VD).astype(low_type)
    branch = jnp.dot(mixed_low, aout_full, preferred_element_type=wide_type)
    residual = inputs + residual_scale * branch
    normed_ffn, norm_f_back = jax.vjp(rms_scale, residual, gain_f_full.astype(wide_type))
    ffn_low = normed_ffn.astype(low_type)
    gate_full, up_full, down_full = (
        lax.all_gather(w_gate, "shard", axis=0, tiled=True),
        lax.all_gather(w_up, "shard", axis=0, tiled=True),
        lax.all_gather(w_down, "shard", axis=0, tiled=True),
    )
    gate_pre = jnp.dot(ffn_low, gate_full, preferred_element_type=wide_type)
    up_pre = jnp.dot(ffn_low, up_full, preferred_element_type=wide_type)
    hidden, act_back = jax.vjp(swiglu, gate_pre, up_pre)
    hidden_low = hidden.astype(low_type)
    ffn_branch = jnp.dot(hidden_low, down_full, preferred_element_type=wide_type)
    layer_out = residual + residual_scale * ffn_branch
    grad_out = cotangent[0].astype(wide_type)
    grad_down_in = (residual_scale * grad_out).astype(low_type)
    gate_back_w, up_back_w, down_back_w = (
        lax.all_gather(w_gate, "shard", axis=0, tiled=True),
        lax.all_gather(w_up, "shard", axis=0, tiled=True),
        lax.all_gather(w_down, "shard", axis=0, tiled=True),
    )
    grad_hidden = outer_cols(grad_down_in, down_back_w)
    grad_gate_f, grad_up_f = act_back(grad_hidden)
    grad_gate = grad_gate_f.astype(low_type)
    grad_up = grad_up_f.astype(low_type)
    grad_ffn_in = outer_cols(grad_gate, gate_back_w) + outer_cols(grad_up, up_back_w)
    down_grad = lax.psum_scatter(
        inner_rows(hidden_low, grad_down_in).astype(jnp.bfloat16),
        "shard",
        scatter_dimension=0,
        tiled=True,
    )
    gate_up_in = jnp.concatenate([grad_gate, grad_up], axis=1)
    gate_up_grad = lax.psum_scatter(
        inner_rows(ffn_low, gate_up_in).astype(jnp.bfloat16),
        "shard",
        scatter_dimension=0,
        tiled=True,
    ).astype(jnp.float32)
    gate_grad = gate_up_grad[:, :FF]
    up_grad = gate_up_grad[:, FF:]
    grad_res_norm, grad_gain_ffn = norm_f_back(grad_ffn_in)
    grad_resid = grad_out + grad_res_norm
    qdown_back, qup_back, ldown_back, lup_back, aout_back = (
        lax.all_gather(query_down, "shard", axis=0, tiled=True),
        lax.all_gather(query_up, "shard", axis=0, tiled=True),
        lax.all_gather(latent_down, "shard", axis=0, tiled=True),
        lax.all_gather(latent_up, "shard", axis=0, tiled=True),
        lax.all_gather(attn_out, "shard", axis=0, tiled=True),
    )
    grad_branch = (residual_scale * grad_resid).astype(low_type)
    aout_grad = inner_rows(mixed_low, grad_branch)
    grad_mixed = outer_cols(grad_branch, aout_back).astype(low_type)
    grad_groups = grad_mixed.reshape(tok_rows, group_count, group_size, VD).transpose(1, 0, 2, 3)

    def backward_group(rope_acc, blocks):
        query_blk, key_blk, grad_blk, log_blk = blocks
        scores = scores_of(query_blk, key_blk)
        probs = jnp.exp(scores - log_blk)
        grad_probs = jnp.einsum(
            "thd,shd->hts", grad_blk, key_blk[..., ND:], preferred_element_type=wide_type
        )
        delta = jnp.sum(probs * grad_probs, axis=-1, keepdims=True)
        grad_scores = (probs * (grad_probs - delta)).astype(low_type)
        grad_query = (
            jnp.concatenate(
                [
                    jnp.einsum(
                        "hts,shd->thd",
                        grad_scores,
                        key_blk[..., :ND],
                        preferred_element_type=wide_type,
                    ),
                    jnp.einsum(
                        "hts,sd->thd", grad_scores, all_rope, preferred_element_type=wide_type
                    ),
                ],
                axis=-1,
            )
            * softmax_scale
        )
        grad_key = (
            jnp.einsum(
                "hts,thd->shd", grad_scores, query_blk[..., :ND], preferred_element_type=wide_type
            )
            * softmax_scale
        )
        grad_value = jnp.einsum(
            "hts,thd->shd", probs.astype(low_type), grad_blk, preferred_element_type=wide_type
        )
        rope_acc = (
            rope_acc
            + jnp.einsum(
                "hts,thd->sd", grad_scores, query_blk[..., ND:], preferred_element_type=wide_type
            )
            * softmax_scale
        )
        return (rope_acc, (grad_query, jnp.concatenate([grad_key, grad_value], axis=-1)))

    rope_start = jnp.zeros((seq_len, RD), wide_type)
    rope_sum, (grad_q_groups, grad_kv_groups) = lax.scan(
        backward_group, rope_start, (queries, key_groups, grad_groups, log_totals)
    )
    grad_kv_all = grad_kv_groups.transpose(1, 0, 2, 3).reshape(seq_len, H * (ND + VD))
    grad_kv_own, grad_rope_own = (
        lax.psum_scatter(
            grad_kv_all.astype(jnp.bfloat16), "rep", scatter_dimension=0, tiled=True
        ).astype(jnp.float32),
        lax.psum_scatter(
            rope_sum.astype(jnp.bfloat16), "rep", scatter_dimension=0, tiled=True
        ).astype(jnp.float32),
    )
    grad_q_full = grad_q_groups.transpose(1, 0, 2, 3).reshape(tok_rows, H, head_dim)
    grad_q_proj = query_back(grad_q_full)[0].reshape(tok_rows, H * head_dim).astype(low_type)
    qup_grad = inner_rows(query_low, grad_q_proj)
    grad_q_lat_f, grad_gain_query = norm_q_back(outer_cols(grad_q_proj, qup_back))
    grad_q_lat = grad_q_lat_f.astype(low_type)
    grad_kv_low = grad_kv_own.astype(low_type)
    lup_grad = inner_rows(latent_low, grad_kv_low)
    grad_lat_c, grad_gain_latent = norm_l_back(outer_cols(grad_kv_low, lup_back))
    grad_lat_r = key_back(grad_rope_own)[0]
    grad_lat = jnp.concatenate([grad_lat_c, grad_lat_r], axis=1).astype(low_type)
    qdown_grad = inner_rows(normed_low, grad_q_lat)
    ldown_grad = inner_rows(normed_low, grad_lat)
    grad_normed = outer_cols(grad_q_lat, qdown_back) + outer_cols(grad_lat, ldown_back)
    grad_in_norm, grad_gain_attn = norm_in_back(grad_normed)
    tokens_grad = (grad_resid + grad_in_norm).astype(low_type)
    (
        owned_gain_attn,
        owned_qdown,
        owned_gain_query,
        owned_qup,
        owned_ldown,
        owned_gain_latent,
        owned_lup,
        owned_aout,
        owned_gain_ffn,
    ) = (
        lax.psum_scatter(
            grad_gain_attn.astype(jnp.bfloat16), "shard", scatter_dimension=0, tiled=True
        ).astype(jnp.float32),
        lax.psum_scatter(
            qdown_grad.astype(jnp.bfloat16), "shard", scatter_dimension=0, tiled=True
        ).astype(jnp.float32),
        lax.psum_scatter(
            grad_gain_query.astype(jnp.bfloat16), "shard", scatter_dimension=0, tiled=True
        ).astype(jnp.float32),
        lax.psum_scatter(
            qup_grad.astype(jnp.bfloat16), "shard", scatter_dimension=0, tiled=True
        ).astype(jnp.float32),
        lax.psum_scatter(
            ldown_grad.astype(jnp.bfloat16), "shard", scatter_dimension=0, tiled=True
        ).astype(jnp.float32),
        lax.psum_scatter(
            grad_gain_latent.astype(jnp.bfloat16), "shard", scatter_dimension=0, tiled=True
        ).astype(jnp.float32),
        lax.psum_scatter(
            lup_grad.astype(jnp.bfloat16), "shard", scatter_dimension=0, tiled=True
        ).astype(jnp.float32),
        lax.psum_scatter(
            aout_grad.astype(jnp.bfloat16), "shard", scatter_dimension=0, tiled=True
        ).astype(jnp.float32),
        lax.psum_scatter(
            grad_gain_ffn.astype(jnp.bfloat16), "shard", scatter_dimension=0, tiled=True
        ).astype(jnp.float32),
    )
    summed = (
        lax.psum(owned_gain_attn.astype(jnp.bfloat16), "rep").astype(jnp.float32),
        lax.psum(owned_qdown.astype(jnp.bfloat16), "rep").astype(jnp.float32),
        lax.psum(owned_gain_query.astype(jnp.bfloat16), "rep").astype(jnp.float32),
        lax.psum(owned_qup.astype(jnp.bfloat16), "rep").astype(jnp.float32),
        lax.psum(owned_ldown.astype(jnp.bfloat16), "rep").astype(jnp.float32),
        lax.psum(owned_gain_latent.astype(jnp.bfloat16), "rep").astype(jnp.float32),
        lax.psum(owned_lup.astype(jnp.bfloat16), "rep").astype(jnp.float32),
        lax.psum(owned_aout.astype(jnp.bfloat16), "rep").astype(jnp.float32),
        lax.psum(owned_gain_ffn.astype(jnp.bfloat16), "rep").astype(jnp.float32),
        lax.psum(gate_grad.astype(jnp.bfloat16), "rep").astype(jnp.float32),
        lax.psum(up_grad.astype(jnp.bfloat16), "rep").astype(jnp.float32),
        lax.psum(down_grad, "rep").astype(jnp.float32),
    )
    return (
        layer_out.astype(low_type)[None],
        tokens_grad[None],
        summed[0],
        summed[1],
        summed[2],
        summed[3],
        summed[4],
        summed[5],
        summed[6],
        summed[7],
        summed[8],
        summed[9],
        summed[10],
        summed[11],
    )


def solution(mesh):
    placed = (
        P("shard", "rep", None),
        P("shard", "rep", None),
        P("shard", None),
        P("shard"),
        P("shard", None),
        P("shard"),
        P("shard", None),
        P("shard", None),
        P("shard"),
        P("shard", None),
        P("shard", None),
        P("shard"),
        P("shard", None),
        P("shard", None),
        P("shard", None),
    )
    fits = mesh.shape["rep"] == 4 and mesh.shape["shard"] == 8
    return jax.shard_map(
        column_body if fits else body,
        mesh=mesh,
        in_specs=placed,
        out_specs=(
            P("shard", "rep", None),
            P("shard", "rep", None),
            P("shard"),
            P("shard", None),
            P("shard"),
            P("shard", None),
            P("shard", None),
            P("shard"),
            P("shard", None),
            P("shard", None),
            P("shard"),
            P("shard", None),
            P("shard", None),
            P("shard", None),
        ),
        check_vma=False,
    )
```
